32 devices in a mesh: tiles: 16 (over z, x, core), dp: 2 (over y).
Axes of the slice: x: 2, y: 2, z: 4, core: 2. Of those that a mesh axis runs over, the one named last changes fastest.
Arguments:
- fields: bfloat16 [2, 48, 16, 16, 256], P('dp', 'tiles'), may hold values from -6 to 6
- grad_out: bfloat16 [2, 48, 16, 16, 256], P('dp', 'tiles'), may hold values from -6 to 6
- block_count: int32 [16], P('tiles'), may hold values from 1 to 3, as said below
- ocean: int32 [48], P('tiles'), may hold values from 0 to 1, as said below
- kernel: bfloat16 [7, 7, 256], replicated, may hold values from -0.875 to 0.875
- ln_gain: float32 [256], replicated, may hold values from 0.1 to 1.9
- w_in: bfloat16 [256, 1024], replicated, may hold values from -0.375 to 0.375
- w_out: bfloat16 [1024, 256], replicated, may hold values from -0.1875 to 0.1875
- layer_scale: float32 [256], replicated, may hold values from 0.3 to 1.5
Outputs:
- state_next: bfloat16 [2, 48, 16, 16, 256], P('dp', 'tiles')
- grad_fields: bfloat16 [2, 48, 16, 16, 256], P('dp', 'tiles')
- grad_kernel: float32 [7, 7, 256], replicated
- grad_gain: float32 [256], replicated
- grad_w_in: float32 [256, 1024], replicated
- grad_w_out: float32 [1024, 256], replicated
- grad_scale: float32 [256], replicated
The draws below stay inside these ranges and needn't reach their ends.
Inputs may be any that keep to these rules, and one draw needn't show every extreme that they name: Index i of tiles owns block_count[i] consecutive cycle tiles in its first slots, in the cycle order of the first step; index i and index i + H (i < H, H half the number of entries) own equally many; some index owns 3 and some index owns one. 1 marks an ocean tile; the first and the last cycle tile that each index of tiles owns are ocean.
All inputs are finite; a program needn't handle non-finite values.
Results may differ from the reference program's by a relative error of at most 0.0066.
Values may be sent and summed in bfloat16 or wider, within the bound.
No kernel may reach another device: no remote copies, remote signals or barrier semaphores. Data moves between devices by JAX's collectives and lax.ppermute only.
A program may use at most 64 MiB of HBM per device.

```python
import math
import jax
import jax.numpy as jnp
from jax import lax

C = 256
HID = 1024
KSIZE = 7
TILE = 16
SLOTS = 3
SAMPLES = 2
SLOT_TOTAL = 48
CELLS = 24576


def cycle_counts(key):
    key = jax.random.fold_in(key, 11)
    half_cycle = SLOT_TOTAL // SLOTS // 2
    owned_counts = jax.random.randint(jax.random.fold_in(key, 1), (half_cycle,), 1, SLOTS + 1)
    shuffled = jax.random.permutation(jax.random.fold_in(key, 2), half_cycle)
    owned_counts = owned_counts.at[shuffled[0]].set(SLOTS).at[shuffled[1]].set(1)
    return jnp.concatenate([owned_counts, owned_counts]).astype(jnp.int32)


def draw_block_count(key, part):
    return cycle_counts(key)


def draw_ocean(key, part):
    owned_counts = cycle_counts(key)
    key = jax.random.fold_in(key, 12)
    flags = (jax.random.randint(key, (SLOT_TOTAL,), 0, 4) < 3).astype(jnp.int32)
    slot_ids = jnp.arange(SLOT_TOTAL, dtype=jnp.int32)
    position = slot_ids % SLOTS
    owner_count = owned_counts[slot_ids // SLOTS]
    run_end = jnp.logical_or(position == 0, position == owner_count - 1)
    return jnp.where(run_end, 1, flags).astype(jnp.int32)


def levels(key, shape, split, smallest, largest):
    level = 1.0
    for dim, parts in split:
        heights = jax.random.uniform(jax.random.fold_in(jax.random.fold_in(key, 6), dim), (parts,), jnp.float32, smallest / len(split), largest / len(split))
        level = level * jnp.repeat(jnp.exp(heights), shape[dim] // parts).reshape((-1,) + (1,) * (len(shape) - 1 - dim))
    return level


def bell_draw(key, extent, width, bound, shards=(), held_as=jnp.bfloat16):
    drawn = width * jax.random.normal(key, extent, jnp.float32)
    if shards:
        drawn = drawn * levels(key, extent, shards, -0.22, 0.18)
    return jnp.clip(drawn, -bound, bound).astype(held_as)


def setup_inputs(seed: int = 0) -> dict:
    arg_keys = jax.random.split(jax.random.key(seed), 10)
    return {
        "fields": bell_draw(arg_keys[0], (SAMPLES, SLOT_TOTAL, TILE, TILE, C), 1.0, 6.0, ((0, 2), (1, 16))),
        "grad_out": bell_draw(arg_keys[1], (SAMPLES, SLOT_TOTAL, TILE, TILE, C), 1.0, 6.0, ((0, 2), (1, 16))),
        "block_count": draw_block_count(jax.random.fold_in(arg_keys[9], 71), 0),
        "ocean": draw_ocean(jax.random.fold_in(arg_keys[9], 71), 0),
        "kernel": bell_draw(arg_keys[4], (KSIZE, KSIZE, C), (KSIZE * KSIZE) ** -0.5, 0.875),
        "ln_gain": jnp.clip(1.0 + 0.18 * jax.random.normal(arg_keys[5], (C,), jnp.float32), 0.1, 1.9),
        "w_in": bell_draw(arg_keys[6], (C, HID), C ** -0.5, 0.375),
        "w_out": bell_draw(arg_keys[7], (HID, C), HID ** -0.5, 0.1875),
        "layer_scale": jnp.clip(jnp.exp(jax.random.uniform(arg_keys[8], (C,), jnp.float32, math.log(0.3), math.log(1.5))), 0.3, 1.5),
    }


EPS = 1e-06

def gelu_tanh(inputs):
    return jax.nn.gelu(inputs, approximate=True)

def depthwise(padded, kernel_f, tile_rows, tile_cols):
    running = jnp.zeros(padded.shape[:-3] + (tile_rows, tile_cols, padded.shape[-1]), jnp.float32)
    for row_shift in range(KSIZE):
        for col_shift in range(KSIZE):
            window = padded[..., row_shift:row_shift + tile_rows, col_shift:col_shift + tile_cols, :]
            running = running + kernel_f[row_shift, col_shift] * window.astype(jnp.float32)
    return running

def kernel_terms(conv_grad, padded, tile_rows, tile_cols):
    grad_f = conv_grad.astype(jnp.float32)
    leading = tuple(range(grad_f.ndim - 1))
    stacked = []
    for row_shift in range(KSIZE):
        taps = []
        for col_shift in range(KSIZE):
            window = padded[..., row_shift:row_shift + tile_rows, col_shift:col_shift + tile_cols, :]
            taps.append(lax.optimization_barrier(jnp.sum(grad_f * window.astype(jnp.float32), axis=leading)))
        stacked.append(jnp.stack(taps))
    return jnp.stack(stacked)

def spread(conv_grad, kernel_f, tile_rows, tile_cols):
    reach = KSIZE - 1
    widths = [(0, 0)] * (conv_grad.ndim - 3) + [(reach, reach), (reach, reach), (0, 0)]
    grad_f = jnp.pad(conv_grad.astype(jnp.float32), widths)
    running = jnp.zeros(conv_grad.shape[:-3] + (tile_rows + reach, tile_cols + reach, conv_grad.shape[-1]), jnp.float32)
    for row_shift in range(KSIZE):
        for col_shift in range(KSIZE):
            window = grad_f[..., reach - row_shift:reach - row_shift + tile_rows + reach, reach - col_shift:reach - col_shift + tile_cols + reach, :]
            running = running + kernel_f[row_shift, col_shift] * window
    return running

def make_block(ln_gain, w_in, w_out, layer_scale):

    def block_step(totals, inputs):
        convolved, skip_rows, cell_mask, tangent = inputs
        row_mean = lax.optimization_barrier(jnp.mean(convolved, axis=-1, keepdims=True))
        centred = convolved - row_mean
        variance = lax.optimization_barrier(jnp.mean(centred * centred, axis=-1, keepdims=True))
        inverse = lax.rsqrt(variance + EPS)
        yhat = centred * inverse
        normed = (yhat * ln_gain).astype(jnp.bfloat16)
        preact = jnp.dot(normed, w_in, preferred_element_type=jnp.float32)
        activated = gelu_tanh(preact).astype(jnp.bfloat16)
        projected = jnp.dot(activated, w_out, preferred_element_type=jnp.float32)
        tangent_f = tangent.astype(jnp.float32)
        state = (cell_mask * (skip_rows.astype(jnp.float32) + layer_scale * projected)).astype(jnp.bfloat16)
        dproj = (cell_mask * layer_scale * tangent_f).astype(jnp.bfloat16)
        scale_part = lax.optimization_barrier(jnp.sum(cell_mask * tangent_f * projected, axis=0))
        w_out_part = lax.dot_general(activated, dproj, (((0,), (0,)), ((), ())), preferred_element_type=jnp.float32)
        dactivated = lax.dot_general(dproj, w_out, (((1,), (1,)), ((), ())), preferred_element_type=jnp.float32)
        unused, pullback = jax.vjp(gelu_tanh, preact)
        dpreact = pullback(dactivated)[0].astype(jnp.bfloat16)
        w_in_part = lax.dot_general(normed, dpreact, (((0,), (0,)), ((), ())), preferred_element_type=jnp.float32)
        dnormed = lax.dot_general(dpreact, w_in, (((1,), (1,)), ((), ())), preferred_element_type=jnp.float32)
        gain_part = lax.optimization_barrier(jnp.sum(dnormed * yhat, axis=0))
        dhat = dnormed * ln_gain
        conv_grad = inverse * (dhat - lax.optimization_barrier(jnp.mean(dhat, axis=-1, keepdims=True)) - yhat * lax.optimization_barrier(jnp.mean(dhat * yhat, axis=-1, keepdims=True)))
        totals = (totals[0] + gain_part, totals[1] + w_in_part, totals[2] + w_out_part, totals[3] + scale_part)
        return (totals, (state, conv_grad.astype(jnp.bfloat16)))
    return block_step

def pad_tiles(masked, west_slot, east_slot, partner_slot, half_kernel):
    tile_rows = masked.shape[1]
    extended = jnp.concatenate([masked[west_slot][:, :, -half_kernel:], masked, masked[east_slot][:, :, :half_kernel]], axis=2)
    north_rows = extended[partner_slot][:, tile_rows - half_kernel:][:, ::-1, ::-1]
    south_rows = jnp.zeros((masked.shape[0], half_kernel, extended.shape[2], masked.shape[3]), masked.dtype)
    return jnp.concatenate([south_rows, extended, north_rows], axis=1)

def unpad_tiles(dpadded, west_slot, east_slot, partner_slot, half_kernel):
    tile_rows = dpadded.shape[1] - 2 * half_kernel
    tile_cols = dpadded.shape[2] - 2 * half_kernel
    north_rows = dpadded[:, tile_rows + half_kernel:]
    dextended = dpadded[:, half_kernel:tile_rows + half_kernel]
    dextended = dextended.at[:, tile_rows - half_kernel:].add(north_rows[partner_slot][:, ::-1, ::-1])
    core_grad = dextended[:, :, half_kernel:tile_cols + half_kernel]
    core_grad = core_grad.at[:, :, :half_kernel].add(dextended[west_slot][:, :, tile_cols + half_kernel:])
    core_grad = core_grad.at[:, :, tile_cols - half_kernel:].add(dextended[east_slot][:, :, :half_kernel])
    return core_grad

def reference(fields, grad_out, block_count, ocean, kernel, ln_gain, w_in, w_out, layer_scale):
    samples, total_slots, tile_rows, tile_cols, channels = fields.shape
    half_kernel = KSIZE // 2
    blocks = total_slots // SLOTS
    half_blocks = blocks // 2
    cycle_order = jnp.concatenate([jnp.arange(half_blocks, dtype=jnp.int32), jnp.arange(blocks - 1, half_blocks - 1, -1, dtype=jnp.int32)]).astype(jnp.int32)
    counts_by_rank = block_count[cycle_order]
    starts_by_rank = (jnp.cumsum(counts_by_rank) - counts_by_rank).astype(jnp.int32)
    starts = jnp.zeros((blocks,), jnp.int32).at[cycle_order].set(starts_by_rank)
    slot_ids = jnp.arange(total_slots, dtype=jnp.int32)
    owner_index = slot_ids // SLOTS
    position = slot_ids % SLOTS
    cycle_tiles = jnp.sum(block_count).astype(jnp.int32)
    valid = position < block_count[owner_index]
    live = jnp.logical_and(valid, ocean > 0)
    tile_id = jnp.where(valid, starts[owner_index] + position, 0).astype(jnp.int32)
    target = jnp.where(valid, tile_id, total_slots).astype(jnp.int32)
    slot_of_tile = jnp.zeros((total_slots + 1,), jnp.int32).at[target].set(slot_ids)
    west_slot = slot_of_tile[(tile_id + cycle_tiles - 1) % cycle_tiles]
    east_slot = slot_of_tile[(tile_id + 1) % cycle_tiles]
    partner_slot = slot_of_tile[cycle_tiles - 1 - tile_id]
    slot_mask = live.astype(jnp.float32)
    kernel_f = kernel.astype(jnp.float32)
    block_step = make_block(ln_gain, w_in, w_out, layer_scale)
    block_rows = SLOTS * tile_rows * tile_cols

    def one_sample(sample_pair):
        sample_field, tangent = sample_pair
        masked = sample_field * slot_mask.astype(jnp.bfloat16)[:, None, None, None]
        padded = pad_tiles(masked, west_slot, east_slot, partner_slot, half_kernel)
        convolved = depthwise(padded, kernel_f, tile_rows, tile_cols)
        cell_mask = jnp.broadcast_to(slot_mask[:, None], (total_slots, tile_rows * tile_cols)).reshape(blocks, block_rows, 1)
        start_totals = (jnp.zeros((channels,), jnp.float32), jnp.zeros((channels, HID), jnp.float32), jnp.zeros((HID, channels), jnp.float32), jnp.zeros((channels,), jnp.float32))
        totals, outputs = lax.scan(block_step, start_totals, (convolved.reshape(blocks, block_rows, channels), masked.reshape(blocks, block_rows, channels), cell_mask, tangent.reshape(blocks, block_rows, channels)))
        state = outputs[0].reshape(sample_field.shape)
        conv_grad = outputs[1].reshape(sample_field.shape)
        kernel_part = kernel_terms(conv_grad, padded, tile_rows, tile_cols)
        dpadded = spread(conv_grad, kernel_f, tile_rows, tile_cols)
        dmasked = unpad_tiles(dpadded, west_slot, east_slot, partner_slot, half_kernel)
        grad_field = (slot_mask[:, None, None, None] * (tangent.astype(jnp.float32) + dmasked)).astype(jnp.bfloat16)
        return (state, grad_field, kernel_part, totals)
    states, grad_fields, kernel_parts, totals = lax.map(one_sample, (fields, grad_out))
    norm = CELLS ** (-0.5)
    return (states, grad_fields, lax.optimization_barrier(jnp.sum(kernel_parts, axis=0)) * norm, lax.optimization_barrier(jnp.sum(totals[0], axis=0)) * norm, lax.optimization_barrier(jnp.sum(totals[1], axis=0)) * norm, lax.optimization_barrier(jnp.sum(totals[2], axis=0)) * norm, lax.optimization_barrier(jnp.sum(totals[3], axis=0)) * norm)
```

```python
import jax
import jax.numpy as jnp
from jax import lax
from jax.sharding import Mesh, PartitionSpec as P

HID = 1024
KSIZE = 7
TILES = ("chips", "core")


EPS = 1e-06


def passed_along(block, axis, distance):
    devices = range(lax.axis_size(axis))
    route = [(i - distance, i) for i in devices if i - distance in devices]
    return lax.ppermute(block, axis, route)


def from_partner(block, axis, distance):
    count = lax.axis_size(axis)
    route = []
    for low in range(count):
        high = low | 1 << distance
        if high != low and high < count:
            route += [(low, high), (high, low)]
    return lax.ppermute(block, axis, route)


def gelu_tanh(inputs):
    return jax.nn.gelu(inputs, approximate=True)


def depthwise(padded, kernel_f, tile_rows, tile_cols):
    running = jnp.zeros(padded.shape[:-3] + (tile_rows, tile_cols, padded.shape[-1]), jnp.float32)
    for row_shift in range(KSIZE):
        for col_shift in range(KSIZE):
            window = padded[
                ..., row_shift : row_shift + tile_rows, col_shift : col_shift + tile_cols, :
            ]
            running = running + kernel_f[row_shift, col_shift] * window.astype(jnp.float32)
    return running


def kernel_terms(conv_grad, padded, tile_rows, tile_cols):
    grad_f = conv_grad.astype(jnp.float32)
    leading = tuple(range(grad_f.ndim - 1))
    stacked = []
    for row_shift in range(KSIZE):
        taps = []
        for col_shift in range(KSIZE):
            window = padded[
                ..., row_shift : row_shift + tile_rows, col_shift : col_shift + tile_cols, :
            ]
            taps.append(jnp.sum(grad_f * window.astype(jnp.float32), axis=leading))
        stacked.append(jnp.stack(taps))
    return jnp.stack(stacked)


def spread(conv_grad, kernel_f, tile_rows, tile_cols):
    reach = KSIZE - 1
    widths = [(0, 0)] * (conv_grad.ndim - 3) + [(reach, reach), (reach, reach), (0, 0)]
    grad_f = jnp.pad(conv_grad.astype(jnp.float32), widths)
    running = jnp.zeros(
        conv_grad.shape[:-3] + (tile_rows + reach, tile_cols + reach, conv_grad.shape[-1]),
        jnp.float32,
    )
    for row_shift in range(KSIZE):
        for col_shift in range(KSIZE):
            window = grad_f[
                ...,
                reach - row_shift : reach - row_shift + tile_rows + reach,
                reach - col_shift : reach - col_shift + tile_cols + reach,
                :,
            ]
            running = running + kernel_f[row_shift, col_shift] * window
    return running


def make_block(ln_gain, w_in, w_out, layer_scale):

    def block_step(totals, inputs):
        convolved, skip_rows, cell_mask, tangent = inputs
        row_mean = jnp.mean(convolved, axis=-1, keepdims=True)
        centred = convolved - row_mean
        variance = jnp.mean(centred * centred, axis=-1, keepdims=True)
        inverse = lax.rsqrt(variance + EPS)
        yhat = centred * inverse
        normed = (yhat * ln_gain).astype(jnp.bfloat16)
        preact = jnp.dot(normed, w_in, preferred_element_type=jnp.float32)
        activated = gelu_tanh(preact).astype(jnp.bfloat16)
        projected = jnp.dot(activated, w_out, preferred_element_type=jnp.float32)
        tangent_f = tangent.astype(jnp.float32)
        state = (cell_mask * (skip_rows.astype(jnp.float32) + layer_scale * projected)).astype(
            jnp.bfloat16
        )
        dproj = (cell_mask * layer_scale * tangent_f).astype(jnp.bfloat16)
        scale_part = jnp.sum(cell_mask * tangent_f * projected, axis=0)
        w_out_part = lax.dot_general(
            activated, dproj, (((0,), (0,)), ((), ())), preferred_element_type=jnp.float32
        )
        dactivated = lax.dot_general(
            dproj, w_out, (((1,), (1,)), ((), ())), preferred_element_type=jnp.float32
        )
        unused, pullback = jax.vjp(gelu_tanh, preact)
        dpreact = pullback(dactivated)[0].astype(jnp.bfloat16)
        w_in_part = lax.dot_general(
            normed, dpreact, (((0,), (0,)), ((), ())), preferred_element_type=jnp.float32
        )
        dnormed = lax.dot_general(
            dpreact, w_in, (((1,), (1,)), ((), ())), preferred_element_type=jnp.float32
        )
        gain_part = jnp.sum(dnormed * yhat, axis=0)
        dhat = dnormed * ln_gain
        conv_grad = inverse * (
            dhat
            - jnp.mean(dhat, axis=-1, keepdims=True)
            - yhat * jnp.mean(dhat * yhat, axis=-1, keepdims=True)
        )
        totals = (gain_part, w_in_part, w_out_part, scale_part)
        return (totals, (state, conv_grad.astype(jnp.bfloat16)))

    return block_step


def summed(kernel_part, gain_part, w_in_part, w_out_part, scale_part):
    channels = kernel_part.shape[-1]
    chips = lax.axis_size(TILES) // 2 * lax.axis_size("dp")
    core = lax.axis_index(TILES) % 2
    big = jnp.concatenate(
        [w_in_part.reshape(channels, -1, channels).transpose(1, 0, 2).reshape(-1, channels), w_out_part]
    )
    rows = big.shape[0] // 2
    halves = big.reshape(2, rows, channels)
    keep = lax.dynamic_index_in_dim(halves, core, 0, keepdims=False)
    give = lax.dynamic_index_in_dim(halves, 1 - core, 0, keepdims=False).astype(jnp.bfloat16)
    mine = keep + core_swap(give).astype(jnp.float32)
    small = jnp.concatenate(
        [kernel_part.reshape(-1, channels), gain_part[None], scale_part[None]]
    )
    small_rows = -(-small.shape[0] // chips) * chips
    small = jnp.pad(small, ((0, small_rows - small.shape[0]), (0, 0)))
    pieces = jnp.concatenate(
        [mine.reshape(chips, -1, channels), small.reshape(chips, -1, channels)], axis=1
    ).astype(jnp.bfloat16)
    axes = ("chips", "dp")
    got = lax.all_to_all(pieces, axes, 0, 0, tiled=True)
    total = jnp.sum(got.astype(jnp.float32), axis=0).astype(jnp.bfloat16)
    every = lax.all_to_all(jnp.broadcast_to(total, got.shape), axes, 0, 0, tiled=True)
    other = core_swap(every)
    cut = rows // chips
    low = jnp.where(core == 0, every, other)[:, :cut].reshape(rows, channels)
    high = jnp.where(core == 0, other, every)[:, :cut].reshape(rows, channels)
    every_f = every[:, cut:].astype(jnp.float32) + other[:, cut:].astype(jnp.float32)
    small_sum = every_f.reshape(small_rows, channels)
    taps = KSIZE * KSIZE
    w_in_sum = low.reshape(-1, channels, channels).transpose(1, 0, 2).reshape(channels, -1)
    return (
        small_sum[:taps].reshape(kernel_part.shape),
        small_sum[taps],
        w_in_sum.astype(jnp.float32),
        high.astype(jnp.float32),
        small_sum[taps + 1],
    )


def core_swap(block):
    return lax.ppermute(block, "core", [(0, 1), (1, 0)])


def shards(fields, grad_out, block_count, ocean, kernel, ln_gain, w_in, w_out, layer_scale):
    samples, slot_count, tile_rows, tile_cols, channels = fields.shape
    half_kernel = KSIZE // 2
    half_axis = lax.axis_size(TILES) // 2
    top_bit = lax.axis_size(TILES).bit_length() - 2
    here = lax.axis_index(TILES)
    lower_half = here < half_axis
    at_start = here % half_axis == 0
    at_end = here % half_axis == half_axis - 1
    owned = block_count[0]
    strip_width = slot_count * tile_cols
    used_cols = owned * tile_cols
    slot_ids = jnp.arange(slot_count, dtype=jnp.int32)
    slot_mask = jnp.logical_and(slot_ids < owned, ocean > 0).astype(jnp.float32)
    masked = fields * slot_mask.astype(jnp.bfloat16)[None, :, None, None, None]
    strip = jnp.transpose(masked, (0, 2, 1, 3, 4)).reshape(
        samples, tile_rows, strip_width, channels
    )
    tangent = jnp.transpose(grad_out, (0, 2, 1, 3, 4)).reshape(
        samples, tile_rows, strip_width, channels
    )
    mask_strip = jnp.broadcast_to(
        slot_mask[None, None, :, None, None], (samples, tile_rows, slot_count, tile_cols, 1)
    ).reshape(samples, tile_rows, strip_width, 1)
    left_edge = strip[:, :, :half_kernel]
    right_edge = lax.dynamic_slice_in_dim(strip, used_cols - half_kernel, half_kernel, 2)
    up_send = jnp.where(lower_half, right_edge, left_edge)
    down_send = jnp.where(lower_half, left_edge, right_edge)
    from_lower = passed_along(up_send, TILES, 1)
    from_upper = passed_along(down_send, TILES, -1)
    far_edges = from_partner(jnp.stack([down_send, up_send]), TILES, top_bit)
    from_lower = jnp.where(at_start, far_edges[0], from_lower)
    from_upper = jnp.where(at_end, far_edges[1], from_upper)
    from_west = jnp.where(lower_half, from_lower, from_upper)
    from_east = jnp.where(lower_half, from_upper, from_lower)
    blank_cols = jnp.zeros((samples, tile_rows, half_kernel, channels), jnp.bfloat16)
    extended = jnp.concatenate([from_west, strip, blank_cols], axis=2)
    extended = lax.dynamic_update_slice_in_dim(extended, from_east, used_cols + half_kernel, 2)
    mirrored = from_partner(extended[:, tile_rows - half_kernel :], TILES, top_bit)
    north_rows = jnp.roll(mirrored[:, ::-1, ::-1], used_cols - strip_width, axis=2)
    south_rows = jnp.zeros(
        (samples, half_kernel, strip_width + 2 * half_kernel, channels), jnp.bfloat16
    )
    padded = jnp.concatenate([south_rows, extended, north_rows], axis=1)
    kernel_f = kernel.astype(jnp.float32)
    convolved = depthwise(padded, kernel_f, tile_rows, strip_width)
    block_step = make_block(ln_gain, w_in, w_out, layer_scale)
    start_totals = (
        jnp.zeros((channels,), jnp.float32),
        jnp.zeros((channels, HID), jnp.float32),
        jnp.zeros((HID, channels), jnp.float32),
        jnp.zeros((channels,), jnp.float32),
    )
    totals, outputs = block_step(
        start_totals,
        (
            convolved.reshape(-1, channels),
            strip.reshape(-1, channels),
            mask_strip.reshape(-1, 1),
            tangent.reshape(-1, channels),
        ),
    )
    gain_part, w_in_part, w_out_part, scale_part = totals
    conv_grad = outputs[1].reshape(samples, tile_rows, strip_width, channels)
    kernel_part = kernel_terms(conv_grad, padded, tile_rows, strip_width)
    dpadded = spread(conv_grad, kernel_f, tile_rows, strip_width)
    north_grad = dpadded[:, tile_rows + half_kernel :]
    returned = from_partner(
        jnp.roll(north_grad[:, ::-1, ::-1], used_cols - strip_width, axis=2).astype(jnp.bfloat16),
        TILES,
        top_bit,
    ).astype(jnp.float32)
    dextended = dpadded[:, half_kernel : tile_rows + half_kernel]
    dextended = dextended.at[:, tile_rows - half_kernel :].add(returned)
    west_grad = dextended[:, :, :half_kernel]
    east_grad = lax.dynamic_slice_in_dim(dextended, used_cols + half_kernel, half_kernel, 2)
    core_grad = dextended[:, :, half_kernel : strip_width + half_kernel]
    up_grad = jnp.where(lower_half, east_grad, west_grad)
    down_grad = jnp.where(lower_half, west_grad, east_grad)
    grad_lower = passed_along(up_grad.astype(jnp.bfloat16), TILES, 1).astype(up_grad.dtype)
    grad_upper = passed_along(down_grad.astype(jnp.bfloat16), TILES, -1).astype(down_grad.dtype)
    far_grads = from_partner(
        jnp.stack([down_grad, up_grad]).astype(jnp.bfloat16), TILES, top_bit
    ).astype(jnp.float32)
    grad_lower = jnp.where(at_start, far_grads[0], grad_lower)
    grad_upper = jnp.where(at_end, far_grads[1], grad_upper)
    to_head = jnp.where(lower_half, grad_lower, grad_upper)
    to_tail = jnp.where(lower_half, grad_upper, grad_lower)
    core_grad = core_grad.at[:, :, :half_kernel].add(to_head)
    tail_cols = (
        lax.dynamic_slice_in_dim(core_grad, used_cols - half_kernel, half_kernel, 2) + to_tail
    )
    core_grad = lax.dynamic_update_slice_in_dim(core_grad, tail_cols, used_cols - half_kernel, 2)
    grad_strip = (mask_strip * (tangent.astype(jnp.float32) + core_grad)).astype(jnp.bfloat16)
    kernel_sum, gain_sum, w_in_sum, w_out_sum, scale_sum = summed(
        kernel_part, gain_part, w_in_part, w_out_part, scale_part
    )
    norm = (
        samples * lax.axis_size("dp") * slot_count * lax.axis_size(TILES) * tile_rows * tile_cols
    ) ** (-0.5)
    state_next = jnp.transpose(
        outputs[0].reshape(samples, tile_rows, slot_count, tile_cols, channels), (0, 2, 1, 3, 4)
    )
    grad_fields = jnp.transpose(
        grad_strip.reshape(samples, tile_rows, slot_count, tile_cols, channels), (0, 2, 1, 3, 4)
    )
    return (
        state_next,
        grad_fields,
        kernel_sum * norm,
        gain_sum * norm,
        w_in_sum * norm,
        w_out_sum * norm,
        scale_sum * norm,
    )


def solution(mesh):
    cores = Mesh(mesh.devices.reshape(-1, 2, mesh.devices.shape[1]), ("chips", "core", "dp"))
    placed = (
        P("dp", TILES, None, None, None),
        P("dp", TILES, None, None, None),
        P(TILES),
        P(TILES),
        P(),
        P(),
        P(),
        P(),
        P(),
    )
    return jax.shard_map(
        shards,
        mesh=cores,
        in_specs=placed,
        out_specs=(
            P("dp", TILES, None, None, None),
            P("dp", TILES, None, None, None),
            P(),
            P(),
            P(),
            P(),
            P(),
        ),
        check_vma=False,
    )
```

```python
import functools

import jax
import jax.numpy as jnp
from jax import lax
from jax.experimental import pallas as pl
from jax.experimental.pallas import tpu as pltpu
from jax.sharding import Mesh, PartitionSpec as P

KSIZE = 7
HALF = KSIZE // 2
TILE = 16
EPS = 1e-06
TILES = ("chips", "core")
F32 = jnp.float32
BF16 = jnp.bfloat16
LANES = 128
LEFT = 8
GELU_C = 0.7978845608028654
GELU_A = 0.044715


def dot(lhs, rhs, lhs_dim, rhs_dim):
    return lax.dot_general(
        lhs, rhs, (((lhs_dim,), (rhs_dim,)), ((), ())), preferred_element_type=F32
    )


def cycle_rank():
    count = lax.axis_size(TILES)
    here = lax.axis_index("chips") * lax.axis_size("core") + lax.axis_index("core")
    return jnp.where(here < count // 2, here, count - 1 + count // 2 - here)


def is_even():
    return lax.rem(cycle_rank(), 2) == 0


def slot_flag(count_ref, ocean_ref, slot):
    live = jnp.logical_and(slot < count_ref[0], ocean_ref[slot] > 0)
    return jnp.where(live, 1.0, 0.0).astype(F32)


class Shape:
    def __init__(self, slots, channels):
        self.slots = slots
        self.channels = channels
        self.parts = channels // LANES
        self.columns = slots * TILE
        self.pitch = self.columns + 2 * LEFT
        self.cells = slots * TILE * TILE
        self.padded_rows = TILE + 2 * HALF
        self.edge_rows = HALF * TILE
        self.fold_rows = HALF * self.columns

    def lanes(self, part):
        return slice(part * LANES, (part + 1) * LANES)


def edge_planes(shape, source, start, stride, out):
    for part in range(shape.parts):
        for col in range(HALF):
            plane = source[part, pl.ds(start + col, TILE, stride=stride), :]
            out[pl.ds(col * TILE, TILE), shape.lanes(part)] = plane.astype(BF16)


def flip_matrix(shape, used):
    to = lax.broadcasted_iota(jnp.int32, (shape.columns, shape.columns), 0)
    frm = lax.broadcasted_iota(jnp.int32, (shape.columns, shape.columns), 1)
    return jnp.where(to + frm == used - 1, 1.0, 0.0).astype(BF16)


def by_parity(left_ref, right_ref, first_ref, second_ref):
    even = is_even()
    left = left_ref[...].astype(F32)
    right = right_ref[...].astype(F32)
    first_ref[...] = jnp.where(even, right, left).astype(BF16)
    second_ref[...] = jnp.where(even, left, right).astype(BF16)


def prep_kernel(shape, count_ref, ocean_ref, fields, left, right, first, second, fold, work):
    owned = count_ref[0]
    per_slot = TILE * TILE
    for slot in range(shape.slots):
        flag = slot_flag(count_ref, ocean_ref, slot)
        cells = fields[pl.ds(slot * per_slot, per_slot), :].astype(F32) * flag
        for part in range(shape.parts):
            work[part, pl.ds(slot * per_slot, per_slot), :] = cells[:, shape.lanes(part)]
    edge_planes(shape, work, 0, TILE, left)
    edge_planes(shape, work, (owned - 1) * per_slot + TILE - HALF, TILE, right)
    by_parity(left, right, first, second)
    flip = flip_matrix(shape, owned * TILE)
    for k in range(HALF):
        row = jnp.concatenate(
            [
                fields[pl.ds(slot * per_slot + (TILE - 1 - k) * TILE, TILE), :].astype(F32)
                * slot_flag(count_ref, ocean_ref, slot)
                for slot in range(shape.slots)
            ]
        ).astype(BF16)
        fold[pl.ds(k * shape.columns, shape.columns), :] = dot(flip, row, 1, 0).astype(BF16)


def build_padded(shape, count_ref, ocean_ref, fields, halo, padded, edges):
    first, second, fold, corner_west, corner_east = halo
    used = count_ref[0] * TILE
    even = is_even()
    blank = jnp.zeros((LEFT, LANES), F32)
    per_slot = TILE * TILE
    flags = [slot_flag(count_ref, ocean_ref, slot) for slot in range(shape.slots)]
    for part in range(shape.parts):
        padded[part, pl.ds(0, HALF * shape.pitch), :] = jnp.zeros((HALF * shape.pitch, LANES), F32)
        for row in range(TILE + HALF):
            base = (row + HALF) * shape.pitch
            padded[part, pl.ds(base, LEFT), :] = blank
            padded[part, pl.ds(base + LEFT + shape.columns, LEFT), :] = blank
            for slot in range(shape.slots):
                if row < TILE:
                    cells = fields[pl.ds(slot * per_slot + row * TILE, TILE), shape.lanes(part)]
                    cells = cells.astype(F32) * flags[slot]
                else:
                    start = (row - TILE) * shape.columns + slot * TILE
                    cells = fold[pl.ds(start, TILE), shape.lanes(part)].astype(F32)
                padded[part, pl.ds(base + LEFT + slot * TILE, TILE), :] = cells
        band = HALF * shape.pitch
        for col in range(HALF):
            rows = pl.ds(col * TILE, TILE)
            one = first[rows, shape.lanes(part)].astype(F32)
            two = second[rows, shape.lanes(part)].astype(F32)
            west = jnp.where(even, two, one)
            east = jnp.where(even, one, two)
            start = band + LEFT - HALF + col
            padded[part, pl.ds(start, TILE, stride=shape.pitch), :] = west
            padded[part, pl.ds(band + LEFT + used + col, TILE, stride=shape.pitch), :] = east
        edges[0, part] = corner_west[:, shape.lanes(part)].astype(F32)
        edges[1, part] = corner_east[:, shape.lanes(part)].astype(F32)
        for k in range(HALF):
            base = (TILE + HALF + k) * shape.pitch + LEFT
            for col in range(HALF):
                cell = pl.ds(col * TILE + TILE - 1 - k, 1)
                padded[part, pl.ds(base - 1 - col, 1), :] = edges[0, part, cell, :]
                padded[part, pl.ds(base + used + HALF - 1 - col, 1), :] = edges[1, part, cell, :]


def spread_taps(shape, kernel, taps):
    for part in range(shape.parts):
        for tap in range(KSIZE * KSIZE):
            row = kernel[pl.ds(tap, 1), shape.lanes(part)]
            taps[part, tap] = jnp.broadcast_to(row, (8, LANES))


def convolve(shape, padded, taps, convolved):
    run = shape.columns // 8
    pair = 2
    origin = LEFT - HALF

    def two_rows(step, carry):
        row = step * pair
        for part in range(shape.parts):
            sums = [[None] * run for _ in range(pair)]
            for above in range(KSIZE + pair - 1):
                base = (row + above) * shape.pitch + origin
                loaded = [
                    padded[part, pl.ds(base + at, 8, stride=run), :]
                    for at in range(run + KSIZE - 1)
                ]
                for which in range(pair):
                    tap_row = above - which
                    if not 0 <= tap_row < KSIZE:
                        continue
                    for shift in range(KSIZE):
                        weight = taps[part, tap_row * KSIZE + shift]
                        for at in range(run):
                            term = weight * loaded[at + shift]
                            old = sums[which][at]
                            sums[which][at] = term if old is None else old + term
            for which in range(pair):
                for at in range(run):
                    start = (row + which) * shape.columns + at
                    convolved[part, pl.ds(start, 8, stride=run), :] = sums[which][at]
        return carry

    lax.fori_loop(0, TILE // pair, two_rows, 0)


def normalise(shape, convolved, gain, normed, yhat, inverse):
    def one_row(row, carry):
        for slot in range(shape.slots):
            start = pl.multiple_of(row * shape.columns + slot * TILE, TILE)
            out = pl.ds(pl.multiple_of(slot * TILE * TILE + row * TILE, TILE), TILE)
            parts = [convolved[part, pl.ds(start, TILE), :] for part in range(shape.parts)]
            mean = jnp.sum(sum(parts), axis=-1, keepdims=True) * (1.0 / shape.channels)
            parts = [value - mean for value in parts]
            spread_of = jnp.sum(
                sum(value * value for value in parts), axis=-1, keepdims=True
            ) * (1.0 / shape.channels)
            scale = lax.rsqrt(spread_of + EPS)
            inverse[out, :] = jnp.broadcast_to(scale, (TILE, LANES))
            for part in range(shape.parts):
                value = parts[part] * scale
                yhat[out, shape.lanes(part)] = value
                normed[out, shape.lanes(part)] = (value * gain[:, shape.lanes(part)]).astype(BF16)
        return carry

    lax.fori_loop(0, TILE, one_row, 0)


def forward_kernel(
    shape, count_ref, ocean_ref, fields, first, second, fold, corner_west, corner_east,
    tangent, kernel, gain, w_in, w_out, layer_scale,
    keep, give, activated, dpreact, yhat, inverse,
    padded, edges, taps, convolved, normed, dproj,
):
    halo = (first, second, fold, corner_west, corner_east)
    build_padded(shape, count_ref, ocean_ref, fields, halo, padded, edges)
    spread_taps(shape, kernel, taps)
    convolve(shape, padded, taps, convolved)
    normalise(shape, convolved, gain, normed, yhat, inverse)
    per_slot = TILE * TILE
    for slot in range(shape.slots):
        rows = pl.ds(slot * per_slot, per_slot)
        flag = slot_flag(count_ref, ocean_ref, slot)
        scaled = tangent[rows, :].astype(F32) * (layer_scale[...] * flag)
        dproj[rows, :] = scaled.astype(BF16)
    hidden = w_in.shape[1]
    block = shape.channels
    chunk = 128

    for h in range(hidden // block):
        cols = slice(h * block, (h + 1) * block)

        def one_chunk(step, carry, cols=cols):
            rows = pl.ds(pl.multiple_of(step * chunk, chunk), chunk)
            pre = dot(normed[rows, :], w_in[:, cols], 1, 0)
            dact = dot(dproj[rows, :], w_out[cols, :], 1, 1)
            square = pre * pre
            inner = pre * (GELU_C + (GELU_C * GELU_A) * square)
            gate = 0.5 + 0.5 * jnp.tanh(inner)
            activated[rows, cols] = (pre * gate).astype(BF16)
            slope = pre * (2.0 * GELU_C + (6.0 * GELU_C * GELU_A) * square)
            dpreact[rows, cols] = (dact * (gate + slope * (gate - gate * gate))).astype(BF16)
            return carry

        lax.fori_loop(0, shape.cells // chunk, one_chunk, 0)

    keeps_in = lax.axis_index("core") == 0
    for h in range(hidden // block):
        cols = slice(h * block, (h + 1) * block)
        rows = slice(h * block, (h + 1) * block)
        of_in = dot(normed[...], dpreact[:, cols], 0, 0)
        of_out = dot(dproj[...], activated[:, cols], 0, 0)
        keep[rows, :] = jnp.where(keeps_in, of_in, of_out)
        give[rows, :] = jnp.where(keeps_in, of_out, of_in).astype(BF16)


def fold_sum(value):
    return jnp.sum(value.reshape(-1, 8, value.shape[-1]), axis=0)


def place_grad(shape, conv_grad, spaced):
    blank = jnp.zeros((LEFT, LANES), F32)
    for part in range(shape.parts):
        for row in range(TILE):
            base = row * shape.pitch
            spaced[part, pl.ds(base, LEFT), :] = blank
            spaced[part, pl.ds(base + LEFT + shape.columns, LEFT), :] = blank
            for slot in range(shape.slots):
                cells = conv_grad[pl.ds(slot * TILE * TILE + row * TILE, TILE), shape.lanes(part)]
                spaced[part, pl.ds(base + LEFT + slot * TILE, TILE), :] = cells.astype(F32)


def middle_kernel(
    shape, count_ref, ocean_ref, fields, first, second, fold, corner_west, corner_east,
    tangent, gain, w_in, w_out, layer_scale, activated, dpreact, yhat, inverse,
    state, conv_grad, small,
    padded, edges, spaced, totals,
):
    halo = (first, second, fold, corner_west, corner_east)
    build_padded(shape, count_ref, ocean_ref, fields, halo, padded, edges)
    taps = KSIZE * KSIZE
    chunk = 128
    per_chunk = TILE * TILE // chunk
    small[...] = jnp.zeros_like(small)
    gain_sum = jnp.zeros((8, shape.channels), F32)
    scale_sum = jnp.zeros((8, shape.channels), F32)
    for step in range(shape.cells // chunk):
        rows = pl.ds(step * chunk, chunk)
        flag = slot_flag(count_ref, ocean_ref, step // per_chunk)
        projected = dot(activated[rows, :], w_out[...], 1, 0)
        state[rows, :] = (
            flag * (fields[rows, :].astype(F32) + layer_scale[...] * projected)
        ).astype(BF16)
        scale_sum += fold_sum(flag * tangent[rows, :].astype(F32) * projected)
        dnormed = dot(dpreact[rows, :], w_in[...], 1, 1)
        unit = yhat[rows, :]
        gain_sum += fold_sum(dnormed * unit)
        dhat = dnormed * gain[...]
        mean = jnp.sum(dhat, axis=-1, keepdims=True) * (1.0 / shape.channels)
        along = jnp.sum(dhat * unit, axis=-1, keepdims=True) * (1.0 / shape.channels)
        scale = jnp.concatenate([inverse[rows, :]] * shape.parts, axis=1)
        conv_grad[rows, :] = (scale * (dhat - mean - unit * along)).astype(BF16)
    small[pl.ds(taps, 1), :] = jnp.sum(gain_sum, axis=0, keepdims=True)
    small[pl.ds(taps + 1, 1), :] = jnp.sum(scale_sum, axis=0, keepdims=True)
    place_grad(shape, conv_grad, spaced)
    run = shape.columns // 8
    origin = LEFT - HALF
    for part in range(shape.parts):
        for above in range(KSIZE):

            def one_row(row, sums, part=part, above=above):
                base = (row + above) * shape.pitch + origin
                loaded = [
                    padded[part, pl.ds(base + at, 8, stride=run), :]
                    for at in range(run + KSIZE - 1)
                ]
                grads = [
                    spaced[part, pl.ds(row * shape.pitch + LEFT + at, 8, stride=run), :]
                    for at in range(run)
                ]
                sums = list(sums)
                for shift in range(KSIZE):
                    for at in range(run):
                        sums[shift] = sums[shift] + grads[at] * loaded[at + shift]
                return tuple(sums)

            sums = lax.fori_loop(
                0, TILE, one_row, tuple(jnp.zeros((8, LANES), F32) for _ in range(KSIZE))
            )
            for shift in range(KSIZE):
                small[pl.ds(above * KSIZE + shift, 1), shape.lanes(part)] = jnp.sum(
                    sums[shift], axis=0, keepdims=True
                )


def back_kernel(
    shape, count_ref, conv_grad, kernel,
    core_grad, west, east, first, second, fold, corner_west, corner_east,
    spaced, taps,
):
    used = count_ref[0] * TILE
    place_grad(shape, conv_grad, spaced)
    spread_taps(shape, kernel, taps)
    run = -(-(shape.columns + 2 * HALF) // 8)

    def one_row(row, tap_rows):
        for part in range(shape.parts):
            sums = [None] * run
            for above in tap_rows:
                base = (row - above) * shape.pitch + LEFT
                loaded = [
                    spaced[part, pl.ds(base + at - KSIZE + 1, 8, stride=run), :]
                    for at in range(run + KSIZE - 1)
                ]
                for shift in range(KSIZE):
                    weight = taps[part, above * KSIZE + shift]
                    for at in range(run):
                        term = weight * loaded[at - shift + KSIZE - 1]
                        sums[at] = term if sums[at] is None else sums[at] + term
            start = (row - HALF) * shape.pitch + LEFT - HALF
            for at in range(run):
                core_grad[part, pl.ds(start + at, 8, stride=run), :] = sums[at]

    last = TILE + 2 * HALF - 1
    inner = (KSIZE - 1, TILE - 1)
    for row in range(HALF, last + 1):
        if not inner[0] <= row <= inner[1]:
            low = max(0, row - TILE + 1)
            one_row(row, range(low, min(KSIZE - 1, row) + 1))

    def inner_row(step, carry):
        one_row(step, range(KSIZE))
        return carry

    lax.fori_loop(inner[0], inner[1] + 1, inner_row, 0)
    edge_planes(shape, core_grad, LEFT - HALF, shape.pitch, west)
    edge_planes(shape, core_grad, LEFT + used, shape.pitch, east)
    by_parity(west, east, first, second)
    skip = HALF * shape.pitch
    edge_planes(shape, core_grad, skip + LEFT - HALF, shape.pitch, corner_west)
    edge_planes(shape, core_grad, skip + LEFT + used, shape.pitch, corner_east)
    flip = flip_matrix(shape, used)
    for k in range(HALF):
        rows = pl.ds((TILE + k) * shape.pitch + LEFT, shape.columns)
        row = jnp.concatenate(
            [core_grad[part, rows, :] for part in range(shape.parts)], axis=1
        ).astype(BF16)
        fold[pl.ds(k * shape.columns, shape.columns), :] = dot(flip, row, 1, 0).astype(BF16)


def final_kernel(
    shape, count_ref, ocean_ref, tangent, core_grad, first, second, fold, corner_west, corner_east,
    grad_fields, work, edges,
):
    used = count_ref[0] * TILE
    even = is_even()
    for part in range(shape.parts):
        work[part] = core_grad[part, pl.ds(0, TILE * shape.pitch), :]
        for k in range(HALF):
            rows = pl.ds((TILE - 1 - k) * shape.pitch + LEFT, shape.columns)
            returned = fold[pl.ds(k * shape.columns, shape.columns), shape.lanes(part)]
            work[part, rows, :] += returned.astype(F32)
        for col in range(HALF):
            planes = pl.ds(col * TILE, TILE)
            one = first[planes, shape.lanes(part)].astype(F32)
            two = second[planes, shape.lanes(part)].astype(F32)
            to_tail = jnp.where(even, one, two)
            to_head = jnp.where(even, two, one)
            head = pl.ds(LEFT + col, TILE, stride=shape.pitch)
            work[part, head, :] = work[part, head, :] + to_head
            tail = pl.ds(LEFT + used - HALF + col, TILE, stride=shape.pitch)
            work[part, tail, :] = work[part, tail, :] + to_tail
        edges[0, part] = corner_west[:, shape.lanes(part)].astype(F32)
        edges[1, part] = corner_east[:, shape.lanes(part)].astype(F32)
        for k in range(HALF):
            base = (TILE - 1 - k) * shape.pitch + LEFT
            for col in range(HALF):
                cell = pl.ds(col * TILE + TILE - HALF + k, 1)
                head = pl.ds(base + HALF - 1 - col, 1)
                work[part, head, :] = work[part, head, :] + edges[0, part, cell, :]
                tail = pl.ds(base + used - 1 - col, 1)
                work[part, tail, :] = work[part, tail, :] + edges[1, part, cell, :]
        for slot in range(shape.slots):
            flag = slot_flag(count_ref, ocean_ref, slot)
            for row in range(TILE):
                rows = pl.ds(slot * TILE * TILE + row * TILE, TILE)
                cells = work[part, pl.ds(row * shape.pitch + LEFT + slot * TILE, TILE), :]
                total = tangent[rows, shape.lanes(part)].astype(F32) + cells
                grad_fields[rows, shape.lanes(part)] = (flag * total).astype(BF16)


def unpack_kernel(norm, rows, own, other, w_in, w_out):
    is_first = lax.axis_index("core") == 0
    channels = own.shape[-1]
    per_block = channels // rows
    for h in range(w_out.shape[0] // channels):
        mine = own[pl.ds(h * per_block, per_block), pl.ds(0, rows), :].astype(F32) * norm
        theirs = other[pl.ds(h * per_block, per_block), pl.ds(0, rows), :].astype(F32) * norm
        mine = mine.reshape(channels, channels)
        theirs = theirs.reshape(channels, channels)
        w_in[:, h * channels : (h + 1) * channels] = jnp.where(is_first, mine, theirs)
        w_out[h * channels : (h + 1) * channels, :] = jnp.where(is_first, theirs, mine).T


def pairs_of(kind):
    count = lax.axis_size(TILES)
    half = count // 2
    place = [rank if rank < half else count - 1 + half - rank for rank in range(count)]
    partner = {
        "first": lambda rank: rank ^ 1,
        "second": lambda rank: ((rank + 1) ^ 1) - 1,
        "fold": lambda rank: count - 1 - rank,
        "west": lambda rank: count - rank,
        "east": lambda rank: count - 2 - rank,
    }[kind]
    return [(place[rank], place[partner(rank) % count]) for rank in range(count)]


def exchange(first, second, fold, corner_west, corner_east):
    def swap(block, kind):
        return lax.ppermute(block, TILES, pairs_of(kind))

    fold = swap(fold, "fold")
    first = swap(first, "first")
    second = swap(second, "second")
    corner_west = swap(corner_west, "west")
    corner_east = swap(corner_east, "east")
    return first, second, fold, corner_west, corner_east


def core_swap(block):
    return lax.ppermute(block, "core", [(0, 1), (1, 0)])


def summed(keep, give, small):
    channels = keep.shape[-1]
    chips = lax.axis_size("chips") * lax.axis_size("dp")
    rows = keep.shape[0] // chips
    mine = keep + core_swap(give).astype(F32)
    share = -(-small.shape[0] // chips)
    small = jnp.pad(small, ((0, share * chips - small.shape[0]), (0, 0))).reshape(chips, share, channels)
    high = lax.reduce_precision(small, 8, 7)
    low = (small - high).astype(BF16)
    high = high.astype(BF16)
    pieces = jnp.concatenate([mine.reshape(chips, rows, channels).astype(BF16), high, low], axis=1)
    axes = ("chips", "dp")
    got = lax.all_to_all(pieces, axes, 0, 0, tiled=True)
    total = jnp.sum(got.astype(F32), axis=0)
    exact = total[rows : rows + share] + total[rows + share :]
    high = lax.reduce_precision(exact, 8, 7)
    low = (exact - high).astype(BF16)
    high = high.astype(BF16)
    total = jnp.concatenate([total[:rows].astype(BF16), high, low])
    every = lax.all_to_all(jnp.broadcast_to(total, got.shape), axes, 0, 0, tiled=True)
    other = core_swap(every)
    ends = every[:, rows:].astype(F32) + other[:, rows:].astype(F32)
    small = (ends[:, :share] + ends[:, share:]).reshape(chips * share, channels)
    return every, other, small, rows


def call(kernel, outs, scratch, *args, scalars=2, limit=40):
    smem = pl.BlockSpec(memory_space=pltpu.SMEM)
    vmem = pl.BlockSpec(memory_space=pltpu.VMEM)
    return pl.pallas_call(
        kernel,
        out_shape=[jax.ShapeDtypeStruct(*out) for out in outs],
        in_specs=[smem] * scalars + [vmem] * (len(args) - scalars),
        out_specs=[vmem] * len(outs),
        scratch_shapes=[pltpu.VMEM(*one) for one in scratch],
        compiler_params=pltpu.CompilerParams(vmem_limit_bytes=limit * 1024 * 1024),
    )(*args)


def shards(fields, grad_out, block_count, ocean, kernel, ln_gain, w_in, w_out, layer_scale):
    samples, slots, tile_rows, tile_cols, channels = fields.shape
    hidden = w_in.shape[1]
    shape = Shape(slots, channels)
    cells = shape.cells
    grid = fields.shape
    fields = fields.reshape(cells, channels)
    tangent = grad_out.reshape(cells, channels)
    taps_in = kernel.reshape(KSIZE * KSIZE, channels).astype(F32)
    gain = ln_gain.reshape(1, channels)
    scale = layer_scale.reshape(1, channels)
    edge = ((shape.edge_rows, channels), BF16)
    fold = ((shape.fold_rows, channels), BF16)
    whole = ((cells, channels), BF16)
    parts = shape.parts
    padded = ((parts, shape.padded_rows * shape.pitch, LANES), F32)
    edges = ((2, parts, shape.edge_rows, LANES), F32)
    taps = ((parts, KSIZE * KSIZE, 8, LANES), F32)
    spaced = ((parts, TILE * shape.pitch, LANES), F32)

    left, right, first, second, up = call(
        functools.partial(prep_kernel, shape),
        [edge, edge, edge, edge, fold],
        [((parts, cells, LANES), F32)],
        block_count, ocean, fields,
    )
    halo = exchange(first, second, up, left, right)
    keep, give, activated, dpreact, yhat, inverse = call(
        functools.partial(forward_kernel, shape),
        [
            ((hidden, channels), F32),
            ((hidden, channels), BF16),
            ((cells, hidden), BF16),
            ((cells, hidden), BF16),
            ((cells, channels), F32),
            ((cells, LANES), F32),
        ],
        [padded, edges, taps, ((parts, cells, LANES), F32), whole, whole],
        block_count, ocean, fields, *halo, tangent, taps_in, gain, w_in, w_out, scale,
    )
    small_rows = -(-(KSIZE * KSIZE + 2) // 8) * 8
    state, conv_grad, small = call(
        functools.partial(middle_kernel, shape),
        [whole, whole, ((small_rows, channels), F32)],
        [padded, edges, spaced, ((8, channels), F32)],
        block_count, ocean, fields, *halo, tangent, gain, w_in, w_out, scale,
        activated, dpreact, yhat, inverse,
    )
    every, other, small_sum, rows = summed(keep, give, small)
    core_grad, _, _, first, second, up, corner_west, corner_east = call(
        functools.partial(back_kernel, shape),
        [((parts, (TILE + HALF) * shape.pitch, LANES), F32), edge, edge, edge, edge, fold, edge, edge],
        [spaced, taps],
        block_count, conv_grad, taps_in, scalars=1,
    )
    back = exchange(first, second, up, corner_west, corner_east)
    (grad_fields,) = call(
        functools.partial(final_kernel, shape),
        [whole],
        [spaced, edges],
        block_count, ocean, tangent, core_grad, *back,
    )
    count = samples * lax.axis_size("dp") * slots * lax.axis_size(TILES) * tile_rows * tile_cols
    norm = count ** (-0.5)
    w_in_sum, w_out_sum = call(
        functools.partial(unpack_kernel, norm, rows),
        [((channels, hidden), F32), ((hidden, channels), F32)],
        [],
        every, other, scalars=0,
    )
    small_sum = small_sum * norm
    count = KSIZE * KSIZE
    return (
        state.reshape(grid),
        grad_fields.reshape(grid),
        small_sum[:count].reshape(kernel.shape),
        small_sum[count],
        w_in_sum,
        w_out_sum,
        small_sum[count + 1],
    )


def solution(mesh):
    cores = Mesh(mesh.devices.reshape(-1, 2, mesh.devices.shape[1]), ("chips", "core", "dp"))
    banded = P("dp", TILES, None, None, None)
    placed = (banded, banded, P(TILES), P(TILES), P(), P(), P(), P(), P())
    return jax.shard_map(
        shards,
        mesh=cores,
        in_specs=placed,
        out_specs=(banded, banded, P(), P(), P(), P(), P()),
        check_vma=False,
    )
```

```python
import functools

import jax
import jax.numpy as jnp
from jax import lax
from jax.experimental import pallas as pl
from jax.experimental.pallas import tpu as pltpu
from jax.sharding import Mesh, PartitionSpec as P

KSIZE = 7
HALF = KSIZE // 2
TILE = 16
EPS = 1e-06
TILES = ("chips", "core")
F32 = jnp.float32
BF16 = jnp.bfloat16
LANES = 128
LEFT = 8
GELU_C = 0.7978845608028654
GELU_A = 0.044715


def dot(lhs, rhs, lhs_dim, rhs_dim):
    return lax.dot_general(
        lhs, rhs, (((lhs_dim,), (rhs_dim,)), ((), ())), preferred_element_type=F32
    )


def cycle_rank():
    count = lax.axis_size(TILES)
    here = lax.axis_index("chips") * lax.axis_size("core") + lax.axis_index("core")
    return jnp.where(here < count // 2, here, count - 1 + count // 2 - here)


def is_even():
    return lax.rem(cycle_rank(), 2) == 0


class Fetch:
    def __init__(self, sems, *pairs):
        self.copies = [
            pltpu.make_async_copy(source, target, sems.at[at]) for at, (source, target) in enumerate(pairs)
        ]
        for copy in self.copies:
            copy.start()

    def wait(self, *which):
        for at in which:
            self.copies[at].wait()


def slot_flag(count_ref, ocean_ref, slot):
    live = jnp.logical_and(slot < count_ref[0], ocean_ref[slot] > 0)
    return jnp.where(live, 1.0, 0.0).astype(F32)


class Shape:
    def __init__(self, slots, channels, hidden):
        self.slots = slots
        self.channels = channels
        self.hidden = hidden
        self.parts = channels // LANES
        self.columns = slots * TILE
        self.pitch = self.columns + 2 * LEFT
        self.cells = slots * TILE * TILE
        self.edge_rows = HALF * TILE
        self.early = 12

    def lanes(self, part):
        return slice(part * LANES, (part + 1) * LANES)


def edge_planes(shape, source, start, stride):
    return [
        jnp.concatenate(
            [source[part, pl.ds(start + col, TILE, stride=stride), :] for part in range(shape.parts)], axis=1
        )
        for col in range(HALF)
    ]


def send_edges(shape, left, right, first, second):
    even = is_even()
    for col in range(HALF):
        rows = pl.ds(col * TILE, TILE)
        first[rows, :] = jnp.where(even, right[col], left[col]).astype(BF16)
        second[rows, :] = jnp.where(even, left[col], right[col]).astype(BF16)


def flip_matrix(shape, used):
    to = lax.broadcasted_iota(jnp.int32, (shape.pitch, shape.pitch), 0)
    frm = lax.broadcasted_iota(jnp.int32, (shape.pitch, shape.pitch), 1)
    return jnp.where(to + frm == used + 2 * LEFT - 1, 1.0, 0.0).astype(BF16)


def prep_kernel(shape, count_hbm, ocean_hbm, fields_hbm, first, second, count, ocean, fields, work, sems):
    fetch = Fetch(sems, (fields_hbm, fields), (count_hbm, count), (ocean_hbm, ocean))
    fetch.wait(0, 1, 2)
    owned = count[0]
    per_slot = TILE * TILE
    for slot in range(shape.slots):
        flag = slot_flag(count, ocean, slot)
        cells = fields[pl.ds(slot * per_slot, per_slot), :].astype(F32) * flag
        for part in range(shape.parts):
            work[part, pl.ds(slot * per_slot, per_slot), :] = cells[:, shape.lanes(part)]
    left = edge_planes(shape, work, 0, TILE)
    right = edge_planes(shape, work, (owned - 1) * per_slot + TILE - HALF, TILE)
    send_edges(shape, left, right, first, second)


def cotangent_kernel(
    shape, count_hbm, ocean_hbm, tangent_hbm, scale_hbm, w_out_hbm,
    dproj, dproj_t, dact,
    count, ocean, tangent, scale, w_out, sems,
):
    fetch = Fetch(
        sems, (tangent_hbm, tangent), (count_hbm, count), (ocean_hbm, ocean), (scale_hbm, scale), (w_out_hbm, w_out)
    )
    fetch.wait(0, 1, 2, 3)
    per_slot = TILE * TILE
    for slot in range(shape.slots):
        rows = pl.ds(slot * per_slot, per_slot)
        flag = slot_flag(count, ocean, slot)
        scaled = (tangent[rows, :].astype(F32) * (scale[...] * flag)).astype(BF16)
        dproj[rows, :] = scaled
        dproj_t[:, slot * per_slot : (slot + 1) * per_slot] = scaled.T
    fetch.wait(4)
    for slot in range(shape.slots):
        rows = pl.ds(slot * per_slot, per_slot)
        for h in range(shape.hidden // shape.channels):
            cols = slice(h * shape.channels, (h + 1) * shape.channels)
            dact[rows, cols] = dot(dproj[rows, :], w_out[cols, :], 1, 1)


def band_kernel(shape, count_hbm, ocean_hbm, fields_hbm, first, second, band, fold, count, ocean, fields, sems):
    fetch = Fetch(sems, (fields_hbm, fields), (count_hbm, count), (ocean_hbm, ocean))
    even = is_even()
    blank = jnp.zeros((LEFT, LANES), F32)
    per_slot = TILE * TILE
    for part in range(shape.parts):
        band[part, pl.ds(0, HALF * shape.pitch), :] = jnp.zeros((HALF * shape.pitch, LANES), F32)
        for row in range(TILE):
            base = (row + HALF) * shape.pitch
            band[part, pl.ds(base, LEFT), :] = blank
            band[part, pl.ds(base + LEFT + shape.columns, LEFT), :] = blank
    fetch.wait(0, 1, 2)
    used = count[0] * TILE
    flags = [slot_flag(count, ocean, slot) for slot in range(shape.slots)]
    top = HALF * shape.pitch
    for part in range(shape.parts):
        for row in range(TILE):
            base = (row + HALF) * shape.pitch
            for slot in range(shape.slots):
                cells = fields[pl.ds(slot * per_slot + row * TILE, TILE), shape.lanes(part)]
                band[part, pl.ds(base + LEFT + slot * TILE, TILE), :] = cells.astype(F32) * flags[slot]
        for col in range(HALF):
            rows = pl.ds(col * TILE, TILE)
            one = first[rows, shape.lanes(part)].astype(F32)
            two = second[rows, shape.lanes(part)].astype(F32)
            west = jnp.where(even, two, one)
            east = jnp.where(even, one, two)
            band[part, pl.ds(top + LEFT - HALF + col, TILE, stride=shape.pitch), :] = west
            band[part, pl.ds(top + LEFT + used + col, TILE, stride=shape.pitch), :] = east
    turn_rows(shape, used, band, (HALF + TILE - 1, HALF + TILE - 2, HALF + TILE - 3), fold)


def turn_rows(shape, used, source, rows, fold):
    flip = flip_matrix(shape, used)
    for k, row in enumerate(rows):
        at = pl.ds(row * shape.pitch, shape.pitch)
        cells = jnp.concatenate([source[part, at, :] for part in range(shape.parts)], axis=1)
        turned = dot(flip, cells.astype(BF16), 1, 0)
        fold[pl.ds(k * shape.pitch, shape.pitch), :] = turned.astype(BF16)


def put_fold(shape, fold, padded, first_row):
    for part in range(shape.parts):
        rows = pl.ds(first_row * shape.pitch, HALF * shape.pitch)
        padded[part, rows, :] = fold[:, shape.lanes(part)].astype(F32)


def spread_taps(shape, kernel, taps):
    for part in range(shape.parts):
        for tap in range(KSIZE * KSIZE):
            row = kernel[pl.ds(tap, 1), shape.lanes(part)].astype(F32)
            taps[part, tap] = jnp.broadcast_to(row, (8, LANES))


def convolve(shape, rows, padded, taps, convolved):
    run = shape.columns // 8
    pair = 2
    origin = LEFT - HALF

    def two_rows(step, carry):
        row = step * pair
        for part in range(shape.parts):
            sums = [[None] * run for _ in range(pair)]
            for above in range(KSIZE + pair - 1):
                base = (row + above) * shape.pitch + origin
                loaded = [
                    padded[part, pl.ds(base + at, 8, stride=run), :]
                    for at in range(run + KSIZE - 1)
                ]
                for which in range(pair):
                    tap_row = above - which
                    if not 0 <= tap_row < KSIZE:
                        continue
                    for shift in range(KSIZE):
                        weight = taps[part, tap_row * KSIZE + shift]
                        for at in range(run):
                            term = weight * loaded[at + shift]
                            old = sums[which][at]
                            sums[which][at] = term if old is None else old + term
            for which in range(pair):
                for at in range(run):
                    start = (row + which) * shape.columns + at
                    convolved[part, pl.ds(start, 8, stride=run), :] = sums[which][at]
        return carry

    lax.fori_loop(0, rows // pair, two_rows, 0)


def normalise(shape, rows, first_row, convolved, gain, normed, yhat, inverse):
    def one_row(row, carry):
        for slot in range(shape.slots):
            start = pl.multiple_of(row * shape.columns + slot * TILE, TILE)
            at = slot * TILE * TILE + (first_row + row) * TILE
            out = pl.ds(pl.multiple_of(at, TILE), TILE)
            parts = [convolved[part, pl.ds(start, TILE), :] for part in range(shape.parts)]
            mean = jnp.sum(sum(parts), axis=-1, keepdims=True) * (1.0 / shape.channels)
            parts = [value - mean for value in parts]
            square = jnp.sum(sum(value * value for value in parts), axis=-1, keepdims=True)
            scale = lax.rsqrt(square * (1.0 / shape.channels) + EPS)
            inverse[out, :] = jnp.broadcast_to(scale, (TILE, LANES))
            for part in range(shape.parts):
                value = parts[part] * scale
                yhat[out, shape.lanes(part)] = value
                normed[out, shape.lanes(part)] = (value * gain[:, shape.lanes(part)]).astype(BF16)
        return carry

    lax.fori_loop(0, rows, one_row, 0, unroll=2)


def early_kernel(
    shape, taps_hbm, gain_hbm, band,
    normed, yhat, inverse,
    kernel, gain, taps, convolved, sems,
):
    fetch = Fetch(sems, (taps_hbm, kernel), (gain_hbm, gain))
    fetch.wait(0, 1)
    spread_taps(shape, kernel, taps)
    convolve(shape, shape.early, band, taps, convolved)
    normalise(shape, shape.early, 0, convolved, gain, normed, yhat, inverse)


def late_kernel(
    shape, taps_hbm, gain_hbm, w_in_hbm, band, fold, normed_in, yhat_in, inverse_in, dproj_t, dact,
    keep, give, activated, dpreact, yhat, inverse,
    kernel, gain, w_in, taps, padded, convolved, normed, normed_t, sems,
):
    fetch = Fetch(sems, (taps_hbm, kernel), (gain_hbm, gain), (w_in_hbm, w_in))
    late = TILE - shape.early
    kept = late + HALF
    for part in range(shape.parts):
        rows = pl.ds(shape.early * shape.pitch, kept * shape.pitch)
        padded[part, pl.ds(0, kept * shape.pitch), :] = band[part, rows, :]
    put_fold(shape, fold, padded, kept)
    done = shape.early * TILE
    for slot in range(shape.slots):
        rows = pl.ds(slot * TILE * TILE, done)
        normed[rows, :] = normed_in[rows, :]
        yhat[rows, :] = yhat_in[rows, :]
        inverse[rows, :] = inverse_in[rows, :]
    fetch.wait(0, 1)
    spread_taps(shape, kernel, taps)
    convolve(shape, late, padded, taps, convolved)
    normalise(shape, late, shape.early, convolved, gain, normed, yhat, inverse)
    per_slot = TILE * TILE
    for slot in range(shape.slots):
        normed_t[:, slot * per_slot : (slot + 1) * per_slot] = normed[pl.ds(slot * per_slot, per_slot), :].T
    fetch.wait(2)
    keeps_in = lax.axis_index("core") == 0
    block = shape.channels
    for h in range(shape.hidden // block):
        cols = slice(h * block, (h + 1) * block)
        for slot in range(shape.slots):
            rows = pl.ds(slot * per_slot, per_slot)
            pre = dot(normed[rows, :], w_in[:, cols], 1, 0)
            square = pre * pre
            inner = pre * (GELU_C + (GELU_C * GELU_A) * square)
            gate = 0.5 + 0.5 * jnp.tanh(inner)
            activated[rows, cols] = (pre * gate).astype(BF16)
            slope = pre * (2.0 * GELU_C + (6.0 * GELU_C * GELU_A) * square)
            grown = gate + slope * (gate - gate * gate)
            dpreact[rows, cols] = (dact[rows, cols] * grown).astype(BF16)
        rows = slice(h * block, (h + 1) * block)
        of_in = dot(normed_t[...], dpreact[:, cols], 1, 0)
        of_out = dot(dproj_t[...], activated[:, cols], 1, 0)
        keep[rows, :] = jnp.where(keeps_in, of_in, of_out)
        give[rows, :] = jnp.where(keeps_in, of_out, of_in).astype(BF16)


def fold_sum(value):
    return jnp.sum(value.reshape(-1, 8, value.shape[-1]), axis=0)


def norm_grad_kernel(shape, w_in_hbm, gain_hbm, dpreact, yhat, inverse, conv_grad, gain_part, w_in, gain, sems):
    fetch = Fetch(sems, (w_in_hbm, w_in), (gain_hbm, gain))
    fetch.wait(0, 1)
    chunk = TILE * TILE
    total = jnp.zeros((8, shape.channels), F32)
    for slot in range(shape.slots):
        rows = pl.ds(slot * chunk, chunk)
        dnormed = dot(dpreact[rows, :], w_in[...], 1, 1)
        unit = yhat[rows, :]
        total += fold_sum(dnormed * unit)
        dhat = dnormed * gain[...]
        mean = jnp.sum(dhat, axis=-1, keepdims=True) * (1.0 / shape.channels)
        along = jnp.sum(dhat * unit, axis=-1, keepdims=True) * (1.0 / shape.channels)
        scale = jnp.concatenate([inverse[rows, :]] * shape.parts, axis=1)
        conv_grad[rows, :] = (scale * (dhat - mean - unit * along)).astype(BF16)
    gain_part[...] = total


def state_kernel(
    shape, count_hbm, ocean_hbm, fields_hbm, tangent_hbm, w_out_hbm, scale_hbm, activated,
    state, scale_part,
    count, ocean, fields, tangent, w_out, scale, sems,
):
    fetch = Fetch(
        sems, (w_out_hbm, w_out), (fields_hbm, fields), (tangent_hbm, tangent),
        (scale_hbm, scale), (count_hbm, count), (ocean_hbm, ocean),
    )
    fetch.wait(0, 1, 2, 3, 4, 5)
    chunk = TILE * TILE
    total = jnp.zeros((8, shape.channels), F32)
    for slot in range(shape.slots):
        rows = pl.ds(slot * chunk, chunk)
        flag = slot_flag(count, ocean, slot)
        projected = dot(activated[rows, :], w_out[...], 1, 0)
        kept = fields[rows, :].astype(F32) + scale[...] * projected
        state[rows, :] = (flag * kept).astype(BF16)
        total += fold_sum(flag * tangent[rows, :].astype(F32) * projected)
    scale_part[...] = total


def place_grad(shape, conv_grad, spaced):
    blank = jnp.zeros((LEFT, LANES), F32)
    for part in range(shape.parts):
        for row in range(TILE):
            base = row * shape.pitch
            spaced[part, pl.ds(base, LEFT), :] = blank
            spaced[part, pl.ds(base + LEFT + shape.columns, LEFT), :] = blank
            for slot in range(shape.slots):
                cells = conv_grad[pl.ds(slot * TILE * TILE + row * TILE, TILE), shape.lanes(part)]
                spaced[part, pl.ds(base + LEFT + slot * TILE, TILE), :] = cells.astype(F32)


def taps_kernel(shape, band, fold, conv_grad, gain_part, scale_part, small, padded, spaced):
    taps = KSIZE * KSIZE
    small[...] = jnp.zeros_like(small)
    small[pl.ds(taps, 1), :] = jnp.sum(gain_part[...], axis=0, keepdims=True)
    small[pl.ds(taps + 1, 1), :] = jnp.sum(scale_part[...], axis=0, keepdims=True)
    place_grad(shape, conv_grad, spaced)
    kept = TILE + HALF
    for part in range(shape.parts):
        padded[part, pl.ds(0, kept * shape.pitch), :] = band[part]
    put_fold(shape, fold, padded, kept)
    run = shape.columns // 8
    origin = LEFT - HALF
    for part in range(shape.parts):
        for above in range(KSIZE):

            def one_row(row, sums, part=part, above=above):
                base = (row + above) * shape.pitch + origin
                loaded = [
                    padded[part, pl.ds(base + at, 8, stride=run), :] for at in range(run + KSIZE - 1)
                ]
                grads = [
                    spaced[part, pl.ds(row * shape.pitch + LEFT + at, 8, stride=run), :] for at in range(run)
                ]
                sums = list(sums)
                for shift in range(KSIZE):
                    for at in range(run):
                        sums[shift] = sums[shift] + grads[at] * loaded[at + shift]
                return tuple(sums)

            blank = tuple(jnp.zeros((8, LANES), F32) for _ in range(KSIZE))
            sums = lax.fori_loop(0, TILE, one_row, blank, unroll=2)
            for shift in range(KSIZE):
                small[pl.ds(above * KSIZE + shift, 1), shape.lanes(part)] = jnp.sum(
                    sums[shift], axis=0, keepdims=True
                )


def back_kernel(shape, count_hbm, taps_hbm, conv_grad, core_grad, fold, count, kernel, spaced, taps, sems):
    fetch = Fetch(sems, (count_hbm, count), (taps_hbm, kernel))
    place_grad(shape, conv_grad, spaced)
    blank = jnp.zeros((LEFT, LANES), F32)
    for part in range(shape.parts):
        for row in range(TILE + HALF):
            core_grad[part, pl.ds(row * shape.pitch, LEFT), :] = blank
            core_grad[part, pl.ds((row + 1) * shape.pitch - LEFT, LEFT), :] = blank
    fetch.wait(0, 1)
    spread_taps(shape, kernel, taps)
    run = -(-(shape.columns + 2 * HALF) // 8)

    def one_row(row, tap_rows):
        for part in range(shape.parts):
            sums = [None] * run
            for above in tap_rows:
                base = (row - above) * shape.pitch + LEFT
                loaded = [
                    spaced[part, pl.ds(base + at - KSIZE + 1, 8, stride=run), :]
                    for at in range(run + KSIZE - 1)
                ]
                for shift in range(KSIZE):
                    weight = taps[part, above * KSIZE + shift]
                    for at in range(run):
                        term = weight * loaded[at - shift + KSIZE - 1]
                        sums[at] = term if sums[at] is None else sums[at] + term
            start = (row - HALF) * shape.pitch + LEFT - HALF
            for at in range(run):
                core_grad[part, pl.ds(start + at, 8, stride=run), :] = sums[at]

    inner = (KSIZE - 1, TILE - 1)
    for row in range(HALF, TILE + 2 * HALF):
        if not inner[0] <= row <= inner[1]:
            low = max(0, row - TILE + 1)
            one_row(row, range(low, min(KSIZE - 1, row) + 1))

    def inner_row(step, carry):
        one_row(step, range(KSIZE))
        return carry

    lax.fori_loop(inner[0], inner[1] + 1, inner_row, 0)
    turn_rows(shape, count[0] * TILE, core_grad, (TILE, TILE + 1, TILE + 2), fold)


def rims_kernel(shape, count_hbm, core_grad, fold, folded, first, second, count, sems):
    fetch = Fetch(sems, (count_hbm, count))
    for part in range(shape.parts):
        folded[part] = core_grad[part, pl.ds(0, TILE * shape.pitch), :]
        for k in range(HALF):
            rows = pl.ds((TILE - 1 - k) * shape.pitch, shape.pitch)
            returned = fold[pl.ds(k * shape.pitch, shape.pitch), shape.lanes(part)]
            folded[part, rows, :] += returned.astype(F32)
    fetch.wait(0)
    west = edge_planes(shape, folded, LEFT - HALF, shape.pitch)
    east = edge_planes(shape, folded, LEFT + count[0] * TILE, shape.pitch)
    send_edges(shape, west, east, first, second)


def final_kernel(
    shape, count_hbm, ocean_hbm, tangent_hbm, folded, first, second,
    grad_fields,
    count, ocean, tangent, work, sems,
):
    fetch = Fetch(sems, (tangent_hbm, tangent), (count_hbm, count), (ocean_hbm, ocean))
    even = is_even()
    work[...] = folded[...]
    fetch.wait(0, 1, 2)
    used = count[0] * TILE
    for part in range(shape.parts):
        for col in range(HALF):
            planes = pl.ds(col * TILE, TILE)
            one = first[planes, shape.lanes(part)].astype(F32)
            two = second[planes, shape.lanes(part)].astype(F32)
            to_tail = jnp.where(even, one, two)
            to_head = jnp.where(even, two, one)
            head = pl.ds(LEFT + col, TILE, stride=shape.pitch)
            work[part, head, :] = work[part, head, :] + to_head
            tail = pl.ds(LEFT + used - HALF + col, TILE, stride=shape.pitch)
            work[part, tail, :] = work[part, tail, :] + to_tail
        for slot in range(shape.slots):
            flag = slot_flag(count, ocean, slot)
            for row in range(TILE):
                rows = pl.ds(slot * TILE * TILE + row * TILE, TILE)
                cells = work[part, pl.ds(row * shape.pitch + LEFT + slot * TILE, TILE), :]
                total = tangent[rows, shape.lanes(part)].astype(F32) + cells
                grad_fields[rows, shape.lanes(part)] = (flag * total).astype(BF16)


def unpack_kernel(norm, own, other, small, w_in, w_out, kernel_sum, gain_sum, scale_sum):
    is_first = lax.axis_index("core") == 0
    channels = own.shape[-1]
    for h in range(w_out.shape[0] // channels):
        rows = slice(h * channels, (h + 1) * channels)
        mine = own[rows, :].astype(F32) * norm
        theirs = other[rows, :].astype(F32) * norm
        w_in[:, rows] = jnp.where(is_first, mine, theirs)
        w_out[rows, :] = jnp.where(is_first, theirs, mine).T
    for above in range(KSIZE):
        kernel_sum[above] = small[pl.ds(above * KSIZE, KSIZE), :] * norm
    gain_sum[...] = small[pl.ds(KSIZE * KSIZE, 1), :] * norm
    scale_sum[...] = small[pl.ds(KSIZE * KSIZE + 1, 1), :] * norm


def pairs_of(kind):
    count = lax.axis_size(TILES)
    half = count // 2
    place = [rank if rank < half else count - 1 + half - rank for rank in range(count)]
    partner = {
        "first": lambda rank: rank ^ 1,
        "second": lambda rank: ((rank + 1) ^ 1) - 1,
        "fold": lambda rank: count - 1 - rank,
    }[kind]
    return [(place[rank], place[partner(rank) % count]) for rank in range(count)]


def swap(block, kind):
    return lax.ppermute(block, TILES, pairs_of(kind))


def core_swap(block):
    return lax.ppermute(block, "core", [(0, 1), (1, 0)])


def stages():
    chip_bits = lax.axis_size("chips").bit_length() - 1
    rest = list(range(2, chip_bits))
    return list(zip([0, -1, 1] + rest, [1, 0, -1] + rest))


def bit_swap(block, stage):
    chips, cores, samples = (lax.axis_size(axis) for axis in ("chips", "core", "dp"))
    pairs = []
    for chip in range(chips):
        for core in range(cores):
            for sample in range(samples):
                bit = stage[core]
                to = (chip, sample ^ 1) if bit < 0 else (chip ^ (1 << bit), sample)
                pairs.append(
                    ((chip * cores + core) * samples + sample, (to[0] * cores + core) * samples + to[1])
                )
    return lax.ppermute(block, ("chips", "core", "dp"), pairs)


def bit_here(stage):
    bits = [
        lax.axis_index("dp") if bit < 0 else lax.axis_index("chips") >> bit & 1 for bit in stage
    ]
    return jnp.where(lax.axis_index("core") == 0, bits[0], bits[1])


def halved(keep, give):
    mine = keep + core_swap(give).astype(F32)
    for stage in stages():
        bit = bit_here(stage)
        halves = mine.reshape(2, -1, mine.shape[-1])
        send = lax.dynamic_index_in_dim(halves, 1 - bit, 0, keepdims=False).astype(BF16)
        mine = lax.dynamic_index_in_dim(halves, bit, 0, keepdims=False) + bit_swap(send, stage).astype(F32)
    return mine.astype(BF16)


def doubled(mine, small):
    for stage in reversed(stages()):
        rows = mine.shape[0]
        rounded = small.astype(BF16)
        came = bit_swap(jnp.concatenate([mine, rounded]), stage)
        first = bit_here(stage) == 0
        other = came[:rows]
        mine = jnp.concatenate([jnp.where(first, mine, other), jnp.where(first, other, mine)])
        small = lax.reduce_precision(small, 8, 7) + came[rows:].astype(F32)
    rows = mine.shape[0]
    high = lax.reduce_precision(small, 8, 7)
    low = lax.reduce_precision(small - high, 8, 7)
    came = core_swap(jnp.concatenate([mine, high.astype(BF16), low.astype(BF16)]))
    extra = came[rows:].astype(F32).reshape(2, -1, small.shape[-1])
    small = (high + low) + (extra[0] + extra[1])
    return mine, came[:rows], small


def call(kernel, outs, scratch, hbm, vmem, copies=0, micros=1.0):
    in_specs = [pl.BlockSpec(memory_space=pl.ANY)] * len(hbm)
    in_specs += [pl.BlockSpec(memory_space=pltpu.VMEM)] * len(vmem)
    shapes = [pltpu.SMEM(*one) if one[1] == jnp.int32 else pltpu.VMEM(*one) for one in scratch]
    if copies:
        shapes.append(pltpu.SemaphoreType.DMA((copies,)))
    return pl.pallas_call(
        kernel,
        out_shape=[jax.ShapeDtypeStruct(*out) for out in outs],
        in_specs=in_specs,
        out_specs=[pl.BlockSpec(memory_space=pltpu.VMEM)] * len(outs),
        scratch_shapes=shapes,
        cost_estimate=pl.CostEstimate(flops=int(micros * 1e9), bytes_accessed=0, transcendentals=0),
        compiler_params=pltpu.CompilerParams(vmem_limit_bytes=24 * 1024 * 1024),
    )(*hbm, *vmem)


def shards(fields, grad_out, block_count, ocean, kernel, ln_gain, w_in, w_out, layer_scale):
    samples, slots, tile_rows, tile_cols, channels = fields.shape
    hidden = w_in.shape[1]
    shape = Shape(slots, channels, hidden)
    cells, parts, pitch = shape.cells, shape.parts, shape.pitch
    grid = fields.shape
    fields = fields.reshape(cells, channels)
    tangent = grad_out.reshape(cells, channels)
    taps_in = kernel.reshape(KSIZE * KSIZE, channels)
    gain = ln_gain.reshape(1, channels)
    scale = layer_scale.reshape(1, channels)

    def bind(body):
        return functools.partial(body, shape)

    def strip(rows):
        return ((parts, rows * pitch, LANES), F32)

    edge = ((shape.edge_rows, channels), BF16)
    turned = ((HALF * pitch, channels), BF16)
    whole = ((cells, channels), BF16)
    whole_f = ((cells, channels), F32)
    wide = ((cells, hidden), BF16)
    narrow = ((cells, LANES), F32)
    row = ((1, channels), F32)
    eight = ((8, channels), F32)
    taps = ((parts, KSIZE * KSIZE, 8, LANES), F32)
    taps_raw = (taps_in.shape, BF16)
    count_s = (block_count.shape, jnp.int32)
    ocean_s = (ocean.shape, jnp.int32)
    w_in_s = (w_in.shape, BF16)
    w_out_s = (w_out.shape, BF16)
    flat = ((channels, cells), BF16)
    late = TILE - shape.early

    first, second = call(
        bind(prep_kernel), [edge, edge], [count_s, ocean_s, whole, ((parts, cells, LANES), F32)],
        [block_count, ocean, fields], [], 3, 1.5,
    )
    first, second = swap(first, "first"), swap(second, "second")
    dproj, dproj_t, dact = call(
        bind(cotangent_kernel), [whole, flat, ((cells, hidden), F32)],
        [count_s, ocean_s, whole, row, w_out_s],
        [block_count, ocean, tangent, scale, w_out], [], 5, 2.5,
    )
    band, fold = call(
        bind(band_kernel), [strip(TILE + HALF), turned], [count_s, ocean_s, whole],
        [block_count, ocean, fields], [first, second], 3, 1.0,
    )
    fold = swap(fold, "fold")
    normed, yhat, inverse = call(
        bind(early_kernel), [whole, whole_f, narrow],
        [taps_raw, row, taps, ((parts, shape.early * shape.columns, LANES), F32)],
        [taps_in, gain], [band], 2, 4.0,
    )
    keep, give, activated, dpreact, yhat, inverse = call(
        bind(late_kernel),
        [((hidden, channels), F32), ((hidden, channels), BF16), wide, wide, whole_f, narrow],
        [
            taps_raw, row, w_in_s, taps, strip(late + 2 * HALF),
            ((parts, late * shape.columns, LANES), F32), whole, flat,
        ],
        [taps_in, gain, w_in], [band, fold, normed, yhat, inverse, dproj_t, dact], 3, 6.0,
    )
    conv_grad, gain_part = call(
        bind(norm_grad_kernel), [whole, eight], [w_in_s, row], [w_in, gain], [dpreact, yhat, inverse], 2, 1.5,
    )
    mine = halved(keep, give)
    core_grad, fold_back = call(
        bind(back_kernel), [strip(TILE + HALF), turned],
        [count_s, taps_raw, strip(TILE), taps],
        [block_count, taps_in], [conv_grad], 2, 4.0,
    )
    fold_back = swap(fold_back, "fold")
    state, scale_part = call(
        bind(state_kernel), [whole, eight], [count_s, ocean_s, whole, whole, w_out_s, row],
        [block_count, ocean, fields, tangent, w_out, scale], [activated], 6, 1.5,
    )
    small_rows = -(-(KSIZE * KSIZE + 2) // 16) * 16
    (small,) = call(
        bind(taps_kernel), [((small_rows, channels), F32)], [strip(TILE + 2 * HALF), strip(TILE)],
        [], [band, fold, conv_grad, gain_part, scale_part], 0, 3.5,
    )
    folded, first, second = call(
        bind(rims_kernel), [strip(TILE), edge, edge], [count_s], [block_count], [core_grad, fold_back], 1, 1.0,
    )
    first, second = swap(first, "first"), swap(second, "second")
    (grad_fields,) = call(
        bind(final_kernel), [whole], [count_s, ocean_s, whole, strip(TILE)],
        [block_count, ocean, tangent], [folded, first, second], 3, 1.5,
    )
    own, other, small = doubled(mine, small)
    total = samples * lax.axis_size("dp") * slots * lax.axis_size(TILES) * tile_rows * tile_cols
    w_in_sum, w_out_sum, kernel_sum, gain_sum, scale_sum = call(
        functools.partial(unpack_kernel, total ** (-0.5)),
        [((channels, hidden), F32), ((hidden, channels), F32), (kernel.shape, F32), row, row],
        [], [], [own, other, small], 0, 1.5,
    )
    return (
        state.reshape(grid),
        grad_fields.reshape(grid),
        kernel_sum,
        gain_sum.reshape(ln_gain.shape),
        w_in_sum,
        w_out_sum,
        scale_sum.reshape(layer_scale.shape),
    )


def solution(mesh):
    cores = Mesh(mesh.devices.reshape(-1, 2, mesh.devices.shape[1]), ("chips", "core", "dp"))
    banded = P("dp", TILES, None, None, None)
    placed = (banded, banded, P(TILES), P(TILES), P(), P(), P(), P(), P())
    return jax.shard_map(
        shards,
        mesh=cores,
        in_specs=placed,
        out_specs=(banded, banded, P(), P(), P(), P(), P()),
        check_vma=False,
    )
```

```python
import functools

import jax
import jax.numpy as jnp
from jax import lax
from jax.experimental import pallas as pl
from jax.experimental.pallas import tpu as pltpu
from jax.sharding import Mesh, PartitionSpec as P

KSIZE = 7
HALF = KSIZE // 2
TILE = 16
EPS = 1e-06
TILES = ("chips", "core")
F32 = jnp.float32
BF16 = jnp.bfloat16
LANES = 128
LEFT = 8
GELU_C = 0.7978845608028654
GELU_A = 0.044715


def dot(lhs, rhs, lhs_dim, rhs_dim):
    return lax.dot_general(
        lhs, rhs, (((lhs_dim,), (rhs_dim,)), ((), ())), preferred_element_type=F32
    )


def cycle_rank():
    count = lax.axis_size(TILES)
    here = lax.axis_index("chips") * lax.axis_size("core") + lax.axis_index("core")
    return jnp.where(here < count // 2, here, count - 1 + count // 2 - here)


def is_even():
    return lax.rem(cycle_rank(), 2) == 0


class Fetch:
    def __init__(self, sems, *pairs):
        self.copies = [
            pltpu.make_async_copy(source, target, sems.at[at]) for at, (source, target) in enumerate(pairs)
        ]
        for copy in self.copies:
            copy.start()

    def wait(self, *which):
        for at in which:
            self.copies[at].wait()


def slot_flag(count_ref, ocean_ref, slot):
    live = jnp.logical_and(slot < count_ref[0], ocean_ref[slot] > 0)
    return jnp.where(live, 1.0, 0.0).astype(F32)


class Shape:
    def __init__(self, slots, channels, hidden):
        self.slots = slots
        self.channels = channels
        self.hidden = hidden
        self.parts = channels // LANES
        self.columns = slots * TILE
        self.pitch = self.columns + 2 * LEFT
        self.cells = slots * TILE * TILE
        self.edge_rows = HALF * TILE
        self.early = 12

    def lanes(self, part):
        return slice(part * LANES, (part + 1) * LANES)


def edge_planes(shape, source, start, stride):
    return [
        jnp.concatenate(
            [source[part, pl.ds(start + col, TILE, stride=stride), :] for part in range(shape.parts)], axis=1
        )
        for col in range(HALF)
    ]


def send_edges(shape, left, right, first, second):
    even = is_even()
    for col in range(HALF):
        rows = pl.ds(col * TILE, TILE)
        first[rows, :] = jnp.where(even, right[col], left[col]).astype(BF16)
        second[rows, :] = jnp.where(even, left[col], right[col]).astype(BF16)


def flip_matrix(shape, used):
    to = lax.broadcasted_iota(jnp.int32, (shape.pitch, shape.pitch), 0)
    frm = lax.broadcasted_iota(jnp.int32, (shape.pitch, shape.pitch), 1)
    return jnp.where(to + frm == used + 2 * LEFT - 1, 1.0, 0.0).astype(BF16)


def prep_kernel(shape, count_hbm, fields, first, second, count, work, sems):
    fetch = Fetch(sems, (count_hbm, count))
    for part in range(shape.parts):
        work[part] = fields[:, shape.lanes(part)].astype(F32)
    left = edge_planes(shape, work, 0, TILE)
    fetch.wait(0)
    right = edge_planes(shape, work, (count[0] - 1) * TILE * TILE + TILE - HALF, TILE)
    send_edges(shape, left, right, first, second)


def cotangent_kernel(
    shape, count_hbm, ocean_hbm, tangent, scale, dproj, dproj_t, count, ocean, sems
):
    fetch = Fetch(sems, (count_hbm, count), (ocean_hbm, ocean))
    fetch.wait(0, 1)
    per_slot = TILE * TILE
    for slot in range(shape.slots):
        rows = pl.ds(slot * per_slot, per_slot)
        flag = slot_flag(count, ocean, slot)
        scaled = (tangent[rows, :].astype(F32) * (scale[...] * flag)).astype(BF16)
        dproj[rows, :] = scaled
        dproj_t[:, slot * per_slot : (slot + 1) * per_slot] = scaled.T


def band_kernel(shape, count_hbm, ocean_hbm, fields, first, second, band, fold, count, ocean, sems):
    fetch = Fetch(sems, (count_hbm, count), (ocean_hbm, ocean))
    even = is_even()
    blank = jnp.zeros((LEFT, LANES), F32)
    per_slot = TILE * TILE
    for part in range(shape.parts):
        band[part, pl.ds(0, HALF * shape.pitch), :] = jnp.zeros((HALF * shape.pitch, LANES), F32)
        for row in range(TILE):
            base = (row + HALF) * shape.pitch
            band[part, pl.ds(base, LEFT), :] = blank
            band[part, pl.ds(base + LEFT + shape.columns, LEFT), :] = blank
    fetch.wait(0, 1)
    used = count[0] * TILE
    flags = [slot_flag(count, ocean, slot) for slot in range(shape.slots)]
    top = HALF * shape.pitch
    for part in range(shape.parts):
        for row in range(TILE):
            base = (row + HALF) * shape.pitch
            for slot in range(shape.slots):
                cells = fields[pl.ds(slot * per_slot + row * TILE, TILE), shape.lanes(part)]
                band[part, pl.ds(base + LEFT + slot * TILE, TILE), :] = cells.astype(F32) * flags[slot]
        for col in range(HALF):
            rows = pl.ds(col * TILE, TILE)
            one = first[rows, shape.lanes(part)].astype(F32)
            two = second[rows, shape.lanes(part)].astype(F32)
            west = jnp.where(even, two, one)
            east = jnp.where(even, one, two)
            band[part, pl.ds(top + LEFT - HALF + col, TILE, stride=shape.pitch), :] = west
            band[part, pl.ds(top + LEFT + used + col, TILE, stride=shape.pitch), :] = east
    turn_rows(shape, used, band, (HALF + TILE - 1, HALF + TILE - 2, HALF + TILE - 3), fold)


def turn_rows(shape, used, source, rows, fold):
    flip = flip_matrix(shape, used)
    for k, row in enumerate(rows):
        at = pl.ds(row * shape.pitch, shape.pitch)
        cells = jnp.concatenate([source[part, at, :] for part in range(shape.parts)], axis=1)
        turned = dot(flip, cells.astype(BF16), 1, 0)
        fold[pl.ds(k * shape.pitch, shape.pitch), :] = turned.astype(BF16)


def put_fold(shape, fold, padded, first_row):
    for part in range(shape.parts):
        rows = pl.ds(first_row * shape.pitch, HALF * shape.pitch)
        padded[part, rows, :] = fold[:, shape.lanes(part)].astype(F32)


def spread_taps(shape, kernel, taps):
    for above in range(KSIZE):
        rows = kernel[above].astype(F32)
        for part in range(shape.parts):
            for shift in range(KSIZE):
                row = rows[shift : shift + 1, shape.lanes(part)]
                taps[part, above * KSIZE + shift] = jnp.broadcast_to(row, (8, LANES))


def convolve(shape, rows, padded, taps, convolved):
    run = shape.columns // 8
    pair = 2
    origin = LEFT - HALF

    def two_rows(step, carry):
        row = step * pair
        for part in range(shape.parts):
            sums = [[None] * run for _ in range(pair)]
            for above in range(KSIZE + pair - 1):
                base = (row + above) * shape.pitch + origin
                loaded = [
                    padded[part, pl.ds(base + at, 8, stride=run), :]
                    for at in range(run + KSIZE - 1)
                ]
                for which in range(pair):
                    tap_row = above - which
                    if not 0 <= tap_row < KSIZE:
                        continue
                    for shift in range(KSIZE):
                        weight = taps[part, tap_row * KSIZE + shift]
                        for at in range(run):
                            term = weight * loaded[at + shift]
                            old = sums[which][at]
                            sums[which][at] = term if old is None else old + term
            for which in range(pair):
                for at in range(run):
                    start = (row + which) * shape.columns + at
                    convolved[part, pl.ds(start, 8, stride=run), :] = sums[which][at]
        return carry

    lax.fori_loop(0, rows // pair, two_rows, 0)


def normalise(shape, rows, first_row, convolved, gain, normed, yhat, inverse):
    def one_row(row, carry):
        for slot in range(shape.slots):
            start = pl.multiple_of(row * shape.columns + slot * TILE, TILE)
            at = slot * TILE * TILE + (first_row + row) * TILE
            out = pl.ds(pl.multiple_of(at, TILE), TILE)
            parts = [convolved[part, pl.ds(start, TILE), :] for part in range(shape.parts)]
            mean = jnp.sum(sum(parts), axis=-1, keepdims=True) * (1.0 / shape.channels)
            parts = [value - mean for value in parts]
            square = jnp.sum(sum(value * value for value in parts), axis=-1, keepdims=True)
            scale = lax.rsqrt(square * (1.0 / shape.channels) + EPS)
            inverse[out, :] = jnp.broadcast_to(scale, (TILE, LANES))
            for part in range(shape.parts):
                value = parts[part] * scale
                yhat[out, shape.lanes(part)] = value
                normed[out, shape.lanes(part)] = (value * gain[:, shape.lanes(part)]).astype(BF16)
        return carry

    lax.fori_loop(0, rows, one_row, 0, unroll=2)


def early_kernel(
    shape, kernel, gain, w_out, band, dproj,
    normed, yhat, inverse, dact,
    taps, convolved,
):
    spread_taps(shape, kernel, taps)
    convolve(shape, shape.early, band, taps, convolved)
    normalise(shape, shape.early, 0, convolved, gain, normed, yhat, inverse)
    per_slot = TILE * TILE
    for slot in range(shape.slots):
        rows = pl.ds(slot * per_slot, per_slot)
        for h in range(shape.hidden // shape.channels):
            cols = slice(h * shape.channels, (h + 1) * shape.channels)
            dact[rows, cols] = dot(dproj[rows, :], w_out[cols, :], 1, 1)


def late_kernel(
    shape, kernel, gain, w_in, band, fold, normed_in, yhat_in, inverse_in, dproj_t, dact,
    keep, give, activated, dpreact, yhat, inverse,
    taps, padded, convolved, normed, normed_t,
):
    late = TILE - shape.early
    kept = late + HALF
    for part in range(shape.parts):
        rows = pl.ds(shape.early * shape.pitch, kept * shape.pitch)
        padded[part, pl.ds(0, kept * shape.pitch), :] = band[part, rows, :]
    put_fold(shape, fold, padded, kept)
    done = shape.early * TILE
    for slot in range(shape.slots):
        rows = pl.ds(slot * TILE * TILE, done)
        normed[rows, :] = normed_in[rows, :]
        yhat[rows, :] = yhat_in[rows, :]
        inverse[rows, :] = inverse_in[rows, :]
    spread_taps(shape, kernel, taps)
    convolve(shape, late, padded, taps, convolved)
    normalise(shape, late, shape.early, convolved, gain, normed, yhat, inverse)
    per_slot = TILE * TILE
    for slot in range(shape.slots):
        normed_t[:, slot * per_slot : (slot + 1) * per_slot] = normed[pl.ds(slot * per_slot, per_slot), :].T
    keeps_in = lax.axis_index("core") == 0
    block = shape.channels
    for h in range(shape.hidden // block):
        cols = slice(h * block, (h + 1) * block)
        for slot in range(shape.slots):
            rows = pl.ds(slot * per_slot, per_slot)
            pre = dot(normed[rows, :], w_in[:, cols], 1, 0)
            square = pre * pre
            inner = pre * (GELU_C + (GELU_C * GELU_A) * square)
            gate = 0.5 + 0.5 * jnp.tanh(inner)
            activated[rows, cols] = (pre * gate).astype(BF16)
            slope = pre * (2.0 * GELU_C + (6.0 * GELU_C * GELU_A) * square)
            grown = gate + slope * (gate - gate * gate)
            dpreact[rows, cols] = (dact[rows, cols] * grown).astype(BF16)
        rows = slice(h * block, (h + 1) * block)
        of_in = dot(normed_t[...], dpreact[:, cols], 1, 0)
        of_out = dot(dproj_t[...], activated[:, cols], 1, 0)
        keep[rows, :] = jnp.where(keeps_in, of_in, of_out)
        give[rows, :] = jnp.where(keeps_in, of_out, of_in).astype(BF16)


def fold_sum(value):
    return jnp.sum(value.reshape(-1, 8, value.shape[-1]), axis=0)


def norm_grad_kernel(shape, w_in, gain, dpreact, yhat, inverse, conv_grad, gain_part):
    chunk = TILE * TILE
    total = jnp.zeros((8, shape.channels), F32)
    for slot in range(shape.slots):
        rows = pl.ds(slot * chunk, chunk)
        dnormed = dot(dpreact[rows, :], w_in[...], 1, 1)
        unit = yhat[rows, :]
        total += fold_sum(dnormed * unit)
        dhat = dnormed * gain[...]
        mean = jnp.sum(dhat, axis=-1, keepdims=True) * (1.0 / shape.channels)
        along = jnp.sum(dhat * unit, axis=-1, keepdims=True) * (1.0 / shape.channels)
        scale = jnp.concatenate([inverse[rows, :]] * shape.parts, axis=1)
        conv_grad[rows, :] = (scale * (dhat - mean - unit * along)).astype(BF16)
    gain_part[...] = total


def state_kernel(
    shape, count_hbm, ocean_hbm, fields, tangent, w_out, scale, activated,
    state, scale_part,
    count, ocean, sems,
):
    fetch = Fetch(sems, (count_hbm, count), (ocean_hbm, ocean))
    fetch.wait(0, 1)
    chunk = TILE * TILE
    total = jnp.zeros((8, shape.channels), F32)
    for slot in range(shape.slots):
        rows = pl.ds(slot * chunk, chunk)
        flag = slot_flag(count, ocean, slot)
        projected = dot(activated[rows, :], w_out[...], 1, 0)
        kept = fields[rows, :].astype(F32) + scale[...] * projected
        state[rows, :] = (flag * kept).astype(BF16)
        total += fold_sum(flag * tangent[rows, :].astype(F32) * projected)
    scale_part[...] = total


def place_grad(shape, conv_grad, spaced):
    blank = jnp.zeros((LEFT, LANES), F32)
    for part in range(shape.parts):
        for row in range(TILE):
            base = row * shape.pitch
            spaced[part, pl.ds(base, LEFT), :] = blank
            spaced[part, pl.ds(base + LEFT + shape.columns, LEFT), :] = blank
            for slot in range(shape.slots):
                cells = conv_grad[pl.ds(slot * TILE * TILE + row * TILE, TILE), shape.lanes(part)]
                spaced[part, pl.ds(base + LEFT + slot * TILE, TILE), :] = cells.astype(F32)


def taps_kernel(shape, band, fold, conv_grad, gain_part, scale_part, small, padded, spaced):
    taps = KSIZE * KSIZE
    small[...] = jnp.zeros_like(small)
    small[pl.ds(taps, 1), :] = jnp.sum(gain_part[...], axis=0, keepdims=True)
    small[pl.ds(taps + 1, 1), :] = jnp.sum(scale_part[...], axis=0, keepdims=True)
    place_grad(shape, conv_grad, spaced)
    kept = TILE + HALF
    for part in range(shape.parts):
        padded[part, pl.ds(0, kept * shape.pitch), :] = band[part]
    put_fold(shape, fold, padded, kept)
    run = shape.columns // 8
    origin = LEFT - HALF
    for part in range(shape.parts):
        for above in range(KSIZE):

            def one_row(row, sums, part=part, above=above):
                base = (row + above) * shape.pitch + origin
                loaded = [
                    padded[part, pl.ds(base + at, 8, stride=run), :] for at in range(run + KSIZE - 1)
                ]
                grads = [
                    spaced[part, pl.ds(row * shape.pitch + LEFT + at, 8, stride=run), :] for at in range(run)
                ]
                sums = list(sums)
                for shift in range(KSIZE):
                    for at in range(run):
                        sums[shift] = sums[shift] + grads[at] * loaded[at + shift]
                return tuple(sums)

            blank = tuple(jnp.zeros((8, LANES), F32) for _ in range(KSIZE))
            sums = lax.fori_loop(0, TILE, one_row, blank, unroll=2)
            for shift in range(KSIZE):
                small[pl.ds(above * KSIZE + shift, 1), shape.lanes(part)] = jnp.sum(
                    sums[shift], axis=0, keepdims=True
                )


def back_kernel(shape, count_hbm, kernel, conv_grad, core_grad, fold, count, spaced, taps, sems):
    fetch = Fetch(sems, (count_hbm, count))
    place_grad(shape, conv_grad, spaced)
    blank = jnp.zeros((LEFT, LANES), F32)
    for part in range(shape.parts):
        for row in range(TILE + HALF):
            core_grad[part, pl.ds(row * shape.pitch, LEFT), :] = blank
            core_grad[part, pl.ds((row + 1) * shape.pitch - LEFT, LEFT), :] = blank
    fetch.wait(0)
    spread_taps(shape, kernel, taps)
    run = -(-(shape.columns + 2 * HALF) // 8)

    def one_row(row, tap_rows):
        for part in range(shape.parts):
            sums = [None] * run
            for above in tap_rows:
                base = (row - above) * shape.pitch + LEFT
                loaded = [
                    spaced[part, pl.ds(base + at - KSIZE + 1, 8, stride=run), :]
                    for at in range(run + KSIZE - 1)
                ]
                for shift in range(KSIZE):
                    weight = taps[part, above * KSIZE + shift]
                    for at in range(run):
                        term = weight * loaded[at - shift + KSIZE - 1]
                        sums[at] = term if sums[at] is None else sums[at] + term
            start = (row - HALF) * shape.pitch + LEFT - HALF
            for at in range(run):
                core_grad[part, pl.ds(start + at, 8, stride=run), :] = sums[at]

    inner = (KSIZE - 1, TILE - 1)
    for row in range(HALF, TILE + 2 * HALF):
        if not inner[0] <= row <= inner[1]:
            low = max(0, row - TILE + 1)
            one_row(row, range(low, min(KSIZE - 1, row) + 1))

    def inner_row(step, carry):
        one_row(step, range(KSIZE))
        return carry

    lax.fori_loop(inner[0], inner[1] + 1, inner_row, 0)
    turn_rows(shape, count[0] * TILE, core_grad, (TILE, TILE + 1, TILE + 2), fold)


def rims_kernel(shape, count_hbm, core_grad, fold, folded, first, second, count, sems):
    fetch = Fetch(sems, (count_hbm, count))
    for part in range(shape.parts):
        folded[part] = core_grad[part, pl.ds(0, TILE * shape.pitch), :]
        for k in range(HALF):
            rows = pl.ds((TILE - 1 - k) * shape.pitch, shape.pitch)
            returned = fold[pl.ds(k * shape.pitch, shape.pitch), shape.lanes(part)]
            folded[part, rows, :] += returned.astype(F32)
    fetch.wait(0)
    west = edge_planes(shape, folded, LEFT - HALF, shape.pitch)
    east = edge_planes(shape, folded, LEFT + count[0] * TILE, shape.pitch)
    send_edges(shape, west, east, first, second)


def final_kernel(
    shape, count_hbm, ocean_hbm, tangent, folded, first, second,
    grad_fields, done,
    count, ocean, work, sems,
):
    fetch = Fetch(sems, (count_hbm, count), (ocean_hbm, ocean))
    even = is_even()
    done[...] = jnp.zeros_like(done)
    work[...] = folded[...]
    fetch.wait(0, 1)
    used = count[0] * TILE
    for part in range(shape.parts):
        for col in range(HALF):
            planes = pl.ds(col * TILE, TILE)
            one = first[planes, shape.lanes(part)].astype(F32)
            two = second[planes, shape.lanes(part)].astype(F32)
            to_tail = jnp.where(even, one, two)
            to_head = jnp.where(even, two, one)
            head = pl.ds(LEFT + col, TILE, stride=shape.pitch)
            work[part, head, :] = work[part, head, :] + to_head
            tail = pl.ds(LEFT + used - HALF + col, TILE, stride=shape.pitch)
            work[part, tail, :] = work[part, tail, :] + to_tail
        for slot in range(shape.slots):
            flag = slot_flag(count, ocean, slot)
            for row in range(TILE):
                rows = pl.ds(slot * TILE * TILE + row * TILE, TILE)
                cells = work[part, pl.ds(row * shape.pitch + LEFT + slot * TILE, TILE), :]
                total = tangent[rows, shape.lanes(part)].astype(F32) + cells
                grad_fields[rows, shape.lanes(part)] = (flag * total).astype(BF16)


def unpack_kernel(norm, own, came, w_in, w_out, kernel_sum, gain_sum, scale_sum):
    is_first = lax.axis_index("core") == 0
    channels = own.shape[-1]
    hidden = w_out.shape[0]
    for h in range(hidden // channels):
        rows = slice(h * channels, (h + 1) * channels)
        mine = own[rows, :].astype(F32) * norm
        theirs = came[rows, :].astype(F32) * norm
        w_in[:, rows] = jnp.where(is_first, mine, theirs)
        w_out[rows, :] = jnp.where(is_first, theirs, mine).T
    extra = (own.shape[0] - hidden) // 2
    high, low = pl.ds(hidden, extra), pl.ds(hidden + extra, extra)
    small = own[high, :].astype(F32) + own[low, :].astype(F32)
    small = (small + (came[high, :].astype(F32) + came[low, :].astype(F32))) * norm
    for above in range(KSIZE):
        kernel_sum[above] = small[above * KSIZE : (above + 1) * KSIZE, :]
    gain_sum[...] = small[KSIZE * KSIZE : KSIZE * KSIZE + 1, :]
    scale_sum[...] = small[KSIZE * KSIZE + 1 : KSIZE * KSIZE + 2, :]


def pairs_of(kind):
    count = lax.axis_size(TILES)
    half = count // 2
    place = [rank if rank < half else count - 1 + half - rank for rank in range(count)]
    partner = {
        "first": lambda rank: rank ^ 1,
        "second": lambda rank: ((rank + 1) ^ 1) - 1,
        "fold": lambda rank: count - 1 - rank,
    }[kind]
    return [(place[rank], place[partner(rank) % count]) for rank in range(count)]


def swap(block, kind):
    return lax.ppermute(block, TILES, pairs_of(kind))


def core_swap(block):
    return lax.ppermute(block, "core", [(0, 1), (1, 0)])


def stages():
    chip_bits = lax.axis_size("chips").bit_length() - 1
    rest = list(range(2, chip_bits))
    return list(zip([0, -1, 1] + rest, [1, 0, -1] + rest))


def bit_swap(block, stage):
    chips, cores, samples = (lax.axis_size(axis) for axis in ("chips", "core", "dp"))
    pairs = []
    for chip in range(chips):
        for core in range(cores):
            for sample in range(samples):
                bit = stage[core]
                to = (chip, sample ^ 1) if bit < 0 else (chip ^ (1 << bit), sample)
                pairs.append(
                    ((chip * cores + core) * samples + sample, (to[0] * cores + core) * samples + to[1])
                )
    return lax.ppermute(block, ("chips", "core", "dp"), pairs)


def bit_here(stage):
    bits = [
        lax.axis_index("dp") if bit < 0 else lax.axis_index("chips") >> bit & 1 for bit in stage
    ]
    return jnp.where(lax.axis_index("core") == 0, bits[0], bits[1])


def half_rows(bit, rows):
    return pl.ds(pl.multiple_of(bit * rows, rows), rows)


def join_kernel(stage, keep, came, mine, send):
    rows = send.shape[0]
    mine[...] = keep[...] + came[...].astype(F32)
    send[...] = mine[half_rows(1 - bit_here(stage), rows), :].astype(BF16)


def halve_kernel(stage, following, whole, came, mine, send):
    rows = mine.shape[0]
    mine[...] = whole[half_rows(bit_here(stage), rows), :] + came[...].astype(F32)
    send[...] = mine[half_rows(1 - bit_here(following), rows // 2), :].astype(BF16)


def turn_kernel(stage, whole, came, small, payload):
    rows = came.shape[0]
    share = whole[half_rows(bit_here(stage), rows), :] + came[...].astype(F32)
    payload[pl.ds(0, rows), :] = share.astype(BF16)
    payload[pl.ds(rows, small.shape[0]), :] = small[...].astype(BF16)


def double_kernel(stage, extra, own, came, payload):
    rows = own.shape[0] - extra
    bit = bit_here(stage)
    payload[half_rows(bit, rows), :] = own[pl.ds(0, rows), :]
    payload[half_rows(1 - bit, rows), :] = came[pl.ds(0, rows), :]
    total = own[pl.ds(rows, extra), :].astype(F32) + came[pl.ds(rows, extra), :].astype(F32)
    high = total.astype(BF16)
    payload[pl.ds(2 * rows, extra), :] = high
    if payload.shape[0] > 2 * rows + extra:
        payload[pl.ds(2 * rows + extra, extra), :] = (total - high.astype(F32)).astype(BF16)


def halved(mine, send, order):
    for at, stage in enumerate(order[:-1]):
        came = bit_swap(send, stage)
        rows = came.shape[0]
        bit = bit_here(stage)
        mine = lax.dynamic_index_in_dim(mine.reshape(2, rows, -1), bit, 0, keepdims=False) + came.astype(F32)
        bit = bit_here(order[at + 1])
        halves = mine.reshape(2, rows // 2, -1)
        send = lax.dynamic_index_in_dim(halves, 1 - bit, 0, keepdims=False).astype(BF16)
    return mine, send


def call(kernel, outs, scratch, hbm, vmem, copies=0, micros=1.0, after=(), limit=20):
    in_specs = [pl.BlockSpec(memory_space=pl.ANY)] * len(hbm)
    in_specs += [pl.BlockSpec(memory_space=pltpu.VMEM)] * len(vmem)
    in_specs += [pl.BlockSpec(memory_space=pl.ANY)] * len(after)
    shapes = [pltpu.SMEM(*one) if one[1] == jnp.int32 else pltpu.VMEM(*one) for one in scratch]
    if copies:
        shapes.append(pltpu.SemaphoreType.DMA((copies,)))
    taken = len(hbm) + len(vmem)

    def body(*refs):
        kernel(*refs[:taken], *refs[taken + len(after) :])

    return pl.pallas_call(
        body,
        out_shape=[jax.ShapeDtypeStruct(*out) for out in outs],
        in_specs=in_specs,
        out_specs=[pl.BlockSpec(memory_space=pltpu.VMEM)] * len(outs),
        scratch_shapes=shapes,
        cost_estimate=pl.CostEstimate(flops=int(micros * 1e9), bytes_accessed=0, transcendentals=0),
        compiler_params=pltpu.CompilerParams(vmem_limit_bytes=limit * 1024 * 1024),
    )(*hbm, *vmem, *after)


def shards(fields, grad_out, block_count, ocean, kernel, ln_gain, w_in, w_out, layer_scale):
    samples, slots, tile_rows, tile_cols, channels = fields.shape
    hidden = w_in.shape[1]
    shape = Shape(slots, channels, hidden)
    cells, parts, pitch = shape.cells, shape.parts, shape.pitch
    grid = fields.shape
    fields = fields.reshape(cells, channels)
    tangent = grad_out.reshape(cells, channels)
    taps_in = kernel
    gain = ln_gain.reshape(1, channels)
    scale = layer_scale.reshape(1, channels)

    def bind(body):
        return functools.partial(body, shape)

    def strip(rows):
        return ((parts, rows * pitch, LANES), F32)

    edge = ((shape.edge_rows, channels), BF16)
    turned = ((HALF * pitch, channels), BF16)
    whole = ((cells, channels), BF16)
    whole_f = ((cells, channels), F32)
    wide = ((cells, hidden), BF16)
    narrow = ((cells, LANES), F32)
    row = ((1, channels), F32)
    eight = ((8, channels), F32)
    taps = ((parts, KSIZE * KSIZE, 8, LANES), F32)
    count_s = (block_count.shape, jnp.int32)
    ocean_s = (ocean.shape, jnp.int32)
    flat = ((channels, cells), BF16)
    late = TILE - shape.early

    first, second = call(
        bind(prep_kernel), [edge, edge], [count_s, ((parts, cells, LANES), F32)],
        [block_count], [fields], 1, 1.0,
    )
    dproj, dproj_t = call(
        bind(cotangent_kernel), [whole, flat], [count_s, ocean_s],
        [block_count, ocean], [tangent, scale], 2, 1.0, after=[first],
    )
    first, second = swap(first, "first"), swap(second, "second")
    band, fold = call(
        bind(band_kernel), [strip(TILE + HALF), turned], [count_s, ocean_s],
        [block_count, ocean], [fields, first, second], 2, 1.0, after=[dproj],
    )
    fold = swap(fold, "fold")
    normed, yhat, inverse, dact = call(
        bind(early_kernel), [whole, whole_f, narrow, ((cells, hidden), F32)],
        [taps, ((parts, shape.early * shape.columns, LANES), F32)],
        [], [taps_in, gain, w_out, band, dproj], 0, 4.5,
    )
    keep, give, activated, dpreact, yhat, inverse = call(
        bind(late_kernel),
        [((hidden, channels), F32), ((hidden, channels), BF16), wide, wide, whole_f, narrow],
        [
            taps, strip(late + 2 * HALF), ((parts, late * shape.columns, LANES), F32), whole, flat,
        ],
        [], [taps_in, gain, w_in, band, fold, normed, yhat, inverse, dproj_t, dact], 0, 5.0,
    )

    order = stages()
    rows = hidden // 2

    def half_step(at, rows):
        return functools.partial(halve_kernel, order[at], order[at + 1]), [
            ((rows, channels), F32), ((rows // 2, channels), BF16),
        ]

    came = core_swap(give)
    conv_grad, gain_part = call(
        bind(norm_grad_kernel), [whole, eight], [], [], [w_in, gain, dpreact, yhat, inverse], 0, 1.0,
    )
    mine, send = call(
        functools.partial(join_kernel, order[0]),
        [((hidden, channels), F32), ((rows, channels), BF16)], [], [], [keep, came], after=[conv_grad], micros=0.3,
    )
    came = bit_swap(send, order[0])
    core_grad, fold_back = call(
        bind(back_kernel), [strip(TILE + HALF), turned], [count_s, strip(TILE), taps],
        [block_count], [taps_in, conv_grad], 1, 4.0, after=[send],
    )
    body, outs = half_step(0, rows)
    mine, send = call(body, outs, [], [], [mine, came], after=[fold_back], micros=0.3)
    came = bit_swap(send, order[1])
    fold_back = swap(fold_back, "fold")
    state, scale_part = call(
        bind(state_kernel), [whole, eight], [count_s, ocean_s],
        [block_count, ocean], [fields, tangent, w_out, scale, activated], 2, 1.5, after=[send],
    )
    rows //= 2
    body, outs = half_step(1, rows)
    mine, send = call(body, outs, [], [], [mine, came], after=[scale_part], micros=0.3)
    came = bit_swap(send, order[2])
    small_rows = -(-(KSIZE * KSIZE + 2) // 16) * 16
    (small,) = call(
        bind(taps_kernel), [((small_rows, channels), F32)], [strip(TILE + 2 * HALF), strip(TILE)],
        [], [band, fold, conv_grad, gain_part, scale_part], 0, 3.5, after=[send],
    )
    rows //= 2
    body, outs = half_step(2, rows)
    mine, send = call(body, outs, [], [], [mine, came], after=[small], micros=0.3)
    mine, send = halved(mine, send, order[3:])
    came = bit_swap(send, order[-1])
    folded, first, second = call(
        bind(rims_kernel), [strip(TILE), edge, edge], [count_s], [block_count], [core_grad, fold_back], 1, 1.0,
        after=[send],
    )
    rows = came.shape[0]
    if rows % 16 == 0:
        (payload,) = call(
            functools.partial(turn_kernel, order[-1]), [((rows + small_rows, channels), BF16)],
            [], [], [mine, came, small], after=[first], micros=0.3,
        )
    else:
        bit = bit_here(order[-1])
        share = lax.dynamic_index_in_dim(mine.reshape(2, rows, channels), bit, 0, keepdims=False)
        payload = jnp.concatenate([share + came.astype(F32), small]).astype(BF16)
    came = bit_swap(payload, order[-1])
    first, second = swap(first, "first"), swap(second, "second")
    grad_fields, done = call(
        bind(final_kernel), [whole, ((8, LANES), F32)], [count_s, ocean_s, strip(TILE)],
        [block_count, ocean], [tangent, folded, first, second], 2, 1.5, after=[payload],
    )
    after = [done]
    for at in reversed(range(len(order))):
        copies = 2 if at == 0 else 1
        if rows % 16 == 0:
            (payload,) = call(
                functools.partial(double_kernel, order[at], small_rows),
                [((2 * rows + copies * small_rows, channels), BF16)],
                [], [], [payload, came], after=after, micros=0.3,
            )
        else:
            first = bit_here(order[at]) == 0
            low, high = payload[:rows], came[:rows]
            small = payload[rows:].astype(F32) + came[rows:].astype(F32)
            joined = [jnp.where(first, low, high), jnp.where(first, high, low), small.astype(BF16)]
            payload = jnp.concatenate(joined)
        after = []
        rows *= 2
        came = bit_swap(payload, order[at - 1]) if at else core_swap(payload)
    total = samples * lax.axis_size("dp") * slots * lax.axis_size(TILES) * tile_rows * tile_cols
    w_in_sum, w_out_sum, kernel_sum, gain_sum, scale_sum = call(
        functools.partial(unpack_kernel, total ** (-0.5)),
        [((channels, hidden), F32), ((hidden, channels), F32), (kernel.shape, F32), row, row],
        [], [], [payload, came], 0, 1.5,
    )
    return (
        state.reshape(grid),
        grad_fields.reshape(grid),
        kernel_sum,
        gain_sum.reshape(ln_gain.shape),
        w_in_sum,
        w_out_sum,
        scale_sum.reshape(layer_scale.shape),
    )


def solution(mesh):
    cores = Mesh(mesh.devices.reshape(-1, 2, mesh.devices.shape[1]), ("chips", "core", "dp"))
    banded = P("dp", TILES, None, None, None)
    placed = (banded, banded, P(TILES), P(TILES), P(), P(), P(), P(), P())
    return jax.shard_map(
        shards,
        mesh=cores,
        in_specs=placed,
        out_specs=(banded, banded, P(), P(), P(), P(), P()),
        check_vma=False,
    )
```

```python
import functools

import jax
import jax.numpy as jnp
from jax import lax
from jax.experimental import pallas as pl
from jax.experimental.pallas import tpu as pltpu
from jax.sharding import Mesh, PartitionSpec as P

KSIZE = 7
HALF = KSIZE // 2
TILE = 16
EPS = 1e-06
TILES = ("chips", "core")
F32 = jnp.float32
BF16 = jnp.bfloat16
LANES = 128
LEFT = 8
GELU_C = 0.7978845608028654
GELU_A = 0.044715


def dot(lhs, rhs, lhs_dim, rhs_dim):
    return lax.dot_general(
        lhs, rhs, (((lhs_dim,), (rhs_dim,)), ((), ())), preferred_element_type=F32
    )


def cycle_rank():
    count = lax.axis_size(TILES)
    here = lax.axis_index("chips") * lax.axis_size("core") + lax.axis_index("core")
    return jnp.where(here < count // 2, here, count - 1 + count // 2 - here)


def is_even():
    return lax.rem(cycle_rank(), 2) == 0


class Fetch:
    def __init__(self, sems, *pairs):
        self.copies = [
            pltpu.make_async_copy(source, target, sems.at[at]) for at, (source, target) in enumerate(pairs)
        ]
        for copy in self.copies:
            copy.start()

    def wait(self, *which):
        for at in which:
            self.copies[at].wait()


def slot_flag(count_ref, ocean_ref, slot):
    live = jnp.logical_and(slot < count_ref[0], ocean_ref[slot] > 0)
    return jnp.where(live, 1.0, 0.0).astype(F32)


class Shape:
    def __init__(self, slots, channels, hidden):
        self.slots = slots
        self.channels = channels
        self.hidden = hidden
        self.parts = channels // LANES
        self.columns = slots * TILE
        self.pitch = self.columns + 2 * LEFT
        self.cells = slots * TILE * TILE
        self.edge_rows = HALF * TILE
        self.early = 12

    def lanes(self, part):
        return slice(part * LANES, (part + 1) * LANES)


def edge_planes(shape, source, start, stride):
    return [
        jnp.concatenate(
            [source[part, pl.ds(start + col, TILE, stride=stride), :] for part in range(shape.parts)], axis=1
        )
        for col in range(HALF)
    ]


def send_edges(shape, left, right, first, second):
    even = is_even()
    for col in range(HALF):
        rows = pl.ds(col * TILE, TILE)
        first[rows, :] = jnp.where(even, right[col], left[col]).astype(BF16)
        second[rows, :] = jnp.where(even, left[col], right[col]).astype(BF16)


def flip_matrix(size, last):
    to = lax.broadcasted_iota(jnp.int32, (size, size), 0)
    frm = lax.broadcasted_iota(jnp.int32, (size, size), 1)
    return jnp.where(to + frm == last, 1.0, 0.0).astype(BF16)


def prep_kernel(shape, count_hbm, fields, first, second, count, work, sems):
    fetch = Fetch(sems, (count_hbm, count))
    for part in range(shape.parts):
        work[part] = fields[:, shape.lanes(part)].astype(F32)
    left = edge_planes(shape, work, 0, TILE)
    fetch.wait(0)
    right = edge_planes(shape, work, (count[0] - 1) * TILE * TILE + TILE - HALF, TILE)
    send_edges(shape, left, right, first, second)


def top_kernel(shape, count_hbm, ocean_hbm, fields, fold, count, ocean, sems):
    fetch = Fetch(sems, (count_hbm, count), (ocean_hbm, ocean))
    fetch.wait(0, 1)
    flip = flip_matrix(shape.columns, count[0] * TILE - 1)
    for k in range(HALF):
        cells = jnp.concatenate(
            [
                fields[pl.ds(slot * TILE * TILE + (TILE - 1 - k) * TILE, TILE), :].astype(F32)
                * slot_flag(count, ocean, slot)
                for slot in range(shape.slots)
            ]
        )
        turned = dot(flip, cells.astype(BF16), 1, 0)
        fold[pl.ds(k * shape.columns, shape.columns), :] = turned.astype(BF16)


def band_kernel(shape, count_hbm, ocean_hbm, fields, first, second, band, rims, count, ocean, sems):
    fetch = Fetch(sems, (count_hbm, count), (ocean_hbm, ocean))
    even = is_even()
    blank = jnp.zeros((LEFT, LANES), F32)
    per_slot = TILE * TILE
    for part in range(shape.parts):
        band[part, pl.ds(0, HALF * shape.pitch), :] = jnp.zeros((HALF * shape.pitch, LANES), F32)
        for row in range(TILE):
            base = (row + HALF) * shape.pitch
            band[part, pl.ds(base, LEFT), :] = blank
            band[part, pl.ds(base + LEFT + shape.columns, LEFT), :] = blank
    fetch.wait(0, 1)
    used = count[0] * TILE
    flags = [slot_flag(count, ocean, slot) for slot in range(shape.slots)]
    top = HALF * shape.pitch
    for part in range(shape.parts):
        for row in range(TILE):
            base = (row + HALF) * shape.pitch
            for slot in range(shape.slots):
                cells = fields[pl.ds(slot * per_slot + row * TILE, TILE), shape.lanes(part)]
                band[part, pl.ds(base + LEFT + slot * TILE, TILE), :] = cells.astype(F32) * flags[slot]
        for col in range(HALF):
            rows = pl.ds(col * TILE, TILE)
            one = first[rows, shape.lanes(part)].astype(F32)
            two = second[rows, shape.lanes(part)].astype(F32)
            west = jnp.where(even, two, one)
            east = jnp.where(even, one, two)
            band[part, pl.ds(top + LEFT - HALF + col, TILE, stride=shape.pitch), :] = west
            band[part, pl.ds(top + LEFT + used + col, TILE, stride=shape.pitch), :] = east
    for k in range(HALF):
        base = (HALF + TILE - 1 - k) * shape.pitch
        east = pl.multiple_of(base + LEFT + used, LEFT)
        for part in range(shape.parts):
            ends = jnp.concatenate([band[part, pl.ds(base, LEFT), :], band[part, pl.ds(east, LEFT), :]])
            rims[pl.ds(k * 2 * LEFT, 2 * LEFT), shape.lanes(part)] = ends.astype(BF16)


def turn_rows(shape, used, source, rows, fold):
    flip = flip_matrix(shape.pitch, used + 2 * LEFT - 1)
    for k, row in enumerate(rows):
        at = pl.ds(row * shape.pitch, shape.pitch)
        cells = jnp.concatenate([source[part, at, :] for part in range(shape.parts)], axis=1)
        turned = dot(flip, cells.astype(BF16), 1, 0)
        fold[pl.ds(k * shape.pitch, shape.pitch), :] = turned.astype(BF16)


def put_fold(shape, used, fold, rims, parts, padded, first_row, work):
    blank = jnp.zeros((LEFT, LANES), F32)
    for at, part in enumerate(parts):
        work[at] = rims[:, shape.lanes(part)].astype(F32)
        for k in range(HALF):
            base = (first_row + k) * shape.pitch
            padded[at, pl.ds(base, LEFT), :] = blank
            padded[at, pl.ds(base + LEFT + shape.columns, LEFT), :] = blank
            cells = fold[pl.ds(k * shape.columns, shape.columns), shape.lanes(part)]
            padded[at, pl.ds(base + LEFT, shape.columns), :] = cells.astype(F32)
            for col in range(HALF):
                west = work[at, pl.ds(k * 2 * LEFT + LEFT - 1 - col, 1), :]
                east = work[at, pl.ds(k * 2 * LEFT + LEFT + col, 1), :]
                padded[at, pl.ds(base + LEFT - 1 - col, 1), :] = east
                padded[at, pl.ds(base + LEFT + used + col, 1), :] = west


def spread_taps(shape, kernel, taps):
    for above in range(KSIZE):
        rows = kernel[above].astype(F32)
        for part in range(shape.parts):
            for shift in range(KSIZE):
                row = rows[shift : shift + 1, shape.lanes(part)]
                taps[part, above * KSIZE + shift] = jnp.broadcast_to(row, (8, LANES))


def convolve(shape, rows, padded, taps, convolved):
    run = shape.columns // 8
    pair = 2
    origin = LEFT - HALF

    def two_rows(step, carry):
        row = step * pair
        for part in range(shape.parts):
            sums = [[None] * run for _ in range(pair)]
            for above in range(KSIZE + pair - 1):
                base = (row + above) * shape.pitch + origin
                loaded = [
                    padded[part, pl.ds(base + at, 8, stride=run), :]
                    for at in range(run + KSIZE - 1)
                ]
                for which in range(pair):
                    tap_row = above - which
                    if not 0 <= tap_row < KSIZE:
                        continue
                    for shift in range(KSIZE):
                        weight = taps[part, tap_row * KSIZE + shift]
                        for at in range(run):
                            term = weight * loaded[at + shift]
                            old = sums[which][at]
                            sums[which][at] = term if old is None else old + term
            for which in range(pair):
                for at in range(run):
                    start = (row + which) * shape.columns + at
                    convolved[part, pl.ds(start, 8, stride=run), :] = sums[which][at]
        return carry

    lax.fori_loop(0, rows // pair, two_rows, 0)


def normalise(shape, rows, first_row, convolved, gain, normed, yhat, inverse):
    def one_row(row, carry):
        for slot in range(shape.slots):
            start = pl.multiple_of(row * shape.columns + slot * TILE, TILE)
            at = slot * TILE * TILE + (first_row + row) * TILE
            out = pl.ds(pl.multiple_of(at, TILE), TILE)
            parts = [convolved[part, pl.ds(start, TILE), :] for part in range(shape.parts)]
            mean = jnp.sum(sum(parts), axis=-1, keepdims=True) * (1.0 / shape.channels)
            parts = [value - mean for value in parts]
            square = jnp.sum(sum(value * value for value in parts), axis=-1, keepdims=True)
            scale = lax.rsqrt(square * (1.0 / shape.channels) + EPS)
            inverse[out, :] = jnp.broadcast_to(scale, (TILE, LANES))
            for part in range(shape.parts):
                value = parts[part] * scale
                yhat[out, shape.lanes(part)] = value
                normed[out, shape.lanes(part)] = (value * gain[:, shape.lanes(part)]).astype(BF16)
        return carry

    lax.fori_loop(0, rows, one_row, 0, unroll=2)


def early_kernel(
    shape, count_hbm, ocean_hbm, kernel, gain, w_out, scale, tangent, band,
    normed, yhat, inverse, dproj_t, dact,
    count, ocean, taps, convolved, dproj, sems,
):
    fetch = Fetch(sems, (count_hbm, count), (ocean_hbm, ocean))
    spread_taps(shape, kernel, taps)
    convolve(shape, shape.early, band, taps, convolved)
    normalise(shape, shape.early, 0, convolved, gain, normed, yhat, inverse)
    fetch.wait(0, 1)
    per_slot = TILE * TILE
    for slot in range(shape.slots):
        rows = pl.ds(slot * per_slot, per_slot)
        flag = slot_flag(count, ocean, slot)
        scaled = (tangent[rows, :].astype(F32) * (scale[...] * flag)).astype(BF16)
        dproj[rows, :] = scaled
        dproj_t[:, slot * per_slot : (slot + 1) * per_slot] = scaled.T
        for h in range(shape.hidden // shape.channels):
            cols = slice(h * shape.channels, (h + 1) * shape.channels)
            dact[rows, cols] = dot(dproj[rows, :], w_out[cols, :], 1, 1)


def late_kernel(
    shape, count_hbm, kernel, gain, w_in, band, fold, rims, normed_in, yhat_in, inverse_in, dproj_t, dact,
    keep, give, activated, dpreact, yhat, inverse,
    count, taps, padded, convolved, normed, normed_t, work, sems,
):
    fetch = Fetch(sems, (count_hbm, count))
    late = TILE - shape.early
    kept = late + HALF
    for part in range(shape.parts):
        rows = pl.ds(shape.early * shape.pitch, kept * shape.pitch)
        padded[part, pl.ds(0, kept * shape.pitch), :] = band[part, rows, :]
    done = shape.early * TILE
    for slot in range(shape.slots):
        rows = pl.ds(slot * TILE * TILE, done)
        normed[rows, :] = normed_in[rows, :]
        yhat[rows, :] = yhat_in[rows, :]
        inverse[rows, :] = inverse_in[rows, :]
    spread_taps(shape, kernel, taps)
    fetch.wait(0)
    put_fold(shape, count[0] * TILE, fold, rims, range(shape.parts), padded, kept, work)
    convolve(shape, late, padded, taps, convolved)
    normalise(shape, late, shape.early, convolved, gain, normed, yhat, inverse)
    per_slot = TILE * TILE
    for slot in range(shape.slots):
        normed_t[:, slot * per_slot : (slot + 1) * per_slot] = normed[pl.ds(slot * per_slot, per_slot), :].T
    keeps_in = lax.axis_index("core") == 0
    block = shape.channels
    for h in range(shape.hidden // block):
        cols = slice(h * block, (h + 1) * block)
        for slot in range(shape.slots):
            rows = pl.ds(slot * per_slot, per_slot)
            pre = dot(normed[rows, :], w_in[:, cols], 1, 0)
            square = pre * pre
            inner = pre * (GELU_C + (GELU_C * GELU_A) * square)
            gate = 0.5 + 0.5 * jnp.tanh(inner)
            activated[rows, cols] = (pre * gate).astype(BF16)
            slope = pre * (2.0 * GELU_C + (6.0 * GELU_C * GELU_A) * square)
            grown = gate + slope * (gate - gate * gate)
            dpreact[rows, cols] = (dact[rows, cols] * grown).astype(BF16)
        rows = slice(h * block, (h + 1) * block)
        of_in = dot(normed_t[...], dpreact[:, cols], 1, 0)
        of_out = dot(dproj_t[...], activated[:, cols], 1, 0)
        keep[rows, :] = jnp.where(keeps_in, of_in, of_out)
        give[rows, :] = jnp.where(keeps_in, of_out, of_in).astype(BF16)


def fold_sum(value):
    return jnp.sum(value.reshape(-1, 8, value.shape[-1]), axis=0)


def norm_grad_kernel(shape, w_in, gain, dpreact, yhat, inverse, conv_grad, gain_part):
    chunk = TILE * TILE
    total = jnp.zeros((8, shape.channels), F32)
    for slot in range(shape.slots):
        rows = pl.ds(slot * chunk, chunk)
        dnormed = dot(dpreact[rows, :], w_in[...], 1, 1)
        unit = yhat[rows, :]
        total += fold_sum(dnormed * unit)
        dhat = dnormed * gain[...]
        mean = jnp.sum(dhat, axis=-1, keepdims=True) * (1.0 / shape.channels)
        along = jnp.sum(dhat * unit, axis=-1, keepdims=True) * (1.0 / shape.channels)
        scale = jnp.concatenate([inverse[rows, :]] * shape.parts, axis=1)
        conv_grad[rows, :] = (scale * (dhat - mean - unit * along)).astype(BF16)
    gain_part[...] = total


def state_kernel(
    shape, count_hbm, ocean_hbm, fields, tangent, w_out, scale, activated,
    state, scale_part,
    count, ocean, sems,
):
    fetch = Fetch(sems, (count_hbm, count), (ocean_hbm, ocean))
    fetch.wait(0, 1)
    chunk = TILE * TILE
    total = jnp.zeros((8, shape.channels), F32)
    for slot in range(shape.slots):
        rows = pl.ds(slot * chunk, chunk)
        flag = slot_flag(count, ocean, slot)
        projected = dot(activated[rows, :], w_out[...], 1, 0)
        kept = fields[rows, :].astype(F32) + scale[...] * projected
        state[rows, :] = (flag * kept).astype(BF16)
        total += fold_sum(flag * tangent[rows, :].astype(F32) * projected)
    scale_part[...] = total


def place_grad(shape, conv_grad, parts, spaced):
    blank = jnp.zeros((LEFT, LANES), F32)
    for at, part in enumerate(parts):
        for row in range(TILE):
            base = row * shape.pitch
            spaced[at, pl.ds(base, LEFT), :] = blank
            spaced[at, pl.ds(base + LEFT + shape.columns, LEFT), :] = blank
            for slot in range(shape.slots):
                cells = conv_grad[pl.ds(slot * TILE * TILE + row * TILE, TILE), shape.lanes(part)]
                spaced[at, pl.ds(base + LEFT + slot * TILE, TILE), :] = cells.astype(F32)


def taps_kernel(
    shape, part, count_hbm, band, fold, rims, conv_grad, gain_part, scale_part, small, count, padded, spaced, work, sems
):
    fetch = Fetch(sems, (count_hbm, count))
    taps = KSIZE * KSIZE
    lanes = shape.lanes(part)
    small[...] = jnp.zeros_like(small)
    small[pl.ds(taps, 1), :] = jnp.sum(gain_part[:, lanes], axis=0, keepdims=True)
    small[pl.ds(taps + 1, 1), :] = jnp.sum(scale_part[:, lanes], axis=0, keepdims=True)
    place_grad(shape, conv_grad, [part], spaced)
    kept = TILE + HALF
    padded[0, pl.ds(0, kept * shape.pitch), :] = band[part]
    fetch.wait(0)
    put_fold(shape, count[0] * TILE, fold, rims, [part], padded, kept, work)
    run = shape.columns // 8
    origin = LEFT - HALF
    for above in range(KSIZE):

        def one_row(row, sums, above=above):
            base = (row + above) * shape.pitch + origin
            loaded = [padded[0, pl.ds(base + at, 8, stride=run), :] for at in range(run + KSIZE - 1)]
            start = row * shape.pitch + LEFT
            grads = [spaced[0, pl.ds(start + at, 8, stride=run), :] for at in range(run)]
            sums = list(sums)
            for shift in range(KSIZE):
                for at in range(run):
                    sums[shift] = sums[shift] + grads[at] * loaded[at + shift]
            return tuple(sums)

        blank = tuple(jnp.zeros((8, LANES), F32) for _ in range(KSIZE))
        sums = lax.fori_loop(0, TILE, one_row, blank, unroll=2)
        for shift in range(KSIZE):
            small[pl.ds(above * KSIZE + shift, 1), :] = jnp.sum(sums[shift], axis=0, keepdims=True)


def back_kernel(shape, count_hbm, kernel, conv_grad, core_grad, fold, count, spaced, taps, sems):
    fetch = Fetch(sems, (count_hbm, count))
    place_grad(shape, conv_grad, range(shape.parts), spaced)
    blank = jnp.zeros((LEFT, LANES), F32)
    for part in range(shape.parts):
        for row in range(TILE + HALF):
            core_grad[part, pl.ds(row * shape.pitch, LEFT), :] = blank
            core_grad[part, pl.ds((row + 1) * shape.pitch - LEFT, LEFT), :] = blank
    fetch.wait(0)
    spread_taps(shape, kernel, taps)
    run = -(-(shape.columns + 2 * HALF) // 8)

    def one_row(row, tap_rows):
        for part in range(shape.parts):
            sums = [None] * run
            for above in tap_rows:
                base = (row - above) * shape.pitch + LEFT
                loaded = [
                    spaced[part, pl.ds(base + at - KSIZE + 1, 8, stride=run), :]
                    for at in range(run + KSIZE - 1)
                ]
                for shift in range(KSIZE):
                    weight = taps[part, above * KSIZE + shift]
                    for at in range(run):
                        term = weight * loaded[at - shift + KSIZE - 1]
                        sums[at] = term if sums[at] is None else sums[at] + term
            start = (row - HALF) * shape.pitch + LEFT - HALF
            for at in range(run):
                core_grad[part, pl.ds(start + at, 8, stride=run), :] = sums[at]

    inner = (KSIZE - 1, TILE - 1)
    for row in range(HALF, TILE + 2 * HALF):
        if not inner[0] <= row <= inner[1]:
            low = max(0, row - TILE + 1)
            one_row(row, range(low, min(KSIZE - 1, row) + 1))

    def inner_row(step, carry):
        one_row(step, range(KSIZE))
        return carry

    lax.fori_loop(inner[0], inner[1] + 1, inner_row, 0)
    turn_rows(shape, count[0] * TILE, core_grad, (TILE, TILE + 1, TILE + 2), fold)


def rims_kernel(shape, count_hbm, core_grad, fold, folded, first, second, count, sems):
    fetch = Fetch(sems, (count_hbm, count))
    for part in range(shape.parts):
        folded[part] = core_grad[part, pl.ds(0, TILE * shape.pitch), :]
        for k in range(HALF):
            rows = pl.ds((TILE - 1 - k) * shape.pitch, shape.pitch)
            returned = fold[pl.ds(k * shape.pitch, shape.pitch), shape.lanes(part)]
            folded[part, rows, :] += returned.astype(F32)
    fetch.wait(0)
    west = edge_planes(shape, folded, LEFT - HALF, shape.pitch)
    east = edge_planes(shape, folded, LEFT + count[0] * TILE, shape.pitch)
    send_edges(shape, west, east, first, second)


def final_kernel(
    shape, count_hbm, ocean_hbm, tangent, folded, first, second,
    grad_fields, done,
    count, ocean, work, sems,
):
    fetch = Fetch(sems, (count_hbm, count), (ocean_hbm, ocean))
    even = is_even()
    done[...] = jnp.zeros_like(done)
    work[...] = folded[...]
    fetch.wait(0, 1)
    used = count[0] * TILE
    for part in range(shape.parts):
        for col in range(HALF):
            planes = pl.ds(col * TILE, TILE)
            one = first[planes, shape.lanes(part)].astype(F32)
            two = second[planes, shape.lanes(part)].astype(F32)
            to_tail = jnp.where(even, one, two)
            to_head = jnp.where(even, two, one)
            head = pl.ds(LEFT + col, TILE, stride=shape.pitch)
            work[part, head, :] = work[part, head, :] + to_head
            tail = pl.ds(LEFT + used - HALF + col, TILE, stride=shape.pitch)
            work[part, tail, :] = work[part, tail, :] + to_tail
        for slot in range(shape.slots):
            flag = slot_flag(count, ocean, slot)
            for row in range(TILE):
                rows = pl.ds(slot * TILE * TILE + row * TILE, TILE)
                cells = work[part, pl.ds(row * shape.pitch + LEFT + slot * TILE, TILE), :]
                total = tangent[rows, shape.lanes(part)].astype(F32) + cells
                grad_fields[rows, shape.lanes(part)] = (flag * total).astype(BF16)


def unpack_kernel(norm, own, came, w_in, w_out, kernel_sum, gain_sum, scale_sum):
    is_first = lax.axis_index("core") == 0
    channels = own.shape[-1]
    hidden = w_out.shape[0]
    for h in range(hidden // channels):
        rows = slice(h * channels, (h + 1) * channels)
        mine = own[rows, :].astype(F32) * norm
        theirs = came[rows, :].astype(F32) * norm
        w_in[:, rows] = jnp.where(is_first, mine, theirs)
        w_out[rows, :] = jnp.where(is_first, theirs, mine).T
    extra = (own.shape[0] - hidden) // 2
    high, low = pl.ds(hidden, extra), pl.ds(hidden + extra, extra)
    small = own[high, :].astype(F32) + own[low, :].astype(F32)
    small = (small + (came[high, :].astype(F32) + came[low, :].astype(F32))) * norm
    for above in range(KSIZE):
        kernel_sum[above] = small[above * KSIZE : (above + 1) * KSIZE, :]
    gain_sum[...] = small[KSIZE * KSIZE : KSIZE * KSIZE + 1, :]
    scale_sum[...] = small[KSIZE * KSIZE + 1 : KSIZE * KSIZE + 2, :]


def pairs_of(kind):
    count = lax.axis_size(TILES)
    half = count // 2
    place = [rank if rank < half else count - 1 + half - rank for rank in range(count)]
    partner = {
        "first": lambda rank: rank ^ 1,
        "second": lambda rank: ((rank + 1) ^ 1) - 1,
        "fold": lambda rank: count - 1 - rank,
    }[kind]
    return [(place[rank], place[partner(rank) % count]) for rank in range(count)]


def swap(block, kind):
    return lax.ppermute(block, TILES, pairs_of(kind))


def core_swap(block):
    return lax.ppermute(block, "core", [(0, 1), (1, 0)])


def stages():
    chip_bits = lax.axis_size("chips").bit_length() - 1
    rest = list(range(2, chip_bits))
    return list(zip([0, -1, 1] + rest, [1, 0, -1] + rest))


def bit_swap(block, stage):
    chips, cores, samples = (lax.axis_size(axis) for axis in ("chips", "core", "dp"))
    pairs = []
    for chip in range(chips):
        for core in range(cores):
            for sample in range(samples):
                bit = stage[core]
                to = (chip, sample ^ 1) if bit < 0 else (chip ^ (1 << bit), sample)
                pairs.append(
                    ((chip * cores + core) * samples + sample, (to[0] * cores + core) * samples + to[1])
                )
    return lax.ppermute(block, ("chips", "core", "dp"), pairs)


def bit_here(stage):
    bits = [
        lax.axis_index("dp") if bit < 0 else lax.axis_index("chips") >> bit & 1 for bit in stage
    ]
    return jnp.where(lax.axis_index("core") == 0, bits[0], bits[1])


def half_rows(bit, rows):
    return pl.ds(pl.multiple_of(bit * rows, rows), rows)


def join_kernel(stage, keep, came, mine, send):
    rows = send.shape[0]
    mine[...] = keep[...] + came[...].astype(F32)
    send[...] = mine[half_rows(1 - bit_here(stage), rows), :].astype(BF16)


def halve_kernel(stage, following, whole, came, mine, send):
    rows = mine.shape[0]
    mine[...] = whole[half_rows(bit_here(stage), rows), :] + came[...].astype(F32)
    send[...] = mine[half_rows(1 - bit_here(following), rows // 2), :].astype(BF16)


def turn_kernel(stage, whole, came, *refs):
    small, payload = refs[:-1], refs[-1]
    rows = came.shape[0]
    share = whole[half_rows(bit_here(stage), rows), :] + came[...].astype(F32)
    payload[pl.ds(0, rows), :] = share.astype(BF16)
    for part, ref in enumerate(small):
        payload[pl.ds(rows, ref.shape[0]), part * LANES : (part + 1) * LANES] = ref[...].astype(BF16)


def add_kernel(own, came, payload):
    payload[...] = (own[...].astype(F32) + came[...].astype(F32)).astype(BF16)


def double_kernel(stage, extra, own, came, payload):
    rows = own.shape[0] - extra
    bit = bit_here(stage)
    payload[half_rows(bit, rows), :] = own[pl.ds(0, rows), :]
    payload[half_rows(1 - bit, rows), :] = came[pl.ds(0, rows), :]
    total = own[pl.ds(rows, extra), :].astype(F32) + came[pl.ds(rows, extra), :].astype(F32)
    high = total.astype(BF16)
    payload[pl.ds(2 * rows, extra), :] = high
    if payload.shape[0] > 2 * rows + extra:
        payload[pl.ds(2 * rows + extra, extra), :] = (total - high.astype(F32)).astype(BF16)


def halved(mine, send, order):
    for at, stage in enumerate(order[:-1]):
        came = bit_swap(send, stage)
        rows = came.shape[0]
        bit = bit_here(stage)
        mine = lax.dynamic_index_in_dim(mine.reshape(2, rows, -1), bit, 0, keepdims=False) + came.astype(F32)
        bit = bit_here(order[at + 1])
        halves = mine.reshape(2, rows // 2, -1)
        send = lax.dynamic_index_in_dim(halves, 1 - bit, 0, keepdims=False).astype(BF16)
    return mine, send


def call(kernel, outs, scratch, hbm, vmem, copies=0, micros=1.0, after=(), limit=20):
    in_specs = [pl.BlockSpec(memory_space=pl.ANY)] * len(hbm)
    in_specs += [pl.BlockSpec(memory_space=pltpu.VMEM)] * len(vmem)
    in_specs += [pl.BlockSpec(memory_space=pl.ANY)] * len(after)
    shapes = [pltpu.SMEM(*one) if one[1] == jnp.int32 else pltpu.VMEM(*one) for one in scratch]
    if copies:
        shapes.append(pltpu.SemaphoreType.DMA((copies,)))
    taken = len(hbm) + len(vmem)

    def body(*refs):
        kernel(*refs[:taken], *refs[taken + len(after) :])

    return pl.pallas_call(
        body,
        out_shape=[jax.ShapeDtypeStruct(*out) for out in outs],
        in_specs=in_specs,
        out_specs=[pl.BlockSpec(memory_space=pltpu.VMEM)] * len(outs),
        scratch_shapes=shapes,
        cost_estimate=pl.CostEstimate(flops=int(micros * 1e9), bytes_accessed=0, transcendentals=0),
        compiler_params=pltpu.CompilerParams(vmem_limit_bytes=limit * 1024 * 1024),
    )(*hbm, *vmem, *after)


def shards(fields, grad_out, block_count, ocean, kernel, ln_gain, w_in, w_out, layer_scale):
    samples, slots, tile_rows, tile_cols, channels = fields.shape
    hidden = w_in.shape[1]
    shape = Shape(slots, channels, hidden)
    cells, parts, pitch = shape.cells, shape.parts, shape.pitch
    grid = fields.shape
    fields = fields.reshape(cells, channels)
    tangent = grad_out.reshape(cells, channels)
    taps_in = kernel
    gain = ln_gain.reshape(1, channels)
    scale = layer_scale.reshape(1, channels)

    def bind(body):
        return functools.partial(body, shape)

    def strip(rows):
        return ((parts, rows * pitch, LANES), F32)

    edge = ((shape.edge_rows, channels), BF16)
    turned = ((HALF * pitch, channels), BF16)
    whole = ((cells, channels), BF16)
    whole_f = ((cells, channels), F32)
    wide = ((cells, hidden), BF16)
    narrow = ((cells, LANES), F32)
    row = ((1, channels), F32)
    eight = ((8, channels), F32)
    taps = ((parts, KSIZE * KSIZE, 8, LANES), F32)
    count_s = (block_count.shape, jnp.int32)
    ocean_s = (ocean.shape, jnp.int32)
    flat = ((channels, cells), BF16)
    ends = ((HALF * 2 * LEFT, channels), BF16)
    ends_f = ((parts, HALF * 2 * LEFT, LANES), F32)
    late = TILE - shape.early

    first, second = call(
        bind(prep_kernel), [edge, edge], [count_s, ((parts, cells, LANES), F32)],
        [block_count], [fields], 1, 1.0,
    )
    (fold,) = call(
        bind(top_kernel), [((HALF * shape.columns, channels), BF16)], [count_s, ocean_s],
        [block_count, ocean], [fields], 2, 0.5, after=[first],
    )
    first, second = swap(first, "first"), swap(second, "second")
    band, rims = call(
        bind(band_kernel), [strip(TILE + HALF), ends], [count_s, ocean_s],
        [block_count, ocean], [fields, first, second], 2, 1.0, after=[fold],
    )
    fold, rims = swap(fold, "fold"), swap(rims, "fold")
    normed, yhat, inverse, dproj_t, dact = call(
        bind(early_kernel), [whole, whole_f, narrow, flat, ((cells, hidden), F32)],
        [count_s, ocean_s, taps, ((parts, shape.early * shape.columns, LANES), F32), whole],
        [block_count, ocean], [taps_in, gain, w_out, scale, tangent, band], 2, 5.0,
    )
    keep, give, activated, dpreact, yhat, inverse = call(
        bind(late_kernel),
        [((hidden, channels), F32), ((hidden, channels), BF16), wide, wide, whole_f, narrow],
        [
            count_s, taps, strip(late + 2 * HALF), ((parts, late * shape.columns, LANES), F32), whole, flat,
            ends_f,
        ],
        [block_count],
        [taps_in, gain, w_in, band, fold, rims, normed, yhat, inverse, dproj_t, dact], 1, 5.0,
    )

    order = stages()
    rows = hidden // 2

    def half_step(at, rows):
        return functools.partial(halve_kernel, order[at], order[at + 1]), [
            ((rows, channels), F32), ((rows // 2, channels), BF16),
        ]

    def taps_part(part, after):
        (small,) = call(
            functools.partial(taps_kernel, shape, part), [((small_rows, LANES), F32)],
            [count_s, ((1, (TILE + 2 * HALF) * pitch, LANES), F32), ((1, TILE * pitch, LANES), F32), ends_f],
            [block_count], [band, fold, rims, conv_grad, gain_part, scale_part], 1, 1.8, after=after,
        )
        return small

    small_rows = -(-(KSIZE * KSIZE + 2) // 16) * 16
    came = core_swap(give)
    conv_grad, gain_part = call(
        bind(norm_grad_kernel), [whole, eight], [], [], [w_in, gain, dpreact, yhat, inverse], 0, 1.0,
    )
    mine, send = call(
        functools.partial(join_kernel, order[0]),
        [((hidden, channels), F32), ((rows, channels), BF16)], [], [], [keep, came], after=[conv_grad], micros=0.3,
    )
    came = bit_swap(send, order[0])
    state, scale_part = call(
        bind(state_kernel), [whole, eight], [count_s, ocean_s],
        [block_count, ocean], [fields, tangent, w_out, scale, activated], 2, 1.5, after=[send],
    )
    small = [taps_part(0, [send])]
    body, outs = half_step(0, rows)
    mine, send = call(body, outs, [], [], [mine, came], after=small, micros=0.3)
    came = bit_swap(send, order[1])
    small += [taps_part(part, [send]) for part in range(1, parts)]
    rows //= 2
    body, outs = half_step(1, rows)
    mine, send = call(body, outs, [], [], [mine, came], after=small[1:], micros=0.3)
    mine, send = halved(mine, send, order[2:-1])
    came = bit_swap(send, order[-2])
    rows = came.shape[0]
    if rows % 16 == 0:
        (payload,) = call(
            functools.partial(turn_kernel, order[-2]), [((rows + small_rows, channels), BF16)],
            [], [], [mine, came, *small], micros=0.3,
        )
    else:
        bit = bit_here(order[-2])
        share = lax.dynamic_index_in_dim(mine.reshape(2, rows, channels), bit, 0, keepdims=False)
        payload = jnp.concatenate([share + came.astype(F32), jnp.concatenate(small, axis=1)]).astype(BF16)
    came = bit_swap(payload, order[-1])
    core_grad, fold_back = call(
        bind(back_kernel), [strip(TILE + HALF), turned], [count_s, strip(TILE), taps],
        [block_count], [taps_in, conv_grad], 1, 4.0, after=[payload],
    )
    (payload,) = call(
        add_kernel, [(payload.shape, BF16)], [], [], [payload, came], after=[fold_back], micros=0.3,
    )
    fold_back = swap(fold_back, "fold")
    came = bit_swap(payload, order[-2])
    after = []
    for at in reversed(range(len(order) - 1)):
        copies = 2 if at == 0 else 1
        if rows % 16 == 0:
            (payload,) = call(
                functools.partial(double_kernel, order[at], small_rows),
                [((2 * rows + copies * small_rows, channels), BF16)],
                [], [], [payload, came], after=after, micros=0.3,
            )
        else:
            first = bit_here(order[at]) == 0
            low, high = payload[:rows], came[:rows]
            both = payload[rows:].astype(F32) + came[rows:].astype(F32)
            joined = [jnp.where(first, low, high), jnp.where(first, high, low), both.astype(BF16)]
            payload = jnp.concatenate(joined)
        after = []
        rows *= 2
        came = bit_swap(payload, order[at - 1]) if at else core_swap(payload)
        if at == 2:
            folded, first, second = call(
                bind(rims_kernel), [strip(TILE), edge, edge], [count_s], [block_count], [core_grad, fold_back], 1, 1.0,
                after=[payload],
            )
            after = [folded]
            first, second = swap(first, "first"), swap(second, "second")
        if at == 1:
            grad_fields, done = call(
                bind(final_kernel), [whole, ((8, LANES), F32)], [count_s, ocean_s, strip(TILE)],
                [block_count, ocean], [tangent, folded, first, second], 2, 1.5, after=[payload],
            )
            after = [done]
    total = samples * lax.axis_size("dp") * slots * lax.axis_size(TILES) * tile_rows * tile_cols
    w_in_sum, w_out_sum, kernel_sum, gain_sum, scale_sum = call(
        functools.partial(unpack_kernel, total ** (-0.5)),
        [((channels, hidden), F32), ((hidden, channels), F32), (kernel.shape, F32), row, row],
        [], [], [payload, came], 0, 1.5,
    )
    return (
        state.reshape(grid),
        grad_fields.reshape(grid),
        kernel_sum,
        gain_sum.reshape(ln_gain.shape),
        w_in_sum,
        w_out_sum,
        scale_sum.reshape(layer_scale.shape),
    )


def solution(mesh):
    cores = Mesh(mesh.devices.reshape(-1, 2, mesh.devices.shape[1]), ("chips", "core", "dp"))
    banded = P("dp", TILES, None, None, None)
    placed = (banded, banded, P(TILES), P(TILES), P(), P(), P(), P(), P())
    return jax.shard_map(
        shards,
        mesh=cores,
        in_specs=placed,
        out_specs=(banded, banded, P(), P(), P(), P(), P()),
        check_vma=False,
    )
```

```python
import functools

import jax
import jax.numpy as jnp
from jax import lax
from jax.experimental import pallas as pl
from jax.experimental.pallas import tpu as pltpu
from jax.sharding import Mesh, PartitionSpec as P

KSIZE = 7
HALF = KSIZE // 2
TILE = 16
EPS = 1e-06
TILES = ("chips", "core")
F32 = jnp.float32
BF16 = jnp.bfloat16
LANES = 128
LEFT = 8
GELU_C = 0.7978845608028654
GELU_A = 0.044715


def dot(lhs, rhs, lhs_dim, rhs_dim):
    return lax.dot_general(
        lhs, rhs, (((lhs_dim,), (rhs_dim,)), ((), ())), preferred_element_type=F32
    )


def cycle_rank():
    count = lax.axis_size(TILES)
    here = lax.axis_index("chips") * lax.axis_size("core") + lax.axis_index("core")
    return jnp.where(here < count // 2, here, count - 1 + count // 2 - here)


def is_even():
    return lax.rem(cycle_rank(), 2) == 0


class Fetch:
    def __init__(self, sems, *pairs):
        self.copies = [
            pltpu.make_async_copy(source, target, sems.at[at]) for at, (source, target) in enumerate(pairs)
        ]
        for copy in self.copies:
            copy.start()

    def wait(self, *which):
        for at in which:
            self.copies[at].wait()


def slot_flag(count_ref, ocean_ref, slot):
    live = jnp.logical_and(slot < count_ref[0], ocean_ref[slot] > 0)
    return jnp.where(live, 1.0, 0.0).astype(F32)


class Shape:
    def __init__(self, slots, channels, hidden):
        self.slots = slots
        self.channels = channels
        self.hidden = hidden
        self.parts = channels // LANES
        self.columns = slots * TILE
        self.pitch = self.columns + 2 * LEFT
        self.cells = slots * TILE * TILE
        self.edge_rows = HALF * TILE
        self.early = 12

    def lanes(self, part):
        return slice(part * LANES, (part + 1) * LANES)


def edge_planes(shape, source, start, stride):
    return [
        jnp.concatenate(
            [source[part, pl.ds(start + col, TILE, stride=stride), :] for part in range(shape.parts)], axis=1
        )
        for col in range(HALF)
    ]


def send_edges(shape, left, right, first, second):
    even = is_even()
    for col in range(HALF):
        rows = pl.ds(col * TILE, TILE)
        first[rows, :] = jnp.where(even, right[col], left[col]).astype(BF16)
        second[rows, :] = jnp.where(even, left[col], right[col]).astype(BF16)


def flip_matrix(size, last):
    to = lax.broadcasted_iota(jnp.int32, (size, size), 0)
    frm = lax.broadcasted_iota(jnp.int32, (size, size), 1)
    return jnp.where(to + frm == last, 1.0, 0.0).astype(BF16)


def prep_kernel(shape, count_hbm, fields, first, second, count, work, sems):
    fetch = Fetch(sems, (count_hbm, count))
    for part in range(shape.parts):
        work[part] = fields[:, shape.lanes(part)].astype(F32)
    left = edge_planes(shape, work, 0, TILE)
    fetch.wait(0)
    right = edge_planes(shape, work, (count[0] - 1) * TILE * TILE + TILE - HALF, TILE)
    send_edges(shape, left, right, first, second)


def top_kernel(shape, count_hbm, ocean_hbm, fields, fold, count, ocean, sems):
    fetch = Fetch(sems, (count_hbm, count), (ocean_hbm, ocean))
    fetch.wait(0, 1)
    flip = flip_matrix(shape.columns, count[0] * TILE - 1)
    for k in range(HALF):
        cells = jnp.concatenate(
            [
                fields[pl.ds(slot * TILE * TILE + (TILE - 1 - k) * TILE, TILE), :].astype(F32)
                * slot_flag(count, ocean, slot)
                for slot in range(shape.slots)
            ]
        )
        turned = dot(flip, cells.astype(BF16), 1, 0)
        fold[pl.ds(k * shape.columns, shape.columns), :] = turned.astype(BF16)


def band_kernel(shape, count_hbm, ocean_hbm, fields, first, second, band, rims, count, ocean, sems):
    fetch = Fetch(sems, (count_hbm, count), (ocean_hbm, ocean))
    even = is_even()
    blank = jnp.zeros((LEFT, LANES), F32)
    per_slot = TILE * TILE
    for part in range(shape.parts):
        band[part, pl.ds(0, HALF * shape.pitch), :] = jnp.zeros((HALF * shape.pitch, LANES), F32)
        for row in range(TILE):
            base = (row + HALF) * shape.pitch
            band[part, pl.ds(base, LEFT), :] = blank
            band[part, pl.ds(base + LEFT + shape.columns, LEFT), :] = blank
    fetch.wait(0, 1)
    used = count[0] * TILE
    flags = [slot_flag(count, ocean, slot) for slot in range(shape.slots)]
    top = HALF * shape.pitch
    for part in range(shape.parts):
        for row in range(TILE):
            base = (row + HALF) * shape.pitch
            for slot in range(shape.slots):
                cells = fields[pl.ds(slot * per_slot + row * TILE, TILE), shape.lanes(part)]
                band[part, pl.ds(base + LEFT + slot * TILE, TILE), :] = cells.astype(F32) * flags[slot]
        for col in range(HALF):
            rows = pl.ds(col * TILE, TILE)
            one = first[rows, shape.lanes(part)].astype(F32)
            two = second[rows, shape.lanes(part)].astype(F32)
            west = jnp.where(even, two, one)
            east = jnp.where(even, one, two)
            band[part, pl.ds(top + LEFT - HALF + col, TILE, stride=shape.pitch), :] = west
            band[part, pl.ds(top + LEFT + used + col, TILE, stride=shape.pitch), :] = east
    for k in range(HALF):
        base = (HALF + TILE - 1 - k) * shape.pitch
        east = pl.multiple_of(base + LEFT + used, LEFT)
        for part in range(shape.parts):
            ends = jnp.concatenate([band[part, pl.ds(base, LEFT), :], band[part, pl.ds(east, LEFT), :]])
            rims[pl.ds(k * 2 * LEFT, 2 * LEFT), shape.lanes(part)] = ends.astype(BF16)


def put_fold(shape, used, fold, rims, parts, padded, first_row, work):
    blank = jnp.zeros((LEFT, LANES), F32)
    for at, part in enumerate(parts):
        work[at] = rims[:, shape.lanes(part)].astype(F32)
        for k in range(HALF):
            base = (first_row + k) * shape.pitch
            padded[at, pl.ds(base, LEFT), :] = blank
            padded[at, pl.ds(base + LEFT + shape.columns, LEFT), :] = blank
            cells = fold[pl.ds(k * shape.columns, shape.columns), shape.lanes(part)]
            padded[at, pl.ds(base + LEFT, shape.columns), :] = cells.astype(F32)
            for col in range(HALF):
                west = work[at, pl.ds(k * 2 * LEFT + LEFT - 1 - col, 1), :]
                east = work[at, pl.ds(k * 2 * LEFT + LEFT + col, 1), :]
                padded[at, pl.ds(base + LEFT - 1 - col, 1), :] = east
                padded[at, pl.ds(base + LEFT + used + col, 1), :] = west


def spread_taps(shape, kernel, parts, taps):
    for above in range(KSIZE):
        rows = kernel[above].astype(F32)
        for at, part in enumerate(parts):
            for shift in range(KSIZE):
                row = rows[shift : shift + 1, shape.lanes(part)]
                taps[at, above * KSIZE + shift] = jnp.broadcast_to(row, (8, LANES))


def convolve(shape, rows, padded, taps, convolved):
    run = shape.columns // 8
    pair = 2
    origin = LEFT - HALF

    def two_rows(step, carry):
        row = step * pair
        for part in range(shape.parts):
            sums = [[None] * run for _ in range(pair)]
            for above in range(KSIZE + pair - 1):
                base = (row + above) * shape.pitch + origin
                loaded = [
                    padded[part, pl.ds(base + at, 8, stride=run), :]
                    for at in range(run + KSIZE - 1)
                ]
                for which in range(pair):
                    tap_row = above - which
                    if not 0 <= tap_row < KSIZE:
                        continue
                    for shift in range(KSIZE):
                        weight = taps[part, tap_row * KSIZE + shift]
                        for at in range(run):
                            term = weight * loaded[at + shift]
                            old = sums[which][at]
                            sums[which][at] = term if old is None else old + term
            for which in range(pair):
                for at in range(run):
                    start = (row + which) * shape.columns + at
                    convolved[part, pl.ds(start, 8, stride=run), :] = sums[which][at]
        return carry

    lax.fori_loop(0, rows // pair, two_rows, 0)


def normalise(shape, rows, first_row, convolved, gain, normed, yhat, inverse):
    def one_row(row, carry):
        for slot in range(shape.slots):
            start = pl.multiple_of(row * shape.columns + slot * TILE, TILE)
            at = slot * TILE * TILE + (first_row + row) * TILE
            out = pl.ds(pl.multiple_of(at, TILE), TILE)
            parts = [convolved[part, pl.ds(start, TILE), :] for part in range(shape.parts)]
            mean = jnp.sum(sum(parts), axis=-1, keepdims=True) * (1.0 / shape.channels)
            parts = [value - mean for value in parts]
            square = jnp.sum(sum(value * value for value in parts), axis=-1, keepdims=True)
            scale = lax.rsqrt(square * (1.0 / shape.channels) + EPS)
            inverse[out, :] = jnp.broadcast_to(scale, (TILE, LANES))
            for part in range(shape.parts):
                value = parts[part] * scale
                yhat[out, shape.lanes(part)] = value
                normed[out, shape.lanes(part)] = (value * gain[:, shape.lanes(part)]).astype(BF16)
        return carry

    lax.fori_loop(0, rows, one_row, 0, unroll=2)


def early_kernel(
    shape, count_hbm, ocean_hbm, kernel, gain, w_out, scale, tangent, band,
    normed, yhat, inverse, dproj_t, dact,
    count, ocean, taps, convolved, dproj, sems,
):
    fetch = Fetch(sems, (count_hbm, count), (ocean_hbm, ocean))
    spread_taps(shape, kernel, range(shape.parts), taps)
    convolve(shape, shape.early, band, taps, convolved)
    normalise(shape, shape.early, 0, convolved, gain, normed, yhat, inverse)
    fetch.wait(0, 1)
    per_slot = TILE * TILE
    for slot in range(shape.slots):
        rows = pl.ds(slot * per_slot, per_slot)
        flag = slot_flag(count, ocean, slot)
        scaled = (tangent[rows, :].astype(F32) * (scale[...] * flag)).astype(BF16)
        dproj[rows, :] = scaled
        dproj_t[:, slot * per_slot : (slot + 1) * per_slot] = scaled.T
        for h in range(shape.hidden // shape.channels):
            cols = slice(h * shape.channels, (h + 1) * shape.channels)
            dact[rows, cols] = dot(dproj[rows, :], w_out[cols, :], 1, 1)


def late_kernel(
    shape, count_hbm, kernel, gain, w_in, band, fold, rims, normed_in, yhat_in, inverse_in, dproj_t, dact,
    keep, give, activated, dpreact, yhat, inverse, padded,
    count, taps, convolved, normed, normed_t, work, sems,
):
    fetch = Fetch(sems, (count_hbm, count))
    late = TILE - shape.early
    kept = late + HALF
    for part in range(shape.parts):
        rows = pl.ds(shape.early * shape.pitch, kept * shape.pitch)
        padded[part, pl.ds(0, kept * shape.pitch), :] = band[part, rows, :]
    done = shape.early * TILE
    for slot in range(shape.slots):
        rows = pl.ds(slot * TILE * TILE, done)
        normed[rows, :] = normed_in[rows, :]
        yhat[rows, :] = yhat_in[rows, :]
        inverse[rows, :] = inverse_in[rows, :]
    spread_taps(shape, kernel, range(shape.parts), taps)
    fetch.wait(0)
    put_fold(shape, count[0] * TILE, fold, rims, range(shape.parts), padded, kept, work)
    convolve(shape, late, padded, taps, convolved)
    normalise(shape, late, shape.early, convolved, gain, normed, yhat, inverse)
    per_slot = TILE * TILE
    for slot in range(shape.slots):
        normed_t[:, slot * per_slot : (slot + 1) * per_slot] = normed[pl.ds(slot * per_slot, per_slot), :].T
    keeps_in = lax.axis_index("core") == 0
    block = shape.channels
    for h in range(shape.hidden // block):
        cols = slice(h * block, (h + 1) * block)
        for slot in range(shape.slots):
            rows = pl.ds(slot * per_slot, per_slot)
            pre = dot(normed[rows, :], w_in[:, cols], 1, 0)
            square = pre * pre
            inner = pre * (GELU_C + (GELU_C * GELU_A) * square)
            gate = 0.5 + 0.5 * jnp.tanh(inner)
            activated[rows, cols] = (pre * gate).astype(BF16)
            slope = pre * (2.0 * GELU_C + (6.0 * GELU_C * GELU_A) * square)
            grown = gate + slope * (gate - gate * gate)
            dpreact[rows, cols] = (dact[rows, cols] * grown).astype(BF16)
        rows = slice(h * block, (h + 1) * block)
        of_in = dot(normed_t[...], dpreact[:, cols], 1, 0)
        of_out = dot(dproj_t[...], activated[:, cols], 1, 0)
        keep[rows, :] = jnp.where(keeps_in, of_in, of_out)
        give[rows, :] = jnp.where(keeps_in, of_out, of_in).astype(BF16)


def fold_sum(value):
    return jnp.sum(value.reshape(-1, 8, value.shape[-1]), axis=0)


def norm_grad_kernel(shape, w_in, gain, dpreact, yhat, inverse, conv_grad, gain_part):
    chunk = TILE * TILE
    total = jnp.zeros((8, shape.channels), F32)
    for slot in range(shape.slots):
        rows = pl.ds(slot * chunk, chunk)
        dnormed = dot(dpreact[rows, :], w_in[...], 1, 1)
        unit = yhat[rows, :]
        total += fold_sum(dnormed * unit)
        dhat = dnormed * gain[...]
        mean = jnp.sum(dhat, axis=-1, keepdims=True) * (1.0 / shape.channels)
        along = jnp.sum(dhat * unit, axis=-1, keepdims=True) * (1.0 / shape.channels)
        scale = jnp.concatenate([inverse[rows, :]] * shape.parts, axis=1)
        conv_grad[rows, :] = (scale * (dhat - mean - unit * along)).astype(BF16)
    gain_part[...] = total


def state_kernel(
    shape, count_hbm, ocean_hbm, fields, tangent, w_out, scale, activated,
    state, scale_part,
    count, ocean, sems,
):
    fetch = Fetch(sems, (count_hbm, count), (ocean_hbm, ocean))
    fetch.wait(0, 1)
    chunk = TILE * TILE
    total = jnp.zeros((8, shape.channels), F32)
    for slot in range(shape.slots):
        rows = pl.ds(slot * chunk, chunk)
        flag = slot_flag(count, ocean, slot)
        projected = dot(activated[rows, :], w_out[...], 1, 0)
        kept = fields[rows, :].astype(F32) + scale[...] * projected
        state[rows, :] = (flag * kept).astype(BF16)
        total += fold_sum(flag * tangent[rows, :].astype(F32) * projected)
    scale_part[...] = total


def place_grad(shape, conv_grad, parts, spaced):
    blank = jnp.zeros((LEFT, LANES), F32)
    for at, part in enumerate(parts):
        for row in range(TILE):
            base = row * shape.pitch
            spaced[at, pl.ds(base, LEFT), :] = blank
            spaced[at, pl.ds(base + LEFT + shape.columns, LEFT), :] = blank
            for slot in range(shape.slots):
                cells = conv_grad[pl.ds(slot * TILE * TILE + row * TILE, TILE), shape.lanes(part)]
                spaced[at, pl.ds(base + LEFT + slot * TILE, TILE), :] = cells.astype(F32)


def taps_kernel(shape, part, band, top, conv_grad, small, padded, spaced):
    place_grad(shape, conv_grad, [part], spaced)
    kept = shape.early * shape.pitch
    padded[0, pl.ds(0, kept), :] = band[part, pl.ds(0, kept), :]
    padded[0, pl.ds(kept, top.shape[1]), :] = top[part]
    run = shape.columns // 8
    origin = LEFT - HALF
    for above in range(KSIZE):

        def one_row(row, sums, above=above):
            base = (row + above) * shape.pitch + origin
            loaded = [padded[0, pl.ds(base + at, 8, stride=run), :] for at in range(run + KSIZE - 1)]
            start = row * shape.pitch + LEFT
            grads = [spaced[0, pl.ds(start + at, 8, stride=run), :] for at in range(run)]
            sums = list(sums)
            for shift in range(KSIZE):
                for at in range(run):
                    sums[shift] = sums[shift] + grads[at] * loaded[at + shift]
            return tuple(sums)

        blank = tuple(jnp.zeros((8, LANES), F32) for _ in range(KSIZE))
        sums = lax.fori_loop(0, TILE, one_row, blank, unroll=2)
        for shift in range(KSIZE):
            small[pl.ds(above * KSIZE + shift, 1), :] = jnp.sum(sums[shift], axis=0, keepdims=True)


def back_kernel(shape, part, count_hbm, kernel, conv_grad, *refs):
    before = refs[:part]
    turns = part == shape.parts - 1
    core_grad, *refs = refs[part:]
    if turns:
        fold, *refs = refs
    count, spaced, taps, sems = refs
    fetch = Fetch(sems, (count_hbm, count))
    place_grad(shape, conv_grad, [part], spaced)
    blank = jnp.zeros((LEFT, LANES), F32)
    for row in range(TILE + HALF):
        core_grad[pl.ds(row * shape.pitch, LEFT), :] = blank
        core_grad[pl.ds((row + 1) * shape.pitch - LEFT, LEFT), :] = blank
    spread_taps(shape, kernel, [part], taps)
    run = -(-(shape.columns + 2 * HALF) // 8)

    def one_row(row, tap_rows):
        sums = [None] * run
        for above in tap_rows:
            base = (row - above) * shape.pitch + LEFT
            loaded = [
                spaced[0, pl.ds(base + at - KSIZE + 1, 8, stride=run), :] for at in range(run + KSIZE - 1)
            ]
            for shift in range(KSIZE):
                weight = taps[0, above * KSIZE + shift]
                for at in range(run):
                    term = weight * loaded[at - shift + KSIZE - 1]
                    sums[at] = term if sums[at] is None else sums[at] + term
        start = (row - HALF) * shape.pitch + LEFT - HALF
        for at in range(run):
            core_grad[pl.ds(start + at, 8, stride=run), :] = sums[at]

    inner = (KSIZE - 1, TILE - 1)
    for row in range(HALF, TILE + 2 * HALF):
        if not inner[0] <= row <= inner[1]:
            low = max(0, row - TILE + 1)
            one_row(row, range(low, min(KSIZE - 1, row) + 1))

    def inner_row(step, carry):
        one_row(step, range(KSIZE))
        return carry

    lax.fori_loop(inner[0], inner[1] + 1, inner_row, 0)
    fetch.wait(0)
    if turns:
        flip = flip_matrix(shape.pitch, count[0] * TILE + 2 * LEFT - 1)
        for k in range(HALF):
            at = pl.ds((TILE + k) * shape.pitch, shape.pitch)
            cells = jnp.concatenate([one[at, :] for one in (*before, core_grad)], axis=1)
            turned = dot(flip, cells.astype(BF16), 1, 0)
            fold[pl.ds(k * shape.pitch, shape.pitch), :] = turned.astype(BF16)


def rims_kernel(shape, count_hbm, fold, *refs):
    core_grad = refs[: shape.parts]
    folded, first, second, count, sems = refs[shape.parts :]
    fetch = Fetch(sems, (count_hbm, count))
    for part in range(shape.parts):
        folded[part] = core_grad[part][pl.ds(0, TILE * shape.pitch), :]
        for k in range(HALF):
            rows = pl.ds((TILE - 1 - k) * shape.pitch, shape.pitch)
            returned = fold[pl.ds(k * shape.pitch, shape.pitch), shape.lanes(part)]
            folded[part, rows, :] += returned.astype(F32)
    fetch.wait(0)
    west = edge_planes(shape, folded, LEFT - HALF, shape.pitch)
    east = edge_planes(shape, folded, LEFT + count[0] * TILE, shape.pitch)
    send_edges(shape, west, east, first, second)


def final_kernel(
    shape, count_hbm, ocean_hbm, tangent, folded, first, second,
    grad_fields, done,
    count, ocean, work, sems,
):
    fetch = Fetch(sems, (count_hbm, count), (ocean_hbm, ocean))
    even = is_even()
    done[...] = jnp.zeros_like(done)
    work[...] = folded[...]
    fetch.wait(0, 1)
    used = count[0] * TILE
    for part in range(shape.parts):
        for col in range(HALF):
            planes = pl.ds(col * TILE, TILE)
            one = first[planes, shape.lanes(part)].astype(F32)
            two = second[planes, shape.lanes(part)].astype(F32)
            to_tail = jnp.where(even, one, two)
            to_head = jnp.where(even, two, one)
            head = pl.ds(LEFT + col, TILE, stride=shape.pitch)
            work[part, head, :] = work[part, head, :] + to_head
            tail = pl.ds(LEFT + used - HALF + col, TILE, stride=shape.pitch)
            work[part, tail, :] = work[part, tail, :] + to_tail
        for slot in range(shape.slots):
            flag = slot_flag(count, ocean, slot)
            for row in range(TILE):
                rows = pl.ds(slot * TILE * TILE + row * TILE, TILE)
                cells = work[part, pl.ds(row * shape.pitch + LEFT + slot * TILE, TILE), :]
                total = tangent[rows, shape.lanes(part)].astype(F32) + cells
                grad_fields[rows, shape.lanes(part)] = (flag * total).astype(BF16)


def write_sums(norm, has_in, sums, w_in, w_out, work_in, work_out, sems):
    channels = sums.shape[-1]
    blocks = w_out.shape[0] // channels

    def written(of_in):
        copies = []
        for h in range(blocks):
            block = slice(h * channels, (h + 1) * channels)
            value = sums[block, :].astype(F32) * norm
            if of_in:
                work_in[:, block] = value
                copy = pltpu.make_async_copy(work_in.at[:, block], w_in.at[:, block], sems.at[h])
            else:
                work_out[block, :] = value.T
                copy = pltpu.make_async_copy(work_out.at[block, :], w_out.at[block, :], sems.at[h])
            copy.start()
            copies.append(copy)
        for copy in copies:
            copy.wait()

    @pl.when(has_in)
    def _():
        written(True)

    @pl.when(jnp.logical_not(has_in))
    def _():
        written(False)


def own_kernel(norm, own, w_in, w_out, work_in, work_out, sems):
    write_sums(norm, lax.axis_index("core") == 0, own, w_in, w_out, work_in, work_out, sems)


def other_kernel(norm, w_in_old, w_out_old, own, came, w_in, w_out, kernel_sum, gain_sum, scale_sum, work_in, work_out, sems):
    is_first = lax.axis_index("core") == 0
    hidden = w_out.shape[0]
    extra = (own.shape[0] - hidden) // 2
    high, low = pl.ds(hidden, extra), pl.ds(hidden + extra, extra)
    mine = (own[high, :].astype(F32) + own[low, :].astype(F32)) * norm
    theirs = (came[high, :].astype(F32) + came[low, :].astype(F32)) * norm
    small = jnp.concatenate([jnp.where(is_first, mine, theirs), jnp.where(is_first, theirs, mine)])
    for above in range(KSIZE):
        kernel_sum[above] = small[above * KSIZE : (above + 1) * KSIZE, :]
    gain_sum[...] = small[KSIZE * KSIZE : KSIZE * KSIZE + 1, :]
    scale_sum[...] = small[KSIZE * KSIZE + 1 : KSIZE * KSIZE + 2, :]
    write_sums(norm, jnp.logical_not(is_first), came, w_in, w_out, work_in, work_out, sems)


def pairs_of(kind):
    count = lax.axis_size(TILES)
    half = count // 2
    place = [rank if rank < half else count - 1 + half - rank for rank in range(count)]
    partner = {
        "first": lambda rank: rank ^ 1,
        "second": lambda rank: ((rank + 1) ^ 1) - 1,
        "fold": lambda rank: count - 1 - rank,
    }[kind]
    return [(place[rank], place[partner(rank) % count]) for rank in range(count)]


def swap(block, kind):
    return lax.ppermute(block, TILES, pairs_of(kind))


def core_swap(block):
    return lax.ppermute(block, "core", [(0, 1), (1, 0)])


def stages():
    chip_bits = lax.axis_size("chips").bit_length() - 1
    rest = list(range(2, chip_bits))
    return list(zip([0, -1, 1] + rest, [1, 0, -1] + rest))


def bit_swap(block, stage):
    chips, cores, samples = (lax.axis_size(axis) for axis in ("chips", "core", "dp"))
    pairs = []
    for chip in range(chips):
        for core in range(cores):
            for sample in range(samples):
                bit = stage[core]
                to = (chip, sample ^ 1) if bit < 0 else (chip ^ (1 << bit), sample)
                pairs.append(
                    ((chip * cores + core) * samples + sample, (to[0] * cores + core) * samples + to[1])
                )
    return lax.ppermute(block, ("chips", "core", "dp"), pairs)


def bit_here(stage):
    bits = [
        lax.axis_index("dp") if bit < 0 else lax.axis_index("chips") >> bit & 1 for bit in stage
    ]
    return jnp.where(lax.axis_index("core") == 0, bits[0], bits[1])


def half_rows(bit, rows):
    return pl.ds(pl.multiple_of(bit * rows, rows), rows)


def join_kernel(stage, keep, came, mine, send):
    rows = send.shape[0]
    mine[...] = keep[...] + came[...].astype(F32)
    send[...] = mine[half_rows(1 - bit_here(stage), rows), :].astype(BF16)


def halve_kernel(stage, following, whole, came, mine, send):
    rows = mine.shape[0]
    mine[...] = whole[half_rows(bit_here(stage), rows), :] + came[...].astype(F32)
    send[...] = mine[half_rows(1 - bit_here(following), rows // 2), :].astype(BF16)


def pack_kernel(gain_part, scale_part, *refs):
    taps, (keep, send, work) = refs[:-3], refs[-3:]
    half = keep.shape[0]
    work[...] = jnp.zeros_like(work)
    for part, ref in enumerate(taps):
        work[pl.ds(0, ref.shape[0]), part * LANES : (part + 1) * LANES] = ref[...]
    work[pl.ds(KSIZE * KSIZE, 1), :] = jnp.sum(gain_part[...], axis=0, keepdims=True)
    work[pl.ds(KSIZE * KSIZE + 1, 1), :] = jnp.sum(scale_part[...], axis=0, keepdims=True)
    core = lax.axis_index("core")
    keep[...] = work[half_rows(core, half), :]
    value = work[half_rows(1 - core, half), :]
    high = value.astype(BF16)
    send[pl.ds(0, half), :] = high
    send[pl.ds(half, half), :] = (value - high.astype(F32)).astype(BF16)


def turn_kernel(stage, whole, came, keep, extra, payload):
    rows, half = came.shape[0], keep.shape[0]
    share = whole[half_rows(bit_here(stage), rows), :] + came[...].astype(F32)
    payload[pl.ds(0, rows), :] = share.astype(BF16)
    small = keep[...] + (extra[pl.ds(0, half), :].astype(F32) + extra[pl.ds(half, half), :].astype(F32))
    payload[pl.ds(rows, half), :] = small.astype(BF16)


def add_kernel(own, came, payload):
    payload[...] = (own[...].astype(F32) + came[...].astype(F32)).astype(BF16)


def double_kernel(stage, extra, own, came, payload):
    rows = own.shape[0] - extra
    bit = bit_here(stage)
    payload[half_rows(bit, rows), :] = own[pl.ds(0, rows), :]
    payload[half_rows(1 - bit, rows), :] = came[pl.ds(0, rows), :]
    total = own[pl.ds(rows, extra), :].astype(F32) + came[pl.ds(rows, extra), :].astype(F32)
    high = total.astype(BF16)
    payload[pl.ds(2 * rows, extra), :] = high
    if payload.shape[0] > 2 * rows + extra:
        payload[pl.ds(2 * rows + extra, extra), :] = (total - high.astype(F32)).astype(BF16)


def halved(mine, send, order):
    for at, stage in enumerate(order[:-1]):
        came = bit_swap(send, stage)
        rows = came.shape[0]
        bit = bit_here(stage)
        mine = lax.dynamic_index_in_dim(mine.reshape(2, rows, -1), bit, 0, keepdims=False) + came.astype(F32)
        bit = bit_here(order[at + 1])
        halves = mine.reshape(2, rows // 2, -1)
        send = lax.dynamic_index_in_dim(halves, 1 - bit, 0, keepdims=False).astype(BF16)
    return mine, send


def call(kernel, outs, scratch, hbm, vmem, copies=0, micros=1.0, after=(), limit=20, in_hbm=0, aliases=None):
    in_specs = [pl.BlockSpec(memory_space=pl.ANY)] * len(hbm)
    in_specs += [pl.BlockSpec(memory_space=pltpu.VMEM)] * len(vmem)
    in_specs += [pl.BlockSpec(memory_space=pl.ANY)] * len(after)
    shapes = [pltpu.SMEM(*one) if one[1] == jnp.int32 else pltpu.VMEM(*one) for one in scratch]
    if copies:
        shapes.append(pltpu.SemaphoreType.DMA((copies,)))
    taken = len(hbm) + len(vmem)

    def body(*refs):
        kernel(*refs[:taken], *refs[taken + len(after) :])

    return pl.pallas_call(
        body,
        out_shape=[jax.ShapeDtypeStruct(*out) for out in outs],
        in_specs=in_specs,
        out_specs=[pl.BlockSpec(memory_space=pl.ANY if at < in_hbm else pltpu.VMEM) for at in range(len(outs))],
        input_output_aliases=aliases or {},
        scratch_shapes=shapes,
        cost_estimate=pl.CostEstimate(flops=int(micros * 1e9), bytes_accessed=0, transcendentals=0),
        compiler_params=pltpu.CompilerParams(vmem_limit_bytes=limit * 1024 * 1024),
    )(*hbm, *vmem, *after)


def shards(fields, grad_out, block_count, ocean, kernel, ln_gain, w_in, w_out, layer_scale):
    samples, slots, tile_rows, tile_cols, channels = fields.shape
    hidden = w_in.shape[1]
    shape = Shape(slots, channels, hidden)
    cells, parts, pitch = shape.cells, shape.parts, shape.pitch
    grid = fields.shape
    fields = fields.reshape(cells, channels)
    tangent = grad_out.reshape(cells, channels)
    taps_in = kernel
    gain = ln_gain.reshape(1, channels)
    scale = layer_scale.reshape(1, channels)

    def bind(body):
        return functools.partial(body, shape)

    def strip(rows):
        return ((parts, rows * pitch, LANES), F32)

    edge = ((shape.edge_rows, channels), BF16)
    turned = ((HALF * pitch, channels), BF16)
    whole = ((cells, channels), BF16)
    whole_f = ((cells, channels), F32)
    wide = ((cells, hidden), BF16)
    narrow = ((cells, LANES), F32)
    row = ((1, channels), F32)
    eight = ((8, channels), F32)
    taps = ((parts, KSIZE * KSIZE, 8, LANES), F32)
    count_s = (block_count.shape, jnp.int32)
    ocean_s = (ocean.shape, jnp.int32)
    flat = ((channels, cells), BF16)
    ends = ((HALF * 2 * LEFT, channels), BF16)
    ends_f = ((parts, HALF * 2 * LEFT, LANES), F32)
    late = TILE - shape.early

    first, second = call(
        bind(prep_kernel), [edge, edge], [count_s, ((parts, cells, LANES), F32)],
        [block_count], [fields], 1, 1.0,
    )
    (fold,) = call(
        bind(top_kernel), [((HALF * shape.columns, channels), BF16)], [count_s, ocean_s],
        [block_count, ocean], [fields], 2, 0.5, after=[first],
    )
    first, second = swap(first, "first"), swap(second, "second")
    band, rims = call(
        bind(band_kernel), [strip(TILE + HALF), ends], [count_s, ocean_s],
        [block_count, ocean], [fields, first, second], 2, 1.0, after=[fold],
    )
    fold, rims = swap(fold, "fold"), swap(rims, "fold")
    normed, yhat, inverse, dproj_t, dact = call(
        bind(early_kernel), [whole, whole_f, narrow, flat, ((cells, hidden), F32)],
        [count_s, ocean_s, taps, ((parts, shape.early * shape.columns, LANES), F32), whole],
        [block_count, ocean], [taps_in, gain, w_out, scale, tangent, band], 2, 5.0,
    )
    keep, give, activated, dpreact, yhat, inverse, top = call(
        bind(late_kernel),
        [((hidden, channels), F32), ((hidden, channels), BF16), wide, wide, whole_f, narrow, strip(late + 2 * HALF)],
        [count_s, taps, ((parts, late * shape.columns, LANES), F32), whole, flat, ends_f],
        [block_count],
        [taps_in, gain, w_in, band, fold, rims, normed, yhat, inverse, dproj_t, dact], 1, 5.0,
    )

    order = stages()
    rows = hidden // 2

    def half_step(at, rows):
        return functools.partial(halve_kernel, order[at], order[at + 1]), [
            ((rows, channels), F32), ((rows // 2, channels), BF16),
        ]

    def taps_part(part, after):
        (small,) = call(
            functools.partial(taps_kernel, shape, part), [((small_rows, LANES), F32)],
            [((1, (TILE + 2 * HALF) * pitch, LANES), F32), ((1, TILE * pitch, LANES), F32)],
            [], [band, top, conv_grad], 0, 1.8, after=after,
        )
        return small

    def back_part(part, before, after):
        outs = [(((TILE + HALF) * pitch, LANES), F32)] + [turned] * (part == parts - 1)
        return call(
            functools.partial(back_kernel, shape, part), outs,
            [count_s, ((1, TILE * pitch, LANES), F32), ((1, KSIZE * KSIZE, 8, LANES), F32)],
            [block_count], [taps_in, conv_grad, *before], 1, 2.0, after=after,
        )

    small_rows = -(-(KSIZE * KSIZE + 2) // 32) * 32
    came = core_swap(give)
    conv_grad, gain_part = call(
        bind(norm_grad_kernel), [whole, eight], [], [], [w_in, gain, dpreact, yhat, inverse], 0, 1.0,
    )
    mine, send = call(
        functools.partial(join_kernel, order[0]),
        [((hidden, channels), F32), ((rows, channels), BF16)], [], [], [keep, came], after=[conv_grad], micros=0.3,
    )
    came = bit_swap(send, order[0])
    taps_parts = [taps_part(0, [send])]
    state, scale_part = call(
        bind(state_kernel), [whole, eight], [count_s, ocean_s],
        [block_count, ocean], [fields, tangent, w_out, scale, activated], 2, 1.5, after=taps_parts,
    )
    body, outs = half_step(0, rows)
    mine, send = call(body, outs, [], [], [mine, came], after=[scale_part], micros=0.3)
    came = bit_swap(send, order[1])
    taps_parts += [taps_part(part, [send]) for part in range(1, parts)]
    small_rows //= 2
    small, extra = call(
        pack_kernel, [((small_rows, channels), F32), ((2 * small_rows, channels), BF16)],
        [((2 * small_rows, channels), F32)], [], [gain_part, scale_part, *taps_parts], micros=0.3,
    )
    rows //= 2
    body, outs = half_step(1, rows)
    mine, send = call(body, outs, [], [], [mine, came], after=[small], micros=0.3)
    extra = core_swap(extra)
    mine, send = halved(mine, send, order[2:-1])
    came = bit_swap(send, order[-2])
    core_grad = []
    for part in range(parts - 1):
        core_grad += back_part(part, core_grad, [send])
    rows = came.shape[0]
    if rows % 16 == 0:
        (payload,) = call(
            functools.partial(turn_kernel, order[-2]), [((rows + small_rows, channels), BF16)],
            [], [], [mine, came, small, extra], after=core_grad, micros=0.3,
        )
    else:
        bit = bit_here(order[-2])
        share = lax.dynamic_index_in_dim(mine.reshape(2, rows, channels), bit, 0, keepdims=False)
        small = small + (extra[:small_rows].astype(F32) + extra[small_rows:].astype(F32))
        payload = jnp.concatenate([share + came.astype(F32), small]).astype(BF16)
    came = bit_swap(payload, order[-1])
    last_grad, fold_back = back_part(parts - 1, core_grad, [payload])
    core_grad += [last_grad]
    fold_back = swap(fold_back, "fold")
    (payload,) = call(
        add_kernel, [(payload.shape, BF16)], [], [], [payload, came], after=[last_grad], micros=0.3,
    )
    came = bit_swap(payload, order[-2])
    folded, first, second = call(
        bind(rims_kernel), [strip(TILE), edge, edge], [count_s], [block_count], [fold_back, *core_grad], 1, 1.0,
        after=[payload],
    )
    first, second = swap(first, "first"), swap(second, "second")
    after = [folded]
    for at in reversed(range(len(order) - 1)):
        copies = 2 if at == 0 else 1
        if rows % 16 == 0:
            (payload,) = call(
                functools.partial(double_kernel, order[at], small_rows),
                [((2 * rows + copies * small_rows, channels), BF16)],
                [], [], [payload, came], after=after, micros=0.3,
            )
        else:
            is_low = bit_here(order[at]) == 0
            low, high = payload[:rows], came[:rows]
            both = payload[rows:].astype(F32) + came[rows:].astype(F32)
            joined = [jnp.where(is_low, low, high), jnp.where(is_low, high, low), both.astype(BF16)]
            payload = jnp.concatenate(joined)
        after = []
        rows *= 2
        came = bit_swap(payload, order[at - 1]) if at else core_swap(payload)
        if at == 2:
            grad_fields, done = call(
                bind(final_kernel), [whole, ((8, LANES), F32)], [count_s, ocean_s, strip(TILE)],
                [block_count, ocean], [tangent, folded, first, second], 2, 1.5, after=[payload],
            )
            after = [done]
    total = samples * lax.axis_size("dp") * slots * lax.axis_size(TILES) * tile_rows * tile_cols
    norm = total ** (-0.5)
    sums = [((channels, hidden), F32), ((hidden, channels), F32)]
    w_in_sum, w_out_sum = call(
        functools.partial(own_kernel, norm), sums, sums, [], [payload], hidden // channels, 1.0, in_hbm=2,
    )
    w_in_sum, w_out_sum, kernel_sum, gain_sum, scale_sum = call(
        functools.partial(other_kernel, norm), sums + [(kernel.shape, F32), row, row], sums,
        [w_in_sum, w_out_sum], [payload, came], hidden // channels, 1.0, in_hbm=2, aliases={0: 0, 1: 1},
    )
    return (
        state.reshape(grid),
        grad_fields.reshape(grid),
        kernel_sum,
        gain_sum.reshape(ln_gain.shape),
        w_in_sum,
        w_out_sum,
        scale_sum.reshape(layer_scale.shape),
    )


def solution(mesh):
    cores = Mesh(mesh.devices.reshape(-1, 2, mesh.devices.shape[1]), ("chips", "core", "dp"))
    banded = P("dp", TILES, None, None, None)
    placed = (banded, banded, P(TILES), P(TILES), P(), P(), P(), P(), P())
    return jax.shard_map(
        shards,
        mesh=cores,
        in_specs=placed,
        out_specs=(banded, banded, P(), P(), P(), P(), P()),
        check_vma=False,
    )
```

```python
import functools

import jax
import jax.numpy as jnp
from jax import lax
from jax.experimental import pallas as pl
from jax.experimental.pallas import tpu as pltpu
from jax.sharding import Mesh, PartitionSpec as P

KSIZE = 7
HALF = KSIZE // 2
TILE = 16
EPS = 1e-06
TILES = ("chips", "core")
F32 = jnp.float32
BF16 = jnp.bfloat16
LANES = 128
LEFT = 8
GELU_C = 0.7978845608028654
GELU_A = 0.044715


def dot(lhs, rhs, lhs_dim, rhs_dim):
    return lax.dot_general(
        lhs, rhs, (((lhs_dim,), (rhs_dim,)), ((), ())), preferred_element_type=F32
    )


def cycle_rank():
    count = lax.axis_size(TILES)
    here = lax.axis_index("chips") * lax.axis_size("core") + lax.axis_index("core")
    return jnp.where(here < count // 2, here, count - 1 + count // 2 - here)


def is_even():
    return lax.rem(cycle_rank(), 2) == 0


class Fetch:
    def __init__(self, sems, *pairs):
        self.copies = [
            pltpu.make_async_copy(source, target, sems.at[at]) for at, (source, target) in enumerate(pairs)
        ]
        for copy in self.copies:
            copy.start()

    def wait(self, *which):
        for at in which:
            self.copies[at].wait()


def slot_flag(count_ref, ocean_ref, slot):
    live = jnp.logical_and(slot < count_ref[0], ocean_ref[slot] > 0)
    return jnp.where(live, 1.0, 0.0).astype(F32)


class Shape:
    def __init__(self, slots, channels, hidden):
        self.slots = slots
        self.channels = channels
        self.hidden = hidden
        self.parts = channels // LANES
        self.columns = slots * TILE
        self.pitch = self.columns + 2 * LEFT
        self.cells = slots * TILE * TILE
        self.edge_rows = HALF * TILE
        self.early = 12

    def lanes(self, part):
        return slice(part * LANES, (part + 1) * LANES)


def edge_planes(shape, source, start, stride):
    return [
        jnp.concatenate(
            [source[part, pl.ds(start + col, TILE, stride=stride), :] for part in range(shape.parts)], axis=1
        )
        for col in range(HALF)
    ]


def send_edges(shape, left, right, first, second):
    even = is_even()
    for col in range(HALF):
        rows = pl.ds(col * TILE, TILE)
        first[rows, :] = jnp.where(even, right[col], left[col]).astype(BF16)
        second[rows, :] = jnp.where(even, left[col], right[col]).astype(BF16)


def flip_matrix(size, last):
    to = lax.broadcasted_iota(jnp.int32, (size, size), 0)
    frm = lax.broadcasted_iota(jnp.int32, (size, size), 1)
    return jnp.where(to + frm == last, 1.0, 0.0).astype(BF16)


def prep_kernel(shape, count_hbm, fields, first, second, count, work, sems):
    fetch = Fetch(sems, (count_hbm, count))
    for part in range(shape.parts):
        work[part] = fields[:, shape.lanes(part)].astype(F32)
    left = edge_planes(shape, work, 0, TILE)
    fetch.wait(0)
    right = edge_planes(shape, work, (count[0] - 1) * TILE * TILE + TILE - HALF, TILE)
    send_edges(shape, left, right, first, second)


def top_kernel(shape, count_hbm, ocean_hbm, fields, fold, count, ocean, sems):
    fetch = Fetch(sems, (count_hbm, count), (ocean_hbm, ocean))
    fetch.wait(0, 1)
    flip = flip_matrix(shape.columns, count[0] * TILE - 1)
    for k in range(HALF):
        cells = jnp.concatenate(
            [
                fields[pl.ds(slot * TILE * TILE + (TILE - 1 - k) * TILE, TILE), :].astype(F32)
                * slot_flag(count, ocean, slot)
                for slot in range(shape.slots)
            ]
        )
        turned = dot(flip, cells.astype(BF16), 1, 0)
        fold[pl.ds(k * shape.columns, shape.columns), :] = turned.astype(BF16)


def band_kernel(shape, count_hbm, ocean_hbm, fields, first, second, band, rims, count, ocean, sems):
    fetch = Fetch(sems, (count_hbm, count), (ocean_hbm, ocean))
    even = is_even()
    blank = jnp.zeros((LEFT, LANES), F32)
    per_slot = TILE * TILE
    for part in range(shape.parts):
        band[part, pl.ds(0, HALF * shape.pitch), :] = jnp.zeros((HALF * shape.pitch, LANES), F32)
        for row in range(TILE):
            base = (row + HALF) * shape.pitch
            band[part, pl.ds(base, LEFT), :] = blank
            band[part, pl.ds(base + LEFT + shape.columns, LEFT), :] = blank
    fetch.wait(0, 1)
    used = count[0] * TILE
    flags = [slot_flag(count, ocean, slot) for slot in range(shape.slots)]
    top = HALF * shape.pitch
    for part in range(shape.parts):
        for row in range(TILE):
            base = (row + HALF) * shape.pitch
            for slot in range(shape.slots):
                cells = fields[pl.ds(slot * per_slot + row * TILE, TILE), shape.lanes(part)]
                band[part, pl.ds(base + LEFT + slot * TILE, TILE), :] = cells.astype(F32) * flags[slot]
        for col in range(HALF):
            rows = pl.ds(col * TILE, TILE)
            one = first[rows, shape.lanes(part)].astype(F32)
            two = second[rows, shape.lanes(part)].astype(F32)
            west = jnp.where(even, two, one)
            east = jnp.where(even, one, two)
            band[part, pl.ds(top + LEFT - HALF + col, TILE, stride=shape.pitch), :] = west
            band[part, pl.ds(top + LEFT + used + col, TILE, stride=shape.pitch), :] = east
    for k in range(HALF):
        base = (HALF + TILE - 1 - k) * shape.pitch
        east = pl.multiple_of(base + LEFT + used, LEFT)
        for part in range(shape.parts):
            ends = jnp.concatenate([band[part, pl.ds(base, LEFT), :], band[part, pl.ds(east, LEFT), :]])
            rims[pl.ds(k * 2 * LEFT, 2 * LEFT), shape.lanes(part)] = ends.astype(BF16)


def put_fold(shape, used, fold, rims, parts, padded, first_row, work):
    blank = jnp.zeros((LEFT, LANES), F32)
    for at, part in enumerate(parts):
        work[at] = rims[:, shape.lanes(part)].astype(F32)
        for k in range(HALF):
            base = (first_row + k) * shape.pitch
            padded[at, pl.ds(base, LEFT), :] = blank
            padded[at, pl.ds(base + LEFT + shape.columns, LEFT), :] = blank
            cells = fold[pl.ds(k * shape.columns, shape.columns), shape.lanes(part)]
            padded[at, pl.ds(base + LEFT, shape.columns), :] = cells.astype(F32)
            for col in range(HALF):
                west = work[at, pl.ds(k * 2 * LEFT + LEFT - 1 - col, 1), :]
                east = work[at, pl.ds(k * 2 * LEFT + LEFT + col, 1), :]
                padded[at, pl.ds(base + LEFT - 1 - col, 1), :] = east
                padded[at, pl.ds(base + LEFT + used + col, 1), :] = west


def spread_taps(shape, kernel, parts, taps):
    for above in range(KSIZE):
        rows = kernel[above].astype(F32)
        for at, part in enumerate(parts):
            for shift in range(KSIZE):
                row = rows[shift : shift + 1, shape.lanes(part)]
                taps[at, above * KSIZE + shift] = jnp.broadcast_to(row, (8, LANES))


def convolve(shape, rows, padded, taps, convolved):
    run = shape.columns // 8
    pair = 2
    origin = LEFT - HALF

    def two_rows(step, carry):
        row = step * pair
        for part in range(shape.parts):
            sums = [[None] * run for _ in range(pair)]
            for above in range(KSIZE + pair - 1):
                base = (row + above) * shape.pitch + origin
                loaded = [
                    padded[part, pl.ds(base + at, 8, stride=run), :]
                    for at in range(run + KSIZE - 1)
                ]
                for which in range(pair):
                    tap_row = above - which
                    if not 0 <= tap_row < KSIZE:
                        continue
                    for shift in range(KSIZE):
                        weight = taps[part, tap_row * KSIZE + shift]
                        for at in range(run):
                            term = weight * loaded[at + shift]
                            old = sums[which][at]
                            sums[which][at] = term if old is None else old + term
            for which in range(pair):
                for at in range(run):
                    start = (row + which) * shape.columns + at
                    convolved[part, pl.ds(start, 8, stride=run), :] = sums[which][at]
        return carry

    lax.fori_loop(0, rows // pair, two_rows, 0)


def normalise(shape, rows, first_row, convolved, gain, normed, yhat, inverse):
    def one_row(row, carry):
        for slot in range(shape.slots):
            start = pl.multiple_of(row * shape.columns + slot * TILE, TILE)
            at = slot * TILE * TILE + (first_row + row) * TILE
            out = pl.ds(pl.multiple_of(at, TILE), TILE)
            parts = [convolved[part, pl.ds(start, TILE), :] for part in range(shape.parts)]
            mean = jnp.sum(sum(parts), axis=-1, keepdims=True) * (1.0 / shape.channels)
            parts = [value - mean for value in parts]
            square = jnp.sum(sum(value * value for value in parts), axis=-1, keepdims=True)
            scale = lax.rsqrt(square * (1.0 / shape.channels) + EPS)
            inverse[out, :] = jnp.broadcast_to(scale, (TILE, LANES))
            for part in range(shape.parts):
                value = parts[part] * scale
                yhat[out, shape.lanes(part)] = value
                normed[out, shape.lanes(part)] = (value * gain[:, shape.lanes(part)]).astype(BF16)
        return carry

    lax.fori_loop(0, rows, one_row, 0, unroll=4)


def early_kernel(
    shape, count_hbm, ocean_hbm, kernel, gain, w_out, scale, tangent, band,
    normed, yhat, inverse, dproj_t, dact,
    count, ocean, taps, convolved, dproj, sems,
):
    fetch = Fetch(sems, (count_hbm, count), (ocean_hbm, ocean))
    spread_taps(shape, kernel, range(shape.parts), taps)
    convolve(shape, shape.early, band, taps, convolved)
    normalise(shape, shape.early, 0, convolved, gain, normed, yhat, inverse)
    fetch.wait(0, 1)
    per_slot = TILE * TILE
    for slot in range(shape.slots):
        rows = pl.ds(slot * per_slot, per_slot)
        flag = slot_flag(count, ocean, slot)
        scaled = (tangent[rows, :].astype(F32) * (scale[...] * flag)).astype(BF16)
        dproj[rows, :] = scaled
        dproj_t[:, slot * per_slot : (slot + 1) * per_slot] = scaled.T
        for h in range(shape.hidden // shape.channels):
            cols = slice(h * shape.channels, (h + 1) * shape.channels)
            dact[rows, cols] = dot(dproj[rows, :], w_out[cols, :], 1, 1)


def late_kernel(
    shape, count_hbm, kernel, gain, w_in, band, fold, rims, normed_in, yhat_in, inverse_in, dproj_t, dact,
    keep, give, activated, dpreact, yhat, inverse, padded,
    count, taps, convolved, normed, normed_t, work, pre, sems,
):
    fetch = Fetch(sems, (count_hbm, count))
    late = TILE - shape.early
    kept = late + HALF
    for part in range(shape.parts):
        rows = pl.ds(shape.early * shape.pitch, kept * shape.pitch)
        padded[part, pl.ds(0, kept * shape.pitch), :] = band[part, rows, :]
    done = shape.early * TILE
    for slot in range(shape.slots):
        rows = pl.ds(slot * TILE * TILE, done)
        normed[rows, :] = normed_in[rows, :]
        yhat[rows, :] = yhat_in[rows, :]
        inverse[rows, :] = inverse_in[rows, :]
    spread_taps(shape, kernel, range(shape.parts), taps)
    fetch.wait(0)
    put_fold(shape, count[0] * TILE, fold, rims, range(shape.parts), padded, kept, work)
    convolve(shape, late, padded, taps, convolved)
    normalise(shape, late, shape.early, convolved, gain, normed, yhat, inverse)
    per_slot = TILE * TILE
    for slot in range(shape.slots):
        normed_t[:, slot * per_slot : (slot + 1) * per_slot] = normed[pl.ds(slot * per_slot, per_slot), :].T
    keeps_in = lax.axis_index("core") == 0
    block = shape.channels
    blocks = shape.hidden // block

    def span(h):
        return slice(h * block, (h + 1) * block)

    def expand(step):
        h, slot = divmod(step, shape.slots)
        pre[step % 3] = dot(normed[pl.ds(slot * per_slot, per_slot), :], w_in[:, span(h)], 1, 0)

    def activate(step):
        h, slot = divmod(step, shape.slots)
        rows, cols = pl.ds(slot * per_slot, per_slot), span(h)
        value = pre[step % 3]
        square = value * value
        gate = 0.5 + 0.5 * jnp.tanh(value * (GELU_C + (GELU_C * GELU_A) * square))
        activated[rows, cols] = (value * gate).astype(BF16)
        slope = value * (2.0 * GELU_C + (6.0 * GELU_C * GELU_A) * square)
        grown = gate + slope * (gate - gate * gate)
        dpreact[rows, cols] = (dact[rows, cols] * grown).astype(BF16)

    def reduce_rows(h):
        of_in = dot(normed_t[...], dpreact[:, span(h)], 1, 0)
        of_out = dot(dproj_t[...], activated[:, span(h)], 1, 0)
        keep[span(h), :] = jnp.where(keeps_in, of_in, of_out)
        give[span(h), :] = jnp.where(keeps_in, of_out, of_in).astype(BF16)

    steps = blocks * shape.slots
    expand(0)
    for step in range(steps):
        if step + 1 < steps:
            expand(step + 1)
        activate(step)
        h, slot = divmod(step, shape.slots)
        if slot == 0 and h:
            reduce_rows(h - 1)
    reduce_rows(blocks - 1)


def fold_sum(value):
    return jnp.sum(value.reshape(-1, 8, value.shape[-1]), axis=0)


def norm_grad_kernel(shape, w_in, gain, dpreact, yhat, inverse, conv_grad, gain_part):
    chunk = TILE * TILE
    total = jnp.zeros((8, shape.channels), F32)
    for slot in range(shape.slots):
        rows = pl.ds(slot * chunk, chunk)
        dnormed = dot(dpreact[rows, :], w_in[...], 1, 1)
        unit = yhat[rows, :]
        total += fold_sum(dnormed * unit)
        dhat = dnormed * gain[...]
        mean = jnp.sum(dhat, axis=-1, keepdims=True) * (1.0 / shape.channels)
        along = jnp.sum(dhat * unit, axis=-1, keepdims=True) * (1.0 / shape.channels)
        scale = jnp.concatenate([inverse[rows, :]] * shape.parts, axis=1)
        conv_grad[rows, :] = (scale * (dhat - mean - unit * along)).astype(BF16)
    gain_part[...] = total


def state_kernel(
    shape, count_hbm, ocean_hbm, fields, tangent, w_out, scale, activated,
    state, scale_part,
    count, ocean, sems,
):
    fetch = Fetch(sems, (count_hbm, count), (ocean_hbm, ocean))
    fetch.wait(0, 1)
    chunk = TILE * TILE
    total = jnp.zeros((8, shape.channels), F32)
    for slot in range(shape.slots):
        rows = pl.ds(slot * chunk, chunk)
        flag = slot_flag(count, ocean, slot)
        projected = dot(activated[rows, :], w_out[...], 1, 0)
        kept = fields[rows, :].astype(F32) + scale[...] * projected
        state[rows, :] = (flag * kept).astype(BF16)
        total += fold_sum(flag * tangent[rows, :].astype(F32) * projected)
    scale_part[...] = total


def place_grad(shape, conv_grad, parts, spaced):
    blank = jnp.zeros((LEFT, LANES), F32)
    for at, part in enumerate(parts):
        for row in range(TILE):
            base = row * shape.pitch
            spaced[at, pl.ds(base, LEFT), :] = blank
            spaced[at, pl.ds(base + LEFT + shape.columns, LEFT), :] = blank
            for slot in range(shape.slots):
                cells = conv_grad[pl.ds(slot * TILE * TILE + row * TILE, TILE), shape.lanes(part)]
                spaced[at, pl.ds(base + LEFT + slot * TILE, TILE), :] = cells.astype(F32)


def taps_kernel(shape, part, band, top, conv_grad, small, padded, spaced):
    place_grad(shape, conv_grad, [part], spaced)
    kept = shape.early * shape.pitch
    padded[0, pl.ds(0, kept), :] = band[part, pl.ds(0, kept), :]
    padded[0, pl.ds(kept, top.shape[1]), :] = top[part]
    run = shape.columns // 8
    origin = LEFT - HALF
    for above in range(KSIZE):

        def one_row(row, sums, above=above):
            base = (row + above) * shape.pitch + origin
            loaded = [padded[0, pl.ds(base + at, 8, stride=run), :] for at in range(run + KSIZE - 1)]
            start = row * shape.pitch + LEFT
            grads = [spaced[0, pl.ds(start + at, 8, stride=run), :] for at in range(run)]
            sums = list(sums)
            for shift in range(KSIZE):
                for at in range(run):
                    sums[shift] = sums[shift] + grads[at] * loaded[at + shift]
            return tuple(sums)

        blank = tuple(jnp.zeros((8, LANES), F32) for _ in range(KSIZE))
        sums = lax.fori_loop(0, TILE, one_row, blank, unroll=2)
        for shift in range(KSIZE):
            small[pl.ds(above * KSIZE + shift, 1), :] = jnp.sum(sums[shift], axis=0, keepdims=True)


def back_kernel(shape, part, count_hbm, kernel, conv_grad, *refs):
    before = refs[:part]
    turns = part == shape.parts - 1
    core_grad, *refs = refs[part:]
    if turns:
        fold, *refs = refs
    count, spaced, taps, sems = refs
    fetch = Fetch(sems, (count_hbm, count))
    place_grad(shape, conv_grad, [part], spaced)
    blank = jnp.zeros((LEFT, LANES), F32)
    for row in range(TILE + HALF):
        core_grad[pl.ds(row * shape.pitch, LEFT), :] = blank
        core_grad[pl.ds((row + 1) * shape.pitch - LEFT, LEFT), :] = blank
    spread_taps(shape, kernel, [part], taps)
    run = -(-(shape.columns + 2 * HALF) // 8)

    def one_row(row, tap_rows):
        sums = [None] * run
        for above in tap_rows:
            base = (row - above) * shape.pitch + LEFT
            loaded = [
                spaced[0, pl.ds(base + at - KSIZE + 1, 8, stride=run), :] for at in range(run + KSIZE - 1)
            ]
            for shift in range(KSIZE):
                weight = taps[0, above * KSIZE + shift]
                for at in range(run):
                    term = weight * loaded[at - shift + KSIZE - 1]
                    sums[at] = term if sums[at] is None else sums[at] + term
        start = (row - HALF) * shape.pitch + LEFT - HALF
        for at in range(run):
            core_grad[pl.ds(start + at, 8, stride=run), :] = sums[at]

    inner = (KSIZE - 1, TILE - 1)
    for row in range(HALF, TILE + 2 * HALF):
        if not inner[0] <= row <= inner[1]:
            low = max(0, row - TILE + 1)
            one_row(row, range(low, min(KSIZE - 1, row) + 1))

    def inner_row(step, carry):
        one_row(step, range(KSIZE))
        return carry

    lax.fori_loop(inner[0], inner[1] + 1, inner_row, 0)
    fetch.wait(0)
    if turns:
        flip = flip_matrix(shape.pitch, count[0] * TILE + 2 * LEFT - 1)
        for k in range(HALF):
            at = pl.ds((TILE + k) * shape.pitch, shape.pitch)
            cells = jnp.concatenate([one[at, :] for one in (*before, core_grad)], axis=1)
            turned = dot(flip, cells.astype(BF16), 1, 0)
            fold[pl.ds(k * shape.pitch, shape.pitch), :] = turned.astype(BF16)


def rims_kernel(shape, count_hbm, fold, *refs):
    core_grad = refs[: shape.parts]
    folded, first, second, count, sems = refs[shape.parts :]
    fetch = Fetch(sems, (count_hbm, count))
    for part in range(shape.parts):
        folded[part] = core_grad[part][pl.ds(0, TILE * shape.pitch), :]
        for k in range(HALF):
            rows = pl.ds((TILE - 1 - k) * shape.pitch, shape.pitch)
            returned = fold[pl.ds(k * shape.pitch, shape.pitch), shape.lanes(part)]
            folded[part, rows, :] += returned.astype(F32)
    fetch.wait(0)
    west = edge_planes(shape, folded, LEFT - HALF, shape.pitch)
    east = edge_planes(shape, folded, LEFT + count[0] * TILE, shape.pitch)
    send_edges(shape, west, east, first, second)


def final_kernel(
    shape, count_hbm, ocean_hbm, tangent, folded, first, second,
    grad_fields, done,
    count, ocean, work, sems,
):
    fetch = Fetch(sems, (count_hbm, count), (ocean_hbm, ocean))
    even = is_even()
    done[...] = jnp.zeros_like(done)
    work[...] = folded[...]
    fetch.wait(0, 1)
    used = count[0] * TILE
    for part in range(shape.parts):
        for col in range(HALF):
            planes = pl.ds(col * TILE, TILE)
            one = first[planes, shape.lanes(part)].astype(F32)
            two = second[planes, shape.lanes(part)].astype(F32)
            to_tail = jnp.where(even, one, two)
            to_head = jnp.where(even, two, one)
            head = pl.ds(LEFT + col, TILE, stride=shape.pitch)
            work[part, head, :] = work[part, head, :] + to_head
            tail = pl.ds(LEFT + used - HALF + col, TILE, stride=shape.pitch)
            work[part, tail, :] = work[part, tail, :] + to_tail
        for slot in range(shape.slots):
            flag = slot_flag(count, ocean, slot)
            for row in range(TILE):
                rows = pl.ds(slot * TILE * TILE + row * TILE, TILE)
                cells = work[part, pl.ds(row * shape.pitch + LEFT + slot * TILE, TILE), :]
                total = tangent[rows, shape.lanes(part)].astype(F32) + cells
                grad_fields[rows, shape.lanes(part)] = (flag * total).astype(BF16)


def unpack_kernel(norm, own, came, w_in, w_out, kernel_sum, gain_sum, scale_sum, work_in, work_out, sems):
    is_first = lax.axis_index("core") == 0
    hidden, channels = w_out.shape
    copies = []
    for h in range(hidden // channels):
        block = slice(h * channels, (h + 1) * channels)
        mine = own[block, :].astype(F32) * norm
        theirs = came[block, :].astype(F32) * norm
        work_in[:, block] = jnp.where(is_first, mine, theirs)
        copies.append(pltpu.make_async_copy(work_in.at[:, block], w_in.at[:, block], sems.at[2 * h]))
        copies[-1].start()
        work_out[block, :] = jnp.where(is_first, theirs, mine).T
        copies.append(pltpu.make_async_copy(work_out.at[block, :], w_out.at[block, :], sems.at[2 * h + 1]))
        copies[-1].start()
    extra = (own.shape[0] - hidden) // 2
    high, low = pl.ds(hidden, extra), pl.ds(hidden + extra, extra)
    mine = (own[high, :].astype(F32) + own[low, :].astype(F32)) * norm
    theirs = (came[high, :].astype(F32) + came[low, :].astype(F32)) * norm
    small = jnp.concatenate([jnp.where(is_first, mine, theirs), jnp.where(is_first, theirs, mine)])
    for above in range(KSIZE):
        kernel_sum[above] = small[above * KSIZE : (above + 1) * KSIZE, :]
    gain_sum[...] = small[KSIZE * KSIZE : KSIZE * KSIZE + 1, :]
    scale_sum[...] = small[KSIZE * KSIZE + 1 : KSIZE * KSIZE + 2, :]
    for copy in copies:
        copy.wait()


def pairs_of(kind):
    count = lax.axis_size(TILES)
    half = count // 2
    place = [rank if rank < half else count - 1 + half - rank for rank in range(count)]
    partner = {
        "first": lambda rank: rank ^ 1,
        "second": lambda rank: ((rank + 1) ^ 1) - 1,
        "fold": lambda rank: count - 1 - rank,
    }[kind]
    return [(place[rank], place[partner(rank) % count]) for rank in range(count)]


def swap(block, kind):
    return lax.ppermute(block, TILES, pairs_of(kind))


def core_swap(block):
    return lax.ppermute(block, "core", [(0, 1), (1, 0)])


def stages():
    chip_bits = lax.axis_size("chips").bit_length() - 1
    rest = list(range(2, chip_bits))
    return list(zip([0, -1, 1] + rest, [1, 0, -1] + rest))


def bit_swap(block, stage):
    chips, cores, samples = (lax.axis_size(axis) for axis in ("chips", "core", "dp"))
    pairs = []
    for chip in range(chips):
        for core in range(cores):
            for sample in range(samples):
                bit = stage[core]
                to = (chip, sample ^ 1) if bit < 0 else (chip ^ (1 << bit), sample)
                pairs.append(
                    ((chip * cores + core) * samples + sample, (to[0] * cores + core) * samples + to[1])
                )
    return lax.ppermute(block, ("chips", "core", "dp"), pairs)


def bit_here(stage):
    bits = [
        lax.axis_index("dp") if bit < 0 else lax.axis_index("chips") >> bit & 1 for bit in stage
    ]
    return jnp.where(lax.axis_index("core") == 0, bits[0], bits[1])


def half_rows(bit, rows):
    return pl.ds(pl.multiple_of(bit * rows, rows), rows)


def join_kernel(stage, keep, came, mine, send):
    rows = send.shape[0]
    mine[...] = keep[...] + came[...].astype(F32)
    send[...] = mine[half_rows(1 - bit_here(stage), rows), :].astype(BF16)


def halve_kernel(stage, following, whole, came, mine, send):
    rows = mine.shape[0]
    mine[...] = whole[half_rows(bit_here(stage), rows), :] + came[...].astype(F32)
    send[...] = mine[half_rows(1 - bit_here(following), rows // 2), :].astype(BF16)


def pack_kernel(gain_part, scale_part, *refs):
    taps, (keep, send, work) = refs[:-3], refs[-3:]
    half = keep.shape[0]
    work[...] = jnp.zeros_like(work)
    for part, ref in enumerate(taps):
        work[pl.ds(0, ref.shape[0]), part * LANES : (part + 1) * LANES] = ref[...]
    work[pl.ds(KSIZE * KSIZE, 1), :] = jnp.sum(gain_part[...], axis=0, keepdims=True)
    work[pl.ds(KSIZE * KSIZE + 1, 1), :] = jnp.sum(scale_part[...], axis=0, keepdims=True)
    core = lax.axis_index("core")
    keep[...] = work[half_rows(core, half), :]
    value = work[half_rows(1 - core, half), :]
    high = value.astype(BF16)
    send[pl.ds(0, half), :] = high
    send[pl.ds(half, half), :] = (value - high.astype(F32)).astype(BF16)


def turn_kernel(stage, whole, came, keep, extra, payload):
    rows, half = came.shape[0], keep.shape[0]
    share = whole[half_rows(bit_here(stage), rows), :] + came[...].astype(F32)
    payload[pl.ds(0, rows), :] = share.astype(BF16)
    small = keep[...] + (extra[pl.ds(0, half), :].astype(F32) + extra[pl.ds(half, half), :].astype(F32))
    payload[pl.ds(rows, half), :] = small.astype(BF16)


def add_kernel(own, came, payload):
    payload[...] = (own[...].astype(F32) + came[...].astype(F32)).astype(BF16)


def double_kernel(stage, extra, own, came, payload):
    rows = own.shape[0] - extra
    bit = bit_here(stage)
    payload[half_rows(bit, rows), :] = own[pl.ds(0, rows), :]
    payload[half_rows(1 - bit, rows), :] = came[pl.ds(0, rows), :]
    total = own[pl.ds(rows, extra), :].astype(F32) + came[pl.ds(rows, extra), :].astype(F32)
    high = total.astype(BF16)
    payload[pl.ds(2 * rows, extra), :] = high
    if payload.shape[0] > 2 * rows + extra:
        payload[pl.ds(2 * rows + extra, extra), :] = (total - high.astype(F32)).astype(BF16)


def halved(mine, send, order):
    for at, stage in enumerate(order[:-1]):
        came = bit_swap(send, stage)
        rows = came.shape[0]
        bit = bit_here(stage)
        mine = lax.dynamic_index_in_dim(mine.reshape(2, rows, -1), bit, 0, keepdims=False) + came.astype(F32)
        bit = bit_here(order[at + 1])
        halves = mine.reshape(2, rows // 2, -1)
        send = lax.dynamic_index_in_dim(halves, 1 - bit, 0, keepdims=False).astype(BF16)
    return mine, send


def call(kernel, outs, scratch, hbm, vmem, copies=0, micros=1.0, after=(), limit=20, in_hbm=0):
    in_specs = [pl.BlockSpec(memory_space=pl.ANY)] * len(hbm)
    in_specs += [pl.BlockSpec(memory_space=pltpu.VMEM)] * len(vmem)
    in_specs += [pl.BlockSpec(memory_space=pl.ANY)] * len(after)
    shapes = [pltpu.SMEM(*one) if one[1] == jnp.int32 else pltpu.VMEM(*one) for one in scratch]
    if copies:
        shapes.append(pltpu.SemaphoreType.DMA((copies,)))
    taken = len(hbm) + len(vmem)

    def body(*refs):
        kernel(*refs[:taken], *refs[taken + len(after) :])

    return pl.pallas_call(
        body,
        out_shape=[jax.ShapeDtypeStruct(*out) for out in outs],
        in_specs=in_specs,
        out_specs=[pl.BlockSpec(memory_space=pl.ANY if at < in_hbm else pltpu.VMEM) for at in range(len(outs))],
        scratch_shapes=shapes,
        cost_estimate=pl.CostEstimate(flops=int(micros * 1e9), bytes_accessed=0, transcendentals=0),
        compiler_params=pltpu.CompilerParams(vmem_limit_bytes=limit * 1024 * 1024),
    )(*hbm, *vmem, *after)


def shards(fields, grad_out, block_count, ocean, kernel, ln_gain, w_in, w_out, layer_scale):
    samples, slots, tile_rows, tile_cols, channels = fields.shape
    hidden = w_in.shape[1]
    shape = Shape(slots, channels, hidden)
    cells, parts, pitch = shape.cells, shape.parts, shape.pitch
    grid = fields.shape
    fields = fields.reshape(cells, channels)
    tangent = grad_out.reshape(cells, channels)
    taps_in = kernel
    gain = ln_gain.reshape(1, channels)
    scale = layer_scale.reshape(1, channels)

    def bind(body):
        return functools.partial(body, shape)

    def strip(rows):
        return ((parts, rows * pitch, LANES), F32)

    edge = ((shape.edge_rows, channels), BF16)
    turned = ((HALF * pitch, channels), BF16)
    whole = ((cells, channels), BF16)
    whole_f = ((cells, channels), F32)
    wide = ((cells, hidden), BF16)
    narrow = ((cells, LANES), F32)
    row = ((1, channels), F32)
    eight = ((8, channels), F32)
    taps = ((parts, KSIZE * KSIZE, 8, LANES), F32)
    count_s = (block_count.shape, jnp.int32)
    ocean_s = (ocean.shape, jnp.int32)
    flat = ((channels, cells), BF16)
    ends = ((HALF * 2 * LEFT, channels), BF16)
    ends_f = ((parts, HALF * 2 * LEFT, LANES), F32)
    late = TILE - shape.early

    first, second = call(
        bind(prep_kernel), [edge, edge], [count_s, ((parts, cells, LANES), F32)],
        [block_count], [fields], 1, 1.0,
    )
    (fold,) = call(
        bind(top_kernel), [((HALF * shape.columns, channels), BF16)], [count_s, ocean_s],
        [block_count, ocean], [fields], 2, 0.5, after=[first],
    )
    first, second = swap(first, "first"), swap(second, "second")
    band, rims = call(
        bind(band_kernel), [strip(TILE + HALF), ends], [count_s, ocean_s],
        [block_count, ocean], [fields, first, second], 2, 1.0, after=[fold],
    )
    fold, rims = swap(fold, "fold"), swap(rims, "fold")
    normed, yhat, inverse, dproj_t, dact = call(
        bind(early_kernel), [whole, whole_f, narrow, flat, ((cells, hidden), F32)],
        [count_s, ocean_s, taps, ((parts, shape.early * shape.columns, LANES), F32), whole],
        [block_count, ocean], [taps_in, gain, w_out, scale, tangent, band], 2, 5.0,
    )
    keep, give, activated, dpreact, yhat, inverse, top = call(
        bind(late_kernel),
        [((hidden, channels), F32), ((hidden, channels), BF16), wide, wide, whole_f, narrow, strip(late + 2 * HALF)],
        [
            count_s, taps, ((parts, late * shape.columns, LANES), F32), whole, flat, ends_f,
            ((3, TILE * TILE, channels), F32),
        ],
        [block_count],
        [taps_in, gain, w_in, band, fold, rims, normed, yhat, inverse, dproj_t, dact], 1, 5.0,
    )

    order = stages()
    rows = hidden // 2

    def half_step(at, rows):
        return functools.partial(halve_kernel, order[at], order[at + 1]), [
            ((rows, channels), F32), ((rows // 2, channels), BF16),
        ]

    def taps_part(part, after):
        (small,) = call(
            functools.partial(taps_kernel, shape, part), [((small_rows, LANES), F32)],
            [((1, (TILE + 2 * HALF) * pitch, LANES), F32), ((1, TILE * pitch, LANES), F32)],
            [], [band, top, conv_grad], 0, 1.8, after=after,
        )
        return small

    def back_part(part, before, after):
        outs = [(((TILE + HALF) * pitch, LANES), F32)] + [turned] * (part == parts - 1)
        return call(
            functools.partial(back_kernel, shape, part), outs,
            [count_s, ((1, TILE * pitch, LANES), F32), ((1, KSIZE * KSIZE, 8, LANES), F32)],
            [block_count], [taps_in, conv_grad, *before], 1, 2.0, after=after,
        )

    small_rows = -(-(KSIZE * KSIZE + 2) // 32) * 32
    came = core_swap(give)
    conv_grad, gain_part = call(
        bind(norm_grad_kernel), [whole, eight], [], [], [w_in, gain, dpreact, yhat, inverse], 0, 1.0,
    )
    mine, send = call(
        functools.partial(join_kernel, order[0]),
        [((hidden, channels), F32), ((rows, channels), BF16)], [], [], [keep, came], after=[conv_grad], micros=0.3,
    )
    came = bit_swap(send, order[0])
    taps_parts = [taps_part(0, [send])]
    state, scale_part = call(
        bind(state_kernel), [whole, eight], [count_s, ocean_s],
        [block_count, ocean], [fields, tangent, w_out, scale, activated], 2, 1.5, after=taps_parts,
    )
    body, outs = half_step(0, rows)
    mine, send = call(body, outs, [], [], [mine, came], after=[scale_part], micros=0.3)
    came = bit_swap(send, order[1])
    taps_parts += [taps_part(part, [send]) for part in range(1, parts)]
    small_rows //= 2
    small, extra = call(
        pack_kernel, [((small_rows, channels), F32), ((2 * small_rows, channels), BF16)],
        [((2 * small_rows, channels), F32)], [], [gain_part, scale_part, *taps_parts], micros=0.3,
    )
    rows //= 2
    body, outs = half_step(1, rows)
    mine, send = call(body, outs, [], [], [mine, came], after=[small], micros=0.3)
    extra = core_swap(extra)
    mine, send = halved(mine, send, order[2:-1])
    came = bit_swap(send, order[-2])
    core_grad = []
    for part in range(parts - 1):
        core_grad += back_part(part, core_grad, [send])
    rows = came.shape[0]
    if rows % 16 == 0:
        (payload,) = call(
            functools.partial(turn_kernel, order[-2]), [((rows + small_rows, channels), BF16)],
            [], [], [mine, came, small, extra], after=core_grad, micros=0.3,
        )
    else:
        bit = bit_here(order[-2])
        share = lax.dynamic_index_in_dim(mine.reshape(2, rows, channels), bit, 0, keepdims=False)
        small = small + (extra[:small_rows].astype(F32) + extra[small_rows:].astype(F32))
        payload = jnp.concatenate([share + came.astype(F32), small]).astype(BF16)
    came = bit_swap(payload, order[-1])
    last_grad, fold_back = back_part(parts - 1, core_grad, [payload])
    core_grad += [last_grad]
    fold_back = swap(fold_back, "fold")
    (payload,) = call(
        add_kernel, [(payload.shape, BF16)], [], [], [payload, came], after=[last_grad], micros=0.3,
    )
    came = bit_swap(payload, order[-2])
    after = [fold_back]
    for at in reversed(range(len(order) - 1)):
        copies = 2 if at == 0 else 1
        if rows % 16 == 0:
            (payload,) = call(
                functools.partial(double_kernel, order[at], small_rows),
                [((2 * rows + copies * small_rows, channels), BF16)],
                [], [], [payload, came], after=after, micros=0.3,
            )
        else:
            is_low = bit_here(order[at]) == 0
            low, high = payload[:rows], came[:rows]
            both = payload[rows:].astype(F32) + came[rows:].astype(F32)
            joined = [jnp.where(is_low, low, high), jnp.where(is_low, high, low), both.astype(BF16)]
            payload = jnp.concatenate(joined)
        after = []
        rows *= 2
        came = bit_swap(payload, order[at - 1]) if at else core_swap(payload)
        if at == 2:
            folded, first, second = call(
                bind(rims_kernel), [strip(TILE), edge, edge], [count_s], [block_count], [fold_back, *core_grad], 1, 1.0,
                after=[payload],
            )
            first, second = swap(first, "first"), swap(second, "second")
            after = [first, second]
        if at == 1:
            grad_fields, done = call(
                bind(final_kernel), [whole, ((8, LANES), F32)], [count_s, ocean_s, strip(TILE)],
                [block_count, ocean], [tangent, folded, first, second], 2, 1.5, after=[payload],
            )
            after = [done]
    total = samples * lax.axis_size("dp") * slots * lax.axis_size(TILES) * tile_rows * tile_cols
    norm = total ** (-0.5)
    sums = [((channels, hidden), F32), ((hidden, channels), F32)]
    w_in_sum, w_out_sum, kernel_sum, gain_sum, scale_sum = call(
        functools.partial(unpack_kernel, norm), sums + [(kernel.shape, F32), row, row], sums,
        [], [payload, came], 2 * hidden // channels, 1.5, in_hbm=2,
    )
    return (
        state.reshape(grid),
        grad_fields.reshape(grid),
        kernel_sum,
        gain_sum.reshape(ln_gain.shape),
        w_in_sum,
        w_out_sum,
        scale_sum.reshape(layer_scale.shape),
    )


def solution(mesh):
    cores = Mesh(mesh.devices.reshape(-1, 2, mesh.devices.shape[1]), ("chips", "core", "dp"))
    banded = P("dp", TILES, None, None, None)
    placed = (banded, banded, P(TILES), P(TILES), P(), P(), P(), P(), P())
    return jax.shard_map(
        shards,
        mesh=cores,
        in_specs=placed,
        out_specs=(banded, banded, P(), P(), P(), P(), P()),
        check_vma=False,
    )
```

```python
import functools

import jax
import jax.numpy as jnp
from jax import lax
from jax.experimental import pallas as pl
from jax.experimental.pallas import tpu as pltpu
from jax.sharding import Mesh, PartitionSpec as P

KSIZE = 7
HALF = KSIZE // 2
TILE = 16
EPS = 1e-06
TILES = ("chips", "core")
F32 = jnp.float32
BF16 = jnp.bfloat16
LANES = 128
LEFT = 8
GELU_C = 0.7978845608028654
GELU_A = 0.044715


def dot(lhs, rhs, lhs_dim, rhs_dim):
    return lax.dot_general(
        lhs, rhs, (((lhs_dim,), (rhs_dim,)), ((), ())), preferred_element_type=F32
    )


def cycle_rank():
    count = lax.axis_size(TILES)
    here = lax.axis_index("chips") * lax.axis_size("core") + lax.axis_index("core")
    return jnp.where(here < count // 2, here, count - 1 + count // 2 - here)


def is_even():
    return lax.rem(cycle_rank(), 2) == 0


class Fetch:
    def __init__(self, sems, *pairs):
        self.copies = [
            pltpu.make_async_copy(source, target, sems.at[at]) for at, (source, target) in enumerate(pairs)
        ]
        for copy in self.copies:
            copy.start()

    def wait(self, *which):
        for at in which:
            self.copies[at].wait()


def slot_flag(count_ref, ocean_ref, slot):
    live = jnp.logical_and(slot < count_ref[0], ocean_ref[slot] > 0)
    return jnp.where(live, 1.0, 0.0).astype(F32)


class Shape:
    def __init__(self, slots, channels, hidden):
        self.slots = slots
        self.channels = channels
        self.hidden = hidden
        self.parts = channels // LANES
        self.columns = slots * TILE
        self.pitch = self.columns + 2 * LEFT
        self.cells = slots * TILE * TILE
        self.edge_rows = HALF * TILE
        self.early = 12

    def lanes(self, part):
        return slice(part * LANES, (part + 1) * LANES)


def edge_planes(shape, source, start, stride):
    return [
        jnp.concatenate(
            [source[part, pl.ds(start + col, TILE, stride=stride), :] for part in range(shape.parts)], axis=1
        )
        for col in range(HALF)
    ]


def send_edges(shape, left, right, first, second):
    even = is_even()
    for col in range(HALF):
        rows = pl.ds(col * TILE, TILE)
        first[rows, :] = jnp.where(even, right[col], left[col]).astype(BF16)
        second[rows, :] = jnp.where(even, left[col], right[col]).astype(BF16)


def flip_matrix(size, last):
    to = lax.broadcasted_iota(jnp.int32, (size, size), 0)
    frm = lax.broadcasted_iota(jnp.int32, (size, size), 1)
    return jnp.where(to + frm == last, 1.0, 0.0).astype(BF16)


def prep_kernel(shape, count_hbm, fields, first, second, count, work, sems):
    fetch = Fetch(sems, (count_hbm, count))
    for part in range(shape.parts):
        work[part] = fields[:, shape.lanes(part)].astype(F32)
    left = edge_planes(shape, work, 0, TILE)
    fetch.wait(0)
    right = edge_planes(shape, work, (count[0] - 1) * TILE * TILE + TILE - HALF, TILE)
    send_edges(shape, left, right, first, second)


def top_kernel(shape, count_hbm, ocean_hbm, fields, fold, count, ocean, sems):
    fetch = Fetch(sems, (count_hbm, count), (ocean_hbm, ocean))
    fetch.wait(0, 1)
    flip = flip_matrix(shape.columns, count[0] * TILE - 1)
    for k in range(HALF):
        cells = jnp.concatenate(
            [
                fields[pl.ds(slot * TILE * TILE + (TILE - 1 - k) * TILE, TILE), :].astype(F32)
                * slot_flag(count, ocean, slot)
                for slot in range(shape.slots)
            ]
        )
        turned = dot(flip, cells.astype(BF16), 1, 0)
        fold[pl.ds(k * shape.columns, shape.columns), :] = turned.astype(BF16)


def band_kernel(shape, count_hbm, ocean_hbm, fields, first, second, band, rims, count, ocean, sems):
    fetch = Fetch(sems, (count_hbm, count), (ocean_hbm, ocean))
    even = is_even()
    blank = jnp.zeros((LEFT, LANES), F32)
    per_slot = TILE * TILE
    for part in range(shape.parts):
        band[part, pl.ds(0, HALF * shape.pitch), :] = jnp.zeros((HALF * shape.pitch, LANES), F32)
        for row in range(TILE):
            base = (row + HALF) * shape.pitch
            band[part, pl.ds(base, LEFT), :] = blank
            band[part, pl.ds(base + LEFT + shape.columns, LEFT), :] = blank
    fetch.wait(0, 1)
    used = count[0] * TILE
    flags = [slot_flag(count, ocean, slot) for slot in range(shape.slots)]
    top = HALF * shape.pitch
    for part in range(shape.parts):
        for row in range(TILE):
            base = (row + HALF) * shape.pitch
            for slot in range(shape.slots):
                cells = fields[pl.ds(slot * per_slot + row * TILE, TILE), shape.lanes(part)]
                band[part, pl.ds(base + LEFT + slot * TILE, TILE), :] = cells.astype(F32) * flags[slot]
        for col in range(HALF):
            rows = pl.ds(col * TILE, TILE)
            one = first[rows, shape.lanes(part)].astype(F32)
            two = second[rows, shape.lanes(part)].astype(F32)
            west = jnp.where(even, two, one)
            east = jnp.where(even, one, two)
            band[part, pl.ds(top + LEFT - HALF + col, TILE, stride=shape.pitch), :] = west
            band[part, pl.ds(top + LEFT + used + col, TILE, stride=shape.pitch), :] = east
    for k in range(HALF):
        base = (HALF + TILE - 1 - k) * shape.pitch
        east = pl.multiple_of(base + LEFT + used, LEFT)
        for part in range(shape.parts):
            ends = jnp.concatenate([band[part, pl.ds(base, LEFT), :], band[part, pl.ds(east, LEFT), :]])
            rims[pl.ds(k * 2 * LEFT, 2 * LEFT), shape.lanes(part)] = ends.astype(BF16)


def put_fold(shape, used, fold, rims, parts, padded, first_row, work):
    blank = jnp.zeros((LEFT, LANES), F32)
    for at, part in enumerate(parts):
        work[at] = rims[:, shape.lanes(part)].astype(F32)
        for k in range(HALF):
            base = (first_row + k) * shape.pitch
            padded[at, pl.ds(base, LEFT), :] = blank
            padded[at, pl.ds(base + LEFT + shape.columns, LEFT), :] = blank
            cells = fold[pl.ds(k * shape.columns, shape.columns), shape.lanes(part)]
            padded[at, pl.ds(base + LEFT, shape.columns), :] = cells.astype(F32)
            for col in range(HALF):
                west = work[at, pl.ds(k * 2 * LEFT + LEFT - 1 - col, 1), :]
                east = work[at, pl.ds(k * 2 * LEFT + LEFT + col, 1), :]
                padded[at, pl.ds(base + LEFT - 1 - col, 1), :] = east
                padded[at, pl.ds(base + LEFT + used + col, 1), :] = west


def spread_taps(shape, kernel, parts, taps):
    for above in range(KSIZE):
        rows = kernel[above].astype(F32)
        for at, part in enumerate(parts):
            for shift in range(KSIZE):
                row = rows[shift : shift + 1, shape.lanes(part)]
                taps[at, above * KSIZE + shift] = jnp.broadcast_to(row, (8, LANES))


def convolve(shape, rows, padded, taps, convolved):
    run = shape.columns // 8
    pair = 2
    origin = LEFT - HALF

    def two_rows(step, carry):
        row = step * pair
        for part in range(shape.parts):
            sums = [[None] * run for _ in range(pair)]
            for above in range(KSIZE + pair - 1):
                base = (row + above) * shape.pitch + origin
                loaded = [
                    padded[part, pl.ds(base + at, 8, stride=run), :]
                    for at in range(run + KSIZE - 1)
                ]
                for which in range(pair):
                    tap_row = above - which
                    if not 0 <= tap_row < KSIZE:
                        continue
                    for shift in range(KSIZE):
                        weight = taps[part, tap_row * KSIZE + shift]
                        for at in range(run):
                            term = weight * loaded[at + shift]
                            old = sums[which][at]
                            sums[which][at] = term if old is None else old + term
            for which in range(pair):
                for at in range(run):
                    start = (row + which) * shape.columns + at
                    convolved[part, pl.ds(start, 8, stride=run), :] = sums[which][at]
        return carry

    lax.fori_loop(0, rows // pair, two_rows, 0)


def normalise(shape, rows, first_row, convolved, gain, normed, yhat, inverse):
    def one_row(row, carry):
        for slot in range(shape.slots):
            start = pl.multiple_of(row * shape.columns + slot * TILE, TILE)
            at = slot * TILE * TILE + (first_row + row) * TILE
            out = pl.ds(pl.multiple_of(at, TILE), TILE)
            parts = [convolved[part, pl.ds(start, TILE), :] for part in range(shape.parts)]
            mean = jnp.sum(sum(parts), axis=-1, keepdims=True) * (1.0 / shape.channels)
            parts = [value - mean for value in parts]
            square = jnp.sum(sum(value * value for value in parts), axis=-1, keepdims=True)
            scale = lax.rsqrt(square * (1.0 / shape.channels) + EPS)
            inverse[out, :] = jnp.broadcast_to(scale, (TILE, LANES))
            for part in range(shape.parts):
                value = parts[part] * scale
                yhat[out, shape.lanes(part)] = value
                normed[out, shape.lanes(part)] = (value * gain[:, shape.lanes(part)]).astype(BF16)
        return carry

    lax.fori_loop(0, rows, one_row, 0, unroll=4)


def early_kernel(
    shape, count_hbm, ocean_hbm, kernel, gain, w_out, scale, tangent, band,
    normed, yhat, inverse, dproj_t, dact, live,
    count, ocean, taps, convolved, dproj, sems,
):
    fetch = Fetch(sems, (count_hbm, count), (ocean_hbm, ocean))
    spread_taps(shape, kernel, range(shape.parts), taps)
    convolve(shape, shape.early, band, taps, convolved)
    normalise(shape, shape.early, 0, convolved, gain, normed, yhat, inverse)
    fetch.wait(0, 1)
    per_slot = TILE * TILE
    for slot in range(shape.slots):
        rows = pl.ds(slot * per_slot, per_slot)
        flag = slot_flag(count, ocean, slot)
        live[slot] = jnp.full((8, shape.channels), flag, F32)
        scaled = (tangent[rows, :].astype(F32) * (scale[...] * flag)).astype(BF16)
        dproj[rows, :] = scaled
        dproj_t[:, slot * per_slot : (slot + 1) * per_slot] = scaled.T
        for h in range(shape.hidden // shape.channels):
            cols = slice(h * shape.channels, (h + 1) * shape.channels)
            dact[rows, cols] = dot(dproj[rows, :], w_out[cols, :], 1, 1)


def late_kernel(
    shape, count_hbm, kernel, gain, w_in, band, fold, rims, normed_in, yhat_in, inverse_in, dproj_t, dact,
    keep, give, activated, dpreact, yhat, inverse, padded,
    count, taps, convolved, normed, normed_t, work, pre, sems,
):
    fetch = Fetch(sems, (count_hbm, count))
    late = TILE - shape.early
    kept = late + HALF
    for part in range(shape.parts):
        rows = pl.ds(shape.early * shape.pitch, kept * shape.pitch)
        padded[part, pl.ds(0, kept * shape.pitch), :] = band[part, rows, :]
    done = shape.early * TILE
    for slot in range(shape.slots):
        rows = pl.ds(slot * TILE * TILE, done)
        normed[rows, :] = normed_in[rows, :]
        yhat[rows, :] = yhat_in[rows, :]
        inverse[rows, :] = inverse_in[rows, :]
    spread_taps(shape, kernel, range(shape.parts), taps)
    fetch.wait(0)
    put_fold(shape, count[0] * TILE, fold, rims, range(shape.parts), padded, kept, work)
    convolve(shape, late, padded, taps, convolved)
    normalise(shape, late, shape.early, convolved, gain, normed, yhat, inverse)
    per_slot = TILE * TILE
    for slot in range(shape.slots):
        normed_t[:, slot * per_slot : (slot + 1) * per_slot] = normed[pl.ds(slot * per_slot, per_slot), :].T
    keeps_in = lax.axis_index("core") == 0
    block = shape.channels
    blocks = shape.hidden // block

    def span(h):
        return slice(h * block, (h + 1) * block)

    def expand(step):
        h, slot = divmod(step, shape.slots)
        pre[step % 3] = dot(normed[pl.ds(slot * per_slot, per_slot), :], w_in[:, span(h)], 1, 0)

    def activate(step):
        h, slot = divmod(step, shape.slots)
        rows, cols = pl.ds(slot * per_slot, per_slot), span(h)
        value = pre[step % 3]
        square = value * value
        gate = 0.5 + 0.5 * jnp.tanh(value * (GELU_C + (GELU_C * GELU_A) * square))
        activated[rows, cols] = (value * gate).astype(BF16)
        slope = value * (2.0 * GELU_C + (6.0 * GELU_C * GELU_A) * square)
        grown = gate + slope * (gate - gate * gate)
        dpreact[rows, cols] = (dact[rows, cols] * grown).astype(BF16)

    def reduce_rows(h):
        of_in = dot(normed_t[...], dpreact[:, span(h)], 1, 0)
        of_out = dot(dproj_t[...], activated[:, span(h)], 1, 0)
        keep[span(h), :] = jnp.where(keeps_in, of_in, of_out)
        give[span(h), :] = jnp.where(keeps_in, of_out, of_in).astype(BF16)

    steps = blocks * shape.slots
    expand(0)
    for step in range(steps):
        if step + 1 < steps:
            expand(step + 1)
        activate(step)
        h, slot = divmod(step, shape.slots)
        if slot == 0 and h:
            reduce_rows(h - 1)
    reduce_rows(blocks - 1)


def fold_sum(value):
    return jnp.sum(value.reshape(-1, 8, value.shape[-1]), axis=0)


def norm_grad_kernel(
    shape, w_in, w_out, gain, dpreact, yhat, inverse, activated, tangent, live,
    conv_grad, projected, gain_part, scale_part,
):
    chunk = TILE * TILE
    of_gain = jnp.zeros((8, shape.channels), F32)
    of_scale = jnp.zeros((8, shape.channels), F32)
    for slot in range(shape.slots):
        rows = pl.ds(slot * chunk, chunk)
        dnormed = dot(dpreact[rows, :], w_in[...], 1, 1)
        unit = yhat[rows, :]
        of_gain += fold_sum(dnormed * unit)
        dhat = dnormed * gain[...]
        mean = jnp.sum(dhat, axis=-1, keepdims=True) * (1.0 / shape.channels)
        along = jnp.sum(dhat * unit, axis=-1, keepdims=True) * (1.0 / shape.channels)
        scale = jnp.concatenate([inverse[rows, :]] * shape.parts, axis=1)
        conv_grad[rows, :] = (scale * (dhat - mean - unit * along)).astype(BF16)
        value = dot(activated[rows, :], w_out[...], 1, 0)
        projected[rows, :] = value
        of_scale += live[slot] * fold_sum(tangent[rows, :].astype(F32) * value)
    gain_part[...] = of_gain
    scale_part[...] = of_scale


def state_kernel(shape, fields, scale, projected, live, state, done):
    done[...] = jnp.zeros_like(done)
    chunk = TILE * TILE
    for slot in range(shape.slots):
        rows = pl.ds(slot * chunk, chunk)
        kept = fields[rows, :].astype(F32) + scale[...] * projected[rows, :]
        state[rows, :] = (live[slot, 0:1, :] * kept).astype(BF16)


def place_grad(shape, conv_grad, parts, spaced):
    blank = jnp.zeros((LEFT, LANES), F32)
    for at, part in enumerate(parts):
        for row in range(TILE):
            base = row * shape.pitch
            spaced[at, pl.ds(base, LEFT), :] = blank
            spaced[at, pl.ds(base + LEFT + shape.columns, LEFT), :] = blank
            for slot in range(shape.slots):
                cells = conv_grad[pl.ds(slot * TILE * TILE + row * TILE, TILE), shape.lanes(part)]
                spaced[at, pl.ds(base + LEFT + slot * TILE, TILE), :] = cells.astype(F32)


def taps_kernel(shape, part, band, top, conv_grad, small, padded, spaced):
    place_grad(shape, conv_grad, [part], spaced)
    kept = shape.early * shape.pitch
    padded[0, pl.ds(0, kept), :] = band[part, pl.ds(0, kept), :]
    padded[0, pl.ds(kept, top.shape[1]), :] = top[part]
    run = shape.columns // 8
    origin = LEFT - HALF
    for above in range(KSIZE):

        def one_row(row, sums, above=above):
            base = (row + above) * shape.pitch + origin
            loaded = [padded[0, pl.ds(base + at, 8, stride=run), :] for at in range(run + KSIZE - 1)]
            start = row * shape.pitch + LEFT
            grads = [spaced[0, pl.ds(start + at, 8, stride=run), :] for at in range(run)]
            sums = list(sums)
            for shift in range(KSIZE):
                for at in range(run):
                    sums[shift] = sums[shift] + grads[at] * loaded[at + shift]
            return tuple(sums)

        blank = tuple(jnp.zeros((8, LANES), F32) for _ in range(KSIZE))
        sums = lax.fori_loop(0, TILE, one_row, blank, unroll=2)
        for shift in range(KSIZE):
            small[pl.ds(above * KSIZE + shift, 1), :] = jnp.sum(sums[shift], axis=0, keepdims=True)


def back_kernel(shape, part, count_hbm, kernel, conv_grad, *refs):
    before = refs[:part]
    turns = part == shape.parts - 1
    core_grad, *refs = refs[part:]
    if turns:
        fold, *refs = refs
    count, spaced, taps, sems = refs
    fetch = Fetch(sems, (count_hbm, count))
    place_grad(shape, conv_grad, [part], spaced)
    blank = jnp.zeros((LEFT, LANES), F32)
    for row in range(TILE + HALF):
        core_grad[pl.ds(row * shape.pitch, LEFT), :] = blank
        core_grad[pl.ds((row + 1) * shape.pitch - LEFT, LEFT), :] = blank
    spread_taps(shape, kernel, [part], taps)
    run = -(-(shape.columns + 2 * HALF) // 8)

    def one_row(row, tap_rows):
        sums = [None] * run
        for above in tap_rows:
            base = (row - above) * shape.pitch + LEFT
            loaded = [
                spaced[0, pl.ds(base + at - KSIZE + 1, 8, stride=run), :] for at in range(run + KSIZE - 1)
            ]
            for shift in range(KSIZE):
                weight = taps[0, above * KSIZE + shift]
                for at in range(run):
                    term = weight * loaded[at - shift + KSIZE - 1]
                    sums[at] = term if sums[at] is None else sums[at] + term
        start = (row - HALF) * shape.pitch + LEFT - HALF
        for at in range(run):
            core_grad[pl.ds(start + at, 8, stride=run), :] = sums[at]

    inner = (KSIZE - 1, TILE - 1)
    for row in range(HALF, TILE + 2 * HALF):
        if not inner[0] <= row <= inner[1]:
            low = max(0, row - TILE + 1)
            one_row(row, range(low, min(KSIZE - 1, row) + 1))

    def inner_row(step, carry):
        one_row(step, range(KSIZE))
        return carry

    lax.fori_loop(inner[0], inner[1] + 1, inner_row, 0)
    fetch.wait(0)
    if turns:
        flip = flip_matrix(shape.pitch, count[0] * TILE + 2 * LEFT - 1)
        for k in range(HALF):
            at = pl.ds((TILE + k) * shape.pitch, shape.pitch)
            cells = jnp.concatenate([one[at, :] for one in (*before, core_grad)], axis=1)
            turned = dot(flip, cells.astype(BF16), 1, 0)
            fold[pl.ds(k * shape.pitch, shape.pitch), :] = turned.astype(BF16)


def rims_kernel(shape, count_hbm, fold, *refs):
    core_grad = refs[: shape.parts]
    folded, first, second, count, sems = refs[shape.parts :]
    fetch = Fetch(sems, (count_hbm, count))
    for part in range(shape.parts):
        folded[part] = core_grad[part][pl.ds(0, TILE * shape.pitch), :]
        for k in range(HALF):
            rows = pl.ds((TILE - 1 - k) * shape.pitch, shape.pitch)
            returned = fold[pl.ds(k * shape.pitch, shape.pitch), shape.lanes(part)]
            folded[part, rows, :] += returned.astype(F32)
    fetch.wait(0)
    west = edge_planes(shape, folded, LEFT - HALF, shape.pitch)
    east = edge_planes(shape, folded, LEFT + count[0] * TILE, shape.pitch)
    send_edges(shape, west, east, first, second)


def final_kernel(
    shape, count_hbm, ocean_hbm, tangent, folded, first, second,
    grad_fields, done,
    count, ocean, work, sems,
):
    fetch = Fetch(sems, (count_hbm, count), (ocean_hbm, ocean))
    even = is_even()
    done[...] = jnp.zeros_like(done)
    work[...] = folded[...]
    fetch.wait(0, 1)
    used = count[0] * TILE
    for part in range(shape.parts):
        for col in range(HALF):
            planes = pl.ds(col * TILE, TILE)
            one = first[planes, shape.lanes(part)].astype(F32)
            two = second[planes, shape.lanes(part)].astype(F32)
            to_tail = jnp.where(even, one, two)
            to_head = jnp.where(even, two, one)
            head = pl.ds(LEFT + col, TILE, stride=shape.pitch)
            work[part, head, :] = work[part, head, :] + to_head
            tail = pl.ds(LEFT + used - HALF + col, TILE, stride=shape.pitch)
            work[part, tail, :] = work[part, tail, :] + to_tail
        for slot in range(shape.slots):
            flag = slot_flag(count, ocean, slot)
            for row in range(TILE):
                rows = pl.ds(slot * TILE * TILE + row * TILE, TILE)
                cells = work[part, pl.ds(row * shape.pitch + LEFT + slot * TILE, TILE), :]
                total = tangent[rows, shape.lanes(part)].astype(F32) + cells
                grad_fields[rows, shape.lanes(part)] = (flag * total).astype(BF16)


def unpack_kernel(norm, own, came, w_in, w_out, kernel_sum, gain_sum, scale_sum):
    is_first = lax.axis_index("core") == 0
    hidden, channels = w_out.shape
    for h in range(hidden // channels):
        block = slice(h * channels, (h + 1) * channels)
        mine = own[block, :].astype(F32) * norm
        theirs = came[block, :].astype(F32) * norm
        w_in[:, block] = jnp.where(is_first, mine, theirs)
        w_out[block, :] = jnp.where(is_first, theirs, mine).T
    extra = (own.shape[0] - hidden) // 2
    high, low = pl.ds(hidden, extra), pl.ds(hidden + extra, extra)
    mine = (own[high, :].astype(F32) + own[low, :].astype(F32)) * norm
    theirs = (came[high, :].astype(F32) + came[low, :].astype(F32)) * norm
    small = jnp.concatenate([jnp.where(is_first, mine, theirs), jnp.where(is_first, theirs, mine)])
    for above in range(KSIZE):
        kernel_sum[above] = small[above * KSIZE : (above + 1) * KSIZE, :]
    gain_sum[...] = small[KSIZE * KSIZE : KSIZE * KSIZE + 1, :]
    scale_sum[...] = small[KSIZE * KSIZE + 1 : KSIZE * KSIZE + 2, :]


def pairs_of(kind):
    count = lax.axis_size(TILES)
    half = count // 2
    place = [rank if rank < half else count - 1 + half - rank for rank in range(count)]
    partner = {
        "first": lambda rank: rank ^ 1,
        "second": lambda rank: ((rank + 1) ^ 1) - 1,
        "fold": lambda rank: count - 1 - rank,
    }[kind]
    return [(place[rank], place[partner(rank) % count]) for rank in range(count)]


def swap(block, kind):
    return lax.ppermute(block, TILES, pairs_of(kind))


def core_swap(block):
    return lax.ppermute(block, "core", [(0, 1), (1, 0)])


def stages():
    chip_bits = lax.axis_size("chips").bit_length() - 1
    rest = list(range(2, chip_bits))
    return list(zip([0, -1, 1] + rest, [1, 0, -1] + rest))


def bit_swap(block, stage):
    chips, cores, samples = (lax.axis_size(axis) for axis in ("chips", "core", "dp"))
    pairs = []
    for chip in range(chips):
        for core in range(cores):
            for sample in range(samples):
                bit = stage[core]
                to = (chip, sample ^ 1) if bit < 0 else (chip ^ (1 << bit), sample)
                pairs.append(
                    ((chip * cores + core) * samples + sample, (to[0] * cores + core) * samples + to[1])
                )
    return lax.ppermute(block, ("chips", "core", "dp"), pairs)


def bit_here(stage):
    bits = [
        lax.axis_index("dp") if bit < 0 else lax.axis_index("chips") >> bit & 1 for bit in stage
    ]
    return jnp.where(lax.axis_index("core") == 0, bits[0], bits[1])


def half_rows(bit, rows):
    return pl.ds(pl.multiple_of(bit * rows, rows), rows)


def join_kernel(stage, keep, came, mine, send):
    rows = send.shape[0]
    mine[...] = keep[...] + came[...].astype(F32)
    send[...] = mine[half_rows(1 - bit_here(stage), rows), :].astype(BF16)


def halve_kernel(stage, following, whole, came, mine, send):
    rows = mine.shape[0]
    mine[...] = whole[half_rows(bit_here(stage), rows), :] + came[...].astype(F32)
    send[...] = mine[half_rows(1 - bit_here(following), rows // 2), :].astype(BF16)


def pack_kernel(gain_part, scale_part, *refs):
    taps, (keep, send, work) = refs[:-3], refs[-3:]
    half = keep.shape[0]
    work[...] = jnp.zeros_like(work)
    for part, ref in enumerate(taps):
        work[pl.ds(0, ref.shape[0]), part * LANES : (part + 1) * LANES] = ref[...]
    work[pl.ds(KSIZE * KSIZE, 1), :] = jnp.sum(gain_part[...], axis=0, keepdims=True)
    work[pl.ds(KSIZE * KSIZE + 1, 1), :] = jnp.sum(scale_part[...], axis=0, keepdims=True)
    core = lax.axis_index("core")
    keep[...] = work[half_rows(core, half), :]
    value = work[half_rows(1 - core, half), :]
    high = value.astype(BF16)
    send[pl.ds(0, half), :] = high
    send[pl.ds(half, half), :] = (value - high.astype(F32)).astype(BF16)


def turn_kernel(stage, whole, came, keep, extra, payload):
    rows, half = came.shape[0], keep.shape[0]
    share = whole[half_rows(bit_here(stage), rows), :] + came[...].astype(F32)
    payload[pl.ds(0, rows), :] = share.astype(BF16)
    small = keep[...] + (extra[pl.ds(0, half), :].astype(F32) + extra[pl.ds(half, half), :].astype(F32))
    payload[pl.ds(rows, half), :] = small.astype(BF16)


def add_kernel(own, came, payload):
    payload[...] = (own[...].astype(F32) + came[...].astype(F32)).astype(BF16)


def double_kernel(stage, extra, own, came, payload):
    rows = own.shape[0] - extra
    bit = bit_here(stage)
    payload[half_rows(bit, rows), :] = own[pl.ds(0, rows), :]
    payload[half_rows(1 - bit, rows), :] = came[pl.ds(0, rows), :]
    total = own[pl.ds(rows, extra), :].astype(F32) + came[pl.ds(rows, extra), :].astype(F32)
    high = total.astype(BF16)
    payload[pl.ds(2 * rows, extra), :] = high
    if payload.shape[0] > 2 * rows + extra:
        payload[pl.ds(2 * rows + extra, extra), :] = (total - high.astype(F32)).astype(BF16)


def halved(mine, send, order):
    for at, stage in enumerate(order[:-1]):
        came = bit_swap(send, stage)
        rows = came.shape[0]
        bit = bit_here(stage)
        mine = lax.dynamic_index_in_dim(mine.reshape(2, rows, -1), bit, 0, keepdims=False) + came.astype(F32)
        bit = bit_here(order[at + 1])
        halves = mine.reshape(2, rows // 2, -1)
        send = lax.dynamic_index_in_dim(halves, 1 - bit, 0, keepdims=False).astype(BF16)
    return mine, send


def call(kernel, outs, scratch, hbm, vmem, copies=0, micros=1.0, after=(), limit=20):
    in_specs = [pl.BlockSpec(memory_space=pl.ANY)] * len(hbm)
    in_specs += [pl.BlockSpec(memory_space=pltpu.VMEM)] * len(vmem)
    in_specs += [pl.BlockSpec(memory_space=pl.ANY)] * len(after)
    shapes = [pltpu.SMEM(*one) if one[1] == jnp.int32 else pltpu.VMEM(*one) for one in scratch]
    if copies:
        shapes.append(pltpu.SemaphoreType.DMA((copies,)))
    taken = len(hbm) + len(vmem)

    def body(*refs):
        kernel(*refs[:taken], *refs[taken + len(after) :])

    return pl.pallas_call(
        body,
        out_shape=[jax.ShapeDtypeStruct(*out) for out in outs],
        in_specs=in_specs,
        out_specs=[pl.BlockSpec(memory_space=pltpu.VMEM)] * len(outs),
        scratch_shapes=shapes,
        cost_estimate=pl.CostEstimate(flops=int(micros * 1e9), bytes_accessed=0, transcendentals=0),
        compiler_params=pltpu.CompilerParams(vmem_limit_bytes=limit * 1024 * 1024),
    )(*hbm, *vmem, *after)


def shards(fields, grad_out, block_count, ocean, kernel, ln_gain, w_in, w_out, layer_scale):
    samples, slots, tile_rows, tile_cols, channels = fields.shape
    hidden = w_in.shape[1]
    shape = Shape(slots, channels, hidden)
    cells, parts, pitch = shape.cells, shape.parts, shape.pitch
    grid = fields.shape
    fields = fields.reshape(cells, channels)
    tangent = grad_out.reshape(cells, channels)
    taps_in = kernel
    gain = ln_gain.reshape(1, channels)
    scale = layer_scale.reshape(1, channels)

    def bind(body):
        return functools.partial(body, shape)

    def strip(rows):
        return ((parts, rows * pitch, LANES), F32)

    edge = ((shape.edge_rows, channels), BF16)
    turned = ((HALF * pitch, channels), BF16)
    whole = ((cells, channels), BF16)
    whole_f = ((cells, channels), F32)
    wide = ((cells, hidden), BF16)
    narrow = ((cells, LANES), F32)
    row = ((1, channels), F32)
    eight = ((8, channels), F32)
    taps = ((parts, KSIZE * KSIZE, 8, LANES), F32)
    count_s = (block_count.shape, jnp.int32)
    ocean_s = (ocean.shape, jnp.int32)
    flat = ((channels, cells), BF16)
    ends = ((HALF * 2 * LEFT, channels), BF16)
    ends_f = ((parts, HALF * 2 * LEFT, LANES), F32)
    late = TILE - shape.early

    first, second = call(
        bind(prep_kernel), [edge, edge], [count_s, ((parts, cells, LANES), F32)],
        [block_count], [fields], 1, 1.0,
    )
    (fold,) = call(
        bind(top_kernel), [((HALF * shape.columns, channels), BF16)], [count_s, ocean_s],
        [block_count, ocean], [fields], 2, 0.5, after=[first],
    )
    first, second = swap(first, "first"), swap(second, "second")
    band, rims = call(
        bind(band_kernel), [strip(TILE + HALF), ends], [count_s, ocean_s],
        [block_count, ocean], [fields, first, second], 2, 1.0, after=[fold],
    )
    fold, rims = swap(fold, "fold"), swap(rims, "fold")
    normed, yhat, inverse, dproj_t, dact, live = call(
        bind(early_kernel), [whole, whole_f, narrow, flat, ((cells, hidden), F32), ((slots, 8, channels), F32)],
        [count_s, ocean_s, taps, ((parts, shape.early * shape.columns, LANES), F32), whole],
        [block_count, ocean], [taps_in, gain, w_out, scale, tangent, band], 2, 5.0,
    )
    keep, give, activated, dpreact, yhat, inverse, top = call(
        bind(late_kernel),
        [((hidden, channels), F32), ((hidden, channels), BF16), wide, wide, whole_f, narrow, strip(late + 2 * HALF)],
        [
            count_s, taps, ((parts, late * shape.columns, LANES), F32), whole, flat, ends_f,
            ((3, TILE * TILE, channels), F32),
        ],
        [block_count],
        [taps_in, gain, w_in, band, fold, rims, normed, yhat, inverse, dproj_t, dact], 1, 5.0,
    )

    order = stages()
    rows = hidden // 2

    def half_step(at, rows):
        return functools.partial(halve_kernel, order[at], order[at + 1]), [
            ((rows, channels), F32), ((rows // 2, channels), BF16),
        ]

    def taps_part(part, after):
        (small,) = call(
            functools.partial(taps_kernel, shape, part), [((small_rows, LANES), F32)],
            [((1, (TILE + 2 * HALF) * pitch, LANES), F32), ((1, TILE * pitch, LANES), F32)],
            [], [band, top, conv_grad], 0, 1.8, after=after,
        )
        return small

    def back_part(part, before, after):
        outs = [(((TILE + HALF) * pitch, LANES), F32)] + [turned] * (part == parts - 1)
        return call(
            functools.partial(back_kernel, shape, part), outs,
            [count_s, ((1, TILE * pitch, LANES), F32), ((1, KSIZE * KSIZE, 8, LANES), F32)],
            [block_count], [taps_in, conv_grad, *before], 1, 2.0, after=after,
        )

    small_rows = -(-(KSIZE * KSIZE + 2) // 32) * 32
    came = core_swap(give)
    conv_grad, projected, gain_part, scale_part = call(
        bind(norm_grad_kernel), [whole, whole_f, eight, eight], [], [],
        [w_in, w_out, gain, dpreact, yhat, inverse, activated, tangent, live], 0, 1.3,
    )
    mine, send = call(
        functools.partial(join_kernel, order[0]),
        [((hidden, channels), F32), ((rows, channels), BF16)], [], [], [keep, came], after=[gain_part], micros=0.3,
    )
    came = bit_swap(send, order[0])
    core_grad = []
    after = [send]
    for part in range(parts):
        one, *fold_back = back_part(part, core_grad, after)
        core_grad += [one]
        after = [one]
    taps_parts = [taps_part(0, after)]
    fold_back = swap(fold_back[0], "fold")
    body, outs = half_step(0, rows)
    mine, send = call(body, outs, [], [], [mine, came], after=taps_parts, micros=0.3)
    came = bit_swap(send, order[1])
    taps_parts += [taps_part(part, [send]) for part in range(1, parts)]
    small_rows //= 2
    small, extra = call(
        pack_kernel, [((small_rows, channels), F32), ((2 * small_rows, channels), BF16)],
        [((2 * small_rows, channels), F32)], [], [gain_part, scale_part, *taps_parts], micros=0.3,
    )
    extra = core_swap(extra)
    rows //= 2
    body, outs = half_step(1, rows)
    mine, send = call(body, outs, [], [], [mine, came], after=[small], micros=0.3)
    mine, send = halved(mine, send, order[2:-1])
    came = bit_swap(send, order[-2])
    folded, first, second = call(
        bind(rims_kernel), [strip(TILE), edge, edge], [count_s], [block_count], [fold_back, *core_grad], 1, 1.0,
        after=[send],
    )
    first, second = swap(first, "first"), swap(second, "second")
    rows = came.shape[0]
    if rows % 16 == 0:
        (payload,) = call(
            functools.partial(turn_kernel, order[-2]), [((rows + small_rows, channels), BF16)],
            [], [], [mine, came, small, extra], after=[folded], micros=0.3,
        )
    else:
        bit = bit_here(order[-2])
        share = lax.dynamic_index_in_dim(mine.reshape(2, rows, channels), bit, 0, keepdims=False)
        small = small + (extra[:small_rows].astype(F32) + extra[small_rows:].astype(F32))
        payload = jnp.concatenate([share + came.astype(F32), small]).astype(BF16)
    came = bit_swap(payload, order[-1])
    grad_fields, done = call(
        bind(final_kernel), [whole, ((8, LANES), F32)], [count_s, ocean_s, strip(TILE)],
        [block_count, ocean], [tangent, folded, first, second], 2, 1.5, after=[payload],
    )
    (payload,) = call(
        add_kernel, [(payload.shape, BF16)], [], [], [payload, came], after=[done], micros=0.3,
    )
    came = bit_swap(payload, order[-2])
    after = []
    for at in reversed(range(len(order) - 1)):
        copies = 2 if at == 0 else 1
        if rows % 16 == 0:
            (payload,) = call(
                functools.partial(double_kernel, order[at], small_rows),
                [((2 * rows + copies * small_rows, channels), BF16)],
                [], [], [payload, came], after=after, micros=0.3,
            )
        else:
            is_low = bit_here(order[at]) == 0
            low, high = payload[:rows], came[:rows]
            both = payload[rows:].astype(F32) + came[rows:].astype(F32)
            joined = [jnp.where(is_low, low, high), jnp.where(is_low, high, low), both.astype(BF16)]
            payload = jnp.concatenate(joined)
        after = []
        rows *= 2
        came = bit_swap(payload, order[at - 1]) if at else core_swap(payload)
        if at == 1:
            state, done = call(
                bind(state_kernel), [whole, ((8, LANES), F32)], [], [], [fields, scale, projected, live], 0, 1.5,
                after=[payload],
            )
            after = [done]
    total = samples * lax.axis_size("dp") * slots * lax.axis_size(TILES) * tile_rows * tile_cols
    norm = total ** (-0.5)
    sums = [((channels, hidden), F32), ((hidden, channels), F32)]
    w_in_sum, w_out_sum, kernel_sum, gain_sum, scale_sum = call(
        functools.partial(unpack_kernel, norm), sums + [(kernel.shape, F32), row, row], [],
        [], [payload, came], 0, 1.5,
    )
    return (
        state.reshape(grid),
        grad_fields.reshape(grid),
        kernel_sum,
        gain_sum.reshape(ln_gain.shape),
        w_in_sum,
        w_out_sum,
        scale_sum.reshape(layer_scale.shape),
    )


def solution(mesh):
    cores = Mesh(mesh.devices.reshape(-1, 2, mesh.devices.shape[1]), ("chips", "core", "dp"))
    banded = P("dp", TILES, None, None, None)
    placed = (banded, banded, P(TILES), P(TILES), P(), P(), P(), P(), P())
    return jax.shard_map(
        shards,
        mesh=cores,
        in_specs=placed,
        out_specs=(banded, banded, P(), P(), P(), P(), P()),
        check_vma=False,
    )
```

```python
import functools

import jax
import jax.numpy as jnp
from jax import lax
from jax.experimental import pallas as pl
from jax.experimental.pallas import tpu as pltpu
from jax.sharding import Mesh, PartitionSpec as P

KSIZE = 7
HALF = KSIZE // 2
TILE = 16
EPS = 1e-06
TILES = ("chips", "core")
F32 = jnp.float32
BF16 = jnp.bfloat16
LANES = 128
LEFT = 8
GELU_C = 0.7978845608028654
GELU_A = 0.044715


def dot(lhs, rhs, lhs_dim, rhs_dim):
    return lax.dot_general(
        lhs, rhs, (((lhs_dim,), (rhs_dim,)), ((), ())), preferred_element_type=F32
    )


def cycle_rank():
    count = lax.axis_size(TILES)
    here = lax.axis_index("chips") * lax.axis_size("core") + lax.axis_index("core")
    return jnp.where(here < count // 2, here, count - 1 + count // 2 - here)


def is_even():
    return lax.rem(cycle_rank(), 2) == 0


class Fetch:
    def __init__(self, sems, *pairs):
        self.copies = [
            pltpu.make_async_copy(source, target, sems.at[at]) for at, (source, target) in enumerate(pairs)
        ]
        for copy in self.copies:
            copy.start()

    def wait(self, *which):
        for at in which:
            self.copies[at].wait()


def slot_flag(count_ref, ocean_ref, slot):
    live = jnp.logical_and(slot < count_ref[0], ocean_ref[slot] > 0)
    return jnp.where(live, 1.0, 0.0).astype(F32)


class Shape:
    def __init__(self, slots, channels, hidden):
        self.slots = slots
        self.channels = channels
        self.hidden = hidden
        self.parts = channels // LANES
        self.columns = slots * TILE
        self.pitch = self.columns + 2 * LEFT
        self.cells = slots * TILE * TILE
        self.edge_rows = HALF * TILE
        self.early = 12

    def lanes(self, part):
        return slice(part * LANES, (part + 1) * LANES)


def edge_planes(shape, source, start, stride):
    return [
        jnp.concatenate(
            [source[part, pl.ds(start + col, TILE, stride=stride), :] for part in range(shape.parts)], axis=1
        )
        for col in range(HALF)
    ]


def send_edges(shape, left, right, first, second):
    even = is_even()
    for col in range(HALF):
        rows = pl.ds(col * TILE, TILE)
        first[rows, :] = jnp.where(even, right[col], left[col]).astype(BF16)
        second[rows, :] = jnp.where(even, left[col], right[col]).astype(BF16)


def flip_matrix(size, last):
    to = lax.broadcasted_iota(jnp.int32, (size, size), 0)
    frm = lax.broadcasted_iota(jnp.int32, (size, size), 1)
    return jnp.where(to + frm == last, 1.0, 0.0).astype(BF16)


def prep_kernel(shape, count_hbm, fields, first, second, count, work, sems):
    fetch = Fetch(sems, (count_hbm, count))
    for part in range(shape.parts):
        work[part] = fields[:, shape.lanes(part)].astype(F32)
    left = edge_planes(shape, work, 0, TILE)
    fetch.wait(0)
    right = edge_planes(shape, work, (count[0] - 1) * TILE * TILE + TILE - HALF, TILE)
    send_edges(shape, left, right, first, second)


def top_kernel(shape, count_hbm, ocean_hbm, fields, fold, count, ocean, sems):
    fetch = Fetch(sems, (count_hbm, count), (ocean_hbm, ocean))
    fetch.wait(0, 1)
    flip = flip_matrix(shape.columns, count[0] * TILE - 1)
    for k in range(HALF):
        cells = jnp.concatenate(
            [
                fields[pl.ds(slot * TILE * TILE + (TILE - 1 - k) * TILE, TILE), :].astype(F32)
                * slot_flag(count, ocean, slot)
                for slot in range(shape.slots)
            ]
        )
        turned = dot(flip, cells.astype(BF16), 1, 0)
        fold[pl.ds(k * shape.columns, shape.columns), :] = turned.astype(BF16)


def band_kernel(shape, count_hbm, ocean_hbm, fields, first, second, band, rims, count, ocean, sems):
    fetch = Fetch(sems, (count_hbm, count), (ocean_hbm, ocean))
    even = is_even()
    blank = jnp.zeros((LEFT, LANES), F32)
    per_slot = TILE * TILE
    for part in range(shape.parts):
        band[part, pl.ds(0, HALF * shape.pitch), :] = jnp.zeros((HALF * shape.pitch, LANES), F32)
        for row in range(TILE):
            base = (row + HALF) * shape.pitch
            band[part, pl.ds(base, LEFT), :] = blank
            band[part, pl.ds(base + LEFT + shape.columns, LEFT), :] = blank
    fetch.wait(0, 1)
    used = count[0] * TILE
    flags = [slot_flag(count, ocean, slot) for slot in range(shape.slots)]
    top = HALF * shape.pitch
    for part in range(shape.parts):
        for row in range(TILE):
            base = (row + HALF) * shape.pitch
            for slot in range(shape.slots):
                cells = fields[pl.ds(slot * per_slot + row * TILE, TILE), shape.lanes(part)]
                band[part, pl.ds(base + LEFT + slot * TILE, TILE), :] = cells.astype(F32) * flags[slot]
        for col in range(HALF):
            rows = pl.ds(col * TILE, TILE)
            one = first[rows, shape.lanes(part)].astype(F32)
            two = second[rows, shape.lanes(part)].astype(F32)
            west = jnp.where(even, two, one)
            east = jnp.where(even, one, two)
            band[part, pl.ds(top + LEFT - HALF + col, TILE, stride=shape.pitch), :] = west
            band[part, pl.ds(top + LEFT + used + col, TILE, stride=shape.pitch), :] = east
    for k in range(HALF):
        base = (HALF + TILE - 1 - k) * shape.pitch
        east = pl.multiple_of(base + LEFT + used, LEFT)
        for part in range(shape.parts):
            ends = jnp.concatenate([band[part, pl.ds(base, LEFT), :], band[part, pl.ds(east, LEFT), :]])
            rims[pl.ds(k * 2 * LEFT, 2 * LEFT), shape.lanes(part)] = ends.astype(BF16)


def put_fold(shape, used, fold, rims, parts, padded, first_row, work):
    blank = jnp.zeros((LEFT, LANES), F32)
    for at, part in enumerate(parts):
        work[at] = rims[:, shape.lanes(part)].astype(F32)
        for k in range(HALF):
            base = (first_row + k) * shape.pitch
            padded[at, pl.ds(base, LEFT), :] = blank
            padded[at, pl.ds(base + LEFT + shape.columns, LEFT), :] = blank
            cells = fold[pl.ds(k * shape.columns, shape.columns), shape.lanes(part)]
            padded[at, pl.ds(base + LEFT, shape.columns), :] = cells.astype(F32)
            for col in range(HALF):
                west = work[at, pl.ds(k * 2 * LEFT + LEFT - 1 - col, 1), :]
                east = work[at, pl.ds(k * 2 * LEFT + LEFT + col, 1), :]
                padded[at, pl.ds(base + LEFT - 1 - col, 1), :] = east
                padded[at, pl.ds(base + LEFT + used + col, 1), :] = west


def spread_taps(shape, kernel, parts, taps):
    for above in range(KSIZE):
        rows = kernel[above].astype(F32)
        for at, part in enumerate(parts):
            for shift in range(KSIZE):
                row = rows[shift : shift + 1, shape.lanes(part)]
                taps[at, above * KSIZE + shift] = jnp.broadcast_to(row, (8, LANES))


def convolve(shape, rows, padded, taps, convolved):
    run = shape.columns // 8
    pair = 2
    origin = LEFT - HALF

    def two_rows(step, carry):
        row = step * pair
        for part in range(shape.parts):
            sums = [[None] * run for _ in range(pair)]
            for above in range(KSIZE + pair - 1):
                base = (row + above) * shape.pitch + origin
                loaded = [
                    padded[part, pl.ds(base + at, 8, stride=run), :]
                    for at in range(run + KSIZE - 1)
                ]
                for which in range(pair):
                    tap_row = above - which
                    if not 0 <= tap_row < KSIZE:
                        continue
                    for shift in range(KSIZE):
                        weight = taps[part, tap_row * KSIZE + shift]
                        for at in range(run):
                            term = weight * loaded[at + shift]
                            old = sums[which][at]
                            sums[which][at] = term if old is None else old + term
            for which in range(pair):
                for at in range(run):
                    start = (row + which) * shape.columns + at
                    convolved[part, pl.ds(start, 8, stride=run), :] = sums[which][at]
        return carry

    lax.fori_loop(0, rows // pair, two_rows, 0)


def normalise(shape, rows, first_row, convolved, gain, normed, yhat, inverse):
    def one_row(row, carry):
        for slot in range(shape.slots):
            start = pl.multiple_of(row * shape.columns + slot * TILE, TILE)
            at = slot * TILE * TILE + (first_row + row) * TILE
            out = pl.ds(pl.multiple_of(at, TILE), TILE)
            parts = [convolved[part, pl.ds(start, TILE), :] for part in range(shape.parts)]
            mean = jnp.sum(sum(parts), axis=-1, keepdims=True) * (1.0 / shape.channels)
            parts = [value - mean for value in parts]
            square = jnp.sum(sum(value * value for value in parts), axis=-1, keepdims=True)
            scale = lax.rsqrt(square * (1.0 / shape.channels) + EPS)
            inverse[out, :] = jnp.broadcast_to(scale, (TILE, LANES))
            for part in range(shape.parts):
                value = parts[part] * scale
                yhat[out, shape.lanes(part)] = value
                normed[out, shape.lanes(part)] = (value * gain[:, shape.lanes(part)]).astype(BF16)
        return carry

    lax.fori_loop(0, rows, one_row, 0, unroll=4)


def early_kernel(
    shape, count_hbm, ocean_hbm, kernel, gain, w_out, scale, tangent, band,
    normed, yhat, inverse, dproj_t, dact, live,
    count, ocean, taps, convolved, dproj, sems,
):
    fetch = Fetch(sems, (count_hbm, count), (ocean_hbm, ocean))
    spread_taps(shape, kernel, range(shape.parts), taps)
    convolve(shape, shape.early, band, taps, convolved)
    normalise(shape, shape.early, 0, convolved, gain, normed, yhat, inverse)
    fetch.wait(0, 1)
    per_slot = TILE * TILE
    for slot in range(shape.slots):
        rows = pl.ds(slot * per_slot, per_slot)
        flag = slot_flag(count, ocean, slot)
        live[slot] = jnp.full((8, shape.channels), flag, F32)
        scaled = (tangent[rows, :].astype(F32) * (scale[...] * flag)).astype(BF16)
        dproj[rows, :] = scaled
        dproj_t[:, slot * per_slot : (slot + 1) * per_slot] = scaled.T
        for h in range(shape.hidden // shape.channels):
            cols = slice(h * shape.channels, (h + 1) * shape.channels)
            dact[rows, cols] = dot(dproj[rows, :], w_out[cols, :], 1, 1)


def late_kernel(
    shape, count_hbm, kernel, gain, w_in, band, fold, rims, normed_in, yhat_in, inverse_in, dproj_t, dact,
    keep, give, activated, dpreact, yhat, inverse, padded,
    count, taps, convolved, normed, normed_t, work, pre, sems,
):
    fetch = Fetch(sems, (count_hbm, count))
    late = TILE - shape.early
    kept = late + HALF
    for part in range(shape.parts):
        rows = pl.ds(shape.early * shape.pitch, kept * shape.pitch)
        padded[part, pl.ds(0, kept * shape.pitch), :] = band[part, rows, :]
    done = shape.early * TILE
    for slot in range(shape.slots):
        rows = pl.ds(slot * TILE * TILE, done)
        normed[rows, :] = normed_in[rows, :]
        yhat[rows, :] = yhat_in[rows, :]
        inverse[rows, :] = inverse_in[rows, :]
    spread_taps(shape, kernel, range(shape.parts), taps)
    fetch.wait(0)
    put_fold(shape, count[0] * TILE, fold, rims, range(shape.parts), padded, kept, work)
    convolve(shape, late, padded, taps, convolved)
    normalise(shape, late, shape.early, convolved, gain, normed, yhat, inverse)
    per_slot = TILE * TILE
    for slot in range(shape.slots):
        normed_t[:, slot * per_slot : (slot + 1) * per_slot] = normed[pl.ds(slot * per_slot, per_slot), :].T
    keeps_in = lax.axis_index("core") == 0
    block = shape.channels
    blocks = shape.hidden // block

    def span(h):
        return slice(h * block, (h + 1) * block)

    def expand(step):
        h, slot = divmod(step, shape.slots)
        pre[step % 3] = dot(normed[pl.ds(slot * per_slot, per_slot), :], w_in[:, span(h)], 1, 0)

    def activate(step):
        h, slot = divmod(step, shape.slots)
        rows, cols = pl.ds(slot * per_slot, per_slot), span(h)
        value = pre[step % 3]
        square = value * value
        gate = 0.5 + 0.5 * jnp.tanh(value * (GELU_C + (GELU_C * GELU_A) * square))
        activated[rows, cols] = (value * gate).astype(BF16)
        slope = value * (2.0 * GELU_C + (6.0 * GELU_C * GELU_A) * square)
        grown = gate + slope * (gate - gate * gate)
        dpreact[rows, cols] = (dact[rows, cols] * grown).astype(BF16)

    def reduce_rows(h):
        of_in = dot(normed_t[...], dpreact[:, span(h)], 1, 0)
        of_out = dot(dproj_t[...], activated[:, span(h)], 1, 0)
        keep[span(h), :] = jnp.where(keeps_in, of_in, of_out)
        give[span(h), :] = jnp.where(keeps_in, of_out, of_in).astype(BF16)

    steps = blocks * shape.slots
    expand(0)
    for step in range(steps):
        if step + 1 < steps:
            expand(step + 1)
        activate(step)
        h, slot = divmod(step, shape.slots)
        if slot == 0 and h:
            reduce_rows(h - 1)
    reduce_rows(blocks - 1)


def fold_sum(value):
    return jnp.sum(value.reshape(-1, 8, value.shape[-1]), axis=0)


def norm_grad_kernel(
    shape, w_in, w_out, gain, dpreact, yhat, inverse, activated, tangent, live,
    conv_grad, projected, gain_part, scale_part,
):
    chunk = TILE * TILE
    of_gain = jnp.zeros((8, shape.channels), F32)
    of_scale = jnp.zeros((8, shape.channels), F32)
    for slot in range(shape.slots):
        rows = pl.ds(slot * chunk, chunk)
        dnormed = dot(dpreact[rows, :], w_in[...], 1, 1)
        unit = yhat[rows, :]
        of_gain += fold_sum(dnormed * unit)
        dhat = dnormed * gain[...]
        mean = jnp.sum(dhat, axis=-1, keepdims=True) * (1.0 / shape.channels)
        along = jnp.sum(dhat * unit, axis=-1, keepdims=True) * (1.0 / shape.channels)
        scale = jnp.concatenate([inverse[rows, :]] * shape.parts, axis=1)
        conv_grad[rows, :] = (scale * (dhat - mean - unit * along)).astype(BF16)
        value = dot(activated[rows, :], w_out[...], 1, 0)
        projected[rows, :] = value
        of_scale += live[slot] * fold_sum(tangent[rows, :].astype(F32) * value)
    gain_part[...] = of_gain
    scale_part[...] = of_scale


def state_kernel(shape, fields, scale, projected, live, state, done):
    done[...] = jnp.zeros_like(done)
    chunk = TILE * TILE
    for slot in range(shape.slots):
        rows = pl.ds(slot * chunk, chunk)
        kept = fields[rows, :].astype(F32) + scale[...] * projected[rows, :]
        state[rows, :] = (live[slot, 0:1, :] * kept).astype(BF16)


def place_grad(shape, conv_grad, parts, spaced):
    blank = jnp.zeros((LEFT, LANES), F32)
    for at, part in enumerate(parts):
        for row in range(TILE):
            base = row * shape.pitch
            spaced[at, pl.ds(base, LEFT), :] = blank
            spaced[at, pl.ds(base + LEFT + shape.columns, LEFT), :] = blank
            for slot in range(shape.slots):
                cells = conv_grad[pl.ds(slot * TILE * TILE + row * TILE, TILE), shape.lanes(part)]
                spaced[at, pl.ds(base + LEFT + slot * TILE, TILE), :] = cells.astype(F32)


def taps_kernel(shape, part, band, top, conv_grad, small, padded, spaced):
    place_grad(shape, conv_grad, [part], spaced)
    kept = shape.early * shape.pitch
    padded[0, pl.ds(0, kept), :] = band[part, pl.ds(0, kept), :]
    padded[0, pl.ds(kept, top.shape[1]), :] = top[part]
    run = shape.columns // 8
    origin = LEFT - HALF
    for above in range(KSIZE):

        def one_row(row, sums, above=above):
            base = (row + above) * shape.pitch + origin
            loaded = [padded[0, pl.ds(base + at, 8, stride=run), :] for at in range(run + KSIZE - 1)]
            start = row * shape.pitch + LEFT
            grads = [spaced[0, pl.ds(start + at, 8, stride=run), :] for at in range(run)]
            sums = list(sums)
            for shift in range(KSIZE):
                for at in range(run):
                    sums[shift] = sums[shift] + grads[at] * loaded[at + shift]
            return tuple(sums)

        blank = tuple(jnp.zeros((8, LANES), F32) for _ in range(KSIZE))
        sums = lax.fori_loop(0, TILE, one_row, blank, unroll=2)
        for shift in range(KSIZE):
            small[pl.ds(above * KSIZE + shift, 1), :] = jnp.sum(sums[shift], axis=0, keepdims=True)


def back_kernel(shape, part, count_hbm, kernel, conv_grad, *refs):
    before = refs[:part]
    turns = part == shape.parts - 1
    core_grad, *refs = refs[part:]
    if turns:
        fold, *refs = refs
    count, spaced, taps, sems = refs
    fetch = Fetch(sems, (count_hbm, count))
    place_grad(shape, conv_grad, [part], spaced)
    blank = jnp.zeros((LEFT, LANES), F32)
    for row in range(TILE + HALF):
        core_grad[pl.ds(row * shape.pitch, LEFT), :] = blank
        core_grad[pl.ds((row + 1) * shape.pitch - LEFT, LEFT), :] = blank
    spread_taps(shape, kernel, [part], taps)
    run = -(-(shape.columns + 2 * HALF) // 8)

    def one_row(row, tap_rows):
        sums = [None] * run
        for above in tap_rows:
            base = (row - above) * shape.pitch + LEFT
            loaded = [
                spaced[0, pl.ds(base + at - KSIZE + 1, 8, stride=run), :] for at in range(run + KSIZE - 1)
            ]
            for shift in range(KSIZE):
                weight = taps[0, above * KSIZE + shift]
                for at in range(run):
                    term = weight * loaded[at - shift + KSIZE - 1]
                    sums[at] = term if sums[at] is None else sums[at] + term
        start = (row - HALF) * shape.pitch + LEFT - HALF
        for at in range(run):
            core_grad[pl.ds(start + at, 8, stride=run), :] = sums[at]

    inner = (KSIZE - 1, TILE - 1)
    for row in range(HALF, TILE + 2 * HALF):
        if not inner[0] <= row <= inner[1]:
            low = max(0, row - TILE + 1)
            one_row(row, range(low, min(KSIZE - 1, row) + 1))

    def inner_row(step, carry):
        one_row(step, range(KSIZE))
        return carry

    lax.fori_loop(inner[0], inner[1] + 1, inner_row, 0)
    fetch.wait(0)
    if turns:
        flip = flip_matrix(shape.pitch, count[0] * TILE + 2 * LEFT - 1)
        for k in range(HALF):
            at = pl.ds((TILE + k) * shape.pitch, shape.pitch)
            cells = jnp.concatenate([one[at, :] for one in (*before, core_grad)], axis=1)
            turned = dot(flip, cells.astype(BF16), 1, 0)
            fold[pl.ds(k * shape.pitch, shape.pitch), :] = turned.astype(BF16)


def rims_kernel(shape, count_hbm, fold, *refs):
    core_grad = refs[: shape.parts]
    folded, first, second, count, sems = refs[shape.parts :]
    fetch = Fetch(sems, (count_hbm, count))
    for part in range(shape.parts):
        folded[part] = core_grad[part][pl.ds(0, TILE * shape.pitch), :]
        for k in range(HALF):
            rows = pl.ds((TILE - 1 - k) * shape.pitch, shape.pitch)
            returned = fold[pl.ds(k * shape.pitch, shape.pitch), shape.lanes(part)]
            folded[part, rows, :] += returned.astype(F32)
    fetch.wait(0)
    west = edge_planes(shape, folded, LEFT - HALF, shape.pitch)
    east = edge_planes(shape, folded, LEFT + count[0] * TILE, shape.pitch)
    send_edges(shape, west, east, first, second)


def final_kernel(
    shape, count_hbm, ocean_hbm, tangent, folded, first, second,
    grad_fields, done,
    count, ocean, work, sems,
):
    fetch = Fetch(sems, (count_hbm, count), (ocean_hbm, ocean))
    even = is_even()
    done[...] = jnp.zeros_like(done)
    work[...] = folded[...]
    fetch.wait(0, 1)
    used = count[0] * TILE
    for part in range(shape.parts):
        for col in range(HALF):
            planes = pl.ds(col * TILE, TILE)
            one = first[planes, shape.lanes(part)].astype(F32)
            two = second[planes, shape.lanes(part)].astype(F32)
            to_tail = jnp.where(even, one, two)
            to_head = jnp.where(even, two, one)
            head = pl.ds(LEFT + col, TILE, stride=shape.pitch)
            work[part, head, :] = work[part, head, :] + to_head
            tail = pl.ds(LEFT + used - HALF + col, TILE, stride=shape.pitch)
            work[part, tail, :] = work[part, tail, :] + to_tail
        for slot in range(shape.slots):
            flag = slot_flag(count, ocean, slot)
            for row in range(TILE):
                rows = pl.ds(slot * TILE * TILE + row * TILE, TILE)
                cells = work[part, pl.ds(row * shape.pitch + LEFT + slot * TILE, TILE), :]
                total = tangent[rows, shape.lanes(part)].astype(F32) + cells
                grad_fields[rows, shape.lanes(part)] = (flag * total).astype(BF16)


def unpack_kernel(norm, own, came, w_in, w_out, kernel_sum, gain_sum, scale_sum):
    is_first = lax.axis_index("core") == 0
    hidden, channels = w_out.shape
    for h in range(hidden // channels):
        block = slice(h * channels, (h + 1) * channels)
        mine = own[block, :].astype(F32) * norm
        theirs = came[block, :].astype(F32) * norm
        w_in[:, block] = jnp.where(is_first, mine, theirs)
        w_out[block, :] = jnp.where(is_first, theirs, mine).T
    extra = (own.shape[0] - hidden) // 2
    high, low = pl.ds(hidden, extra), pl.ds(hidden + extra, extra)
    mine = (own[high, :].astype(F32) + own[low, :].astype(F32)) * norm
    theirs = (came[high, :].astype(F32) + came[low, :].astype(F32)) * norm
    small = jnp.concatenate([jnp.where(is_first, mine, theirs), jnp.where(is_first, theirs, mine)])
    for above in range(KSIZE):
        kernel_sum[above] = small[above * KSIZE : (above + 1) * KSIZE, :]
    gain_sum[...] = small[KSIZE * KSIZE : KSIZE * KSIZE + 1, :]
    scale_sum[...] = small[KSIZE * KSIZE + 1 : KSIZE * KSIZE + 2, :]


def pairs_of(kind):
    count = lax.axis_size(TILES)
    half = count // 2
    place = [rank if rank < half else count - 1 + half - rank for rank in range(count)]
    partner = {
        "first": lambda rank: rank ^ 1,
        "second": lambda rank: ((rank + 1) ^ 1) - 1,
        "fold": lambda rank: count - 1 - rank,
    }[kind]
    return [(place[rank], place[partner(rank) % count]) for rank in range(count)]


def swap(block, kind):
    return lax.ppermute(block, TILES, pairs_of(kind))


def core_swap(block):
    return lax.ppermute(block, "core", [(0, 1), (1, 0)])


def stages():
    chip_bits = lax.axis_size("chips").bit_length() - 1
    rest = list(range(2, chip_bits))
    return list(zip([0, -1, 1] + rest, [1, 0, -1] + rest))


def bit_swap(block, stage):
    chips, cores, samples = (lax.axis_size(axis) for axis in ("chips", "core", "dp"))
    pairs = []
    for chip in range(chips):
        for core in range(cores):
            for sample in range(samples):
                bit = stage[core]
                to = (chip, sample ^ 1) if bit < 0 else (chip ^ (1 << bit), sample)
                pairs.append(
                    ((chip * cores + core) * samples + sample, (to[0] * cores + core) * samples + to[1])
                )
    return lax.ppermute(block, ("chips", "core", "dp"), pairs)


def bit_here(stage):
    bits = [
        lax.axis_index("dp") if bit < 0 else lax.axis_index("chips") >> bit & 1 for bit in stage
    ]
    return jnp.where(lax.axis_index("core") == 0, bits[0], bits[1])


def half_rows(bit, rows):
    return pl.ds(pl.multiple_of(bit * rows, rows), rows)


def join_kernel(stage, keep, came, mine, send):
    rows = send.shape[0]
    mine[...] = keep[...] + came[...].astype(F32)
    send[...] = mine[half_rows(1 - bit_here(stage), rows), :].astype(BF16)


def halve_kernel(stage, following, whole, came, mine, send):
    rows = mine.shape[0]
    mine[...] = whole[half_rows(bit_here(stage), rows), :] + came[...].astype(F32)
    send[...] = mine[half_rows(1 - bit_here(following), rows // 2), :].astype(BF16)


def pack_kernel(gain_part, scale_part, *refs):
    taps, (keep, send, work) = refs[:-3], refs[-3:]
    half = keep.shape[0]
    work[...] = jnp.zeros_like(work)
    for part, ref in enumerate(taps):
        work[pl.ds(0, ref.shape[0]), part * LANES : (part + 1) * LANES] = ref[...]
    work[pl.ds(KSIZE * KSIZE, 1), :] = jnp.sum(gain_part[...], axis=0, keepdims=True)
    work[pl.ds(KSIZE * KSIZE + 1, 1), :] = jnp.sum(scale_part[...], axis=0, keepdims=True)
    core = lax.axis_index("core")
    keep[...] = work[half_rows(core, half), :]
    value = work[half_rows(1 - core, half), :]
    high = value.astype(BF16)
    send[pl.ds(0, half), :] = high
    send[pl.ds(half, half), :] = (value - high.astype(F32)).astype(BF16)


def turn_kernel(stage, whole, came, keep, extra, payload):
    rows, half = came.shape[0], keep.shape[0]
    share = whole[half_rows(bit_here(stage), rows), :] + came[...].astype(F32)
    payload[pl.ds(0, rows), :] = share.astype(BF16)
    small = keep[...] + (extra[pl.ds(0, half), :].astype(F32) + extra[pl.ds(half, half), :].astype(F32))
    payload[pl.ds(rows, half), :] = small.astype(BF16)


def add_kernel(own, came, payload):
    payload[...] = (own[...].astype(F32) + came[...].astype(F32)).astype(BF16)


def double_kernel(stage, extra, own, came, payload):
    rows = own.shape[0] - extra
    bit = bit_here(stage)
    payload[half_rows(bit, rows), :] = own[pl.ds(0, rows), :]
    payload[half_rows(1 - bit, rows), :] = came[pl.ds(0, rows), :]
    total = own[pl.ds(rows, extra), :].astype(F32) + came[pl.ds(rows, extra), :].astype(F32)
    high = total.astype(BF16)
    payload[pl.ds(2 * rows, extra), :] = high
    if payload.shape[0] > 2 * rows + extra:
        payload[pl.ds(2 * rows + extra, extra), :] = (total - high.astype(F32)).astype(BF16)


def halved(mine, send, order):
    for at, stage in enumerate(order[:-1]):
        came = bit_swap(send, stage)
        rows = came.shape[0]
        bit = bit_here(stage)
        mine = lax.dynamic_index_in_dim(mine.reshape(2, rows, -1), bit, 0, keepdims=False) + came.astype(F32)
        bit = bit_here(order[at + 1])
        halves = mine.reshape(2, rows // 2, -1)
        send = lax.dynamic_index_in_dim(halves, 1 - bit, 0, keepdims=False).astype(BF16)
    return mine, send


def call(kernel, outs, scratch, hbm, vmem, copies=0, micros=1.0, after=(), limit=20):
    in_specs = [pl.BlockSpec(memory_space=pl.ANY)] * len(hbm)
    in_specs += [pl.BlockSpec(memory_space=pltpu.VMEM)] * len(vmem)
    in_specs += [pl.BlockSpec(memory_space=pl.ANY)] * len(after)
    shapes = [pltpu.SMEM(*one) if one[1] == jnp.int32 else pltpu.VMEM(*one) for one in scratch]
    if copies:
        shapes.append(pltpu.SemaphoreType.DMA((copies,)))
    taken = len(hbm) + len(vmem)

    def body(*refs):
        kernel(*refs[:taken], *refs[taken + len(after) :])

    return pl.pallas_call(
        body,
        out_shape=[jax.ShapeDtypeStruct(*out) for out in outs],
        in_specs=in_specs,
        out_specs=[pl.BlockSpec(memory_space=pltpu.VMEM)] * len(outs),
        scratch_shapes=shapes,
        cost_estimate=pl.CostEstimate(flops=int(micros * 1e9), bytes_accessed=0, transcendentals=0),
        compiler_params=pltpu.CompilerParams(vmem_limit_bytes=limit * 1024 * 1024),
    )(*hbm, *vmem, *after)


def shards(fields, grad_out, block_count, ocean, kernel, ln_gain, w_in, w_out, layer_scale):
    samples, slots, tile_rows, tile_cols, channels = fields.shape
    hidden = w_in.shape[1]
    shape = Shape(slots, channels, hidden)
    cells, parts, pitch = shape.cells, shape.parts, shape.pitch
    grid = fields.shape
    fields = fields.reshape(cells, channels)
    tangent = grad_out.reshape(cells, channels)
    taps_in = kernel
    gain = ln_gain.reshape(1, channels)
    scale = layer_scale.reshape(1, channels)

    def bind(body):
        return functools.partial(body, shape)

    def strip(rows):
        return ((parts, rows * pitch, LANES), F32)

    edge = ((shape.edge_rows, channels), BF16)
    turned = ((HALF * pitch, channels), BF16)
    whole = ((cells, channels), BF16)
    whole_f = ((cells, channels), F32)
    wide = ((cells, hidden), BF16)
    narrow = ((cells, LANES), F32)
    row = ((1, channels), F32)
    eight = ((8, channels), F32)
    taps = ((parts, KSIZE * KSIZE, 8, LANES), F32)
    count_s = (block_count.shape, jnp.int32)
    ocean_s = (ocean.shape, jnp.int32)
    flat = ((channels, cells), BF16)
    ends = ((HALF * 2 * LEFT, channels), BF16)
    ends_f = ((parts, HALF * 2 * LEFT, LANES), F32)
    late = TILE - shape.early

    first, second = call(
        bind(prep_kernel), [edge, edge], [count_s, ((parts, cells, LANES), F32)],
        [block_count], [fields], 1, 1.0,
    )
    (fold,) = call(
        bind(top_kernel), [((HALF * shape.columns, channels), BF16)], [count_s, ocean_s],
        [block_count, ocean], [fields], 2, 0.5, after=[first],
    )
    first, second = swap(first, "first"), swap(second, "second")
    band, rims = call(
        bind(band_kernel), [strip(TILE + HALF), ends], [count_s, ocean_s],
        [block_count, ocean], [fields, first, second], 2, 1.0, after=[fold],
    )
    fold, rims = swap(fold, "fold"), swap(rims, "fold")
    normed, yhat, inverse, dproj_t, dact, live = call(
        bind(early_kernel), [whole, whole_f, narrow, flat, ((cells, hidden), F32), ((slots, 8, channels), F32)],
        [count_s, ocean_s, taps, ((parts, shape.early * shape.columns, LANES), F32), whole],
        [block_count, ocean], [taps_in, gain, w_out, scale, tangent, band], 2, 5.0,
    )
    keep, give, activated, dpreact, yhat, inverse, top = call(
        bind(late_kernel),
        [((hidden, channels), F32), ((hidden, channels), BF16), wide, wide, whole_f, narrow, strip(late + 2 * HALF)],
        [
            count_s, taps, ((parts, late * shape.columns, LANES), F32), whole, flat, ends_f,
            ((3, TILE * TILE, channels), F32),
        ],
        [block_count],
        [taps_in, gain, w_in, band, fold, rims, normed, yhat, inverse, dproj_t, dact], 1, 5.0,
    )

    order = stages()
    rows = hidden // 2

    def half_step(at, rows):
        return functools.partial(halve_kernel, order[at], order[at + 1]), [
            ((rows, channels), F32), ((rows // 2, channels), BF16),
        ]

    def taps_part(part, after):
        (small,) = call(
            functools.partial(taps_kernel, shape, part), [((small_rows, LANES), F32)],
            [((1, (TILE + 2 * HALF) * pitch, LANES), F32), ((1, TILE * pitch, LANES), F32)],
            [], [band, top, conv_grad], 0, 1.8, after=after,
        )
        return small

    def back_part(part, before, after):
        outs = [(((TILE + HALF) * pitch, LANES), F32)] + [turned] * (part == parts - 1)
        return call(
            functools.partial(back_kernel, shape, part), outs,
            [count_s, ((1, TILE * pitch, LANES), F32), ((1, KSIZE * KSIZE, 8, LANES), F32)],
            [block_count], [taps_in, conv_grad, *before], 1, 2.0, after=after,
        )

    small_rows = -(-(KSIZE * KSIZE + 2) // 32) * 32
    came = core_swap(give)
    conv_grad, projected, gain_part, scale_part = call(
        bind(norm_grad_kernel), [whole, whole_f, eight, eight], [], [],
        [w_in, w_out, gain, dpreact, yhat, inverse, activated, tangent, live], 0, 1.3,
    )
    mine, send = call(
        functools.partial(join_kernel, order[0]),
        [((hidden, channels), F32), ((rows, channels), BF16)], [], [], [keep, came], after=[gain_part], micros=0.3,
    )
    came = bit_swap(send, order[0])
    core_grad = []
    after = [send]
    for part in range(parts):
        one, *fold_back = back_part(part, core_grad, after)
        core_grad += [one]
        after = [one]
    fold_back = swap(fold_back[0], "fold")
    body, outs = half_step(0, rows)
    mine, send = call(body, outs, [], [], [mine, came], after=after, micros=0.3)
    came = bit_swap(send, order[1])
    taps_parts = [taps_part(part, [send]) for part in range(parts)]
    small_rows //= 2
    small, extra = call(
        pack_kernel, [((small_rows, channels), F32), ((2 * small_rows, channels), BF16)],
        [((2 * small_rows, channels), F32)], [], [gain_part, scale_part, *taps_parts], micros=0.3,
    )
    extra = core_swap(extra)
    rows //= 2
    body, outs = half_step(1, rows)
    mine, send = call(body, outs, [], [], [mine, came], after=[small], micros=0.3)
    mine, send = halved(mine, send, order[2:-1])
    came = bit_swap(send, order[-2])
    folded, first, second = call(
        bind(rims_kernel), [strip(TILE), edge, edge], [count_s], [block_count], [fold_back, *core_grad], 1, 1.0,
        after=[send],
    )
    first, second = swap(first, "first"), swap(second, "second")
    rows = came.shape[0]
    if rows % 16 == 0:
        (payload,) = call(
            functools.partial(turn_kernel, order[-2]), [((rows + small_rows, channels), BF16)],
            [], [], [mine, came, small, extra], after=[folded], micros=0.3,
        )
    else:
        bit = bit_here(order[-2])
        share = lax.dynamic_index_in_dim(mine.reshape(2, rows, channels), bit, 0, keepdims=False)
        small = small + (extra[:small_rows].astype(F32) + extra[small_rows:].astype(F32))
        payload = jnp.concatenate([share + came.astype(F32), small]).astype(BF16)
    came = bit_swap(payload, order[-1])
    grad_fields, done = call(
        bind(final_kernel), [whole, ((8, LANES), F32)], [count_s, ocean_s, strip(TILE)],
        [block_count, ocean], [tangent, folded, first, second], 2, 1.5, after=[payload],
    )
    (payload,) = call(
        add_kernel, [(payload.shape, BF16)], [], [], [payload, came], after=[done], micros=0.3,
    )
    came = bit_swap(payload, order[-2])
    after = []
    for at in reversed(range(len(order) - 1)):
        copies = 2 if at == 0 else 1
        if rows % 16 == 0:
            (payload,) = call(
                functools.partial(double_kernel, order[at], small_rows),
                [((2 * rows + copies * small_rows, channels), BF16)],
                [], [], [payload, came], after=after, micros=0.3,
            )
        else:
            is_low = bit_here(order[at]) == 0
            low, high = payload[:rows], came[:rows]
            both = payload[rows:].astype(F32) + came[rows:].astype(F32)
            joined = [jnp.where(is_low, low, high), jnp.where(is_low, high, low), both.astype(BF16)]
            payload = jnp.concatenate(joined)
        after = []
        rows *= 2
        came = bit_swap(payload, order[at - 1]) if at else core_swap(payload)
        if at == 1:
            state, done = call(
                bind(state_kernel), [whole, ((8, LANES), F32)], [], [], [fields, scale, projected, live], 0, 1.5,
                after=[payload],
            )
            after = [done]
    total = samples * lax.axis_size("dp") * slots * lax.axis_size(TILES) * tile_rows * tile_cols
    norm = total ** (-0.5)
    sums = [((channels, hidden), F32), ((hidden, channels), F32)]
    w_in_sum, w_out_sum, kernel_sum, gain_sum, scale_sum = call(
        functools.partial(unpack_kernel, norm), sums + [(kernel.shape, F32), row, row], [],
        [], [payload, came], 0, 1.5,
    )
    return (
        state.reshape(grid),
        grad_fields.reshape(grid),
        kernel_sum,
        gain_sum.reshape(ln_gain.shape),
        w_in_sum,
        w_out_sum,
        scale_sum.reshape(layer_scale.shape),
    )


def solution(mesh):
    cores = Mesh(mesh.devices.reshape(-1, 2, mesh.devices.shape[1]), ("chips", "core", "dp"))
    banded = P("dp", TILES, None, None, None)
    placed = (banded, banded, P(TILES), P(TILES), P(), P(), P(), P(), P())
    return jax.shard_map(
        shards,
        mesh=cores,
        in_specs=placed,
        out_specs=(banded, banded, P(), P(), P(), P(), P()),
        check_vma=False,
    )
```

```python
import functools

import jax
import jax.numpy as jnp
from jax import lax
from jax.experimental import pallas as pl
from jax.experimental.pallas import tpu as pltpu
from jax.sharding import Mesh, PartitionSpec as P

KSIZE = 7
HALF = KSIZE // 2
TILE = 16
EPS = 1e-06
CHIPS = ("far", "near")
TILES = CHIPS + ("core",)
F32 = jnp.float32
BF16 = jnp.bfloat16
LANES = 128
LEFT = 8
GELU_C = 0.7978845608028654
GELU_A = 0.044715


def dot(lhs, rhs, lhs_dim, rhs_dim):
    return lax.dot_general(
        lhs, rhs, (((lhs_dim,), (rhs_dim,)), ((), ())), preferred_element_type=F32
    )


def chip_index():
    return lax.axis_index("far") * lax.axis_size("near") + lax.axis_index("near")


def cycle_rank():
    count = lax.axis_size(TILES)
    here = chip_index() * lax.axis_size("core") + lax.axis_index("core")
    return jnp.where(here < count // 2, here, count - 1 + count // 2 - here)


def is_even():
    return lax.rem(cycle_rank(), 2) == 0


class Fetch:
    def __init__(self, sems, *pairs):
        self.copies = [
            pltpu.make_async_copy(source, target, sems.at[at]) for at, (source, target) in enumerate(pairs)
        ]
        for copy in self.copies:
            copy.start()

    def wait(self, *which):
        for at in which:
            self.copies[at].wait()


def slot_flag(count_ref, ocean_ref, slot):
    live = jnp.logical_and(slot < count_ref[0], ocean_ref[slot] > 0)
    return jnp.where(live, 1.0, 0.0).astype(F32)


class Shape:
    def __init__(self, slots, channels, hidden):
        self.slots = slots
        self.channels = channels
        self.hidden = hidden
        self.parts = channels // LANES
        self.columns = slots * TILE
        self.pitch = self.columns + 2 * LEFT
        self.cells = slots * TILE * TILE
        self.edge_rows = HALF * TILE
        self.early = 12

    def lanes(self, part):
        return slice(part * LANES, (part + 1) * LANES)


def edge_planes(shape, source, start, stride):
    return [
        jnp.concatenate(
            [source[part, pl.ds(start + col, TILE, stride=stride), :] for part in range(shape.parts)], axis=1
        )
        for col in range(HALF)
    ]


def send_edges(shape, left, right, first, second):
    even = is_even()
    for col in range(HALF):
        rows = pl.ds(col * TILE, TILE)
        first[rows, :] = jnp.where(even, right[col], left[col]).astype(BF16)
        second[rows, :] = jnp.where(even, left[col], right[col]).astype(BF16)


def flip_matrix(size, last):
    to = lax.broadcasted_iota(jnp.int32, (size, size), 0)
    frm = lax.broadcasted_iota(jnp.int32, (size, size), 1)
    return jnp.where(to + frm == last, 1.0, 0.0).astype(BF16)


def prep_kernel(shape, count_hbm, fields, first, second, count, work, sems):
    fetch = Fetch(sems, (count_hbm, count))
    for part in range(shape.parts):
        work[part] = fields[:, shape.lanes(part)].astype(F32)
    left = edge_planes(shape, work, 0, TILE)
    fetch.wait(0)
    right = edge_planes(shape, work, (count[0] - 1) * TILE * TILE + TILE - HALF, TILE)
    send_edges(shape, left, right, first, second)


def top_kernel(shape, count_hbm, ocean_hbm, fields, fold, count, ocean, sems):
    fetch = Fetch(sems, (count_hbm, count), (ocean_hbm, ocean))
    fetch.wait(0, 1)
    flip = flip_matrix(shape.columns, count[0] * TILE - 1)
    for k in range(HALF):
        cells = jnp.concatenate(
            [
                fields[pl.ds(slot * TILE * TILE + (TILE - 1 - k) * TILE, TILE), :].astype(F32)
                * slot_flag(count, ocean, slot)
                for slot in range(shape.slots)
            ]
        )
        turned = dot(flip, cells.astype(BF16), 1, 0)
        fold[pl.ds(k * shape.columns, shape.columns), :] = turned.astype(BF16)


def band_kernel(shape, count_hbm, ocean_hbm, fields, first, second, band, rims, count, ocean, sems):
    fetch = Fetch(sems, (count_hbm, count), (ocean_hbm, ocean))
    even = is_even()
    blank = jnp.zeros((LEFT, LANES), F32)
    per_slot = TILE * TILE
    for part in range(shape.parts):
        band[part, pl.ds(0, HALF * shape.pitch), :] = jnp.zeros((HALF * shape.pitch, LANES), F32)
        for row in range(TILE):
            base = (row + HALF) * shape.pitch
            band[part, pl.ds(base, LEFT), :] = blank
            band[part, pl.ds(base + LEFT + shape.columns, LEFT), :] = blank
    fetch.wait(0, 1)
    used = count[0] * TILE
    flags = [slot_flag(count, ocean, slot) for slot in range(shape.slots)]
    top = HALF * shape.pitch
    for part in range(shape.parts):
        for row in range(TILE):
            base = (row + HALF) * shape.pitch
            for slot in range(shape.slots):
                cells = fields[pl.ds(slot * per_slot + row * TILE, TILE), shape.lanes(part)]
                band[part, pl.ds(base + LEFT + slot * TILE, TILE), :] = cells.astype(F32) * flags[slot]
        for col in range(HALF):
            rows = pl.ds(col * TILE, TILE)
            one = first[rows, shape.lanes(part)].astype(F32)
            two = second[rows, shape.lanes(part)].astype(F32)
            west = jnp.where(even, two, one)
            east = jnp.where(even, one, two)
            band[part, pl.ds(top + LEFT - HALF + col, TILE, stride=shape.pitch), :] = west
            band[part, pl.ds(top + LEFT + used + col, TILE, stride=shape.pitch), :] = east
    for k in range(HALF):
        base = (HALF + TILE - 1 - k) * shape.pitch
        east = pl.multiple_of(base + LEFT + used, LEFT)
        for part in range(shape.parts):
            ends = jnp.concatenate([band[part, pl.ds(base, LEFT), :], band[part, pl.ds(east, LEFT), :]])
            rims[pl.ds(k * 2 * LEFT, 2 * LEFT), shape.lanes(part)] = ends.astype(BF16)


def put_fold(shape, used, fold, rims, parts, padded, first_row, work):
    blank = jnp.zeros((LEFT, LANES), F32)
    for at, part in enumerate(parts):
        work[at] = rims[:, shape.lanes(part)].astype(F32)
        for k in range(HALF):
            base = (first_row + k) * shape.pitch
            padded[at, pl.ds(base, LEFT), :] = blank
            padded[at, pl.ds(base + LEFT + shape.columns, LEFT), :] = blank
            cells = fold[pl.ds(k * shape.columns, shape.columns), shape.lanes(part)]
            padded[at, pl.ds(base + LEFT, shape.columns), :] = cells.astype(F32)
            for col in range(HALF):
                west = work[at, pl.ds(k * 2 * LEFT + LEFT - 1 - col, 1), :]
                east = work[at, pl.ds(k * 2 * LEFT + LEFT + col, 1), :]
                padded[at, pl.ds(base + LEFT - 1 - col, 1), :] = east
                padded[at, pl.ds(base + LEFT + used + col, 1), :] = west


def spread_taps(shape, kernel, parts, taps):
    for above in range(KSIZE):
        rows = kernel[above].astype(F32)
        for at, part in enumerate(parts):
            for shift in range(KSIZE):
                row = rows[shift : shift + 1, shape.lanes(part)]
                taps[at, above * KSIZE + shift] = jnp.broadcast_to(row, (8, LANES))


def convolve(shape, rows, padded, taps, convolved):
    run = shape.columns // 8
    pair = 2
    origin = LEFT - HALF

    def two_rows(step, carry):
        row = step * pair
        for part in range(shape.parts):
            sums = [[None] * run for _ in range(pair)]
            for above in range(KSIZE + pair - 1):
                base = (row + above) * shape.pitch + origin
                loaded = [
                    padded[part, pl.ds(base + at, 8, stride=run), :]
                    for at in range(run + KSIZE - 1)
                ]
                for which in range(pair):
                    tap_row = above - which
                    if not 0 <= tap_row < KSIZE:
                        continue
                    for shift in range(KSIZE):
                        weight = taps[part, tap_row * KSIZE + shift]
                        for at in range(run):
                            term = weight * loaded[at + shift]
                            old = sums[which][at]
                            sums[which][at] = term if old is None else old + term
            for which in range(pair):
                for at in range(run):
                    start = (row + which) * shape.columns + at
                    convolved[part, pl.ds(start, 8, stride=run), :] = sums[which][at]
        return carry

    lax.fori_loop(0, rows // pair, two_rows, 0)


def normalise(shape, rows, first_row, convolved, gain, normed, yhat, inverse):
    def one_row(row, carry):
        for slot in range(shape.slots):
            start = pl.multiple_of(row * shape.columns + slot * TILE, TILE)
            at = slot * TILE * TILE + (first_row + row) * TILE
            out = pl.ds(pl.multiple_of(at, TILE), TILE)
            parts = [convolved[part, pl.ds(start, TILE), :] for part in range(shape.parts)]
            mean = jnp.sum(sum(parts), axis=-1, keepdims=True) * (1.0 / shape.channels)
            parts = [value - mean for value in parts]
            square = jnp.sum(sum(value * value for value in parts), axis=-1, keepdims=True)
            scale = lax.rsqrt(square * (1.0 / shape.channels) + EPS)
            inverse[out, :] = jnp.broadcast_to(scale, (TILE, LANES))
            for part in range(shape.parts):
                value = parts[part] * scale
                yhat[out, shape.lanes(part)] = value
                normed[out, shape.lanes(part)] = (value * gain[:, shape.lanes(part)]).astype(BF16)
        return carry

    lax.fori_loop(0, rows, one_row, 0, unroll=4)


def early_kernel(
    shape, count_hbm, ocean_hbm, kernel, gain, w_out, scale, tangent, band,
    normed, yhat, inverse, dproj_t, dact, live,
    count, ocean, taps, convolved, dproj, sems,
):
    fetch = Fetch(sems, (count_hbm, count), (ocean_hbm, ocean))
    spread_taps(shape, kernel, range(shape.parts), taps)
    convolve(shape, shape.early, band, taps, convolved)
    normalise(shape, shape.early, 0, convolved, gain, normed, yhat, inverse)
    fetch.wait(0, 1)
    per_slot = TILE * TILE
    for slot in range(shape.slots):
        rows = pl.ds(slot * per_slot, per_slot)
        flag = slot_flag(count, ocean, slot)
        live[slot] = jnp.full((8, shape.channels), flag, F32)
        scaled = (tangent[rows, :].astype(F32) * (scale[...] * flag)).astype(BF16)
        dproj[rows, :] = scaled
        dproj_t[:, slot * per_slot : (slot + 1) * per_slot] = scaled.T
        for h in range(shape.hidden // shape.channels):
            cols = slice(h * shape.channels, (h + 1) * shape.channels)
            dact[rows, cols] = dot(dproj[rows, :], w_out[cols, :], 1, 1)


def late_kernel(
    shape, count_hbm, kernel, gain, w_in, band, fold, rims, normed_in, yhat_in, inverse_in, dproj_t, dact,
    keep, give, activated, dpreact, yhat, inverse, padded,
    count, taps, convolved, normed, normed_t, work, pre, sems,
):
    fetch = Fetch(sems, (count_hbm, count))
    late = TILE - shape.early
    kept = late + HALF
    for part in range(shape.parts):
        rows = pl.ds(shape.early * shape.pitch, kept * shape.pitch)
        padded[part, pl.ds(0, kept * shape.pitch), :] = band[part, rows, :]
    done = shape.early * TILE
    for slot in range(shape.slots):
        rows = pl.ds(slot * TILE * TILE, done)
        normed[rows, :] = normed_in[rows, :]
        yhat[rows, :] = yhat_in[rows, :]
        inverse[rows, :] = inverse_in[rows, :]
    spread_taps(shape, kernel, range(shape.parts), taps)
    fetch.wait(0)
    put_fold(shape, count[0] * TILE, fold, rims, range(shape.parts), padded, kept, work)
    convolve(shape, late, padded, taps, convolved)
    normalise(shape, late, shape.early, convolved, gain, normed, yhat, inverse)
    per_slot = TILE * TILE
    for slot in range(shape.slots):
        normed_t[:, slot * per_slot : (slot + 1) * per_slot] = normed[pl.ds(slot * per_slot, per_slot), :].T
    keeps_in = lax.axis_index("core") == 0
    block = shape.channels
    blocks = shape.hidden // block

    def span(h):
        return slice(h * block, (h + 1) * block)

    def expand(step):
        h, slot = divmod(step, shape.slots)
        pre[step % 3] = dot(normed[pl.ds(slot * per_slot, per_slot), :], w_in[:, span(h)], 1, 0)

    def activate(step):
        h, slot = divmod(step, shape.slots)
        rows, cols = pl.ds(slot * per_slot, per_slot), span(h)
        value = pre[step % 3]
        square = value * value
        gate = 0.5 + 0.5 * jnp.tanh(value * (GELU_C + (GELU_C * GELU_A) * square))
        activated[rows, cols] = (value * gate).astype(BF16)
        slope = value * (2.0 * GELU_C + (6.0 * GELU_C * GELU_A) * square)
        grown = gate + slope * (gate - gate * gate)
        dpreact[rows, cols] = (dact[rows, cols] * grown).astype(BF16)

    def reduce_rows(h):
        of_in = dot(normed_t[...], dpreact[:, span(h)], 1, 0)
        of_out = dot(dproj_t[...], activated[:, span(h)], 1, 0)
        keep[span(h), :] = jnp.where(keeps_in, of_in, of_out)
        give[span(h), :] = jnp.where(keeps_in, of_out, of_in).astype(BF16)

    steps = blocks * shape.slots
    expand(0)
    for step in range(steps):
        if step + 1 < steps:
            expand(step + 1)
        activate(step)
        h, slot = divmod(step, shape.slots)
        if slot == 0 and h:
            reduce_rows(h - 1)
    reduce_rows(blocks - 1)


def fold_sum(value):
    return jnp.sum(value.reshape(-1, 8, value.shape[-1]), axis=0)


def norm_grad_kernel(
    shape, w_in, w_out, gain, dpreact, yhat, inverse, activated, tangent, live,
    conv_grad, projected, gain_part, scale_part,
):
    chunk = TILE * TILE
    of_gain = jnp.zeros((8, shape.channels), F32)
    of_scale = jnp.zeros((8, shape.channels), F32)
    for slot in range(shape.slots):
        rows = pl.ds(slot * chunk, chunk)
        dnormed = dot(dpreact[rows, :], w_in[...], 1, 1)
        unit = yhat[rows, :]
        of_gain += fold_sum(dnormed * unit)
        dhat = dnormed * gain[...]
        mean = jnp.sum(dhat, axis=-1, keepdims=True) * (1.0 / shape.channels)
        along = jnp.sum(dhat * unit, axis=-1, keepdims=True) * (1.0 / shape.channels)
        scale = jnp.concatenate([inverse[rows, :]] * shape.parts, axis=1)
        conv_grad[rows, :] = (scale * (dhat - mean - unit * along)).astype(BF16)
        value = dot(activated[rows, :], w_out[...], 1, 0)
        projected[rows, :] = value
        of_scale += live[slot] * fold_sum(tangent[rows, :].astype(F32) * value)
    gain_part[...] = of_gain
    scale_part[...] = of_scale


def state_kernel(shape, fields, scale, projected, live, state, done):
    done[...] = jnp.zeros_like(done)
    chunk = TILE * TILE
    for slot in range(shape.slots):
        rows = pl.ds(slot * chunk, chunk)
        kept = fields[rows, :].astype(F32) + scale[...] * projected[rows, :]
        state[rows, :] = (live[slot, 0:1, :] * kept).astype(BF16)


def place_grad(shape, conv_grad, parts, spaced):
    blank = jnp.zeros((LEFT, LANES), F32)
    for at, part in enumerate(parts):
        for row in range(TILE):
            base = row * shape.pitch
            spaced[at, pl.ds(base, LEFT), :] = blank
            spaced[at, pl.ds(base + LEFT + shape.columns, LEFT), :] = blank
            for slot in range(shape.slots):
                cells = conv_grad[pl.ds(slot * TILE * TILE + row * TILE, TILE), shape.lanes(part)]
                spaced[at, pl.ds(base + LEFT + slot * TILE, TILE), :] = cells.astype(F32)


def taps_kernel(shape, part, band, top, conv_grad, small, padded, spaced):
    place_grad(shape, conv_grad, [part], spaced)
    kept = shape.early * shape.pitch
    padded[0, pl.ds(0, kept), :] = band[part, pl.ds(0, kept), :]
    padded[0, pl.ds(kept, top.shape[1]), :] = top[part]
    run = shape.columns // 8
    origin = LEFT - HALF
    for above in range(KSIZE):

        def one_row(row, sums, above=above):
            base = (row + above) * shape.pitch + origin
            loaded = [padded[0, pl.ds(base + at, 8, stride=run), :] for at in range(run + KSIZE - 1)]
            start = row * shape.pitch + LEFT
            grads = [spaced[0, pl.ds(start + at, 8, stride=run), :] for at in range(run)]
            sums = list(sums)
            for shift in range(KSIZE):
                for at in range(run):
                    sums[shift] = sums[shift] + grads[at] * loaded[at + shift]
            return tuple(sums)

        blank = tuple(jnp.zeros((8, LANES), F32) for _ in range(KSIZE))
        sums = lax.fori_loop(0, TILE, one_row, blank, unroll=2)
        for shift in range(KSIZE):
            small[pl.ds(above * KSIZE + shift, 1), :] = jnp.sum(sums[shift], axis=0, keepdims=True)


def back_kernel(shape, part, count_hbm, kernel, conv_grad, *refs):
    before = refs[:part]
    turns = part == shape.parts - 1
    core_grad, *refs = refs[part:]
    if turns:
        fold, *refs = refs
    count, spaced, taps, sems = refs
    fetch = Fetch(sems, (count_hbm, count))
    place_grad(shape, conv_grad, [part], spaced)
    blank = jnp.zeros((LEFT, LANES), F32)
    for row in range(TILE + HALF):
        core_grad[pl.ds(row * shape.pitch, LEFT), :] = blank
        core_grad[pl.ds((row + 1) * shape.pitch - LEFT, LEFT), :] = blank
    spread_taps(shape, kernel, [part], taps)
    run = -(-(shape.columns + 2 * HALF) // 8)

    def one_row(row, tap_rows):
        sums = [None] * run
        for above in tap_rows:
            base = (row - above) * shape.pitch + LEFT
            loaded = [
                spaced[0, pl.ds(base + at - KSIZE + 1, 8, stride=run), :] for at in range(run + KSIZE - 1)
            ]
            for shift in range(KSIZE):
                weight = taps[0, above * KSIZE + shift]
                for at in range(run):
                    term = weight * loaded[at - shift + KSIZE - 1]
                    sums[at] = term if sums[at] is None else sums[at] + term
        start = (row - HALF) * shape.pitch + LEFT - HALF
        for at in range(run):
            core_grad[pl.ds(start + at, 8, stride=run), :] = sums[at]

    inner = (KSIZE - 1, TILE - 1)
    for row in range(HALF, TILE + 2 * HALF):
        if not inner[0] <= row <= inner[1]:
            low = max(0, row - TILE + 1)
            one_row(row, range(low, min(KSIZE - 1, row) + 1))

    def inner_row(step, carry):
        one_row(step, range(KSIZE))
        return carry

    lax.fori_loop(inner[0], inner[1] + 1, inner_row, 0)
    fetch.wait(0)
    if turns:
        flip = flip_matrix(shape.pitch, count[0] * TILE + 2 * LEFT - 1)
        for k in range(HALF):
            at = pl.ds((TILE + k) * shape.pitch, shape.pitch)
            cells = jnp.concatenate([one[at, :] for one in (*before, core_grad)], axis=1)
            turned = dot(flip, cells.astype(BF16), 1, 0)
            fold[pl.ds(k * shape.pitch, shape.pitch), :] = turned.astype(BF16)


def rims_kernel(shape, count_hbm, fold, *refs):
    core_grad = refs[: shape.parts]
    folded, first, second, count, sems = refs[shape.parts :]
    fetch = Fetch(sems, (count_hbm, count))
    for part in range(shape.parts):
        folded[part] = core_grad[part][pl.ds(0, TILE * shape.pitch), :]
        for k in range(HALF):
            rows = pl.ds((TILE - 1 - k) * shape.pitch, shape.pitch)
            returned = fold[pl.ds(k * shape.pitch, shape.pitch), shape.lanes(part)]
            folded[part, rows, :] += returned.astype(F32)
    fetch.wait(0)
    west = edge_planes(shape, folded, LEFT - HALF, shape.pitch)
    east = edge_planes(shape, folded, LEFT + count[0] * TILE, shape.pitch)
    send_edges(shape, west, east, first, second)


def final_kernel(
    shape, count_hbm, ocean_hbm, tangent, folded, first, second,
    grad_fields, done,
    count, ocean, work, sems,
):
    fetch = Fetch(sems, (count_hbm, count), (ocean_hbm, ocean))
    even = is_even()
    done[...] = jnp.zeros_like(done)
    work[...] = folded[...]
    fetch.wait(0, 1)
    used = count[0] * TILE
    for part in range(shape.parts):
        for col in range(HALF):
            planes = pl.ds(col * TILE, TILE)
            one = first[planes, shape.lanes(part)].astype(F32)
            two = second[planes, shape.lanes(part)].astype(F32)
            to_tail = jnp.where(even, one, two)
            to_head = jnp.where(even, two, one)
            head = pl.ds(LEFT + col, TILE, stride=shape.pitch)
            work[part, head, :] = work[part, head, :] + to_head
            tail = pl.ds(LEFT + used - HALF + col, TILE, stride=shape.pitch)
            work[part, tail, :] = work[part, tail, :] + to_tail
        for slot in range(shape.slots):
            flag = slot_flag(count, ocean, slot)
            for row in range(TILE):
                rows = pl.ds(slot * TILE * TILE + row * TILE, TILE)
                cells = work[part, pl.ds(row * shape.pitch + LEFT + slot * TILE, TILE), :]
                total = tangent[rows, shape.lanes(part)].astype(F32) + cells
                grad_fields[rows, shape.lanes(part)] = (flag * total).astype(BF16)


def unpack_kernel(norm, own, came, w_in, w_out, kernel_sum, gain_sum, scale_sum):
    is_first = lax.axis_index("core") == 0
    hidden, channels = w_out.shape
    for h in range(hidden // channels):
        block = slice(h * channels, (h + 1) * channels)
        mine = own[block, :].astype(F32) * norm
        theirs = came[block, :].astype(F32) * norm
        w_in[:, block] = jnp.where(is_first, mine, theirs)
        w_out[block, :] = jnp.where(is_first, theirs, mine).T
    extra = (own.shape[0] - hidden) // 2
    high, low = pl.ds(hidden, extra), pl.ds(hidden + extra, extra)
    mine = (own[high, :].astype(F32) + own[low, :].astype(F32)) * norm
    theirs = (came[high, :].astype(F32) + came[low, :].astype(F32)) * norm
    small = jnp.concatenate([jnp.where(is_first, mine, theirs), jnp.where(is_first, theirs, mine)])
    for above in range(KSIZE):
        kernel_sum[above] = small[above * KSIZE : (above + 1) * KSIZE, :]
    gain_sum[...] = small[KSIZE * KSIZE : KSIZE * KSIZE + 1, :]
    scale_sum[...] = small[KSIZE * KSIZE + 1 : KSIZE * KSIZE + 2, :]


def pairs_of(kind):
    count = lax.axis_size(TILES)
    half = count // 2
    place = [rank if rank < half else count - 1 + half - rank for rank in range(count)]
    partner = {
        "first": lambda rank: rank ^ 1,
        "second": lambda rank: ((rank + 1) ^ 1) - 1,
        "fold": lambda rank: count - 1 - rank,
    }[kind]
    return [(place[rank], place[partner(rank) % count]) for rank in range(count)]


def swap(block, kind):
    return lax.ppermute(block, TILES, pairs_of(kind))


def core_swap(block):
    return lax.ppermute(block, "core", [(0, 1), (1, 0)])


def stages():
    chip_bits = lax.axis_size(CHIPS).bit_length() - 1
    rest = list(range(2, chip_bits))
    return list(zip([0, -1, 1] + rest, [1, 0, -1] + rest))


def bit_swap(block, stage):
    chips, cores, samples = (lax.axis_size(axis) for axis in (CHIPS, "core", "dp"))
    pairs = []
    for chip in range(chips):
        for core in range(cores):
            for sample in range(samples):
                bit = stage[core]
                to = (chip, sample ^ 1) if bit < 0 else (chip ^ (1 << bit), sample)
                pairs.append(
                    ((chip * cores + core) * samples + sample, (to[0] * cores + core) * samples + to[1])
                )
    return lax.ppermute(block, TILES + ("dp",), pairs)


def bit_here(stage):
    bits = [
        lax.axis_index("dp") if bit < 0 else chip_index() >> bit & 1 for bit in stage
    ]
    return jnp.where(lax.axis_index("core") == 0, bits[0], bits[1])


def half_rows(bit, rows):
    return pl.ds(pl.multiple_of(bit * rows, rows), rows)


def join_kernel(stage, keep, came, mine, send):
    rows = send.shape[0]
    mine[...] = keep[...] + came[...].astype(F32)
    send[...] = mine[half_rows(1 - bit_here(stage), rows), :].astype(BF16)


def halve_kernel(stage, following, whole, came, mine, send):
    rows = mine.shape[0]
    mine[...] = whole[half_rows(bit_here(stage), rows), :] + came[...].astype(F32)
    send[...] = mine[half_rows(1 - bit_here(following), rows // 2), :].astype(BF16)


def pack_kernel(gain_part, scale_part, *refs):
    taps, (keep, send, work) = refs[:-3], refs[-3:]
    half = keep.shape[0]
    work[...] = jnp.zeros_like(work)
    for part, ref in enumerate(taps):
        work[pl.ds(0, ref.shape[0]), part * LANES : (part + 1) * LANES] = ref[...]
    work[pl.ds(KSIZE * KSIZE, 1), :] = jnp.sum(gain_part[...], axis=0, keepdims=True)
    work[pl.ds(KSIZE * KSIZE + 1, 1), :] = jnp.sum(scale_part[...], axis=0, keepdims=True)
    core = lax.axis_index("core")
    keep[...] = work[half_rows(core, half), :]
    value = work[half_rows(1 - core, half), :]
    high = value.astype(BF16)
    send[pl.ds(0, half), :] = high
    send[pl.ds(half, half), :] = (value - high.astype(F32)).astype(BF16)


def turn_kernel(stage, whole, came, keep, extra, payload):
    rows, half = came.shape[0], keep.shape[0]
    share = whole[half_rows(bit_here(stage), rows), :] + came[...].astype(F32)
    payload[pl.ds(0, rows), :] = share.astype(BF16)
    small = keep[...] + (extra[pl.ds(0, half), :].astype(F32) + extra[pl.ds(half, half), :].astype(F32))
    payload[pl.ds(rows, half), :] = small.astype(BF16)


def add_kernel(own, came, payload):
    total = (own[...].astype(F32) + came[...].astype(F32)).astype(BF16)
    if payload.shape == total.shape:
        payload[...] = total
    else:
        for at in range(payload.shape[0]):
            payload[at] = total


def gather_kernel(order, extra, came, payload):
    rows = came.shape[1] - extra
    samples = lax.axis_size("dp")
    is_first = lax.axis_index("core") == 0
    total = jnp.zeros((extra, came.shape[2]), F32)
    for at in range(came.shape[0]):
        near, sample = divmod(at, samples)
        places = []
        for core in range(2):
            place = 0
            for stage in order:
                place = 2 * place + (sample if stage[core] < 0 else near >> stage[core] & 1)
            places.append(place)
        place = jnp.where(is_first, places[0], places[1])
        payload[half_rows(place, rows), :] = came[at, pl.ds(0, rows), :]
        total += came[at, pl.ds(rows, extra), :].astype(F32)
    high = total.astype(BF16)
    full = rows * came.shape[0]
    payload[pl.ds(full, extra), :] = high
    payload[pl.ds(full + extra, extra), :] = (total - high.astype(F32)).astype(BF16)


def double_kernel(stage, extra, own, came, payload):
    rows = own.shape[0] - extra
    bit = bit_here(stage)
    payload[half_rows(bit, rows), :] = own[pl.ds(0, rows), :]
    payload[half_rows(1 - bit, rows), :] = came[pl.ds(0, rows), :]
    total = own[pl.ds(rows, extra), :].astype(F32) + came[pl.ds(rows, extra), :].astype(F32)
    high = total.astype(BF16)
    payload[pl.ds(2 * rows, extra), :] = high
    if payload.shape[0] > 2 * rows + extra:
        payload[pl.ds(2 * rows + extra, extra), :] = (total - high.astype(F32)).astype(BF16)


def halved(mine, send, order):
    for at, stage in enumerate(order[:-1]):
        came = bit_swap(send, stage)
        rows = came.shape[0]
        bit = bit_here(stage)
        mine = lax.dynamic_index_in_dim(mine.reshape(2, rows, -1), bit, 0, keepdims=False) + came.astype(F32)
        bit = bit_here(order[at + 1])
        halves = mine.reshape(2, rows // 2, -1)
        send = lax.dynamic_index_in_dim(halves, 1 - bit, 0, keepdims=False).astype(BF16)
    return mine, send


def call(kernel, outs, scratch, hbm, vmem, copies=0, micros=1.0, after=(), limit=20):
    in_specs = [pl.BlockSpec(memory_space=pl.ANY)] * len(hbm)
    in_specs += [pl.BlockSpec(memory_space=pltpu.VMEM)] * len(vmem)
    in_specs += [pl.BlockSpec(memory_space=pl.ANY)] * len(after)
    shapes = [pltpu.SMEM(*one) if one[1] == jnp.int32 else pltpu.VMEM(*one) for one in scratch]
    if copies:
        shapes.append(pltpu.SemaphoreType.DMA((copies,)))
    taken = len(hbm) + len(vmem)

    def body(*refs):
        kernel(*refs[:taken], *refs[taken + len(after) :])

    return pl.pallas_call(
        body,
        out_shape=[jax.ShapeDtypeStruct(*out) for out in outs],
        in_specs=in_specs,
        out_specs=[pl.BlockSpec(memory_space=pltpu.VMEM)] * len(outs),
        scratch_shapes=shapes,
        cost_estimate=pl.CostEstimate(flops=int(micros * 1e9), bytes_accessed=0, transcendentals=0),
        compiler_params=pltpu.CompilerParams(vmem_limit_bytes=limit * 1024 * 1024),
    )(*hbm, *vmem, *after)


def shards(fields, grad_out, block_count, ocean, kernel, ln_gain, w_in, w_out, layer_scale):
    samples, slots, tile_rows, tile_cols, channels = fields.shape
    hidden = w_in.shape[1]
    shape = Shape(slots, channels, hidden)
    cells, parts, pitch = shape.cells, shape.parts, shape.pitch
    grid = fields.shape
    fields = fields.reshape(cells, channels)
    tangent = grad_out.reshape(cells, channels)
    taps_in = kernel
    gain = ln_gain.reshape(1, channels)
    scale = layer_scale.reshape(1, channels)

    def bind(body):
        return functools.partial(body, shape)

    def strip(rows):
        return ((parts, rows * pitch, LANES), F32)

    edge = ((shape.edge_rows, channels), BF16)
    turned = ((HALF * pitch, channels), BF16)
    whole = ((cells, channels), BF16)
    whole_f = ((cells, channels), F32)
    wide = ((cells, hidden), BF16)
    narrow = ((cells, LANES), F32)
    row = ((1, channels), F32)
    eight = ((8, channels), F32)
    taps = ((parts, KSIZE * KSIZE, 8, LANES), F32)
    count_s = (block_count.shape, jnp.int32)
    ocean_s = (ocean.shape, jnp.int32)
    flat = ((channels, cells), BF16)
    ends = ((HALF * 2 * LEFT, channels), BF16)
    ends_f = ((parts, HALF * 2 * LEFT, LANES), F32)
    late = TILE - shape.early

    first, second = call(
        bind(prep_kernel), [edge, edge], [count_s, ((parts, cells, LANES), F32)],
        [block_count], [fields], 1, 1.0,
    )
    (fold,) = call(
        bind(top_kernel), [((HALF * shape.columns, channels), BF16)], [count_s, ocean_s],
        [block_count, ocean], [fields], 2, 0.5, after=[first],
    )
    first, second = swap(first, "first"), swap(second, "second")
    band, rims = call(
        bind(band_kernel), [strip(TILE + HALF), ends], [count_s, ocean_s],
        [block_count, ocean], [fields, first, second], 2, 1.0, after=[fold],
    )
    fold, rims = swap(fold, "fold"), swap(rims, "fold")
    normed, yhat, inverse, dproj_t, dact, live = call(
        bind(early_kernel), [whole, whole_f, narrow, flat, ((cells, hidden), F32), ((slots, 8, channels), F32)],
        [count_s, ocean_s, taps, ((parts, shape.early * shape.columns, LANES), F32), whole],
        [block_count, ocean], [taps_in, gain, w_out, scale, tangent, band], 2, 5.0,
    )
    keep, give, activated, dpreact, yhat, inverse, top = call(
        bind(late_kernel),
        [((hidden, channels), F32), ((hidden, channels), BF16), wide, wide, whole_f, narrow, strip(late + 2 * HALF)],
        [
            count_s, taps, ((parts, late * shape.columns, LANES), F32), whole, flat, ends_f,
            ((3, TILE * TILE, channels), F32),
        ],
        [block_count],
        [taps_in, gain, w_in, band, fold, rims, normed, yhat, inverse, dproj_t, dact], 1, 5.0,
    )

    order = stages()
    rows = hidden // 2

    def half_step(at, rows):
        return functools.partial(halve_kernel, order[at], order[at + 1]), [
            ((rows, channels), F32), ((rows // 2, channels), BF16),
        ]

    def taps_part(part, after):
        (small,) = call(
            functools.partial(taps_kernel, shape, part), [((small_rows, LANES), F32)],
            [((1, (TILE + 2 * HALF) * pitch, LANES), F32), ((1, TILE * pitch, LANES), F32)],
            [], [band, top, conv_grad], 0, 1.8, after=after,
        )
        return small

    def back_part(part, before, after):
        outs = [(((TILE + HALF) * pitch, LANES), F32)] + [turned] * (part == parts - 1)
        return call(
            functools.partial(back_kernel, shape, part), outs,
            [count_s, ((1, TILE * pitch, LANES), F32), ((1, KSIZE * KSIZE, 8, LANES), F32)],
            [block_count], [taps_in, conv_grad, *before], 1, 2.0, after=after,
        )

    small_rows = -(-(KSIZE * KSIZE + 2) // 32) * 32
    came = core_swap(give)
    conv_grad, projected, gain_part, scale_part = call(
        bind(norm_grad_kernel), [whole, whole_f, eight, eight], [], [],
        [w_in, w_out, gain, dpreact, yhat, inverse, activated, tangent, live], 0, 1.3,
    )
    mine, send = call(
        functools.partial(join_kernel, order[0]),
        [((hidden, channels), F32), ((rows, channels), BF16)], [], [], [keep, came], after=[gain_part], micros=0.3,
    )
    came = bit_swap(send, order[0])
    core_grad = []
    after = [send]
    for part in range(parts):
        one, *fold_back = back_part(part, core_grad, after)
        core_grad += [one]
        after = [one]
    fold_back = swap(fold_back[0], "fold")
    body, outs = half_step(0, rows)
    mine, send = call(body, outs, [], [], [mine, came], after=after, micros=0.3)
    came = bit_swap(send, order[1])
    taps_parts = [taps_part(part, [send]) for part in range(parts)]
    small_rows //= 2
    small, extra = call(
        pack_kernel, [((small_rows, channels), F32), ((2 * small_rows, channels), BF16)],
        [((2 * small_rows, channels), F32)], [], [gain_part, scale_part, *taps_parts], micros=0.3,
    )
    extra = core_swap(extra)
    rows //= 2
    body, outs = half_step(1, rows)
    mine, send = call(body, outs, [], [], [mine, came], after=[small], micros=0.3)
    mine, send = halved(mine, send, order[2:-1])
    came = bit_swap(send, order[-2])
    folded, first, second = call(
        bind(rims_kernel), [strip(TILE), edge, edge], [count_s], [block_count], [fold_back, *core_grad], 1, 1.0,
        after=[send],
    )
    first, second = swap(first, "first"), swap(second, "second")
    rows = came.shape[0]
    if rows % 16 == 0:
        (payload,) = call(
            functools.partial(turn_kernel, order[-2]), [((rows + small_rows, channels), BF16)],
            [], [], [mine, came, small, extra], after=[folded], micros=0.3,
        )
    else:
        bit = bit_here(order[-2])
        share = lax.dynamic_index_in_dim(mine.reshape(2, rows, channels), bit, 0, keepdims=False)
        small = small + (extra[:small_rows].astype(F32) + extra[small_rows:].astype(F32))
        payload = jnp.concatenate([share + came.astype(F32), small]).astype(BF16)
    came = bit_swap(payload, order[-1])
    grad_fields, done = call(
        bind(final_kernel), [whole, ((8, LANES), F32)], [count_s, ocean_s, strip(TILE)],
        [block_count, ocean], [tangent, folded, first, second], 2, 1.5, after=[payload],
    )
    state, done_too = call(
        bind(state_kernel), [whole, ((8, LANES), F32)], [], [], [fields, scale, projected, live], 0, 1.0, after=[done],
    )
    block = lax.axis_size("near") * lax.axis_size("dp")
    copied = (block, *payload.shape)
    outer = range(block.bit_length() - 1, len(order) - 1)
    (payload,) = call(
        add_kernel, [(payload.shape if outer else copied, BF16)], [], [], [payload, came], after=[done, done_too],
        micros=0.3,
    )
    for at in reversed(outer):
        came = bit_swap(payload, order[at])
        if rows % 16 == 0:
            (payload,) = call(
                functools.partial(double_kernel, order[at], small_rows),
                [((2 * rows + small_rows, channels), BF16)], [], [], [payload, came], micros=0.3,
            )
        else:
            is_low = bit_here(order[at]) == 0
            low, high = payload[:rows], came[:rows]
            both = payload[rows:].astype(F32) + came[rows:].astype(F32)
            joined = [jnp.where(is_low, low, high), jnp.where(is_low, high, low), both.astype(BF16)]
            payload = jnp.concatenate(joined)
        rows *= 2
    if outer:
        payload = jnp.broadcast_to(payload, (block, *payload.shape))
    came = lax.all_to_all(payload, ("near", "dp"), 0, 0, tiled=True)
    (payload,) = call(
        functools.partial(gather_kernel, order[: block.bit_length() - 1], small_rows),
        [((hidden + 2 * small_rows, channels), BF16)], [], [], [came], micros=0.3,
    )
    came = core_swap(payload)
    total = samples * lax.axis_size("dp") * slots * lax.axis_size(TILES) * tile_rows * tile_cols
    norm = total ** (-0.5)
    sums = [((channels, hidden), F32), ((hidden, channels), F32)]
    w_in_sum, w_out_sum, kernel_sum, gain_sum, scale_sum = call(
        functools.partial(unpack_kernel, norm), sums + [(kernel.shape, F32), row, row], [],
        [], [payload, came], 0, 1.5,
    )
    return (
        state.reshape(grid),
        grad_fields.reshape(grid),
        kernel_sum,
        gain_sum.reshape(ln_gain.shape),
        w_in_sum,
        w_out_sum,
        scale_sum.reshape(layer_scale.shape),
    )


def solution(mesh):
    cores = Mesh(mesh.devices.reshape(-1, 4, 2, mesh.devices.shape[1]), TILES + ("dp",))
    banded = P("dp", TILES, None, None, None)
    placed = (banded, banded, P(TILES), P(TILES), P(), P(), P(), P(), P())
    return jax.shard_map(
        shards,
        mesh=cores,
        in_specs=placed,
        out_specs=(banded, banded, P(), P(), P(), P(), P()),
        check_vma=False,
    )
```

```python
import functools

import jax
import jax.numpy as jnp
from jax import lax
from jax.experimental import pallas as pl
from jax.experimental.pallas import tpu as pltpu
from jax.sharding import Mesh, PartitionSpec as P

KSIZE = 7
HALF = KSIZE // 2
TILE = 16
EPS = 1e-06
CHIPS = ("far", "near")
TILES = CHIPS + ("core",)
F32 = jnp.float32
BF16 = jnp.bfloat16
LANES = 128
LEFT = 8
GELU_C = 0.7978845608028654
GELU_A = 0.044715


def dot(lhs, rhs, lhs_dim, rhs_dim):
    return lax.dot_general(
        lhs, rhs, (((lhs_dim,), (rhs_dim,)), ((), ())), preferred_element_type=F32
    )


def chip_index():
    return lax.axis_index("far") * lax.axis_size("near") + lax.axis_index("near")


def cycle_rank():
    count = lax.axis_size(TILES)
    here = chip_index() * lax.axis_size("core") + lax.axis_index("core")
    return jnp.where(here < count // 2, here, count - 1 + count // 2 - here)


def is_even():
    return lax.rem(cycle_rank(), 2) == 0


class Fetch:
    def __init__(self, sems, *pairs):
        self.copies = [
            pltpu.make_async_copy(source, target, sems.at[at]) for at, (source, target) in enumerate(pairs)
        ]
        for copy in self.copies:
            copy.start()

    def wait(self, *which):
        for at in which:
            self.copies[at].wait()


def slot_flag(count_ref, ocean_ref, slot):
    live = jnp.logical_and(slot < count_ref[0], ocean_ref[slot] > 0)
    return jnp.where(live, 1.0, 0.0).astype(F32)


class Shape:
    def __init__(self, slots, channels, hidden):
        self.slots = slots
        self.channels = channels
        self.hidden = hidden
        self.parts = channels // LANES
        self.columns = slots * TILE
        self.pitch = self.columns + 2 * LEFT
        self.cells = slots * TILE * TILE
        self.edge_rows = HALF * TILE
        self.early = 12

    def lanes(self, part):
        return slice(part * LANES, (part + 1) * LANES)


def edge_planes(shape, source, start, stride):
    return [
        jnp.concatenate(
            [source[part, pl.ds(start + col, TILE, stride=stride), :] for part in range(shape.parts)], axis=1
        )
        for col in range(HALF)
    ]


def send_edges(shape, left, right, first, second):
    even = is_even()
    for col in range(HALF):
        rows = pl.ds(col * TILE, TILE)
        first[rows, :] = jnp.where(even, right[col], left[col]).astype(BF16)
        second[rows, :] = jnp.where(even, left[col], right[col]).astype(BF16)


def flip_matrix(size, last):
    to = lax.broadcasted_iota(jnp.int32, (size, size), 0)
    frm = lax.broadcasted_iota(jnp.int32, (size, size), 1)
    return jnp.where(to + frm == last, 1.0, 0.0).astype(BF16)


def prep_kernel(shape, count_hbm, fields, first, second, count, work, sems):
    fetch = Fetch(sems, (count_hbm, count))
    for part in range(shape.parts):
        work[part] = fields[:, shape.lanes(part)].astype(F32)
    left = edge_planes(shape, work, 0, TILE)
    fetch.wait(0)
    right = edge_planes(shape, work, (count[0] - 1) * TILE * TILE + TILE - HALF, TILE)
    send_edges(shape, left, right, first, second)


def top_kernel(shape, count_hbm, ocean_hbm, fields, fold, count, ocean, sems):
    fetch = Fetch(sems, (count_hbm, count), (ocean_hbm, ocean))
    fetch.wait(0, 1)
    flip = flip_matrix(shape.columns, count[0] * TILE - 1)
    for k in range(HALF):
        cells = jnp.concatenate(
            [
                fields[pl.ds(slot * TILE * TILE + (TILE - 1 - k) * TILE, TILE), :].astype(F32)
                * slot_flag(count, ocean, slot)
                for slot in range(shape.slots)
            ]
        )
        turned = dot(flip, cells.astype(BF16), 1, 0)
        fold[pl.ds(k * shape.columns, shape.columns), :] = turned.astype(BF16)


def band_kernel(shape, count_hbm, ocean_hbm, fields, first, second, band, rims, count, ocean, sems):
    fetch = Fetch(sems, (count_hbm, count), (ocean_hbm, ocean))
    even = is_even()
    blank = jnp.zeros((LEFT, LANES), F32)
    per_slot = TILE * TILE
    for part in range(shape.parts):
        band[part, pl.ds(0, HALF * shape.pitch), :] = jnp.zeros((HALF * shape.pitch, LANES), F32)
        for row in range(TILE):
            base = (row + HALF) * shape.pitch
            band[part, pl.ds(base, LEFT), :] = blank
            band[part, pl.ds(base + LEFT + shape.columns, LEFT), :] = blank
    fetch.wait(0, 1)
    used = count[0] * TILE
    flags = [slot_flag(count, ocean, slot) for slot in range(shape.slots)]
    top = HALF * shape.pitch
    for part in range(shape.parts):
        for row in range(TILE):
            base = (row + HALF) * shape.pitch
            for slot in range(shape.slots):
                cells = fields[pl.ds(slot * per_slot + row * TILE, TILE), shape.lanes(part)]
                band[part, pl.ds(base + LEFT + slot * TILE, TILE), :] = cells.astype(F32) * flags[slot]
        for col in range(HALF):
            rows = pl.ds(col * TILE, TILE)
            one = first[rows, shape.lanes(part)].astype(F32)
            two = second[rows, shape.lanes(part)].astype(F32)
            west = jnp.where(even, two, one)
            east = jnp.where(even, one, two)
            band[part, pl.ds(top + LEFT - HALF + col, TILE, stride=shape.pitch), :] = west
            band[part, pl.ds(top + LEFT + used + col, TILE, stride=shape.pitch), :] = east
    for k in range(HALF):
        base = (HALF + TILE - 1 - k) * shape.pitch
        east = pl.multiple_of(base + LEFT + used, LEFT)
        for part in range(shape.parts):
            ends = jnp.concatenate([band[part, pl.ds(base, LEFT), :], band[part, pl.ds(east, LEFT), :]])
            rims[pl.ds(k * 2 * LEFT, 2 * LEFT), shape.lanes(part)] = ends.astype(BF16)


def put_fold(shape, used, fold, rims, parts, padded, first_row, work):
    blank = jnp.zeros((LEFT, LANES), F32)
    for at, part in enumerate(parts):
        work[at] = rims[:, shape.lanes(part)].astype(F32)
        for k in range(HALF):
            base = (first_row + k) * shape.pitch
            padded[at, pl.ds(base, LEFT), :] = blank
            padded[at, pl.ds(base + LEFT + shape.columns, LEFT), :] = blank
            cells = fold[pl.ds(k * shape.columns, shape.columns), shape.lanes(part)]
            padded[at, pl.ds(base + LEFT, shape.columns), :] = cells.astype(F32)
            for col in range(HALF):
                west = work[at, pl.ds(k * 2 * LEFT + LEFT - 1 - col, 1), :]
                east = work[at, pl.ds(k * 2 * LEFT + LEFT + col, 1), :]
                padded[at, pl.ds(base + LEFT - 1 - col, 1), :] = east
                padded[at, pl.ds(base + LEFT + used + col, 1), :] = west


def spread_taps(shape, kernel, parts, taps):
    for above in range(KSIZE):
        rows = kernel[above].astype(F32)
        for at, part in enumerate(parts):
            for shift in range(KSIZE):
                row = rows[shift : shift + 1, shape.lanes(part)]
                taps[at, above * KSIZE + shift] = jnp.broadcast_to(row, (8, LANES))


def convolve(shape, rows, padded, taps, convolved):
    run = shape.columns // 8
    pair = 2
    origin = LEFT - HALF

    def two_rows(step, carry):
        row = step * pair
        for part in range(shape.parts):
            sums = [[None] * run for _ in range(pair)]
            for above in range(KSIZE + pair - 1):
                base = (row + above) * shape.pitch + origin
                loaded = [
                    padded[part, pl.ds(base + at, 8, stride=run), :]
                    for at in range(run + KSIZE - 1)
                ]
                for which in range(pair):
                    tap_row = above - which
                    if not 0 <= tap_row < KSIZE:
                        continue
                    for shift in range(KSIZE):
                        weight = taps[part, tap_row * KSIZE + shift]
                        for at in range(run):
                            term = weight * loaded[at + shift]
                            old = sums[which][at]
                            sums[which][at] = term if old is None else old + term
            for which in range(pair):
                for at in range(run):
                    start = (row + which) * shape.columns + at
                    convolved[part, pl.ds(start, 8, stride=run), :] = sums[which][at]
        return carry

    lax.fori_loop(0, rows // pair, two_rows, 0)


def normalise(shape, rows, first_row, convolved, gain, normed, yhat, inverse):
    def one_row(row, carry):
        for slot in range(shape.slots):
            start = pl.multiple_of(row * shape.columns + slot * TILE, TILE)
            at = slot * TILE * TILE + (first_row + row) * TILE
            out = pl.ds(pl.multiple_of(at, TILE), TILE)
            parts = [convolved[part, pl.ds(start, TILE), :] for part in range(shape.parts)]
            mean = jnp.sum(sum(parts), axis=-1, keepdims=True) * (1.0 / shape.channels)
            parts = [value - mean for value in parts]
            square = jnp.sum(sum(value * value for value in parts), axis=-1, keepdims=True)
            scale = lax.rsqrt(square * (1.0 / shape.channels) + EPS)
            inverse[out, :] = jnp.broadcast_to(scale, (TILE, LANES))
            for part in range(shape.parts):
                value = parts[part] * scale
                yhat[out, shape.lanes(part)] = value
                normed[out, shape.lanes(part)] = (value * gain[:, shape.lanes(part)]).astype(BF16)
        return carry

    lax.fori_loop(0, rows, one_row, 0, unroll=4)


def early_kernel(
    shape, count_hbm, ocean_hbm, kernel, gain, w_out, scale, tangent, band,
    normed, yhat, inverse, dproj_t, dact, live,
    count, ocean, taps, convolved, dproj, sems,
):
    fetch = Fetch(sems, (count_hbm, count), (ocean_hbm, ocean))
    spread_taps(shape, kernel, range(shape.parts), taps)
    convolve(shape, shape.early, band, taps, convolved)
    normalise(shape, shape.early, 0, convolved, gain, normed, yhat, inverse)
    fetch.wait(0, 1)
    per_slot = TILE * TILE
    for slot in range(shape.slots):
        rows = pl.ds(slot * per_slot, per_slot)
        flag = slot_flag(count, ocean, slot)
        live[slot] = jnp.full((8, shape.channels), flag, F32)
        scaled = (tangent[rows, :].astype(F32) * (scale[...] * flag)).astype(BF16)
        dproj[rows, :] = scaled
        dproj_t[:, slot * per_slot : (slot + 1) * per_slot] = scaled.T
        for h in range(shape.hidden // shape.channels):
            cols = slice(h * shape.channels, (h + 1) * shape.channels)
            dact[rows, cols] = dot(dproj[rows, :], w_out[cols, :], 1, 1)


def late_kernel(
    shape, count_hbm, kernel, gain, w_in, band, fold, rims, normed_in, yhat_in, inverse_in, dproj_t, dact,
    keep, give, activated, dpreact, yhat, inverse, padded,
    count, taps, convolved, normed, normed_t, work, pre, sems,
):
    fetch = Fetch(sems, (count_hbm, count))
    late = TILE - shape.early
    kept = late + HALF
    for part in range(shape.parts):
        rows = pl.ds(shape.early * shape.pitch, kept * shape.pitch)
        padded[part, pl.ds(0, kept * shape.pitch), :] = band[part, rows, :]
    done = shape.early * TILE
    for slot in range(shape.slots):
        rows = pl.ds(slot * TILE * TILE, done)
        normed[rows, :] = normed_in[rows, :]
        yhat[rows, :] = yhat_in[rows, :]
        inverse[rows, :] = inverse_in[rows, :]
    spread_taps(shape, kernel, range(shape.parts), taps)
    fetch.wait(0)
    put_fold(shape, count[0] * TILE, fold, rims, range(shape.parts), padded, kept, work)
    convolve(shape, late, padded, taps, convolved)
    normalise(shape, late, shape.early, convolved, gain, normed, yhat, inverse)
    per_slot = TILE * TILE
    for slot in range(shape.slots):
        normed_t[:, slot * per_slot : (slot + 1) * per_slot] = normed[pl.ds(slot * per_slot, per_slot), :].T
    keeps_in = lax.axis_index("core") == 0
    block = shape.channels
    blocks = shape.hidden // block

    def span(h):
        return slice(h * block, (h + 1) * block)

    def expand(step):
        h, slot = divmod(step, shape.slots)
        pre[step % 3] = dot(normed[pl.ds(slot * per_slot, per_slot), :], w_in[:, span(h)], 1, 0)

    def activate(step):
        h, slot = divmod(step, shape.slots)
        rows, cols = pl.ds(slot * per_slot, per_slot), span(h)
        value = pre[step % 3]
        square = value * value
        gate = 0.5 + 0.5 * jnp.tanh(value * (GELU_C + (GELU_C * GELU_A) * square))
        activated[rows, cols] = (value * gate).astype(BF16)
        slope = value * (2.0 * GELU_C + (6.0 * GELU_C * GELU_A) * square)
        grown = gate + slope * (gate - gate * gate)
        dpreact[rows, cols] = (dact[rows, cols] * grown).astype(BF16)

    def reduce_rows(h):
        of_in = dot(normed_t[...], dpreact[:, span(h)], 1, 0)
        of_out = dot(dproj_t[...], activated[:, span(h)], 1, 0)
        keep[span(h), :] = jnp.where(keeps_in, of_in, of_out)
        give[span(h), :] = jnp.where(keeps_in, of_out, of_in).astype(BF16)

    steps = blocks * shape.slots
    expand(0)
    for step in range(steps):
        if step + 1 < steps:
            expand(step + 1)
        activate(step)
        h, slot = divmod(step, shape.slots)
        if slot == 0 and h:
            reduce_rows(h - 1)
    reduce_rows(blocks - 1)


def fold_sum(value):
    return jnp.sum(value.reshape(-1, 8, value.shape[-1]), axis=0)


def norm_grad_kernel(
    shape, w_in, w_out, gain, dpreact, yhat, inverse, activated, tangent, live,
    conv_grad, projected, gain_part, scale_part,
):
    chunk = TILE * TILE
    of_gain = jnp.zeros((8, shape.channels), F32)
    of_scale = jnp.zeros((8, shape.channels), F32)
    for slot in range(shape.slots):
        rows = pl.ds(slot * chunk, chunk)
        dnormed = dot(dpreact[rows, :], w_in[...], 1, 1)
        unit = yhat[rows, :]
        of_gain += fold_sum(dnormed * unit)
        dhat = dnormed * gain[...]
        mean = jnp.sum(dhat, axis=-1, keepdims=True) * (1.0 / shape.channels)
        along = jnp.sum(dhat * unit, axis=-1, keepdims=True) * (1.0 / shape.channels)
        scale = jnp.concatenate([inverse[rows, :]] * shape.parts, axis=1)
        conv_grad[rows, :] = (scale * (dhat - mean - unit * along)).astype(BF16)
        value = dot(activated[rows, :], w_out[...], 1, 0)
        projected[rows, :] = value
        of_scale += live[slot] * fold_sum(tangent[rows, :].astype(F32) * value)
    gain_part[...] = of_gain
    scale_part[...] = of_scale


def state_kernel(shape, fields, scale, projected, live, state, done):
    done[...] = jnp.zeros_like(done)
    chunk = TILE * TILE
    for slot in range(shape.slots):
        rows = pl.ds(slot * chunk, chunk)
        kept = fields[rows, :].astype(F32) + scale[...] * projected[rows, :]
        state[rows, :] = (live[slot, 0:1, :] * kept).astype(BF16)


def place_grad(shape, conv_grad, parts, spaced):
    blank = jnp.zeros((LEFT, LANES), F32)
    for at, part in enumerate(parts):
        for row in range(TILE):
            base = row * shape.pitch
            spaced[at, pl.ds(base, LEFT), :] = blank
            spaced[at, pl.ds(base + LEFT + shape.columns, LEFT), :] = blank
            for slot in range(shape.slots):
                cells = conv_grad[pl.ds(slot * TILE * TILE + row * TILE, TILE), shape.lanes(part)]
                spaced[at, pl.ds(base + LEFT + slot * TILE, TILE), :] = cells.astype(F32)


def taps_kernel(shape, part, band, top, conv_grad, small, padded, spaced):
    place_grad(shape, conv_grad, [part], spaced)
    kept = shape.early * shape.pitch
    padded[0, pl.ds(0, kept), :] = band[part, pl.ds(0, kept), :]
    padded[0, pl.ds(kept, top.shape[1]), :] = top[part]
    run = shape.columns // 8
    origin = LEFT - HALF
    for above in range(KSIZE):

        def one_row(row, sums, above=above):
            base = (row + above) * shape.pitch + origin
            loaded = [padded[0, pl.ds(base + at, 8, stride=run), :] for at in range(run + KSIZE - 1)]
            start = row * shape.pitch + LEFT
            grads = [spaced[0, pl.ds(start + at, 8, stride=run), :] for at in range(run)]
            sums = list(sums)
            for shift in range(KSIZE):
                for at in range(run):
                    sums[shift] = sums[shift] + grads[at] * loaded[at + shift]
            return tuple(sums)

        blank = tuple(jnp.zeros((8, LANES), F32) for _ in range(KSIZE))
        sums = lax.fori_loop(0, TILE, one_row, blank, unroll=2)
        for shift in range(KSIZE):
            small[pl.ds(above * KSIZE + shift, 1), :] = jnp.sum(sums[shift], axis=0, keepdims=True)


def back_kernel(shape, part, count_hbm, kernel, conv_grad, *refs):
    before = refs[:part]
    turns = part == shape.parts - 1
    core_grad, *refs = refs[part:]
    if turns:
        fold, *refs = refs
    count, spaced, taps, sems = refs
    fetch = Fetch(sems, (count_hbm, count))
    place_grad(shape, conv_grad, [part], spaced)
    blank = jnp.zeros((LEFT, LANES), F32)
    for row in range(TILE + HALF):
        core_grad[pl.ds(row * shape.pitch, LEFT), :] = blank
        core_grad[pl.ds((row + 1) * shape.pitch - LEFT, LEFT), :] = blank
    spread_taps(shape, kernel, [part], taps)
    run = -(-(shape.columns + 2 * HALF) // 8)

    def one_row(row, tap_rows):
        sums = [None] * run
        for above in tap_rows:
            base = (row - above) * shape.pitch + LEFT
            loaded = [
                spaced[0, pl.ds(base + at - KSIZE + 1, 8, stride=run), :] for at in range(run + KSIZE - 1)
            ]
            for shift in range(KSIZE):
                weight = taps[0, above * KSIZE + shift]
                for at in range(run):
                    term = weight * loaded[at - shift + KSIZE - 1]
                    sums[at] = term if sums[at] is None else sums[at] + term
        start = (row - HALF) * shape.pitch + LEFT - HALF
        for at in range(run):
            core_grad[pl.ds(start + at, 8, stride=run), :] = sums[at]

    inner = (KSIZE - 1, TILE - 1)
    for row in range(HALF, TILE + 2 * HALF):
        if not inner[0] <= row <= inner[1]:
            low = max(0, row - TILE + 1)
            one_row(row, range(low, min(KSIZE - 1, row) + 1))

    def inner_row(step, carry):
        one_row(step, range(KSIZE))
        return carry

    lax.fori_loop(inner[0], inner[1] + 1, inner_row, 0)
    fetch.wait(0)
    if turns:
        flip = flip_matrix(shape.pitch, count[0] * TILE + 2 * LEFT - 1)
        for k in range(HALF):
            at = pl.ds((TILE + k) * shape.pitch, shape.pitch)
            cells = jnp.concatenate([one[at, :] for one in (*before, core_grad)], axis=1)
            turned = dot(flip, cells.astype(BF16), 1, 0)
            fold[pl.ds(k * shape.pitch, shape.pitch), :] = turned.astype(BF16)


def rims_kernel(shape, count_hbm, fold, *refs):
    core_grad = refs[: shape.parts]
    folded, first, second, count, sems = refs[shape.parts :]
    fetch = Fetch(sems, (count_hbm, count))
    for part in range(shape.parts):
        folded[part] = core_grad[part][pl.ds(0, TILE * shape.pitch), :]
        for k in range(HALF):
            rows = pl.ds((TILE - 1 - k) * shape.pitch, shape.pitch)
            returned = fold[pl.ds(k * shape.pitch, shape.pitch), shape.lanes(part)]
            folded[part, rows, :] += returned.astype(F32)
    fetch.wait(0)
    west = edge_planes(shape, folded, LEFT - HALF, shape.pitch)
    east = edge_planes(shape, folded, LEFT + count[0] * TILE, shape.pitch)
    send_edges(shape, west, east, first, second)


def final_kernel(
    shape, count_hbm, ocean_hbm, tangent, folded, first, second,
    grad_fields, done,
    count, ocean, work, sems,
):
    fetch = Fetch(sems, (count_hbm, count), (ocean_hbm, ocean))
    even = is_even()
    done[...] = jnp.zeros_like(done)
    work[...] = folded[...]
    fetch.wait(0, 1)
    used = count[0] * TILE
    for part in range(shape.parts):
        for col in range(HALF):
            planes = pl.ds(col * TILE, TILE)
            one = first[planes, shape.lanes(part)].astype(F32)
            two = second[planes, shape.lanes(part)].astype(F32)
            to_tail = jnp.where(even, one, two)
            to_head = jnp.where(even, two, one)
            head = pl.ds(LEFT + col, TILE, stride=shape.pitch)
            work[part, head, :] = work[part, head, :] + to_head
            tail = pl.ds(LEFT + used - HALF + col, TILE, stride=shape.pitch)
            work[part, tail, :] = work[part, tail, :] + to_tail
        for slot in range(shape.slots):
            flag = slot_flag(count, ocean, slot)
            for row in range(TILE):
                rows = pl.ds(slot * TILE * TILE + row * TILE, TILE)
                cells = work[part, pl.ds(row * shape.pitch + LEFT + slot * TILE, TILE), :]
                total = tangent[rows, shape.lanes(part)].astype(F32) + cells
                grad_fields[rows, shape.lanes(part)] = (flag * total).astype(BF16)


def unpack_kernel(norm, own, came, w_in, w_out, kernel_sum, gain_sum, scale_sum):
    is_first = lax.axis_index("core") == 0
    hidden, channels = w_out.shape
    for h in range(hidden // channels):
        block = slice(h * channels, (h + 1) * channels)
        mine = own[block, :].astype(F32) * norm
        theirs = came[block, :].astype(F32) * norm
        w_in[:, block] = jnp.where(is_first, mine, theirs)
        w_out[block, :] = jnp.where(is_first, theirs, mine).T
    extra = (own.shape[0] - hidden) // 2
    high, low = pl.ds(hidden, extra), pl.ds(hidden + extra, extra)
    mine = (own[high, :].astype(F32) + own[low, :].astype(F32)) * norm
    theirs = (came[high, :].astype(F32) + came[low, :].astype(F32)) * norm
    small = jnp.concatenate([jnp.where(is_first, mine, theirs), jnp.where(is_first, theirs, mine)])
    for above in range(KSIZE):
        kernel_sum[above] = small[above * KSIZE : (above + 1) * KSIZE, :]
    gain_sum[...] = small[KSIZE * KSIZE : KSIZE * KSIZE + 1, :]
    scale_sum[...] = small[KSIZE * KSIZE + 1 : KSIZE * KSIZE + 2, :]


def pairs_of(kind):
    count = lax.axis_size(TILES)
    half = count // 2
    place = [rank if rank < half else count - 1 + half - rank for rank in range(count)]
    partner = {
        "first": lambda rank: rank ^ 1,
        "second": lambda rank: ((rank + 1) ^ 1) - 1,
        "fold": lambda rank: count - 1 - rank,
    }[kind]
    return [(place[rank], place[partner(rank) % count]) for rank in range(count)]


def swap(block, kind):
    return lax.ppermute(block, TILES, pairs_of(kind))


def core_swap(block):
    return lax.ppermute(block, "core", [(0, 1), (1, 0)])


def stages():
    chip_bits = lax.axis_size(CHIPS).bit_length() - 1
    rest = list(range(2, chip_bits))
    return list(zip([0, -1, 1] + rest, [1, 0, -1] + rest))


def bit_swap(block, stage):
    chips, cores, samples = (lax.axis_size(axis) for axis in (CHIPS, "core", "dp"))
    pairs = []
    for chip in range(chips):
        for core in range(cores):
            for sample in range(samples):
                bit = stage[core]
                to = (chip, sample ^ 1) if bit < 0 else (chip ^ (1 << bit), sample)
                pairs.append(
                    ((chip * cores + core) * samples + sample, (to[0] * cores + core) * samples + to[1])
                )
    return lax.ppermute(block, TILES + ("dp",), pairs)


def bit_here(stage):
    bits = [
        lax.axis_index("dp") if bit < 0 else chip_index() >> bit & 1 for bit in stage
    ]
    return jnp.where(lax.axis_index("core") == 0, bits[0], bits[1])


def half_rows(bit, rows):
    return pl.ds(pl.multiple_of(bit * rows, rows), rows)


def place_of(order, at):
    near, sample = divmod(at, lax.axis_size("dp"))
    places = []
    for core in range(2):
        place = 0
        for stage in order:
            place = 2 * place + (sample if stage[core] < 0 else near >> stage[core] & 1)
        places.append(place)
    return jnp.where(lax.axis_index("core") == 0, places[0], places[1])


def join_kernel(order, keep, came, pieces):
    rows = pieces.shape[1]
    for at in range(pieces.shape[0]):
        share = half_rows(place_of(order, at), rows)
        pieces[at] = (keep[share, :] + came[share, :].astype(F32)).astype(BF16)


def pack_kernel(gain_part, scale_part, *refs):
    taps, (keep, send, work) = refs[:-3], refs[-3:]
    half = keep.shape[0]
    work[...] = jnp.zeros_like(work)
    for part, ref in enumerate(taps):
        work[pl.ds(0, ref.shape[0]), part * LANES : (part + 1) * LANES] = ref[...]
    work[pl.ds(KSIZE * KSIZE, 1), :] = jnp.sum(gain_part[...], axis=0, keepdims=True)
    work[pl.ds(KSIZE * KSIZE + 1, 1), :] = jnp.sum(scale_part[...], axis=0, keepdims=True)
    core = lax.axis_index("core")
    keep[...] = work[half_rows(core, half), :]
    value = work[half_rows(1 - core, half), :]
    high = value.astype(BF16)
    send[pl.ds(0, half), :] = high
    send[pl.ds(half, half), :] = (value - high.astype(F32)).astype(BF16)


def turn_kernel(came, keep, extra, payload):
    rows, half = came.shape[1], keep.shape[0]
    share = sum(came[at].astype(F32) for at in range(came.shape[0]))
    payload[pl.ds(0, rows), :] = share.astype(BF16)
    small = keep[...] + (extra[pl.ds(0, half), :].astype(F32) + extra[pl.ds(half, half), :].astype(F32))
    payload[pl.ds(rows, half), :] = small.astype(BF16)


def add_kernel(own, came, payload):
    total = (own[...].astype(F32) + came[...].astype(F32)).astype(BF16)
    if payload.shape == total.shape:
        payload[...] = total
    else:
        for at in range(payload.shape[0]):
            payload[at] = total


def gather_kernel(order, extra, came, payload):
    rows = came.shape[1] - extra
    total = jnp.zeros((extra, came.shape[2]), F32)
    for at in range(came.shape[0]):
        payload[half_rows(place_of(order, at), rows), :] = came[at, pl.ds(0, rows), :]
        total += came[at, pl.ds(rows, extra), :].astype(F32)
    high = total.astype(BF16)
    full = rows * came.shape[0]
    payload[pl.ds(full, extra), :] = high
    payload[pl.ds(full + extra, extra), :] = (total - high.astype(F32)).astype(BF16)


def double_kernel(stage, extra, own, came, payload):
    rows = own.shape[0] - extra
    bit = bit_here(stage)
    payload[half_rows(bit, rows), :] = own[pl.ds(0, rows), :]
    payload[half_rows(1 - bit, rows), :] = came[pl.ds(0, rows), :]
    total = own[pl.ds(rows, extra), :].astype(F32) + came[pl.ds(rows, extra), :].astype(F32)
    high = total.astype(BF16)
    payload[pl.ds(2 * rows, extra), :] = high
    if payload.shape[0] > 2 * rows + extra:
        payload[pl.ds(2 * rows + extra, extra), :] = (total - high.astype(F32)).astype(BF16)


def halved(mine, order):
    for stage in order:
        bit = bit_here(stage)
        halves = mine.reshape(2, -1, mine.shape[-1])
        send = lax.dynamic_index_in_dim(halves, 1 - bit, 0, keepdims=False).astype(BF16)
        mine = lax.dynamic_index_in_dim(halves, bit, 0, keepdims=False) + bit_swap(send, stage).astype(F32)
    return mine


def call(kernel, outs, scratch, hbm, vmem, copies=0, micros=1.0, after=(), limit=20):
    in_specs = [pl.BlockSpec(memory_space=pl.ANY)] * len(hbm)
    in_specs += [pl.BlockSpec(memory_space=pltpu.VMEM)] * len(vmem)
    in_specs += [pl.BlockSpec(memory_space=pl.ANY)] * len(after)
    shapes = [pltpu.SMEM(*one) if one[1] == jnp.int32 else pltpu.VMEM(*one) for one in scratch]
    if copies:
        shapes.append(pltpu.SemaphoreType.DMA((copies,)))
    taken = len(hbm) + len(vmem)

    def body(*refs):
        kernel(*refs[:taken], *refs[taken + len(after) :])

    return pl.pallas_call(
        body,
        out_shape=[jax.ShapeDtypeStruct(*out) for out in outs],
        in_specs=in_specs,
        out_specs=[pl.BlockSpec(memory_space=pltpu.VMEM)] * len(outs),
        scratch_shapes=shapes,
        cost_estimate=pl.CostEstimate(flops=int(micros * 1e9), bytes_accessed=0, transcendentals=0),
        compiler_params=pltpu.CompilerParams(vmem_limit_bytes=limit * 1024 * 1024),
    )(*hbm, *vmem, *after)


def shards(fields, grad_out, block_count, ocean, kernel, ln_gain, w_in, w_out, layer_scale):
    samples, slots, tile_rows, tile_cols, channels = fields.shape
    hidden = w_in.shape[1]
    shape = Shape(slots, channels, hidden)
    cells, parts, pitch = shape.cells, shape.parts, shape.pitch
    grid = fields.shape
    fields = fields.reshape(cells, channels)
    tangent = grad_out.reshape(cells, channels)
    taps_in = kernel
    gain = ln_gain.reshape(1, channels)
    scale = layer_scale.reshape(1, channels)

    def bind(body):
        return functools.partial(body, shape)

    def strip(rows):
        return ((parts, rows * pitch, LANES), F32)

    edge = ((shape.edge_rows, channels), BF16)
    turned = ((HALF * pitch, channels), BF16)
    whole = ((cells, channels), BF16)
    whole_f = ((cells, channels), F32)
    wide = ((cells, hidden), BF16)
    narrow = ((cells, LANES), F32)
    row = ((1, channels), F32)
    eight = ((8, channels), F32)
    taps = ((parts, KSIZE * KSIZE, 8, LANES), F32)
    count_s = (block_count.shape, jnp.int32)
    ocean_s = (ocean.shape, jnp.int32)
    flat = ((channels, cells), BF16)
    ends = ((HALF * 2 * LEFT, channels), BF16)
    ends_f = ((parts, HALF * 2 * LEFT, LANES), F32)
    late = TILE - shape.early

    first, second = call(
        bind(prep_kernel), [edge, edge], [count_s, ((parts, cells, LANES), F32)],
        [block_count], [fields], 1, 1.0,
    )
    (fold,) = call(
        bind(top_kernel), [((HALF * shape.columns, channels), BF16)], [count_s, ocean_s],
        [block_count, ocean], [fields], 2, 0.5, after=[first],
    )
    first, second = swap(first, "first"), swap(second, "second")
    band, rims = call(
        bind(band_kernel), [strip(TILE + HALF), ends], [count_s, ocean_s],
        [block_count, ocean], [fields, first, second], 2, 1.0, after=[fold],
    )
    fold, rims = swap(fold, "fold"), swap(rims, "fold")
    normed, yhat, inverse, dproj_t, dact, live = call(
        bind(early_kernel), [whole, whole_f, narrow, flat, ((cells, hidden), F32), ((slots, 8, channels), F32)],
        [count_s, ocean_s, taps, ((parts, shape.early * shape.columns, LANES), F32), whole],
        [block_count, ocean], [taps_in, gain, w_out, scale, tangent, band], 2, 5.0,
    )
    keep, give, activated, dpreact, yhat, inverse, top = call(
        bind(late_kernel),
        [((hidden, channels), F32), ((hidden, channels), BF16), wide, wide, whole_f, narrow, strip(late + 2 * HALF)],
        [
            count_s, taps, ((parts, late * shape.columns, LANES), F32), whole, flat, ends_f,
            ((3, TILE * TILE, channels), F32),
        ],
        [block_count],
        [taps_in, gain, w_in, band, fold, rims, normed, yhat, inverse, dproj_t, dact], 1, 5.0,
    )

    order = stages()
    block = lax.axis_size("near") * lax.axis_size("dp")
    inner = block.bit_length() - 1
    rows = hidden // block

    def taps_part(part, after):
        (small,) = call(
            functools.partial(taps_kernel, shape, part), [((small_rows, LANES), F32)],
            [((1, (TILE + 2 * HALF) * pitch, LANES), F32), ((1, TILE * pitch, LANES), F32)],
            [], [band, top, conv_grad], 0, 1.8, after=after,
        )
        return small

    def back_part(part, before, after):
        outs = [(((TILE + HALF) * pitch, LANES), F32)] + [turned] * (part == parts - 1)
        return call(
            functools.partial(back_kernel, shape, part), outs,
            [count_s, ((1, TILE * pitch, LANES), F32), ((1, KSIZE * KSIZE, 8, LANES), F32)],
            [block_count], [taps_in, conv_grad, *before], 1, 2.0, after=after,
        )

    small_rows = -(-(KSIZE * KSIZE + 2) // 32) * 32
    came = core_swap(give)
    conv_grad, projected, gain_part, scale_part = call(
        bind(norm_grad_kernel), [whole, whole_f, eight, eight], [], [],
        [w_in, w_out, gain, dpreact, yhat, inverse, activated, tangent, live], 0, 1.3,
    )
    (send,) = call(
        functools.partial(join_kernel, order[:inner]), [((block, rows, channels), BF16)],
        [], [], [keep, came], after=[gain_part], micros=0.3,
    )
    came = lax.all_to_all(send, ("near", "dp"), 0, 0, tiled=True)
    core_grad = []
    after = [send]
    for part in range(parts):
        one, *fold_back = back_part(part, core_grad, after)
        core_grad += [one]
        after = [one]
    fold_back = swap(fold_back[0], "fold")
    taps_parts = [taps_part(part, after) for part in range(parts)]
    small_rows //= 2
    small, extra = call(
        pack_kernel, [((small_rows, channels), F32), ((2 * small_rows, channels), BF16)],
        [((2 * small_rows, channels), F32)], [], [gain_part, scale_part, *taps_parts], micros=0.3,
    )
    extra = core_swap(extra)
    folded, first, second = call(
        bind(rims_kernel), [strip(TILE), edge, edge], [count_s], [block_count], [fold_back, *core_grad], 1, 1.0,
        after=[small],
    )
    first, second = swap(first, "first"), swap(second, "second")
    if len(order) == inner + 1:
        (payload,) = call(
            turn_kernel, [((rows + small_rows, channels), BF16)], [], [], [came, small, extra], after=[folded], micros=0.3,
        )
    else:
        share = halved(jnp.sum(came.astype(F32), axis=0), order[inner:-1])
        rows = share.shape[0]
        small = small + (extra[:small_rows].astype(F32) + extra[small_rows:].astype(F32))
        payload = jnp.concatenate([share, small]).astype(BF16)
    came = bit_swap(payload, order[-1])
    grad_fields, done = call(
        bind(final_kernel), [whole, ((8, LANES), F32)], [count_s, ocean_s, strip(TILE)],
        [block_count, ocean], [tangent, folded, first, second], 2, 1.5, after=[payload],
    )
    state, done_too = call(
        bind(state_kernel), [whole, ((8, LANES), F32)], [], [], [fields, scale, projected, live], 0, 1.0, after=[done],
    )
    copied = (block, *payload.shape)
    outer = range(inner, len(order) - 1)
    (payload,) = call(
        add_kernel, [(payload.shape if outer else copied, BF16)], [], [], [payload, came], after=[done, done_too],
        micros=0.3,
    )
    for at in reversed(outer):
        came = bit_swap(payload, order[at])
        if rows % 16 == 0:
            (payload,) = call(
                functools.partial(double_kernel, order[at], small_rows),
                [((2 * rows + small_rows, channels), BF16)], [], [], [payload, came], micros=0.3,
            )
        else:
            is_low = bit_here(order[at]) == 0
            low, high = payload[:rows], came[:rows]
            both = payload[rows:].astype(F32) + came[rows:].astype(F32)
            joined = [jnp.where(is_low, low, high), jnp.where(is_low, high, low), both.astype(BF16)]
            payload = jnp.concatenate(joined)
        rows *= 2
    if outer:
        payload = jnp.broadcast_to(payload, (block, *payload.shape))
    came = lax.all_to_all(payload, ("near", "dp"), 0, 0, tiled=True)
    (payload,) = call(
        functools.partial(gather_kernel, order[:inner], small_rows),
        [((hidden + 2 * small_rows, channels), BF16)], [], [], [came], micros=0.3,
    )
    came = core_swap(payload)
    total = samples * lax.axis_size("dp") * slots * lax.axis_size(TILES) * tile_rows * tile_cols
    norm = total ** (-0.5)
    sums = [((channels, hidden), F32), ((hidden, channels), F32)]
    w_in_sum, w_out_sum, kernel_sum, gain_sum, scale_sum = call(
        functools.partial(unpack_kernel, norm), sums + [(kernel.shape, F32), row, row], [],
        [], [payload, came], 0, 1.5,
    )
    return (
        state.reshape(grid),
        grad_fields.reshape(grid),
        kernel_sum,
        gain_sum.reshape(ln_gain.shape),
        w_in_sum,
        w_out_sum,
        scale_sum.reshape(layer_scale.shape),
    )


def solution(mesh):
    cores = Mesh(mesh.devices.reshape(-1, 4, 2, mesh.devices.shape[1]), TILES + ("dp",))
    banded = P("dp", TILES, None, None, None)
    placed = (banded, banded, P(TILES), P(TILES), P(), P(), P(), P(), P())
    return jax.shard_map(
        shards,
        mesh=cores,
        in_specs=placed,
        out_specs=(banded, banded, P(), P(), P(), P(), P()),
        check_vma=False,
    )
```

```python
import functools

import jax
import jax.numpy as jnp
from jax import lax
from jax.experimental import pallas as pl
from jax.experimental.pallas import tpu as pltpu
from jax.sharding import Mesh, PartitionSpec as P

KSIZE = 7
HALF = KSIZE // 2
TILE = 16
EPS = 1e-06
CHIPS = ("far", "near")
TILES = CHIPS + ("core",)
F32 = jnp.float32
BF16 = jnp.bfloat16
LANES = 128
LEFT = 8
GELU_C = 0.7978845608028654
GELU_A = 0.044715


def dot(lhs, rhs, lhs_dim, rhs_dim):
    return lax.dot_general(
        lhs, rhs, (((lhs_dim,), (rhs_dim,)), ((), ())), preferred_element_type=F32
    )


def chip_index():
    return lax.axis_index("far") * lax.axis_size("near") + lax.axis_index("near")


def cycle_rank():
    count = lax.axis_size(TILES)
    here = chip_index() * lax.axis_size("core") + lax.axis_index("core")
    return jnp.where(here < count // 2, here, count - 1 + count // 2 - here)


def is_even():
    return lax.rem(cycle_rank(), 2) == 0


class Fetch:
    def __init__(self, sems, *pairs):
        self.copies = [
            pltpu.make_async_copy(source, target, sems.at[at]) for at, (source, target) in enumerate(pairs)
        ]
        for copy in self.copies:
            copy.start()

    def wait(self, *which):
        for at in which:
            self.copies[at].wait()


def slot_flag(count_ref, ocean_ref, slot):
    live = jnp.logical_and(slot < count_ref[0], ocean_ref[slot] > 0)
    return jnp.where(live, 1.0, 0.0).astype(F32)


class Shape:
    def __init__(self, slots, channels, hidden):
        self.slots = slots
        self.channels = channels
        self.hidden = hidden
        self.parts = channels // LANES
        self.columns = slots * TILE
        self.pitch = self.columns + 2 * LEFT
        self.cells = slots * TILE * TILE
        self.edge_rows = HALF * TILE
        self.early = 12

    def lanes(self, part):
        return slice(part * LANES, (part + 1) * LANES)


def edge_planes(shape, source, start, stride):
    return [
        jnp.concatenate(
            [source[part, pl.ds(start + col, TILE, stride=stride), :] for part in range(shape.parts)], axis=1
        )
        for col in range(HALF)
    ]


def send_edges(shape, left, right, first, second):
    even = is_even()
    for col in range(HALF):
        rows = pl.ds(col * TILE, TILE)
        first[rows, :] = jnp.where(even, right[col], left[col]).astype(BF16)
        second[rows, :] = jnp.where(even, left[col], right[col]).astype(BF16)


def flip_matrix(size, last):
    to = lax.broadcasted_iota(jnp.int32, (size, size), 0)
    frm = lax.broadcasted_iota(jnp.int32, (size, size), 1)
    return jnp.where(to + frm == last, 1.0, 0.0).astype(BF16)


def prep_kernel(shape, count_hbm, fields, first, second, count, work, sems):
    fetch = Fetch(sems, (count_hbm, count))
    for part in range(shape.parts):
        work[part] = fields[:, shape.lanes(part)].astype(F32)
    left = edge_planes(shape, work, 0, TILE)
    fetch.wait(0)
    right = edge_planes(shape, work, (count[0] - 1) * TILE * TILE + TILE - HALF, TILE)
    send_edges(shape, left, right, first, second)


def top_kernel(shape, count_hbm, ocean_hbm, fields, fold, count, ocean, sems):
    fetch = Fetch(sems, (count_hbm, count), (ocean_hbm, ocean))
    fetch.wait(0, 1)
    flip = flip_matrix(shape.columns, count[0] * TILE - 1)
    for k in range(HALF):
        cells = jnp.concatenate(
            [
                fields[pl.ds(slot * TILE * TILE + (TILE - 1 - k) * TILE, TILE), :].astype(F32)
                * slot_flag(count, ocean, slot)
                for slot in range(shape.slots)
            ]
        )
        turned = dot(flip, cells.astype(BF16), 1, 0)
        fold[pl.ds(k * shape.columns, shape.columns), :] = turned.astype(BF16)


def band_kernel(shape, count_hbm, ocean_hbm, fields, first, second, band, rims, count, ocean, sems):
    fetch = Fetch(sems, (count_hbm, count), (ocean_hbm, ocean))
    even = is_even()
    blank = jnp.zeros((LEFT, LANES), F32)
    per_slot = TILE * TILE
    for part in range(shape.parts):
        band[part, pl.ds(0, HALF * shape.pitch), :] = jnp.zeros((HALF * shape.pitch, LANES), F32)
        for row in range(TILE):
            base = (row + HALF) * shape.pitch
            band[part, pl.ds(base, LEFT), :] = blank
            band[part, pl.ds(base + LEFT + shape.columns, LEFT), :] = blank
    fetch.wait(0, 1)
    used = count[0] * TILE
    flags = [slot_flag(count, ocean, slot) for slot in range(shape.slots)]
    top = HALF * shape.pitch
    for part in range(shape.parts):
        for row in range(TILE):
            base = (row + HALF) * shape.pitch
            for slot in range(shape.slots):
                cells = fields[pl.ds(slot * per_slot + row * TILE, TILE), shape.lanes(part)]
                band[part, pl.ds(base + LEFT + slot * TILE, TILE), :] = cells.astype(F32) * flags[slot]
        for col in range(HALF):
            rows = pl.ds(col * TILE, TILE)
            one = first[rows, shape.lanes(part)].astype(F32)
            two = second[rows, shape.lanes(part)].astype(F32)
            west = jnp.where(even, two, one)
            east = jnp.where(even, one, two)
            band[part, pl.ds(top + LEFT - HALF + col, TILE, stride=shape.pitch), :] = west
            band[part, pl.ds(top + LEFT + used + col, TILE, stride=shape.pitch), :] = east
    for k in range(HALF):
        base = (HALF + TILE - 1 - k) * shape.pitch
        east = pl.multiple_of(base + LEFT + used, LEFT)
        for part in range(shape.parts):
            ends = jnp.concatenate([band[part, pl.ds(base, LEFT), :], band[part, pl.ds(east, LEFT), :]])
            rims[pl.ds(k * 2 * LEFT, 2 * LEFT), shape.lanes(part)] = ends.astype(BF16)


def put_fold(shape, used, fold, rims, parts, padded, first_row, work):
    blank = jnp.zeros((LEFT, LANES), F32)
    for at, part in enumerate(parts):
        work[at] = rims[:, shape.lanes(part)].astype(F32)
        for k in range(HALF):
            base = (first_row + k) * shape.pitch
            padded[at, pl.ds(base, LEFT), :] = blank
            padded[at, pl.ds(base + LEFT + shape.columns, LEFT), :] = blank
            cells = fold[pl.ds(k * shape.columns, shape.columns), shape.lanes(part)]
            padded[at, pl.ds(base + LEFT, shape.columns), :] = cells.astype(F32)
            for col in range(HALF):
                west = work[at, pl.ds(k * 2 * LEFT + LEFT - 1 - col, 1), :]
                east = work[at, pl.ds(k * 2 * LEFT + LEFT + col, 1), :]
                padded[at, pl.ds(base + LEFT - 1 - col, 1), :] = east
                padded[at, pl.ds(base + LEFT + used + col, 1), :] = west


def spread_taps(shape, kernel, parts, taps):
    for above in range(KSIZE):
        rows = kernel[above].astype(F32)
        for at, part in enumerate(parts):
            for shift in range(KSIZE):
                row = rows[shift : shift + 1, shape.lanes(part)]
                taps[at, above * KSIZE + shift] = jnp.broadcast_to(row, (8, LANES))


def convolve(shape, rows, padded, taps, convolved):
    run = shape.columns // 8
    pair = 2
    origin = LEFT - HALF

    def two_rows(step, carry):
        row = step * pair
        for part in range(shape.parts):
            sums = [[None] * run for _ in range(pair)]
            for above in range(KSIZE + pair - 1):
                base = (row + above) * shape.pitch + origin
                loaded = [
                    padded[part, pl.ds(base + at, 8, stride=run), :]
                    for at in range(run + KSIZE - 1)
                ]
                for which in range(pair):
                    tap_row = above - which
                    if not 0 <= tap_row < KSIZE:
                        continue
                    for shift in range(KSIZE):
                        weight = taps[part, tap_row * KSIZE + shift]
                        for at in range(run):
                            term = weight * loaded[at + shift]
                            old = sums[which][at]
                            sums[which][at] = term if old is None else old + term
            for which in range(pair):
                for at in range(run):
                    start = (row + which) * shape.columns + at
                    convolved[part, pl.ds(start, 8, stride=run), :] = sums[which][at]
        return carry

    lax.fori_loop(0, rows // pair, two_rows, 0)


def normalise(shape, rows, first_row, convolved, gain, normed, yhat, inverse):
    def one_row(row, carry):
        for slot in range(shape.slots):
            start = pl.multiple_of(row * shape.columns + slot * TILE, TILE)
            at = slot * TILE * TILE + (first_row + row) * TILE
            out = pl.ds(pl.multiple_of(at, TILE), TILE)
            parts = [convolved[part, pl.ds(start, TILE), :] for part in range(shape.parts)]
            mean = jnp.sum(sum(parts), axis=-1, keepdims=True) * (1.0 / shape.channels)
            parts = [value - mean for value in parts]
            square = jnp.sum(sum(value * value for value in parts), axis=-1, keepdims=True)
            scale = lax.rsqrt(square * (1.0 / shape.channels) + EPS)
            inverse[out, :] = jnp.broadcast_to(scale, (TILE, LANES))
            for part in range(shape.parts):
                value = parts[part] * scale
                yhat[out, shape.lanes(part)] = value
                normed[out, shape.lanes(part)] = (value * gain[:, shape.lanes(part)]).astype(BF16)
        return carry

    lax.fori_loop(0, rows, one_row, 0, unroll=4)


def early_kernel(
    shape, count_hbm, ocean_hbm, kernel, gain, w_out, scale, tangent, band,
    normed, yhat, inverse, dproj_t, dact, live,
    count, ocean, taps, convolved, dproj, sems,
):
    fetch = Fetch(sems, (count_hbm, count), (ocean_hbm, ocean))
    spread_taps(shape, kernel, range(shape.parts), taps)
    convolve(shape, shape.early, band, taps, convolved)
    normalise(shape, shape.early, 0, convolved, gain, normed, yhat, inverse)
    fetch.wait(0, 1)
    per_slot = TILE * TILE
    for slot in range(shape.slots):
        rows = pl.ds(slot * per_slot, per_slot)
        flag = slot_flag(count, ocean, slot)
        live[slot] = jnp.full((8, shape.channels), flag, F32)
        scaled = (tangent[rows, :].astype(F32) * (scale[...] * flag)).astype(BF16)
        dproj[rows, :] = scaled
        dproj_t[:, slot * per_slot : (slot + 1) * per_slot] = scaled.T
        for h in range(shape.hidden // shape.channels):
            cols = slice(h * shape.channels, (h + 1) * shape.channels)
            dact[rows, cols] = dot(dproj[rows, :], w_out[cols, :], 1, 1)


def late_kernel(
    shape, count_hbm, kernel, gain, w_in, band, fold, rims, normed_in, yhat_in, inverse_in, dproj_t, dact,
    keep, give, activated, dpreact, yhat, inverse, padded,
    count, taps, convolved, normed, normed_t, work, pre, sems,
):
    fetch = Fetch(sems, (count_hbm, count))
    late = TILE - shape.early
    kept = late + HALF
    for part in range(shape.parts):
        rows = pl.ds(shape.early * shape.pitch, kept * shape.pitch)
        padded[part, pl.ds(0, kept * shape.pitch), :] = band[part, rows, :]
    done = shape.early * TILE
    for slot in range(shape.slots):
        rows = pl.ds(slot * TILE * TILE, done)
        normed[rows, :] = normed_in[rows, :]
        yhat[rows, :] = yhat_in[rows, :]
        inverse[rows, :] = inverse_in[rows, :]
    spread_taps(shape, kernel, range(shape.parts), taps)
    fetch.wait(0)
    put_fold(shape, count[0] * TILE, fold, rims, range(shape.parts), padded, kept, work)
    convolve(shape, late, padded, taps, convolved)
    normalise(shape, late, shape.early, convolved, gain, normed, yhat, inverse)
    per_slot = TILE * TILE
    for slot in range(shape.slots):
        normed_t[:, slot * per_slot : (slot + 1) * per_slot] = normed[pl.ds(slot * per_slot, per_slot), :].T
    keeps_in = lax.axis_index("core") == 0
    block = shape.channels
    blocks = shape.hidden // block

    def span(h):
        return slice(h * block, (h + 1) * block)

    def expand(step):
        h, slot = divmod(step, shape.slots)
        pre[step % 3] = dot(normed[pl.ds(slot * per_slot, per_slot), :], w_in[:, span(h)], 1, 0)

    def activate(step):
        h, slot = divmod(step, shape.slots)
        rows, cols = pl.ds(slot * per_slot, per_slot), span(h)
        value = pre[step % 3]
        square = value * value
        gate = 0.5 + 0.5 * jnp.tanh(value * (GELU_C + (GELU_C * GELU_A) * square))
        activated[rows, cols] = (value * gate).astype(BF16)
        slope = value * (2.0 * GELU_C + (6.0 * GELU_C * GELU_A) * square)
        grown = gate + slope * (gate - gate * gate)
        dpreact[rows, cols] = (dact[rows, cols] * grown).astype(BF16)

    def reduce_rows(h):
        of_in = dot(normed_t[...], dpreact[:, span(h)], 1, 0)
        of_out = dot(dproj_t[...], activated[:, span(h)], 1, 0)
        keep[span(h), :] = jnp.where(keeps_in, of_in, of_out)
        give[span(h), :] = jnp.where(keeps_in, of_out, of_in).astype(BF16)

    steps = blocks * shape.slots
    expand(0)
    for step in range(steps):
        if step + 1 < steps:
            expand(step + 1)
        activate(step)
        h, slot = divmod(step, shape.slots)
        if slot == 0 and h:
            reduce_rows(h - 1)
    reduce_rows(blocks - 1)


def fold_sum(value):
    return jnp.sum(value.reshape(-1, 8, value.shape[-1]), axis=0)


def norm_grad_kernel(
    shape, w_in, w_out, gain, dpreact, yhat, inverse, activated, tangent, live,
    conv_grad, projected, gain_part, scale_part,
):
    chunk = TILE * TILE
    of_gain = jnp.zeros((8, shape.channels), F32)
    of_scale = jnp.zeros((8, shape.channels), F32)
    for slot in range(shape.slots):
        rows = pl.ds(slot * chunk, chunk)
        dnormed = dot(dpreact[rows, :], w_in[...], 1, 1)
        unit = yhat[rows, :]
        of_gain += fold_sum(dnormed * unit)
        dhat = dnormed * gain[...]
        mean = jnp.sum(dhat, axis=-1, keepdims=True) * (1.0 / shape.channels)
        along = jnp.sum(dhat * unit, axis=-1, keepdims=True) * (1.0 / shape.channels)
        scale = jnp.concatenate([inverse[rows, :]] * shape.parts, axis=1)
        conv_grad[rows, :] = (scale * (dhat - mean - unit * along)).astype(BF16)
        value = dot(activated[rows, :], w_out[...], 1, 0)
        projected[rows, :] = value
        of_scale += live[slot] * fold_sum(tangent[rows, :].astype(F32) * value)
    gain_part[...] = of_gain
    scale_part[...] = of_scale


def state_kernel(shape, fields, scale, projected, live, state, done):
    done[...] = jnp.zeros_like(done)
    chunk = TILE * TILE
    for slot in range(shape.slots):
        rows = pl.ds(slot * chunk, chunk)
        kept = fields[rows, :].astype(F32) + scale[...] * projected[rows, :]
        state[rows, :] = (live[slot, 0:1, :] * kept).astype(BF16)


def place_grad(shape, conv_grad, parts, spaced):
    blank = jnp.zeros((LEFT, LANES), F32)
    for at, part in enumerate(parts):
        for row in range(TILE):
            base = row * shape.pitch
            spaced[at, pl.ds(base, LEFT), :] = blank
            spaced[at, pl.ds(base + LEFT + shape.columns, LEFT), :] = blank
            for slot in range(shape.slots):
                cells = conv_grad[pl.ds(slot * TILE * TILE + row * TILE, TILE), shape.lanes(part)]
                spaced[at, pl.ds(base + LEFT + slot * TILE, TILE), :] = cells.astype(F32)


def taps_kernel(shape, part, band, top, conv_grad, small, padded, spaced):
    place_grad(shape, conv_grad, [part], spaced)
    kept = shape.early * shape.pitch
    padded[0, pl.ds(0, kept), :] = band[part, pl.ds(0, kept), :]
    padded[0, pl.ds(kept, top.shape[1]), :] = top[part]
    run = shape.columns // 8
    origin = LEFT - HALF
    for above in range(KSIZE):

        def one_row(row, sums, above=above):
            base = (row + above) * shape.pitch + origin
            loaded = [padded[0, pl.ds(base + at, 8, stride=run), :] for at in range(run + KSIZE - 1)]
            start = row * shape.pitch + LEFT
            grads = [spaced[0, pl.ds(start + at, 8, stride=run), :] for at in range(run)]
            sums = list(sums)
            for shift in range(KSIZE):
                for at in range(run):
                    sums[shift] = sums[shift] + grads[at] * loaded[at + shift]
            return tuple(sums)

        blank = tuple(jnp.zeros((8, LANES), F32) for _ in range(KSIZE))
        sums = lax.fori_loop(0, TILE, one_row, blank, unroll=2)
        for shift in range(KSIZE):
            small[pl.ds(above * KSIZE + shift, 1), :] = jnp.sum(sums[shift], axis=0, keepdims=True)


def back_kernel(shape, part, count_hbm, kernel, conv_grad, *refs):
    before = refs[:part]
    turns = part == shape.parts - 1
    core_grad, *refs = refs[part:]
    if turns:
        fold, *refs = refs
    count, spaced, taps, sems = refs
    fetch = Fetch(sems, (count_hbm, count))
    place_grad(shape, conv_grad, [part], spaced)
    blank = jnp.zeros((LEFT, LANES), F32)
    for row in range(TILE + HALF):
        core_grad[pl.ds(row * shape.pitch, LEFT), :] = blank
        core_grad[pl.ds((row + 1) * shape.pitch - LEFT, LEFT), :] = blank
    spread_taps(shape, kernel, [part], taps)
    run = -(-(shape.columns + 2 * HALF) // 8)

    def one_row(row, tap_rows):
        sums = [None] * run
        for above in tap_rows:
            base = (row - above) * shape.pitch + LEFT
            loaded = [
                spaced[0, pl.ds(base + at - KSIZE + 1, 8, stride=run), :] for at in range(run + KSIZE - 1)
            ]
            for shift in range(KSIZE):
                weight = taps[0, above * KSIZE + shift]
                for at in range(run):
                    term = weight * loaded[at - shift + KSIZE - 1]
                    sums[at] = term if sums[at] is None else sums[at] + term
        start = (row - HALF) * shape.pitch + LEFT - HALF
        for at in range(run):
            core_grad[pl.ds(start + at, 8, stride=run), :] = sums[at]

    inner = (KSIZE - 1, TILE - 1)
    for row in range(HALF, TILE + 2 * HALF):
        if not inner[0] <= row <= inner[1]:
            low = max(0, row - TILE + 1)
            one_row(row, range(low, min(KSIZE - 1, row) + 1))

    def inner_row(step, carry):
        one_row(step, range(KSIZE))
        return carry

    lax.fori_loop(inner[0], inner[1] + 1, inner_row, 0)
    fetch.wait(0)
    if turns:
        flip = flip_matrix(shape.pitch, count[0] * TILE + 2 * LEFT - 1)
        for k in range(HALF):
            at = pl.ds((TILE + k) * shape.pitch, shape.pitch)
            cells = jnp.concatenate([one[at, :] for one in (*before, core_grad)], axis=1)
            turned = dot(flip, cells.astype(BF16), 1, 0)
            fold[pl.ds(k * shape.pitch, shape.pitch), :] = turned.astype(BF16)


def rims_kernel(shape, count_hbm, fold, *refs):
    core_grad = refs[: shape.parts]
    folded, first, second, count, sems = refs[shape.parts :]
    fetch = Fetch(sems, (count_hbm, count))
    for part in range(shape.parts):
        folded[part] = core_grad[part][pl.ds(0, TILE * shape.pitch), :]
        for k in range(HALF):
            rows = pl.ds((TILE - 1 - k) * shape.pitch, shape.pitch)
            returned = fold[pl.ds(k * shape.pitch, shape.pitch), shape.lanes(part)]
            folded[part, rows, :] += returned.astype(F32)
    fetch.wait(0)
    west = edge_planes(shape, folded, LEFT - HALF, shape.pitch)
    east = edge_planes(shape, folded, LEFT + count[0] * TILE, shape.pitch)
    send_edges(shape, west, east, first, second)


def final_kernel(
    shape, count_hbm, ocean_hbm, tangent, folded, first, second,
    grad_fields, done,
    count, ocean, work, sems,
):
    fetch = Fetch(sems, (count_hbm, count), (ocean_hbm, ocean))
    even = is_even()
    done[...] = jnp.zeros_like(done)
    work[...] = folded[...]
    fetch.wait(0, 1)
    used = count[0] * TILE
    for part in range(shape.parts):
        for col in range(HALF):
            planes = pl.ds(col * TILE, TILE)
            one = first[planes, shape.lanes(part)].astype(F32)
            two = second[planes, shape.lanes(part)].astype(F32)
            to_tail = jnp.where(even, one, two)
            to_head = jnp.where(even, two, one)
            head = pl.ds(LEFT + col, TILE, stride=shape.pitch)
            work[part, head, :] = work[part, head, :] + to_head
            tail = pl.ds(LEFT + used - HALF + col, TILE, stride=shape.pitch)
            work[part, tail, :] = work[part, tail, :] + to_tail
        for slot in range(shape.slots):
            flag = slot_flag(count, ocean, slot)
            for row in range(TILE):
                rows = pl.ds(slot * TILE * TILE + row * TILE, TILE)
                cells = work[part, pl.ds(row * shape.pitch + LEFT + slot * TILE, TILE), :]
                total = tangent[rows, shape.lanes(part)].astype(F32) + cells
                grad_fields[rows, shape.lanes(part)] = (flag * total).astype(BF16)


def unpack_kernel(norm, own, came, w_in, w_out, kernel_sum, gain_sum, scale_sum):
    is_first = lax.axis_index("core") == 0
    hidden, channels = w_out.shape
    for h in range(hidden // channels):
        block = slice(h * channels, (h + 1) * channels)
        mine = own[block, :].astype(F32) * norm
        theirs = came[block, :].astype(F32) * norm
        w_in[:, block] = jnp.where(is_first, mine, theirs)
        w_out[block, :] = jnp.where(is_first, theirs, mine).T
    extra = (own.shape[0] - hidden) // 2
    high, low = pl.ds(hidden, extra), pl.ds(hidden + extra, extra)
    mine = (own[high, :].astype(F32) + own[low, :].astype(F32)) * norm
    theirs = (came[high, :].astype(F32) + came[low, :].astype(F32)) * norm
    small = jnp.concatenate([jnp.where(is_first, mine, theirs), jnp.where(is_first, theirs, mine)])
    for above in range(KSIZE):
        kernel_sum[above] = small[above * KSIZE : (above + 1) * KSIZE, :]
    gain_sum[...] = small[KSIZE * KSIZE : KSIZE * KSIZE + 1, :]
    scale_sum[...] = small[KSIZE * KSIZE + 1 : KSIZE * KSIZE + 2, :]


def pairs_of(kind):
    count = lax.axis_size(TILES)
    half = count // 2
    place = [rank if rank < half else count - 1 + half - rank for rank in range(count)]
    partner = {
        "first": lambda rank: rank ^ 1,
        "second": lambda rank: ((rank + 1) ^ 1) - 1,
        "fold": lambda rank: count - 1 - rank,
    }[kind]
    return [(place[rank], place[partner(rank) % count]) for rank in range(count)]


def swap(block, kind):
    return lax.ppermute(block, TILES, pairs_of(kind))


def core_swap(block):
    return lax.ppermute(block, "core", [(0, 1), (1, 0)])


def stages():
    chip_bits = lax.axis_size(CHIPS).bit_length() - 1
    rest = list(range(2, chip_bits))
    return list(zip([0, -1, 1] + rest, [1, 0, -1] + rest))


def bit_swap(block, stage):
    chips, cores, samples = (lax.axis_size(axis) for axis in (CHIPS, "core", "dp"))
    pairs = []
    for chip in range(chips):
        for core in range(cores):
            for sample in range(samples):
                bit = stage[core]
                to = (chip, sample ^ 1) if bit < 0 else (chip ^ (1 << bit), sample)
                pairs.append(
                    ((chip * cores + core) * samples + sample, (to[0] * cores + core) * samples + to[1])
                )
    return lax.ppermute(block, TILES + ("dp",), pairs)


def bit_here(stage):
    bits = [
        lax.axis_index("dp") if bit < 0 else chip_index() >> bit & 1 for bit in stage
    ]
    return jnp.where(lax.axis_index("core") == 0, bits[0], bits[1])


def half_rows(bit, rows):
    return pl.ds(pl.multiple_of(bit * rows, rows), rows)


def place_of(order, at):
    near, sample = divmod(at, lax.axis_size("dp"))
    places = []
    for core in range(2):
        place = 0
        for stage in order:
            place = 2 * place + (sample if stage[core] < 0 else near >> stage[core] & 1)
        places.append(place)
    return jnp.where(lax.axis_index("core") == 0, places[0], places[1])


def join_kernel(order, keep, came, pieces):
    rows = pieces.shape[1]
    for at in range(pieces.shape[0]):
        share = half_rows(place_of(order, at), rows)
        pieces[at] = (keep[share, :] + came[share, :].astype(F32)).astype(BF16)


def pack_kernel(gain_part, scale_part, *refs):
    taps, (keep, send, work) = refs[:-3], refs[-3:]
    half = keep.shape[0]
    work[...] = jnp.zeros_like(work)
    for part, ref in enumerate(taps):
        work[pl.ds(0, ref.shape[0]), part * LANES : (part + 1) * LANES] = ref[...]
    work[pl.ds(KSIZE * KSIZE, 1), :] = jnp.sum(gain_part[...], axis=0, keepdims=True)
    work[pl.ds(KSIZE * KSIZE + 1, 1), :] = jnp.sum(scale_part[...], axis=0, keepdims=True)
    core = lax.axis_index("core")
    keep[...] = work[half_rows(core, half), :]
    value = work[half_rows(1 - core, half), :]
    high = value.astype(BF16)
    send[pl.ds(0, half), :] = high
    send[pl.ds(half, half), :] = (value - high.astype(F32)).astype(BF16)


def turn_kernel(came, keep, extra, payload):
    rows, half = came.shape[1], keep.shape[0]
    share = sum(came[at].astype(F32) for at in range(came.shape[0]))
    payload[pl.ds(0, rows), :] = share.astype(BF16)
    small = keep[...] + (extra[pl.ds(0, half), :].astype(F32) + extra[pl.ds(half, half), :].astype(F32))
    payload[pl.ds(rows, half), :] = small.astype(BF16)


def add_kernel(own, came, payload):
    total = (own[...].astype(F32) + came[...].astype(F32)).astype(BF16)
    if payload.shape == total.shape:
        payload[...] = total
    else:
        for at in range(payload.shape[0]):
            payload[at] = total


def gather_kernel(order, extra, came, payload):
    rows = came.shape[1] - extra
    total = jnp.zeros((extra, came.shape[2]), F32)
    for at in range(came.shape[0]):
        payload[half_rows(place_of(order, at), rows), :] = came[at, pl.ds(0, rows), :]
        total += came[at, pl.ds(rows, extra), :].astype(F32)
    high = total.astype(BF16)
    full = rows * came.shape[0]
    payload[pl.ds(full, extra), :] = high
    payload[pl.ds(full + extra, extra), :] = (total - high.astype(F32)).astype(BF16)


def double_kernel(stage, extra, own, came, payload):
    rows = own.shape[0] - extra
    bit = bit_here(stage)
    payload[half_rows(bit, rows), :] = own[pl.ds(0, rows), :]
    payload[half_rows(1 - bit, rows), :] = came[pl.ds(0, rows), :]
    total = own[pl.ds(rows, extra), :].astype(F32) + came[pl.ds(rows, extra), :].astype(F32)
    high = total.astype(BF16)
    payload[pl.ds(2 * rows, extra), :] = high
    if payload.shape[0] > 2 * rows + extra:
        payload[pl.ds(2 * rows + extra, extra), :] = (total - high.astype(F32)).astype(BF16)


def halved(mine, order):
    for stage in order:
        bit = bit_here(stage)
        halves = mine.reshape(2, -1, mine.shape[-1])
        send = lax.dynamic_index_in_dim(halves, 1 - bit, 0, keepdims=False).astype(BF16)
        mine = lax.dynamic_index_in_dim(halves, bit, 0, keepdims=False) + bit_swap(send, stage).astype(F32)
    return mine


def call(kernel, outs, scratch, hbm, vmem, copies=0, micros=1.0, after=(), limit=20):
    in_specs = [pl.BlockSpec(memory_space=pl.ANY)] * len(hbm)
    in_specs += [pl.BlockSpec(memory_space=pltpu.VMEM)] * len(vmem)
    in_specs += [pl.BlockSpec(memory_space=pl.ANY)] * len(after)
    shapes = [pltpu.SMEM(*one) if one[1] == jnp.int32 else pltpu.VMEM(*one) for one in scratch]
    if copies:
        shapes.append(pltpu.SemaphoreType.DMA((copies,)))
    taken = len(hbm) + len(vmem)

    def body(*refs):
        kernel(*refs[:taken], *refs[taken + len(after) :])

    return pl.pallas_call(
        body,
        out_shape=[jax.ShapeDtypeStruct(*out) for out in outs],
        in_specs=in_specs,
        out_specs=[pl.BlockSpec(memory_space=pltpu.VMEM)] * len(outs),
        scratch_shapes=shapes,
        cost_estimate=pl.CostEstimate(flops=int(micros * 1e9), bytes_accessed=0, transcendentals=0),
        compiler_params=pltpu.CompilerParams(vmem_limit_bytes=limit * 1024 * 1024),
    )(*hbm, *vmem, *after)


def shards(fields, grad_out, block_count, ocean, kernel, ln_gain, w_in, w_out, layer_scale):
    samples, slots, tile_rows, tile_cols, channels = fields.shape
    hidden = w_in.shape[1]
    shape = Shape(slots, channels, hidden)
    cells, parts, pitch = shape.cells, shape.parts, shape.pitch
    grid = fields.shape
    fields = fields.reshape(cells, channels)
    tangent = grad_out.reshape(cells, channels)
    taps_in = kernel
    gain = ln_gain.reshape(1, channels)
    scale = layer_scale.reshape(1, channels)

    def bind(body):
        return functools.partial(body, shape)

    def strip(rows):
        return ((parts, rows * pitch, LANES), F32)

    edge = ((shape.edge_rows, channels), BF16)
    turned = ((HALF * pitch, channels), BF16)
    whole = ((cells, channels), BF16)
    whole_f = ((cells, channels), F32)
    wide = ((cells, hidden), BF16)
    narrow = ((cells, LANES), F32)
    row = ((1, channels), F32)
    eight = ((8, channels), F32)
    taps = ((parts, KSIZE * KSIZE, 8, LANES), F32)
    count_s = (block_count.shape, jnp.int32)
    ocean_s = (ocean.shape, jnp.int32)
    flat = ((channels, cells), BF16)
    ends = ((HALF * 2 * LEFT, channels), BF16)
    ends_f = ((parts, HALF * 2 * LEFT, LANES), F32)
    late = TILE - shape.early

    first, second = call(
        bind(prep_kernel), [edge, edge], [count_s, ((parts, cells, LANES), F32)],
        [block_count], [fields], 1, 1.0,
    )
    (fold,) = call(
        bind(top_kernel), [((HALF * shape.columns, channels), BF16)], [count_s, ocean_s],
        [block_count, ocean], [fields], 2, 0.5, after=[first],
    )
    first, second = swap(first, "first"), swap(second, "second")
    band, rims = call(
        bind(band_kernel), [strip(TILE + HALF), ends], [count_s, ocean_s],
        [block_count, ocean], [fields, first, second], 2, 1.0, after=[fold],
    )
    fold, rims = swap(fold, "fold"), swap(rims, "fold")
    normed, yhat, inverse, dproj_t, dact, live = call(
        bind(early_kernel), [whole, whole_f, narrow, flat, ((cells, hidden), F32), ((slots, 8, channels), F32)],
        [count_s, ocean_s, taps, ((parts, shape.early * shape.columns, LANES), F32), whole],
        [block_count, ocean], [taps_in, gain, w_out, scale, tangent, band], 2, 5.0,
    )
    keep, give, activated, dpreact, yhat, inverse, top = call(
        bind(late_kernel),
        [((hidden, channels), F32), ((hidden, channels), BF16), wide, wide, whole_f, narrow, strip(late + 2 * HALF)],
        [
            count_s, taps, ((parts, late * shape.columns, LANES), F32), whole, flat, ends_f,
            ((3, TILE * TILE, channels), F32),
        ],
        [block_count],
        [taps_in, gain, w_in, band, fold, rims, normed, yhat, inverse, dproj_t, dact], 1, 5.0,
    )

    order = stages()
    block = lax.axis_size("near") * lax.axis_size("dp")
    inner = block.bit_length() - 1
    rows = hidden // block

    def taps_part(part, after):
        (small,) = call(
            functools.partial(taps_kernel, shape, part), [((small_rows, LANES), F32)],
            [((1, (TILE + 2 * HALF) * pitch, LANES), F32), ((1, TILE * pitch, LANES), F32)],
            [], [band, top, conv_grad], 0, 1.8, after=after,
        )
        return small

    def back_part(part, before, after):
        outs = [(((TILE + HALF) * pitch, LANES), F32)] + [turned] * (part == parts - 1)
        return call(
            functools.partial(back_kernel, shape, part), outs,
            [count_s, ((1, TILE * pitch, LANES), F32), ((1, KSIZE * KSIZE, 8, LANES), F32)],
            [block_count], [taps_in, conv_grad, *before], 1, 2.0, after=after,
        )

    small_rows = -(-(KSIZE * KSIZE + 2) // 32) * 32
    came = core_swap(give)
    conv_grad, projected, gain_part, scale_part = call(
        bind(norm_grad_kernel), [whole, whole_f, eight, eight], [], [],
        [w_in, w_out, gain, dpreact, yhat, inverse, activated, tangent, live], 0, 1.3,
    )
    (send,) = call(
        functools.partial(join_kernel, order[:inner]), [((block, rows, channels), BF16)],
        [], [], [keep, came], after=[gain_part], micros=0.3,
    )
    came = lax.all_to_all(send, ("near", "dp"), 0, 0, tiled=True)
    taps_parts = [taps_part(part, [send]) for part in range(parts)]
    small_rows //= 2
    small, extra = call(
        pack_kernel, [((small_rows, channels), F32), ((2 * small_rows, channels), BF16)],
        [((2 * small_rows, channels), F32)], [], [gain_part, scale_part, *taps_parts], micros=0.3,
    )
    extra = core_swap(extra)
    if len(order) == inner + 1:
        (payload,) = call(
            turn_kernel, [((rows + small_rows, channels), BF16)], [], [], [came, small, extra], micros=0.3,
        )
    else:
        share = halved(jnp.sum(came.astype(F32), axis=0), order[inner:-1])
        rows = share.shape[0]
        small = small + (extra[:small_rows].astype(F32) + extra[small_rows:].astype(F32))
        payload = jnp.concatenate([share, small]).astype(BF16)
    came = bit_swap(payload, order[-1])
    core_grad = []
    after = [payload]
    for part in range(parts):
        one, *fold_back = back_part(part, core_grad, after)
        core_grad += [one]
        after = [one]
    fold_back = swap(fold_back[0], "fold")
    copied = (block, *payload.shape)
    outer = range(inner, len(order) - 1)
    (payload,) = call(
        add_kernel, [(payload.shape if outer else copied, BF16)], [], [], [payload, came], after=after, micros=0.3,
    )
    for at in reversed(outer):
        came = bit_swap(payload, order[at])
        if rows % 16 == 0:
            (payload,) = call(
                functools.partial(double_kernel, order[at], small_rows),
                [((2 * rows + small_rows, channels), BF16)], [], [], [payload, came], micros=0.3,
            )
        else:
            is_low = bit_here(order[at]) == 0
            low, high = payload[:rows], came[:rows]
            both = payload[rows:].astype(F32) + came[rows:].astype(F32)
            joined = [jnp.where(is_low, low, high), jnp.where(is_low, high, low), both.astype(BF16)]
            payload = jnp.concatenate(joined)
        rows *= 2
    if outer:
        payload = jnp.broadcast_to(payload, (block, *payload.shape))
    came = lax.all_to_all(payload, ("near", "dp"), 0, 0, tiled=True)
    folded, first, second = call(
        bind(rims_kernel), [strip(TILE), edge, edge], [count_s], [block_count], [fold_back, *core_grad], 1, 1.0,
        after=[payload],
    )
    first, second = swap(first, "first"), swap(second, "second")
    state, done_too = call(
        bind(state_kernel), [whole, ((8, LANES), F32)], [], [], [fields, scale, projected, live], 0, 1.0,
        after=[folded],
    )
    grad_fields, done = call(
        bind(final_kernel), [whole, ((8, LANES), F32)], [count_s, ocean_s, strip(TILE)],
        [block_count, ocean], [tangent, folded, first, second], 2, 1.5, after=[done_too],
    )
    (payload,) = call(
        functools.partial(gather_kernel, order[:inner], small_rows),
        [((hidden + 2 * small_rows, channels), BF16)], [], [], [came], after=[done], micros=0.3,
    )
    came = core_swap(payload)
    total = samples * lax.axis_size("dp") * slots * lax.axis_size(TILES) * tile_rows * tile_cols
    norm = total ** (-0.5)
    sums = [((channels, hidden), F32), ((hidden, channels), F32)]
    w_in_sum, w_out_sum, kernel_sum, gain_sum, scale_sum = call(
        functools.partial(unpack_kernel, norm), sums + [(kernel.shape, F32), row, row], [],
        [], [payload, came], 0, 1.5,
    )
    return (
        state.reshape(grid),
        grad_fields.reshape(grid),
        kernel_sum,
        gain_sum.reshape(ln_gain.shape),
        w_in_sum,
        w_out_sum,
        scale_sum.reshape(layer_scale.shape),
    )


def solution(mesh):
    cores = Mesh(mesh.devices.reshape(-1, 4, 2, mesh.devices.shape[1]), TILES + ("dp",))
    banded = P("dp", TILES, None, None, None)
    placed = (banded, banded, P(TILES), P(TILES), P(), P(), P(), P(), P())
    return jax.shard_map(
        shards,
        mesh=cores,
        in_specs=placed,
        out_specs=(banded, banded, P(), P(), P(), P(), P()),
        check_vma=False,
    )
```

```python
import functools

import jax
import jax.numpy as jnp
from jax import lax
from jax.experimental import pallas as pl
from jax.experimental.pallas import tpu as pltpu
from jax.sharding import Mesh, PartitionSpec as P

KSIZE = 7
HALF = KSIZE // 2
TILE = 16
EPS = 1e-06
CHIPS = ("far", "near")
TILES = CHIPS + ("core",)
F32 = jnp.float32
BF16 = jnp.bfloat16
LANES = 128
LEFT = 8
GELU_C = 0.7978845608028654
GELU_A = 0.044715


def dot(lhs, rhs, lhs_dim, rhs_dim):
    return lax.dot_general(
        lhs, rhs, (((lhs_dim,), (rhs_dim,)), ((), ())), preferred_element_type=F32
    )


def chip_index():
    return lax.axis_index("far") * lax.axis_size("near") + lax.axis_index("near")


def cycle_rank():
    count = lax.axis_size(TILES)
    here = chip_index() * lax.axis_size("core") + lax.axis_index("core")
    return jnp.where(here < count // 2, here, count - 1 + count // 2 - here)


def is_even():
    return lax.rem(cycle_rank(), 2) == 0


class Fetch:
    def __init__(self, sems, *pairs):
        self.copies = [
            pltpu.make_async_copy(source, target, sems.at[at]) for at, (source, target) in enumerate(pairs)
        ]
        for copy in self.copies:
            copy.start()

    def wait(self, *which):
        for at in which:
            self.copies[at].wait()


class Shape:
    def __init__(self, slots, channels, hidden):
        self.slots = slots
        self.channels = channels
        self.hidden = hidden
        self.parts = channels // LANES
        self.columns = slots * TILE
        self.pitch = self.columns + 2 * LEFT
        self.cells = slots * TILE * TILE
        self.edge_rows = HALF * TILE
        self.early = 12

    def lanes(self, part):
        return slice(part * LANES, (part + 1) * LANES)


def edge_planes(shape, source, start, stride):
    return [
        jnp.concatenate(
            [source[part, pl.ds(start + col, TILE, stride=stride), :] for part in range(shape.parts)], axis=1
        )
        for col in range(HALF)
    ]


def send_edges(shape, left, right, first, second):
    even = is_even()
    for col in range(HALF):
        rows = pl.ds(col * TILE, TILE)
        first[rows, :] = jnp.where(even, right[col], left[col]).astype(BF16)
        second[rows, :] = jnp.where(even, left[col], right[col]).astype(BF16)


def flip_matrix(size, last):
    to = lax.broadcasted_iota(jnp.int32, (size, size), 0)
    frm = lax.broadcasted_iota(jnp.int32, (size, size), 1)
    return jnp.where(to + frm == last, 1.0, 0.0).astype(BF16)


def owned_of(info):
    return jnp.max(info[...]).astype(jnp.int32)


def prep_kernel(shape, count_hbm, fields, first, second, info, count, work, sems):
    fetch = Fetch(sems, (count_hbm, count))
    for part in range(shape.parts):
        work[part] = fields[:, shape.lanes(part)].astype(F32)
    left = edge_planes(shape, work, 0, TILE)
    fetch.wait(0)
    right = edge_planes(shape, work, (count[0] - 1) * TILE * TILE + TILE - HALF, TILE)
    send_edges(shape, left, right, first, second)
    info[...] = jnp.full(info.shape, count[0].astype(F32), F32)


def top_kernel(shape, info, ocean, fields, fold, live):
    column = lax.broadcasted_iota(jnp.int32, ocean.shape, 1)
    wet = jnp.where(ocean[...] > 0, 1.0, 0.0).astype(F32)
    for slot in range(shape.slots):
        one = jnp.sum(jnp.where(column == slot, wet, 0.0), axis=1, keepdims=True)
        one = jnp.where(info[0:1, 0:1] > slot + 0.5, one, 0.0)
        live[slot] = jnp.broadcast_to(one, live.shape[1:])
    flip = flip_matrix(shape.columns, owned_of(info) * TILE - 1)
    for k in range(HALF):
        cells = jnp.concatenate(
            [
                fields[pl.ds(slot * TILE * TILE + (TILE - 1 - k) * TILE, TILE), :].astype(F32)
                * live[slot, 0:1, :]
                for slot in range(shape.slots)
            ]
        )
        turned = dot(flip, cells.astype(BF16), 1, 0)
        fold[pl.ds(k * shape.columns, shape.columns), :] = turned.astype(BF16)


def band_kernel(shape, info, live, fields, first, second, band, rims):
    used = owned_of(info) * TILE
    even = is_even()
    blank = jnp.zeros((LEFT, LANES), F32)
    per_slot = TILE * TILE
    for part in range(shape.parts):
        band[part, pl.ds(0, HALF * shape.pitch), :] = jnp.zeros((HALF * shape.pitch, LANES), F32)
        for row in range(TILE):
            base = (row + HALF) * shape.pitch
            band[part, pl.ds(base, LEFT), :] = blank
            band[part, pl.ds(base + LEFT + shape.columns, LEFT), :] = blank
    top = HALF * shape.pitch
    for part in range(shape.parts):
        for row in range(TILE):
            base = (row + HALF) * shape.pitch
            for slot in range(shape.slots):
                cells = fields[pl.ds(slot * per_slot + row * TILE, TILE), shape.lanes(part)]
                band[part, pl.ds(base + LEFT + slot * TILE, TILE), :] = cells.astype(F32) * live[slot, 0:1, shape.lanes(part)]
        for col in range(HALF):
            rows = pl.ds(col * TILE, TILE)
            one = first[rows, shape.lanes(part)].astype(F32)
            two = second[rows, shape.lanes(part)].astype(F32)
            west = jnp.where(even, two, one)
            east = jnp.where(even, one, two)
            band[part, pl.ds(top + LEFT - HALF + col, TILE, stride=shape.pitch), :] = west
            band[part, pl.ds(top + LEFT + used + col, TILE, stride=shape.pitch), :] = east
    for k in range(HALF):
        base = (HALF + TILE - 1 - k) * shape.pitch
        east = pl.multiple_of(base + LEFT + used, LEFT)
        for part in range(shape.parts):
            ends = jnp.concatenate([band[part, pl.ds(base, LEFT), :], band[part, pl.ds(east, LEFT), :]])
            rims[pl.ds(k * 2 * LEFT, 2 * LEFT), shape.lanes(part)] = ends.astype(BF16)


def put_fold(shape, used, fold, rims, parts, padded, first_row, work):
    blank = jnp.zeros((LEFT, LANES), F32)
    for at, part in enumerate(parts):
        work[at] = rims[:, shape.lanes(part)].astype(F32)
        for k in range(HALF):
            base = (first_row + k) * shape.pitch
            padded[at, pl.ds(base, LEFT), :] = blank
            padded[at, pl.ds(base + LEFT + shape.columns, LEFT), :] = blank
            cells = fold[pl.ds(k * shape.columns, shape.columns), shape.lanes(part)]
            padded[at, pl.ds(base + LEFT, shape.columns), :] = cells.astype(F32)
            for col in range(HALF):
                west = work[at, pl.ds(k * 2 * LEFT + LEFT - 1 - col, 1), :]
                east = work[at, pl.ds(k * 2 * LEFT + LEFT + col, 1), :]
                padded[at, pl.ds(base + LEFT - 1 - col, 1), :] = east
                padded[at, pl.ds(base + LEFT + used + col, 1), :] = west


def spread_taps(shape, kernel, parts, taps):
    for above in range(KSIZE):
        rows = kernel[above].astype(F32)
        for at, part in enumerate(parts):
            for shift in range(KSIZE):
                row = rows[shift : shift + 1, shape.lanes(part)]
                taps[at, above * KSIZE + shift] = jnp.broadcast_to(row, (8, LANES))


def convolve(shape, rows, padded, taps, convolved):
    run = shape.columns // 8
    pair = 2
    origin = LEFT - HALF

    def two_rows(step, carry):
        row = step * pair
        for part in range(shape.parts):
            sums = [[None] * run for _ in range(pair)]
            for above in range(KSIZE + pair - 1):
                base = (row + above) * shape.pitch + origin
                loaded = [
                    padded[part, pl.ds(base + at, 8, stride=run), :]
                    for at in range(run + KSIZE - 1)
                ]
                for which in range(pair):
                    tap_row = above - which
                    if not 0 <= tap_row < KSIZE:
                        continue
                    for shift in range(KSIZE):
                        weight = taps[part, tap_row * KSIZE + shift]
                        for at in range(run):
                            term = weight * loaded[at + shift]
                            old = sums[which][at]
                            sums[which][at] = term if old is None else old + term
            for which in range(pair):
                for at in range(run):
                    start = (row + which) * shape.columns + at
                    convolved[part, pl.ds(start, 8, stride=run), :] = sums[which][at]
        return carry

    lax.fori_loop(0, rows // pair, two_rows, 0)


def normalise(shape, rows, first_row, convolved, gain, normed, yhat, inverse):
    def one_row(row, carry):
        for slot in range(shape.slots):
            start = pl.multiple_of(row * shape.columns + slot * TILE, TILE)
            at = slot * TILE * TILE + (first_row + row) * TILE
            out = pl.ds(pl.multiple_of(at, TILE), TILE)
            parts = [convolved[part, pl.ds(start, TILE), :] for part in range(shape.parts)]
            mean = jnp.sum(sum(parts), axis=-1, keepdims=True) * (1.0 / shape.channels)
            parts = [value - mean for value in parts]
            square = jnp.sum(sum(value * value for value in parts), axis=-1, keepdims=True)
            scale = lax.rsqrt(square * (1.0 / shape.channels) + EPS)
            inverse[out, :] = jnp.broadcast_to(scale, (TILE, LANES))
            for part in range(shape.parts):
                value = parts[part] * scale
                yhat[out, shape.lanes(part)] = value
                normed[out, shape.lanes(part)] = (value * gain[:, shape.lanes(part)]).astype(BF16)
        return carry

    lax.fori_loop(0, rows, one_row, 0, unroll=4)


def early_kernel(
    shape, live, kernel, gain, w_out, scale, tangent, band,
    normed, yhat, inverse, dproj_t, dact,
    taps, convolved, dproj,
):
    spread_taps(shape, kernel, range(shape.parts), taps)
    convolve(shape, shape.early, band, taps, convolved)
    normalise(shape, shape.early, 0, convolved, gain, normed, yhat, inverse)
    per_slot = TILE * TILE
    for slot in range(shape.slots):
        rows = pl.ds(slot * per_slot, per_slot)
        scaled = (tangent[rows, :].astype(F32) * (scale[...] * live[slot, 0:1, :])).astype(BF16)
        dproj[rows, :] = scaled
        dproj_t[:, slot * per_slot : (slot + 1) * per_slot] = scaled.T
        for h in range(shape.hidden // shape.channels):
            cols = slice(h * shape.channels, (h + 1) * shape.channels)
            dact[rows, cols] = dot(dproj[rows, :], w_out[cols, :], 1, 1)


def late_kernel(
    shape, info, kernel, gain, w_in, band, fold, rims, normed_in, yhat_in, inverse_in, dproj_t, dact,
    keep, give, activated, dpreact, yhat, inverse, padded,
    taps, convolved, normed, normed_t, work, pre,
):
    late = TILE - shape.early
    kept = late + HALF
    for part in range(shape.parts):
        rows = pl.ds(shape.early * shape.pitch, kept * shape.pitch)
        padded[part, pl.ds(0, kept * shape.pitch), :] = band[part, rows, :]
    done = shape.early * TILE
    for slot in range(shape.slots):
        rows = pl.ds(slot * TILE * TILE, done)
        normed[rows, :] = normed_in[rows, :]
        yhat[rows, :] = yhat_in[rows, :]
        inverse[rows, :] = inverse_in[rows, :]
    spread_taps(shape, kernel, range(shape.parts), taps)
    put_fold(shape, owned_of(info) * TILE, fold, rims, range(shape.parts), padded, kept, work)
    convolve(shape, late, padded, taps, convolved)
    normalise(shape, late, shape.early, convolved, gain, normed, yhat, inverse)
    per_slot = TILE * TILE
    for slot in range(shape.slots):
        normed_t[:, slot * per_slot : (slot + 1) * per_slot] = normed[pl.ds(slot * per_slot, per_slot), :].T
    keeps_in = lax.axis_index("core") == 0
    block = shape.channels
    blocks = shape.hidden // block

    def span(h):
        return slice(h * block, (h + 1) * block)

    def expand(step):
        h, slot = divmod(step, shape.slots)
        pre[step % 3] = dot(normed[pl.ds(slot * per_slot, per_slot), :], w_in[:, span(h)], 1, 0)

    def activate(step):
        h, slot = divmod(step, shape.slots)
        rows, cols = pl.ds(slot * per_slot, per_slot), span(h)
        value = pre[step % 3]
        square = value * value
        gate = 0.5 + 0.5 * jnp.tanh(value * (GELU_C + (GELU_C * GELU_A) * square))
        activated[rows, cols] = (value * gate).astype(BF16)
        slope = value * (2.0 * GELU_C + (6.0 * GELU_C * GELU_A) * square)
        grown = gate + slope * (gate - gate * gate)
        dpreact[rows, cols] = (dact[rows, cols] * grown).astype(BF16)

    def reduce_rows(h):
        of_in = dot(normed_t[...], dpreact[:, span(h)], 1, 0)
        of_out = dot(dproj_t[...], activated[:, span(h)], 1, 0)
        keep[span(h), :] = jnp.where(keeps_in, of_in, of_out)
        give[span(h), :] = jnp.where(keeps_in, of_out, of_in).astype(BF16)

    steps = blocks * shape.slots
    expand(0)
    for step in range(steps):
        if step + 1 < steps:
            expand(step + 1)
        activate(step)
        h, slot = divmod(step, shape.slots)
        if slot == 0 and h:
            reduce_rows(h - 1)
    reduce_rows(blocks - 1)


def fold_sum(value):
    return jnp.sum(value.reshape(-1, 8, value.shape[-1]), axis=0)


def norm_grad_kernel(
    shape, w_in, w_out, gain, dpreact, yhat, inverse, activated, tangent, live,
    conv_grad, projected, gain_part, scale_part,
):
    chunk = TILE * TILE
    of_gain = jnp.zeros((8, shape.channels), F32)
    of_scale = jnp.zeros((8, shape.channels), F32)
    for slot in range(shape.slots):
        rows = pl.ds(slot * chunk, chunk)
        dnormed = dot(dpreact[rows, :], w_in[...], 1, 1)
        unit = yhat[rows, :]
        of_gain += fold_sum(dnormed * unit)
        dhat = dnormed * gain[...]
        mean = jnp.sum(dhat, axis=-1, keepdims=True) * (1.0 / shape.channels)
        along = jnp.sum(dhat * unit, axis=-1, keepdims=True) * (1.0 / shape.channels)
        scale = jnp.concatenate([inverse[rows, :]] * shape.parts, axis=1)
        conv_grad[rows, :] = (scale * (dhat - mean - unit * along)).astype(BF16)
        value = dot(activated[rows, :], w_out[...], 1, 0)
        projected[rows, :] = value
        of_scale += live[slot] * fold_sum(tangent[rows, :].astype(F32) * value)
    gain_part[...] = of_gain
    scale_part[...] = of_scale


def state_kernel(shape, fields, scale, projected, live, state, done):
    done[...] = jnp.zeros_like(done)
    chunk = TILE * TILE
    for slot in range(shape.slots):
        rows = pl.ds(slot * chunk, chunk)
        kept = fields[rows, :].astype(F32) + scale[...] * projected[rows, :]
        state[rows, :] = (live[slot, 0:1, :] * kept).astype(BF16)


def place_grad(shape, conv_grad, parts, spaced):
    blank = jnp.zeros((LEFT, LANES), F32)
    for at, part in enumerate(parts):
        for row in range(TILE):
            base = row * shape.pitch
            spaced[at, pl.ds(base, LEFT), :] = blank
            spaced[at, pl.ds(base + LEFT + shape.columns, LEFT), :] = blank
            for slot in range(shape.slots):
                cells = conv_grad[pl.ds(slot * TILE * TILE + row * TILE, TILE), shape.lanes(part)]
                spaced[at, pl.ds(base + LEFT + slot * TILE, TILE), :] = cells.astype(F32)


def taps_kernel(shape, part, band, top, conv_grad, small, padded, spaced):
    place_grad(shape, conv_grad, [part], spaced)
    kept = shape.early * shape.pitch
    padded[0, pl.ds(0, kept), :] = band[part, pl.ds(0, kept), :]
    padded[0, pl.ds(kept, top.shape[1]), :] = top[part]
    run = shape.columns // 8
    origin = LEFT - HALF
    for above in range(KSIZE):

        def one_row(row, sums, above=above):
            base = (row + above) * shape.pitch + origin
            loaded = [padded[0, pl.ds(base + at, 8, stride=run), :] for at in range(run + KSIZE - 1)]
            start = row * shape.pitch + LEFT
            grads = [spaced[0, pl.ds(start + at, 8, stride=run), :] for at in range(run)]
            sums = list(sums)
            for shift in range(KSIZE):
                for at in range(run):
                    sums[shift] = sums[shift] + grads[at] * loaded[at + shift]
            return tuple(sums)

        blank = tuple(jnp.zeros((8, LANES), F32) for _ in range(KSIZE))
        sums = lax.fori_loop(0, TILE, one_row, blank, unroll=2)
        for shift in range(KSIZE):
            small[pl.ds(above * KSIZE + shift, 1), :] = jnp.sum(sums[shift], axis=0, keepdims=True)


def back_kernel(shape, part, info, kernel, conv_grad, *refs):
    before = refs[:part]
    turns = part == shape.parts - 1
    core_grad, *refs = refs[part:]
    if turns:
        fold, *refs = refs
    spaced, taps = refs
    place_grad(shape, conv_grad, [part], spaced)
    blank = jnp.zeros((LEFT, LANES), F32)
    for row in range(TILE + HALF):
        core_grad[pl.ds(row * shape.pitch, LEFT), :] = blank
        core_grad[pl.ds((row + 1) * shape.pitch - LEFT, LEFT), :] = blank
    spread_taps(shape, kernel, [part], taps)
    run = -(-(shape.columns + 2 * HALF) // 8)

    def one_row(row, tap_rows):
        sums = [None] * run
        for above in tap_rows:
            base = (row - above) * shape.pitch + LEFT
            loaded = [
                spaced[0, pl.ds(base + at - KSIZE + 1, 8, stride=run), :] for at in range(run + KSIZE - 1)
            ]
            for shift in range(KSIZE):
                weight = taps[0, above * KSIZE + shift]
                for at in range(run):
                    term = weight * loaded[at - shift + KSIZE - 1]
                    sums[at] = term if sums[at] is None else sums[at] + term
        start = (row - HALF) * shape.pitch + LEFT - HALF
        for at in range(run):
            core_grad[pl.ds(start + at, 8, stride=run), :] = sums[at]

    inner = (KSIZE - 1, TILE - 1)
    for row in range(HALF, TILE + 2 * HALF):
        if not inner[0] <= row <= inner[1]:
            low = max(0, row - TILE + 1)
            one_row(row, range(low, min(KSIZE - 1, row) + 1))

    def inner_row(step, carry):
        one_row(step, range(KSIZE))
        return carry

    lax.fori_loop(inner[0], inner[1] + 1, inner_row, 0)
    if turns:
        flip = flip_matrix(shape.pitch, owned_of(info) * TILE + 2 * LEFT - 1)
        for k in range(HALF):
            at = pl.ds((TILE + k) * shape.pitch, shape.pitch)
            cells = jnp.concatenate([one[at, :] for one in (*before, core_grad)], axis=1)
            turned = dot(flip, cells.astype(BF16), 1, 0)
            fold[pl.ds(k * shape.pitch, shape.pitch), :] = turned.astype(BF16)


def rims_kernel(shape, info, fold, *refs):
    core_grad = refs[: shape.parts]
    folded, first, second = refs[shape.parts :]
    used = owned_of(info) * TILE
    for part in range(shape.parts):
        folded[part] = core_grad[part][pl.ds(0, TILE * shape.pitch), :]
        for k in range(HALF):
            rows = pl.ds((TILE - 1 - k) * shape.pitch, shape.pitch)
            returned = fold[pl.ds(k * shape.pitch, shape.pitch), shape.lanes(part)]
            folded[part, rows, :] += returned.astype(F32)
    west = edge_planes(shape, folded, LEFT - HALF, shape.pitch)
    east = edge_planes(shape, folded, LEFT + used, shape.pitch)
    send_edges(shape, west, east, first, second)


def final_kernel(
    shape, info, live, tangent, folded, first, second,
    grad_fields, done,
    work,
):
    used = owned_of(info) * TILE
    even = is_even()
    done[...] = jnp.zeros_like(done)
    work[...] = folded[...]
    for part in range(shape.parts):
        for col in range(HALF):
            planes = pl.ds(col * TILE, TILE)
            one = first[planes, shape.lanes(part)].astype(F32)
            two = second[planes, shape.lanes(part)].astype(F32)
            to_tail = jnp.where(even, one, two)
            to_head = jnp.where(even, two, one)
            head = pl.ds(LEFT + col, TILE, stride=shape.pitch)
            work[part, head, :] = work[part, head, :] + to_head
            tail = pl.ds(LEFT + used - HALF + col, TILE, stride=shape.pitch)
            work[part, tail, :] = work[part, tail, :] + to_tail
        for slot in range(shape.slots):
            flag = live[slot, 0:1, shape.lanes(part)]
            for row in range(TILE):
                rows = pl.ds(slot * TILE * TILE + row * TILE, TILE)
                cells = work[part, pl.ds(row * shape.pitch + LEFT + slot * TILE, TILE), :]
                total = tangent[rows, shape.lanes(part)].astype(F32) + cells
                grad_fields[rows, shape.lanes(part)] = (flag * total).astype(BF16)


def unpack_kernel(norm, own, came, w_in, w_out, kernel_sum, gain_sum, scale_sum):
    is_first = lax.axis_index("core") == 0
    hidden, channels = w_out.shape
    for h in range(hidden // channels):
        block = slice(h * channels, (h + 1) * channels)
        mine = own[block, :].astype(F32) * norm
        theirs = came[block, :].astype(F32) * norm
        w_in[:, block] = jnp.where(is_first, mine, theirs)
        w_out[block, :] = jnp.where(is_first, theirs, mine).T
    extra = (own.shape[0] - hidden) // 2
    high, low = pl.ds(hidden, extra), pl.ds(hidden + extra, extra)
    mine = (own[high, :].astype(F32) + own[low, :].astype(F32)) * norm
    theirs = (came[high, :].astype(F32) + came[low, :].astype(F32)) * norm
    small = jnp.concatenate([jnp.where(is_first, mine, theirs), jnp.where(is_first, theirs, mine)])
    for above in range(KSIZE):
        kernel_sum[above] = small[above * KSIZE : (above + 1) * KSIZE, :]
    gain_sum[...] = small[KSIZE * KSIZE : KSIZE * KSIZE + 1, :]
    scale_sum[...] = small[KSIZE * KSIZE + 1 : KSIZE * KSIZE + 2, :]


def pairs_of(kind):
    count = lax.axis_size(TILES)
    half = count // 2
    place = [rank if rank < half else count - 1 + half - rank for rank in range(count)]
    partner = {
        "first": lambda rank: rank ^ 1,
        "second": lambda rank: ((rank + 1) ^ 1) - 1,
        "fold": lambda rank: count - 1 - rank,
    }[kind]
    return [(place[rank], place[partner(rank) % count]) for rank in range(count)]


def swap(block, kind):
    return lax.ppermute(block, TILES, pairs_of(kind))


def core_swap(block):
    return lax.ppermute(block, "core", [(0, 1), (1, 0)])


def stages():
    chip_bits = lax.axis_size(CHIPS).bit_length() - 1
    rest = list(range(2, chip_bits))
    return list(zip([0, -1, 1] + rest, [1, 0, -1] + rest))


def bit_swap(block, stage):
    chips, cores, samples = (lax.axis_size(axis) for axis in (CHIPS, "core", "dp"))
    pairs = []
    for chip in range(chips):
        for core in range(cores):
            for sample in range(samples):
                bit = stage[core]
                to = (chip, sample ^ 1) if bit < 0 else (chip ^ (1 << bit), sample)
                pairs.append(
                    ((chip * cores + core) * samples + sample, (to[0] * cores + core) * samples + to[1])
                )
    return lax.ppermute(block, TILES + ("dp",), pairs)


def bit_here(stage):
    bits = [
        lax.axis_index("dp") if bit < 0 else chip_index() >> bit & 1 for bit in stage
    ]
    return jnp.where(lax.axis_index("core") == 0, bits[0], bits[1])


def half_rows(bit, rows):
    return pl.ds(pl.multiple_of(bit * rows, rows), rows)


def join_kernel(stage, keep, came, mine, send):
    rows = send.shape[0]
    mine[...] = keep[...] + came[...].astype(F32)
    send[...] = mine[half_rows(1 - bit_here(stage), rows), :].astype(BF16)


def halve_kernel(stage, following, whole, came, mine, send):
    rows = mine.shape[0]
    mine[...] = whole[half_rows(bit_here(stage), rows), :] + came[...].astype(F32)
    send[...] = mine[half_rows(1 - bit_here(following), rows // 2), :].astype(BF16)


def pack_kernel(gain_part, scale_part, *refs):
    taps, (keep, send, work) = refs[:-3], refs[-3:]
    half = keep.shape[0]
    work[...] = jnp.zeros_like(work)
    for part, ref in enumerate(taps):
        work[pl.ds(0, ref.shape[0]), part * LANES : (part + 1) * LANES] = ref[...]
    work[pl.ds(KSIZE * KSIZE, 1), :] = jnp.sum(gain_part[...], axis=0, keepdims=True)
    work[pl.ds(KSIZE * KSIZE + 1, 1), :] = jnp.sum(scale_part[...], axis=0, keepdims=True)
    core = lax.axis_index("core")
    keep[...] = work[half_rows(core, half), :]
    value = work[half_rows(1 - core, half), :]
    high = value.astype(BF16)
    send[pl.ds(0, half), :] = high
    send[pl.ds(half, half), :] = (value - high.astype(F32)).astype(BF16)


def turn_kernel(stage, whole, came, keep, extra, payload):
    rows, half = came.shape[0], keep.shape[0]
    share = whole[half_rows(bit_here(stage), rows), :] + came[...].astype(F32)
    payload[pl.ds(0, rows), :] = share.astype(BF16)
    small = keep[...] + (extra[pl.ds(0, half), :].astype(F32) + extra[pl.ds(half, half), :].astype(F32))
    payload[pl.ds(rows, half), :] = small.astype(BF16)


def add_kernel(own, came, payload):
    total = (own[...].astype(F32) + came[...].astype(F32)).astype(BF16)
    if payload.shape == total.shape:
        payload[...] = total
    else:
        for at in range(payload.shape[0]):
            payload[at] = total


def gather_kernel(order, extra, came, payload):
    rows = came.shape[1] - extra
    samples = lax.axis_size("dp")
    is_first = lax.axis_index("core") == 0
    total = jnp.zeros((extra, came.shape[2]), F32)
    for at in range(came.shape[0]):
        near, sample = divmod(at, samples)
        places = []
        for core in range(2):
            place = 0
            for stage in order:
                place = 2 * place + (sample if stage[core] < 0 else near >> stage[core] & 1)
            places.append(place)
        place = jnp.where(is_first, places[0], places[1])
        payload[half_rows(place, rows), :] = came[at, pl.ds(0, rows), :]
        total += came[at, pl.ds(rows, extra), :].astype(F32)
    high = total.astype(BF16)
    full = rows * came.shape[0]
    payload[pl.ds(full, extra), :] = high
    payload[pl.ds(full + extra, extra), :] = (total - high.astype(F32)).astype(BF16)


def double_kernel(stage, extra, own, came, payload):
    rows = own.shape[0] - extra
    bit = bit_here(stage)
    payload[half_rows(bit, rows), :] = own[pl.ds(0, rows), :]
    payload[half_rows(1 - bit, rows), :] = came[pl.ds(0, rows), :]
    total = own[pl.ds(rows, extra), :].astype(F32) + came[pl.ds(rows, extra), :].astype(F32)
    high = total.astype(BF16)
    payload[pl.ds(2 * rows, extra), :] = high
    if payload.shape[0] > 2 * rows + extra:
        payload[pl.ds(2 * rows + extra, extra), :] = (total - high.astype(F32)).astype(BF16)


def halved(mine, send, order):
    for at, stage in enumerate(order[:-1]):
        came = bit_swap(send, stage)
        rows = came.shape[0]
        bit = bit_here(stage)
        mine = lax.dynamic_index_in_dim(mine.reshape(2, rows, -1), bit, 0, keepdims=False) + came.astype(F32)
        bit = bit_here(order[at + 1])
        halves = mine.reshape(2, rows // 2, -1)
        send = lax.dynamic_index_in_dim(halves, 1 - bit, 0, keepdims=False).astype(BF16)
    return mine, send


def call(kernel, outs, scratch, hbm, vmem, copies=0, micros=1.0, after=(), limit=20):
    in_specs = [pl.BlockSpec(memory_space=pl.ANY)] * len(hbm)
    in_specs += [pl.BlockSpec(memory_space=pltpu.VMEM)] * len(vmem)
    in_specs += [pl.BlockSpec(memory_space=pl.ANY)] * len(after)
    shapes = [pltpu.SMEM(*one) if one[1] == jnp.int32 else pltpu.VMEM(*one) for one in scratch]
    if copies:
        shapes.append(pltpu.SemaphoreType.DMA((copies,)))
    taken = len(hbm) + len(vmem)

    def body(*refs):
        kernel(*refs[:taken], *refs[taken + len(after) :])

    return pl.pallas_call(
        body,
        out_shape=[jax.ShapeDtypeStruct(*out) for out in outs],
        in_specs=in_specs,
        out_specs=[pl.BlockSpec(memory_space=pltpu.VMEM)] * len(outs),
        scratch_shapes=shapes,
        cost_estimate=pl.CostEstimate(flops=int(micros * 1e9), bytes_accessed=0, transcendentals=0),
        compiler_params=pltpu.CompilerParams(vmem_limit_bytes=limit * 1024 * 1024),
    )(*hbm, *vmem, *after)


def shards(fields, grad_out, block_count, ocean, kernel, ln_gain, w_in, w_out, layer_scale):
    samples, slots, tile_rows, tile_cols, channels = fields.shape
    hidden = w_in.shape[1]
    shape = Shape(slots, channels, hidden)
    cells, parts, pitch = shape.cells, shape.parts, shape.pitch
    grid = fields.shape
    fields = fields.reshape(cells, channels)
    tangent = grad_out.reshape(cells, channels)
    taps_in = kernel
    gain = ln_gain.reshape(1, channels)
    scale = layer_scale.reshape(1, channels)

    def bind(body):
        return functools.partial(body, shape)

    def strip(rows):
        return ((parts, rows * pitch, LANES), F32)

    edge = ((shape.edge_rows, channels), BF16)
    turned = ((HALF * pitch, channels), BF16)
    whole = ((cells, channels), BF16)
    whole_f = ((cells, channels), F32)
    wide = ((cells, hidden), BF16)
    narrow = ((cells, LANES), F32)
    row = ((1, channels), F32)
    eight = ((8, channels), F32)
    taps = ((parts, KSIZE * KSIZE, 8, LANES), F32)
    count_s = (block_count.shape, jnp.int32)
    flat = ((channels, cells), BF16)
    ends = ((HALF * 2 * LEFT, channels), BF16)
    ends_f = ((parts, HALF * 2 * LEFT, LANES), F32)
    late = TILE - shape.early

    first, second, info = call(
        bind(prep_kernel), [edge, edge, ((8, LANES), F32)],
        [count_s, ((parts, cells, LANES), F32)], [block_count], [fields], 1, 1.0,
    )
    fold, live = call(
        bind(top_kernel), [((HALF * shape.columns, channels), BF16), ((slots, 8, channels), F32)], [],
        [], [info, ocean.reshape(1, slots), fields], 0, 0.5, after=[first],
    )
    first, second = swap(first, "first"), swap(second, "second")
    band, rims = call(
        bind(band_kernel), [strip(TILE + HALF), ends], [],
        [], [info, live, fields, first, second], 0, 1.0, after=[fold],
    )
    fold, rims = swap(fold, "fold"), swap(rims, "fold")
    normed, yhat, inverse, dproj_t, dact = call(
        bind(early_kernel), [whole, whole_f, narrow, flat, ((cells, hidden), F32)],
        [taps, ((parts, shape.early * shape.columns, LANES), F32), whole],
        [], [live, taps_in, gain, w_out, scale, tangent, band], 0, 5.0,
    )
    keep, give, activated, dpreact, yhat, inverse, top = call(
        bind(late_kernel),
        [((hidden, channels), F32), ((hidden, channels), BF16), wide, wide, whole_f, narrow, strip(late + 2 * HALF)],
        [
            taps, ((parts, late * shape.columns, LANES), F32), whole, flat, ends_f,
            ((3, TILE * TILE, channels), F32),
        ],
        [],
        [info, taps_in, gain, w_in, band, fold, rims, normed, yhat, inverse, dproj_t, dact], 0, 5.0,
    )

    order = stages()
    rows = hidden // 2

    def half_step(at, rows):
        return functools.partial(halve_kernel, order[at], order[at + 1]), [
            ((rows, channels), F32), ((rows // 2, channels), BF16),
        ]

    def taps_part(part, after):
        (small,) = call(
            functools.partial(taps_kernel, shape, part), [((small_rows, LANES), F32)],
            [((1, (TILE + 2 * HALF) * pitch, LANES), F32), ((1, TILE * pitch, LANES), F32)],
            [], [band, top, conv_grad], 0, 1.8, after=after,
        )
        return small

    def back_part(part, before, after):
        outs = [(((TILE + HALF) * pitch, LANES), F32)] + [turned] * (part == parts - 1)
        return call(
            functools.partial(back_kernel, shape, part), outs,
            [((1, TILE * pitch, LANES), F32), ((1, KSIZE * KSIZE, 8, LANES), F32)],
            [], [info, taps_in, conv_grad, *before], 0, 2.0, after=after,
        )

    small_rows = -(-(KSIZE * KSIZE + 2) // 32) * 32
    came = core_swap(give)
    conv_grad, projected, gain_part, scale_part = call(
        bind(norm_grad_kernel), [whole, whole_f, eight, eight], [], [],
        [w_in, w_out, gain, dpreact, yhat, inverse, activated, tangent, live], 0, 1.3,
    )
    mine, send = call(
        functools.partial(join_kernel, order[0]),
        [((hidden, channels), F32), ((rows, channels), BF16)], [], [], [keep, came], after=[gain_part], micros=0.3,
    )
    came = bit_swap(send, order[0])
    core_grad = []
    after = [send]
    for part in range(parts):
        one, *fold_back = back_part(part, core_grad, after)
        core_grad += [one]
        after = [one]
    fold_back = swap(fold_back[0], "fold")
    body, outs = half_step(0, rows)
    mine, send = call(body, outs, [], [], [mine, came], after=after, micros=0.3)
    came = bit_swap(send, order[1])
    taps_parts = [taps_part(part, [send]) for part in range(parts)]
    small_rows //= 2
    small, extra = call(
        pack_kernel, [((small_rows, channels), F32), ((2 * small_rows, channels), BF16)],
        [((2 * small_rows, channels), F32)], [], [gain_part, scale_part, *taps_parts], micros=0.3,
    )
    extra = core_swap(extra)
    rows //= 2
    body, outs = half_step(1, rows)
    mine, send = call(body, outs, [], [], [mine, came], after=[small], micros=0.3)
    mine, send = halved(mine, send, order[2:-1])
    came = bit_swap(send, order[-2])
    folded, first, second = call(
        bind(rims_kernel), [strip(TILE), edge, edge], [], [], [info, fold_back, *core_grad], 0, 1.0,
        after=[send],
    )
    first, second = swap(first, "first"), swap(second, "second")
    rows = came.shape[0]
    if rows % 16 == 0:
        (payload,) = call(
            functools.partial(turn_kernel, order[-2]), [((rows + small_rows, channels), BF16)],
            [], [], [mine, came, small, extra], after=[folded], micros=0.3,
        )
    else:
        bit = bit_here(order[-2])
        share = lax.dynamic_index_in_dim(mine.reshape(2, rows, channels), bit, 0, keepdims=False)
        small = small + (extra[:small_rows].astype(F32) + extra[small_rows:].astype(F32))
        payload = jnp.concatenate([share + came.astype(F32), small]).astype(BF16)
    came = bit_swap(payload, order[-1])
    grad_fields, done = call(
        bind(final_kernel), [whole, ((8, LANES), F32)], [strip(TILE)],
        [], [info, live, tangent, folded, first, second], 0, 1.5, after=[payload],
    )
    state, done_too = call(
        bind(state_kernel), [whole, ((8, LANES), F32)], [], [], [fields, scale, projected, live], 0, 1.0, after=[done],
    )
    block = lax.axis_size("near") * lax.axis_size("dp")
    copied = (block, *payload.shape)
    outer = range(block.bit_length() - 1, len(order) - 1)
    (payload,) = call(
        add_kernel, [(payload.shape if outer else copied, BF16)], [], [], [payload, came], after=[done, done_too],
        micros=0.3,
    )
    for at in reversed(outer):
        came = bit_swap(payload, order[at])
        if rows % 16 == 0:
            (payload,) = call(
                functools.partial(double_kernel, order[at], small_rows),
                [((2 * rows + small_rows, channels), BF16)], [], [], [payload, came], micros=0.3,
            )
        else:
            is_low = bit_here(order[at]) == 0
            low, high = payload[:rows], came[:rows]
            both = payload[rows:].astype(F32) + came[rows:].astype(F32)
            joined = [jnp.where(is_low, low, high), jnp.where(is_low, high, low), both.astype(BF16)]
            payload = jnp.concatenate(joined)
        rows *= 2
    if outer:
        payload = jnp.broadcast_to(payload, (block, *payload.shape))
    came = lax.all_to_all(payload, ("near", "dp"), 0, 0, tiled=True)
    (payload,) = call(
        functools.partial(gather_kernel, order[: block.bit_length() - 1], small_rows),
        [((hidden + 2 * small_rows, channels), BF16)], [], [], [came], micros=0.3,
    )
    came = core_swap(payload)
    total = samples * lax.axis_size("dp") * slots * lax.axis_size(TILES) * tile_rows * tile_cols
    norm = total ** (-0.5)
    sums = [((channels, hidden), F32), ((hidden, channels), F32)]
    w_in_sum, w_out_sum, kernel_sum, gain_sum, scale_sum = call(
        functools.partial(unpack_kernel, norm), sums + [(kernel.shape, F32), row, row], [],
        [], [payload, came], 0, 1.5,
    )
    return (
        state.reshape(grid),
        grad_fields.reshape(grid),
        kernel_sum,
        gain_sum.reshape(ln_gain.shape),
        w_in_sum,
        w_out_sum,
        scale_sum.reshape(layer_scale.shape),
    )


def solution(mesh):
    cores = Mesh(mesh.devices.reshape(-1, 4, 2, mesh.devices.shape[1]), TILES + ("dp",))
    banded = P("dp", TILES, None, None, None)
    placed = (banded, banded, P(TILES), P(TILES), P(), P(), P(), P(), P())
    return jax.shard_map(
        shards,
        mesh=cores,
        in_specs=placed,
        out_specs=(banded, banded, P(), P(), P(), P(), P()),
        check_vma=False,
    )
```

```python
import functools

import jax
import jax.numpy as jnp
from jax import lax
from jax.experimental import pallas as pl
from jax.experimental.pallas import tpu as pltpu
from jax.sharding import Mesh, PartitionSpec as P

KSIZE = 7
HALF = KSIZE // 2
TILE = 16
EPS = 1e-06
CHIPS = ("far", "near")
TILES = CHIPS + ("core",)
F32 = jnp.float32
BF16 = jnp.bfloat16
LANES = 128
LEFT = 8
GELU_C = 0.7978845608028654
GELU_A = 0.044715


def dot(lhs, rhs, lhs_dim, rhs_dim):
    return lax.dot_general(
        lhs, rhs, (((lhs_dim,), (rhs_dim,)), ((), ())), preferred_element_type=F32
    )


def chip_index():
    return lax.axis_index("far") * lax.axis_size("near") + lax.axis_index("near")


def cycle_rank():
    count = lax.axis_size(TILES)
    here = chip_index() * lax.axis_size("core") + lax.axis_index("core")
    return jnp.where(here < count // 2, here, count - 1 + count // 2 - here)


def is_even():
    return lax.rem(cycle_rank(), 2) == 0


class Fetch:
    def __init__(self, sems, *pairs):
        self.copies = [
            pltpu.make_async_copy(source, target, sems.at[at]) for at, (source, target) in enumerate(pairs)
        ]
        for copy in self.copies:
            copy.start()

    def wait(self, *which):
        for at in which:
            self.copies[at].wait()


class Shape:
    def __init__(self, slots, channels, hidden):
        self.slots = slots
        self.channels = channels
        self.hidden = hidden
        self.parts = channels // LANES
        self.columns = slots * TILE
        self.pitch = self.columns + 2 * LEFT
        self.cells = slots * TILE * TILE
        self.edge_rows = HALF * TILE
        self.early = 12

    def lanes(self, part):
        return slice(part * LANES, (part + 1) * LANES)


def edge_planes(shape, source, start, stride):
    return [
        jnp.concatenate(
            [source[part, pl.ds(start + col, TILE, stride=stride), :] for part in range(shape.parts)], axis=1
        )
        for col in range(HALF)
    ]


def send_edges(shape, left, right, first, second):
    even = is_even()
    for col in range(HALF):
        rows = pl.ds(col * TILE, TILE)
        first[rows, :] = jnp.where(even, right[col], left[col]).astype(BF16)
        second[rows, :] = jnp.where(even, left[col], right[col]).astype(BF16)


def flip_matrix(size, last):
    to = lax.broadcasted_iota(jnp.int32, (size, size), 0)
    frm = lax.broadcasted_iota(jnp.int32, (size, size), 1)
    return jnp.where(to + frm == last, 1.0, 0.0).astype(BF16)


def owned_of(info):
    return jnp.max(info[...]).astype(jnp.int32)


def prep_kernel(shape, count_hbm, fields, first, second, info, count, work, sems):
    fetch = Fetch(sems, (count_hbm, count))
    for part in range(shape.parts):
        work[part] = fields[:, shape.lanes(part)].astype(F32)
    left = edge_planes(shape, work, 0, TILE)
    fetch.wait(0)
    right = edge_planes(shape, work, (count[0] - 1) * TILE * TILE + TILE - HALF, TILE)
    send_edges(shape, left, right, first, second)
    info[...] = jnp.full(info.shape, count[0].astype(F32), F32)


def top_kernel(shape, info, ocean, fields, fold, live):
    column = lax.broadcasted_iota(jnp.int32, ocean.shape, 1)
    wet = jnp.where(ocean[...] > 0, 1.0, 0.0).astype(F32)
    for slot in range(shape.slots):
        one = jnp.sum(jnp.where(column == slot, wet, 0.0), axis=1, keepdims=True)
        one = jnp.where(info[0:1, 0:1] > slot + 0.5, one, 0.0)
        live[slot] = jnp.broadcast_to(one, live.shape[1:])
    flip = flip_matrix(shape.columns, owned_of(info) * TILE - 1)
    for k in range(HALF):
        cells = jnp.concatenate(
            [
                fields[pl.ds(slot * TILE * TILE + (TILE - 1 - k) * TILE, TILE), :].astype(F32)
                * live[slot, 0:1, :]
                for slot in range(shape.slots)
            ]
        )
        turned = dot(flip, cells.astype(BF16), 1, 0)
        fold[pl.ds(k * shape.columns, shape.columns), :] = turned.astype(BF16)


def band_kernel(shape, info, live, fields, first, second, band, rims):
    used = owned_of(info) * TILE
    even = is_even()
    blank = jnp.zeros((LEFT, LANES), F32)
    per_slot = TILE * TILE
    for part in range(shape.parts):
        band[part, pl.ds(0, HALF * shape.pitch), :] = jnp.zeros((HALF * shape.pitch, LANES), F32)
        for row in range(TILE):
            base = (row + HALF) * shape.pitch
            band[part, pl.ds(base, LEFT), :] = blank
            band[part, pl.ds(base + LEFT + shape.columns, LEFT), :] = blank
    top = HALF * shape.pitch
    for part in range(shape.parts):
        for row in range(TILE):
            base = (row + HALF) * shape.pitch
            for slot in range(shape.slots):
                cells = fields[pl.ds(slot * per_slot + row * TILE, TILE), shape.lanes(part)]
                band[part, pl.ds(base + LEFT + slot * TILE, TILE), :] = cells.astype(F32) * live[slot, 0:1, shape.lanes(part)]
        for col in range(HALF):
            rows = pl.ds(col * TILE, TILE)
            one = first[rows, shape.lanes(part)].astype(F32)
            two = second[rows, shape.lanes(part)].astype(F32)
            west = jnp.where(even, two, one)
            east = jnp.where(even, one, two)
            band[part, pl.ds(top + LEFT - HALF + col, TILE, stride=shape.pitch), :] = west
            band[part, pl.ds(top + LEFT + used + col, TILE, stride=shape.pitch), :] = east
    for k in range(HALF):
        base = (HALF + TILE - 1 - k) * shape.pitch
        east = pl.multiple_of(base + LEFT + used, LEFT)
        for part in range(shape.parts):
            ends = jnp.concatenate([band[part, pl.ds(base, LEFT), :], band[part, pl.ds(east, LEFT), :]])
            rims[pl.ds(k * 2 * LEFT, 2 * LEFT), shape.lanes(part)] = ends.astype(BF16)


def put_fold(shape, used, fold, rims, parts, padded, first_row, work):
    blank = jnp.zeros((LEFT, LANES), F32)
    for at, part in enumerate(parts):
        work[at] = rims[:, shape.lanes(part)].astype(F32)
        for k in range(HALF):
            base = (first_row + k) * shape.pitch
            padded[at, pl.ds(base, LEFT), :] = blank
            padded[at, pl.ds(base + LEFT + shape.columns, LEFT), :] = blank
            cells = fold[pl.ds(k * shape.columns, shape.columns), shape.lanes(part)]
            padded[at, pl.ds(base + LEFT, shape.columns), :] = cells.astype(F32)
            for col in range(HALF):
                west = work[at, pl.ds(k * 2 * LEFT + LEFT - 1 - col, 1), :]
                east = work[at, pl.ds(k * 2 * LEFT + LEFT + col, 1), :]
                padded[at, pl.ds(base + LEFT - 1 - col, 1), :] = east
                padded[at, pl.ds(base + LEFT + used + col, 1), :] = west


def tree_sum(terms):
    while len(terms) > 1:
        pairs = [terms[at] + terms[at + 1] for at in range(0, len(terms) - 1, 2)]
        terms = pairs + terms[len(pairs) * 2 :]
    return terms[0]


def spread_taps(shape, kernel, parts, taps):
    for above in range(KSIZE):
        rows = kernel[above].astype(F32)
        for at, part in enumerate(parts):
            for shift in range(KSIZE):
                row = rows[shift : shift + 1, shape.lanes(part)]
                taps[at, above * KSIZE + shift] = jnp.broadcast_to(row, (8, LANES))


def convolve(shape, rows, padded, taps, convolved):
    run = shape.columns // 8
    pair = 2
    origin = LEFT - HALF

    def two_rows(step, carry):
        row = step * pair
        for part in range(shape.parts):
            sums = [[None] * run for _ in range(pair)]
            for above in range(KSIZE + pair - 1):
                base = (row + above) * shape.pitch + origin
                loaded = [
                    padded[part, pl.ds(base + at, 8, stride=run), :]
                    for at in range(run + KSIZE - 1)
                ]
                for which in range(pair):
                    tap_row = above - which
                    if not 0 <= tap_row < KSIZE:
                        continue
                    for shift in range(KSIZE):
                        weight = taps[part, tap_row * KSIZE + shift]
                        for at in range(run):
                            term = weight * loaded[at + shift]
                            old = sums[which][at]
                            sums[which][at] = term if old is None else old + term
            for which in range(pair):
                for at in range(run):
                    start = (row + which) * shape.columns + at
                    convolved[part, pl.ds(start, 8, stride=run), :] = sums[which][at]
        return carry

    lax.fori_loop(0, rows // pair, two_rows, 0)


def normalise(shape, rows, first_row, convolved, gain, normed, yhat, inverse):
    def one_row(row, carry):
        for slot in range(shape.slots):
            start = pl.multiple_of(row * shape.columns + slot * TILE, TILE)
            at = slot * TILE * TILE + (first_row + row) * TILE
            out = pl.ds(pl.multiple_of(at, TILE), TILE)
            parts = [convolved[part, pl.ds(start, TILE), :] for part in range(shape.parts)]
            mean = jnp.sum(sum(parts), axis=-1, keepdims=True) * (1.0 / shape.channels)
            parts = [value - mean for value in parts]
            square = jnp.sum(sum(value * value for value in parts), axis=-1, keepdims=True)
            scale = lax.rsqrt(square * (1.0 / shape.channels) + EPS)
            inverse[out, :] = jnp.broadcast_to(scale, (TILE, LANES))
            for part in range(shape.parts):
                value = parts[part] * scale
                yhat[out, shape.lanes(part)] = value
                normed[out, shape.lanes(part)] = (value * gain[:, shape.lanes(part)]).astype(BF16)
        return carry

    lax.fori_loop(0, rows, one_row, 0, unroll=4)


def early_kernel(
    shape, live, kernel, gain, w_out, scale, tangent, band,
    normed, yhat, inverse, dproj_t, dact,
    taps, convolved, dproj,
):
    spread_taps(shape, kernel, range(shape.parts), taps)
    convolve(shape, shape.early, band, taps, convolved)
    normalise(shape, shape.early, 0, convolved, gain, normed, yhat, inverse)
    per_slot = TILE * TILE
    for slot in range(shape.slots):
        rows = pl.ds(slot * per_slot, per_slot)
        scaled = (tangent[rows, :].astype(F32) * (scale[...] * live[slot, 0:1, :])).astype(BF16)
        dproj[rows, :] = scaled
        dproj_t[:, slot * per_slot : (slot + 1) * per_slot] = scaled.T
        for h in range(shape.hidden // shape.channels):
            cols = slice(h * shape.channels, (h + 1) * shape.channels)
            dact[rows, cols] = dot(dproj[rows, :], w_out[cols, :], 1, 1)


def late_kernel(
    shape, info, kernel, gain, w_in, band, fold, rims, normed_in, yhat_in, inverse_in, dproj_t, dact,
    keep, give, activated, dpreact, yhat, inverse, padded,
    taps, convolved, normed, normed_t, work, pre,
):
    late = TILE - shape.early
    kept = late + HALF
    for part in range(shape.parts):
        rows = pl.ds(shape.early * shape.pitch, kept * shape.pitch)
        padded[part, pl.ds(0, kept * shape.pitch), :] = band[part, rows, :]
    done = shape.early * TILE
    for slot in range(shape.slots):
        rows = pl.ds(slot * TILE * TILE, done)
        normed[rows, :] = normed_in[rows, :]
        yhat[rows, :] = yhat_in[rows, :]
        inverse[rows, :] = inverse_in[rows, :]
    spread_taps(shape, kernel, range(shape.parts), taps)
    put_fold(shape, owned_of(info) * TILE, fold, rims, range(shape.parts), padded, kept, work)
    convolve(shape, late, padded, taps, convolved)
    normalise(shape, late, shape.early, convolved, gain, normed, yhat, inverse)
    per_slot = TILE * TILE
    for slot in range(shape.slots):
        normed_t[:, slot * per_slot : (slot + 1) * per_slot] = normed[pl.ds(slot * per_slot, per_slot), :].T
    keeps_in = lax.axis_index("core") == 0
    block = shape.channels
    blocks = shape.hidden // block

    def span(h):
        return slice(h * block, (h + 1) * block)

    def expand(step):
        h, slot = divmod(step, shape.slots)
        pre[step % 3] = dot(normed[pl.ds(slot * per_slot, per_slot), :], w_in[:, span(h)], 1, 0)

    def activate(step):
        h, slot = divmod(step, shape.slots)
        rows, cols = pl.ds(slot * per_slot, per_slot), span(h)
        value = pre[step % 3]
        square = value * value
        gate = 0.5 + 0.5 * jnp.tanh(value * (GELU_C + (GELU_C * GELU_A) * square))
        activated[rows, cols] = (value * gate).astype(BF16)
        slope = value * (2.0 * GELU_C + (6.0 * GELU_C * GELU_A) * square)
        grown = gate + slope * (gate - gate * gate)
        dpreact[rows, cols] = (dact[rows, cols] * grown).astype(BF16)

    def reduce_rows(h):
        of_in = dot(normed_t[...], dpreact[:, span(h)], 1, 0)
        of_out = dot(dproj_t[...], activated[:, span(h)], 1, 0)
        keep[span(h), :] = jnp.where(keeps_in, of_in, of_out)
        give[span(h), :] = jnp.where(keeps_in, of_out, of_in).astype(BF16)

    steps = blocks * shape.slots
    expand(0)
    for step in range(steps):
        if step + 1 < steps:
            expand(step + 1)
        activate(step)
        h, slot = divmod(step, shape.slots)
        if slot == 0 and h:
            reduce_rows(h - 1)
    reduce_rows(blocks - 1)


def fold_sum(value):
    return jnp.sum(value.reshape(-1, 8, value.shape[-1]), axis=0)


def norm_grad_kernel(
    shape, w_in, w_out, gain, dpreact, yhat, inverse, activated, tangent, live,
    conv_grad, projected, gain_part, scale_part,
):
    chunk = TILE * TILE
    of_gain = jnp.zeros((8, shape.channels), F32)
    of_scale = jnp.zeros((8, shape.channels), F32)
    for slot in range(shape.slots):
        rows = pl.ds(slot * chunk, chunk)
        dnormed = dot(dpreact[rows, :], w_in[...], 1, 1)
        unit = yhat[rows, :]
        of_gain += fold_sum(dnormed * unit)
        dhat = dnormed * gain[...]
        mean = jnp.sum(dhat, axis=-1, keepdims=True) * (1.0 / shape.channels)
        along = jnp.sum(dhat * unit, axis=-1, keepdims=True) * (1.0 / shape.channels)
        scale = jnp.concatenate([inverse[rows, :]] * shape.parts, axis=1)
        conv_grad[rows, :] = (scale * (dhat - mean - unit * along)).astype(BF16)
        value = dot(activated[rows, :], w_out[...], 1, 0)
        projected[rows, :] = value
        of_scale += live[slot] * fold_sum(tangent[rows, :].astype(F32) * value)
    gain_part[...] = of_gain
    scale_part[...] = of_scale


def state_kernel(shape, fields, scale, projected, live, state, done):
    done[...] = jnp.zeros_like(done)
    chunk = TILE * TILE
    for slot in range(shape.slots):
        rows = pl.ds(slot * chunk, chunk)
        kept = fields[rows, :].astype(F32) + scale[...] * projected[rows, :]
        state[rows, :] = (live[slot, 0:1, :] * kept).astype(BF16)


def place_grad(shape, conv_grad, parts, spaced):
    blank = jnp.zeros((LEFT, LANES), F32)
    for at, part in enumerate(parts):
        for row in range(TILE):
            base = row * shape.pitch
            spaced[at, pl.ds(base, LEFT), :] = blank
            spaced[at, pl.ds(base + LEFT + shape.columns, LEFT), :] = blank
            for slot in range(shape.slots):
                cells = conv_grad[pl.ds(slot * TILE * TILE + row * TILE, TILE), shape.lanes(part)]
                spaced[at, pl.ds(base + LEFT + slot * TILE, TILE), :] = cells.astype(F32)


def taps_kernel(shape, part, band, top, conv_grad, small, padded, spaced):
    place_grad(shape, conv_grad, [part], spaced)
    kept = shape.early * shape.pitch
    padded[0, pl.ds(0, kept), :] = band[part, pl.ds(0, kept), :]
    padded[0, pl.ds(kept, top.shape[1]), :] = top[part]
    run = shape.columns // 8
    origin = LEFT - HALF
    for above in range(KSIZE):

        def one_row(row, sums, above=above):
            base = (row + above) * shape.pitch + origin
            loaded = [padded[0, pl.ds(base + at, 8, stride=run), :] for at in range(run + KSIZE - 1)]
            start = row * shape.pitch + LEFT
            grads = [spaced[0, pl.ds(start + at, 8, stride=run), :] for at in range(run)]
            sums = list(sums)
            for shift in range(KSIZE):
                sums[shift] = sums[shift] + tree_sum([grads[at] * loaded[at + shift] for at in range(run)])
            return tuple(sums)

        blank = tuple(jnp.zeros((8, LANES), F32) for _ in range(KSIZE))
        sums = lax.fori_loop(0, TILE, one_row, blank, unroll=2)
        for shift in range(KSIZE):
            small[pl.ds(above * KSIZE + shift, 1), :] = jnp.sum(sums[shift], axis=0, keepdims=True)


def back_kernel(shape, part, info, kernel, conv_grad, *refs):
    before = refs[:part]
    turns = part == shape.parts - 1
    core_grad, *refs = refs[part:]
    if turns:
        fold, *refs = refs
    spaced, taps = refs
    place_grad(shape, conv_grad, [part], spaced)
    blank = jnp.zeros((LEFT, LANES), F32)
    for row in range(TILE + HALF):
        core_grad[pl.ds(row * shape.pitch, LEFT), :] = blank
        core_grad[pl.ds((row + 1) * shape.pitch - LEFT, LEFT), :] = blank
    spread_taps(shape, kernel, [part], taps)
    run = -(-(shape.columns + 2 * HALF) // 8)

    def one_row(row, tap_rows):
        sums = [None] * run
        for above in tap_rows:
            base = (row - above) * shape.pitch + LEFT
            loaded = [
                spaced[0, pl.ds(base + at - KSIZE + 1, 8, stride=run), :] for at in range(run + KSIZE - 1)
            ]
            weights = [taps[0, above * KSIZE + shift] for shift in range(KSIZE)]
            for at in range(run):
                row_sum = tree_sum([weights[shift] * loaded[at - shift + KSIZE - 1] for shift in range(KSIZE)])
                sums[at] = row_sum if sums[at] is None else sums[at] + row_sum
        start = (row - HALF) * shape.pitch + LEFT - HALF
        for at in range(run):
            core_grad[pl.ds(start + at, 8, stride=run), :] = sums[at]

    inner = (KSIZE - 1, TILE - 1)
    for row in range(HALF, TILE + 2 * HALF):
        if not inner[0] <= row <= inner[1]:
            low = max(0, row - TILE + 1)
            one_row(row, range(low, min(KSIZE - 1, row) + 1))

    def inner_row(step, carry):
        one_row(step, range(KSIZE))
        return carry

    lax.fori_loop(inner[0], inner[1] + 1, inner_row, 0)
    if turns:
        flip = flip_matrix(shape.pitch, owned_of(info) * TILE + 2 * LEFT - 1)
        for k in range(HALF):
            at = pl.ds((TILE + k) * shape.pitch, shape.pitch)
            cells = jnp.concatenate([one[at, :] for one in (*before, core_grad)], axis=1)
            turned = dot(flip, cells.astype(BF16), 1, 0)
            fold[pl.ds(k * shape.pitch, shape.pitch), :] = turned.astype(BF16)


def rims_kernel(shape, info, fold, *refs):
    core_grad = refs[: shape.parts]
    folded, first, second = refs[shape.parts :]
    used = owned_of(info) * TILE
    for part in range(shape.parts):
        folded[part] = core_grad[part][pl.ds(0, TILE * shape.pitch), :]
        for k in range(HALF):
            rows = pl.ds((TILE - 1 - k) * shape.pitch, shape.pitch)
            returned = fold[pl.ds(k * shape.pitch, shape.pitch), shape.lanes(part)]
            folded[part, rows, :] += returned.astype(F32)
    west = edge_planes(shape, folded, LEFT - HALF, shape.pitch)
    east = edge_planes(shape, folded, LEFT + used, shape.pitch)
    send_edges(shape, west, east, first, second)


def final_kernel(
    shape, info, live, tangent, folded, first, second,
    grad_fields, done,
    work,
):
    used = owned_of(info) * TILE
    even = is_even()
    done[...] = jnp.zeros_like(done)
    work[...] = folded[...]
    for part in range(shape.parts):
        for col in range(HALF):
            planes = pl.ds(col * TILE, TILE)
            one = first[planes, shape.lanes(part)].astype(F32)
            two = second[planes, shape.lanes(part)].astype(F32)
            to_tail = jnp.where(even, one, two)
            to_head = jnp.where(even, two, one)
            head = pl.ds(LEFT + col, TILE, stride=shape.pitch)
            work[part, head, :] = work[part, head, :] + to_head
            tail = pl.ds(LEFT + used - HALF + col, TILE, stride=shape.pitch)
            work[part, tail, :] = work[part, tail, :] + to_tail
        for slot in range(shape.slots):
            flag = live[slot, 0:1, shape.lanes(part)]
            for row in range(TILE):
                rows = pl.ds(slot * TILE * TILE + row * TILE, TILE)
                cells = work[part, pl.ds(row * shape.pitch + LEFT + slot * TILE, TILE), :]
                total = tangent[rows, shape.lanes(part)].astype(F32) + cells
                grad_fields[rows, shape.lanes(part)] = (flag * total).astype(BF16)


def unpack_kernel(norm, own, came, w_in, w_out, kernel_sum, gain_sum, scale_sum):
    is_first = lax.axis_index("core") == 0
    hidden, channels = w_out.shape
    for h in range(hidden // channels):
        block = slice(h * channels, (h + 1) * channels)
        mine = own[block, :].astype(F32) * norm
        theirs = came[block, :].astype(F32) * norm
        w_in[:, block] = jnp.where(is_first, mine, theirs)
        w_out[block, :] = jnp.where(is_first, theirs, mine).T
    extra = (own.shape[0] - hidden) // 2
    high, low = pl.ds(hidden, extra), pl.ds(hidden + extra, extra)
    mine = (own[high, :].astype(F32) + own[low, :].astype(F32)) * norm
    theirs = (came[high, :].astype(F32) + came[low, :].astype(F32)) * norm
    small = jnp.concatenate([jnp.where(is_first, mine, theirs), jnp.where(is_first, theirs, mine)])
    for above in range(KSIZE):
        kernel_sum[above] = small[above * KSIZE : (above + 1) * KSIZE, :]
    gain_sum[...] = small[KSIZE * KSIZE : KSIZE * KSIZE + 1, :]
    scale_sum[...] = small[KSIZE * KSIZE + 1 : KSIZE * KSIZE + 2, :]


def pairs_of(kind):
    count = lax.axis_size(TILES)
    half = count // 2
    place = [rank if rank < half else count - 1 + half - rank for rank in range(count)]
    partner = {
        "first": lambda rank: rank ^ 1,
        "second": lambda rank: ((rank + 1) ^ 1) - 1,
        "fold": lambda rank: count - 1 - rank,
    }[kind]
    return [(place[rank], place[partner(rank) % count]) for rank in range(count)]


def swap(block, kind):
    return lax.ppermute(block, TILES, pairs_of(kind))


def core_swap(block):
    return lax.ppermute(block, "core", [(0, 1), (1, 0)])


def stages():
    chip_bits = lax.axis_size(CHIPS).bit_length() - 1
    rest = list(range(2, chip_bits))
    return list(zip([0, -1, 1] + rest, [1, 0, -1] + rest))


def bit_swap(block, stage):
    chips, cores, samples = (lax.axis_size(axis) for axis in (CHIPS, "core", "dp"))
    pairs = []
    for chip in range(chips):
        for core in range(cores):
            for sample in range(samples):
                bit = stage[core]
                to = (chip, sample ^ 1) if bit < 0 else (chip ^ (1 << bit), sample)
                pairs.append(
                    ((chip * cores + core) * samples + sample, (to[0] * cores + core) * samples + to[1])
                )
    return lax.ppermute(block, TILES + ("dp",), pairs)


def bit_here(stage):
    bits = [
        lax.axis_index("dp") if bit < 0 else chip_index() >> bit & 1 for bit in stage
    ]
    return jnp.where(lax.axis_index("core") == 0, bits[0], bits[1])


def half_rows(bit, rows):
    return pl.ds(pl.multiple_of(bit * rows, rows), rows)


def join_kernel(stage, keep, came, mine, send):
    rows = send.shape[0]
    mine[...] = keep[...] + came[...].astype(F32)
    send[...] = mine[half_rows(1 - bit_here(stage), rows), :].astype(BF16)


def halve_kernel(stage, following, whole, came, mine, send):
    rows = mine.shape[0]
    mine[...] = whole[half_rows(bit_here(stage), rows), :] + came[...].astype(F32)
    send[...] = mine[half_rows(1 - bit_here(following), rows // 2), :].astype(BF16)


def pack_kernel(gain_part, scale_part, *refs):
    taps, (keep, send, work) = refs[:-3], refs[-3:]
    half = keep.shape[0]
    work[...] = jnp.zeros_like(work)
    for part, ref in enumerate(taps):
        work[pl.ds(0, ref.shape[0]), part * LANES : (part + 1) * LANES] = ref[...]
    work[pl.ds(KSIZE * KSIZE, 1), :] = jnp.sum(gain_part[...], axis=0, keepdims=True)
    work[pl.ds(KSIZE * KSIZE + 1, 1), :] = jnp.sum(scale_part[...], axis=0, keepdims=True)
    core = lax.axis_index("core")
    keep[...] = work[half_rows(core, half), :]
    value = work[half_rows(1 - core, half), :]
    high = value.astype(BF16)
    send[pl.ds(0, half), :] = high
    send[pl.ds(half, half), :] = (value - high.astype(F32)).astype(BF16)


def turn_kernel(stage, whole, came, keep, extra, payload):
    rows, half = came.shape[0], keep.shape[0]
    share = whole[half_rows(bit_here(stage), rows), :] + came[...].astype(F32)
    payload[pl.ds(0, rows), :] = share.astype(BF16)
    small = keep[...] + (extra[pl.ds(0, half), :].astype(F32) + extra[pl.ds(half, half), :].astype(F32))
    payload[pl.ds(rows, half), :] = small.astype(BF16)


def add_kernel(own, came, payload):
    total = (own[...].astype(F32) + came[...].astype(F32)).astype(BF16)
    if payload.shape == total.shape:
        payload[...] = total
    else:
        for at in range(payload.shape[0]):
            payload[at] = total


def gather_kernel(order, extra, came, payload):
    rows = came.shape[1] - extra
    samples = lax.axis_size("dp")
    is_first = lax.axis_index("core") == 0
    total = jnp.zeros((extra, came.shape[2]), F32)
    for at in range(came.shape[0]):
        near, sample = divmod(at, samples)
        places = []
        for core in range(2):
            place = 0
            for stage in order:
                place = 2 * place + (sample if stage[core] < 0 else near >> stage[core] & 1)
            places.append(place)
        place = jnp.where(is_first, places[0], places[1])
        payload[half_rows(place, rows), :] = came[at, pl.ds(0, rows), :]
        total += came[at, pl.ds(rows, extra), :].astype(F32)
    high = total.astype(BF16)
    full = rows * came.shape[0]
    payload[pl.ds(full, extra), :] = high
    payload[pl.ds(full + extra, extra), :] = (total - high.astype(F32)).astype(BF16)


def double_kernel(stage, extra, own, came, payload):
    rows = own.shape[0] - extra
    bit = bit_here(stage)
    payload[half_rows(bit, rows), :] = own[pl.ds(0, rows), :]
    payload[half_rows(1 - bit, rows), :] = came[pl.ds(0, rows), :]
    total = own[pl.ds(rows, extra), :].astype(F32) + came[pl.ds(rows, extra), :].astype(F32)
    high = total.astype(BF16)
    payload[pl.ds(2 * rows, extra), :] = high
    if payload.shape[0] > 2 * rows + extra:
        payload[pl.ds(2 * rows + extra, extra), :] = (total - high.astype(F32)).astype(BF16)


def halved(mine, send, order):
    for at, stage in enumerate(order[:-1]):
        came = bit_swap(send, stage)
        rows = came.shape[0]
        bit = bit_here(stage)
        mine = lax.dynamic_index_in_dim(mine.reshape(2, rows, -1), bit, 0, keepdims=False) + came.astype(F32)
        bit = bit_here(order[at + 1])
        halves = mine.reshape(2, rows // 2, -1)
        send = lax.dynamic_index_in_dim(halves, 1 - bit, 0, keepdims=False).astype(BF16)
    return mine, send


def call(kernel, outs, scratch, hbm, vmem, copies=0, micros=1.0, after=(), limit=20):
    in_specs = [pl.BlockSpec(memory_space=pl.ANY)] * len(hbm)
    in_specs += [pl.BlockSpec(memory_space=pltpu.VMEM)] * len(vmem)
    in_specs += [pl.BlockSpec(memory_space=pl.ANY)] * len(after)
    shapes = [pltpu.SMEM(*one) if one[1] == jnp.int32 else pltpu.VMEM(*one) for one in scratch]
    if copies:
        shapes.append(pltpu.SemaphoreType.DMA((copies,)))
    taken = len(hbm) + len(vmem)

    def body(*refs):
        kernel(*refs[:taken], *refs[taken + len(after) :])

    return pl.pallas_call(
        body,
        out_shape=[jax.ShapeDtypeStruct(*out) for out in outs],
        in_specs=in_specs,
        out_specs=[pl.BlockSpec(memory_space=pltpu.VMEM)] * len(outs),
        scratch_shapes=shapes,
        cost_estimate=pl.CostEstimate(flops=int(micros * 1e9), bytes_accessed=0, transcendentals=0),
        compiler_params=pltpu.CompilerParams(vmem_limit_bytes=limit * 1024 * 1024),
    )(*hbm, *vmem, *after)


def shards(fields, grad_out, block_count, ocean, kernel, ln_gain, w_in, w_out, layer_scale):
    samples, slots, tile_rows, tile_cols, channels = fields.shape
    hidden = w_in.shape[1]
    shape = Shape(slots, channels, hidden)
    cells, parts, pitch = shape.cells, shape.parts, shape.pitch
    grid = fields.shape
    fields = fields.reshape(cells, channels)
    tangent = grad_out.reshape(cells, channels)
    taps_in = kernel
    gain = ln_gain.reshape(1, channels)
    scale = layer_scale.reshape(1, channels)

    def bind(body):
        return functools.partial(body, shape)

    def strip(rows):
        return ((parts, rows * pitch, LANES), F32)

    edge = ((shape.edge_rows, channels), BF16)
    turned = ((HALF * pitch, channels), BF16)
    whole = ((cells, channels), BF16)
    whole_f = ((cells, channels), F32)
    wide = ((cells, hidden), BF16)
    narrow = ((cells, LANES), F32)
    row = ((1, channels), F32)
    eight = ((8, channels), F32)
    taps = ((parts, KSIZE * KSIZE, 8, LANES), F32)
    count_s = (block_count.shape, jnp.int32)
    flat = ((channels, cells), BF16)
    ends = ((HALF * 2 * LEFT, channels), BF16)
    ends_f = ((parts, HALF * 2 * LEFT, LANES), F32)
    late = TILE - shape.early

    first, second, info = call(
        bind(prep_kernel), [edge, edge, ((8, LANES), F32)],
        [count_s, ((parts, cells, LANES), F32)], [block_count], [fields], 1, 1.0,
    )
    fold, live = call(
        bind(top_kernel), [((HALF * shape.columns, channels), BF16), ((slots, 8, channels), F32)], [],
        [], [info, ocean.reshape(1, slots), fields], 0, 0.5, after=[first],
    )
    first, second = swap(first, "first"), swap(second, "second")
    band, rims = call(
        bind(band_kernel), [strip(TILE + HALF), ends], [],
        [], [info, live, fields, first, second], 0, 1.0, after=[fold],
    )
    fold, rims = swap(fold, "fold"), swap(rims, "fold")
    normed, yhat, inverse, dproj_t, dact = call(
        bind(early_kernel), [whole, whole_f, narrow, flat, ((cells, hidden), F32)],
        [taps, ((parts, shape.early * shape.columns, LANES), F32), whole],
        [], [live, taps_in, gain, w_out, scale, tangent, band], 0, 5.0,
    )
    keep, give, activated, dpreact, yhat, inverse, top = call(
        bind(late_kernel),
        [((hidden, channels), F32), ((hidden, channels), BF16), wide, wide, whole_f, narrow, strip(late + 2 * HALF)],
        [
            taps, ((parts, late * shape.columns, LANES), F32), whole, flat, ends_f,
            ((3, TILE * TILE, channels), F32),
        ],
        [],
        [info, taps_in, gain, w_in, band, fold, rims, normed, yhat, inverse, dproj_t, dact], 0, 5.0,
    )

    order = stages()
    rows = hidden // 2

    def half_step(at, rows):
        return functools.partial(halve_kernel, order[at], order[at + 1]), [
            ((rows, channels), F32), ((rows // 2, channels), BF16),
        ]

    def taps_part(part, after):
        (small,) = call(
            functools.partial(taps_kernel, shape, part), [((small_rows, LANES), F32)],
            [((1, (TILE + 2 * HALF) * pitch, LANES), F32), ((1, TILE * pitch, LANES), F32)],
            [], [band, top, conv_grad], 0, 1.8, after=after,
        )
        return small

    def back_part(part, before, after):
        outs = [(((TILE + HALF) * pitch, LANES), F32)] + [turned] * (part == parts - 1)
        return call(
            functools.partial(back_kernel, shape, part), outs,
            [((1, TILE * pitch, LANES), F32), ((1, KSIZE * KSIZE, 8, LANES), F32)],
            [], [info, taps_in, conv_grad, *before], 0, 2.0, after=after,
        )

    small_rows = -(-(KSIZE * KSIZE + 2) // 32) * 32
    came = core_swap(give)
    conv_grad, projected, gain_part, scale_part = call(
        bind(norm_grad_kernel), [whole, whole_f, eight, eight], [], [],
        [w_in, w_out, gain, dpreact, yhat, inverse, activated, tangent, live], 0, 1.3,
    )
    mine, send = call(
        functools.partial(join_kernel, order[0]),
        [((hidden, channels), F32), ((rows, channels), BF16)], [], [], [keep, came], after=[gain_part], micros=0.3,
    )
    came = bit_swap(send, order[0])
    core_grad = []
    after = [send]
    for part in range(parts):
        one, *fold_back = back_part(part, core_grad, after)
        core_grad += [one]
        after = [one]
    fold_back = swap(fold_back[0], "fold")
    body, outs = half_step(0, rows)
    mine, send = call(body, outs, [], [], [mine, came], after=after, micros=0.3)
    came = bit_swap(send, order[1])
    taps_parts = [taps_part(part, [send]) for part in range(parts)]
    small_rows //= 2
    small, extra = call(
        pack_kernel, [((small_rows, channels), F32), ((2 * small_rows, channels), BF16)],
        [((2 * small_rows, channels), F32)], [], [gain_part, scale_part, *taps_parts], micros=0.3,
    )
    extra = core_swap(extra)
    rows //= 2
    body, outs = half_step(1, rows)
    mine, send = call(body, outs, [], [], [mine, came], after=[small], micros=0.3)
    mine, send = halved(mine, send, order[2:-1])
    came = bit_swap(send, order[-2])
    folded, first, second = call(
        bind(rims_kernel), [strip(TILE), edge, edge], [], [], [info, fold_back, *core_grad], 0, 1.0,
        after=[send],
    )
    first, second = swap(first, "first"), swap(second, "second")
    rows = came.shape[0]
    if rows % 16 == 0:
        (payload,) = call(
            functools.partial(turn_kernel, order[-2]), [((rows + small_rows, channels), BF16)],
            [], [], [mine, came, small, extra], after=[folded], micros=0.3,
        )
    else:
        bit = bit_here(order[-2])
        share = lax.dynamic_index_in_dim(mine.reshape(2, rows, channels), bit, 0, keepdims=False)
        small = small + (extra[:small_rows].astype(F32) + extra[small_rows:].astype(F32))
        payload = jnp.concatenate([share + came.astype(F32), small]).astype(BF16)
    came = bit_swap(payload, order[-1])
    grad_fields, done = call(
        bind(final_kernel), [whole, ((8, LANES), F32)], [strip(TILE)],
        [], [info, live, tangent, folded, first, second], 0, 1.5, after=[payload],
    )
    state, done_too = call(
        bind(state_kernel), [whole, ((8, LANES), F32)], [], [], [fields, scale, projected, live], 0, 1.0, after=[done],
    )
    block = lax.axis_size("near") * lax.axis_size("dp")
    copied = (block, *payload.shape)
    outer = range(block.bit_length() - 1, len(order) - 1)
    (payload,) = call(
        add_kernel, [(payload.shape if outer else copied, BF16)], [], [], [payload, came], after=[done, done_too],
        micros=0.3,
    )
    for at in reversed(outer):
        came = bit_swap(payload, order[at])
        if rows % 16 == 0:
            (payload,) = call(
                functools.partial(double_kernel, order[at], small_rows),
                [((2 * rows + small_rows, channels), BF16)], [], [], [payload, came], micros=0.3,
            )
        else:
            is_low = bit_here(order[at]) == 0
            low, high = payload[:rows], came[:rows]
            both = payload[rows:].astype(F32) + came[rows:].astype(F32)
            joined = [jnp.where(is_low, low, high), jnp.where(is_low, high, low), both.astype(BF16)]
            payload = jnp.concatenate(joined)
        rows *= 2
    if outer:
        payload = jnp.broadcast_to(payload, (block, *payload.shape))
    came = lax.all_to_all(payload, ("near", "dp"), 0, 0, tiled=True)
    (payload,) = call(
        functools.partial(gather_kernel, order[: block.bit_length() - 1], small_rows),
        [((hidden + 2 * small_rows, channels), BF16)], [], [], [came], micros=0.3,
    )
    came = core_swap(payload)
    total = samples * lax.axis_size("dp") * slots * lax.axis_size(TILES) * tile_rows * tile_cols
    norm = total ** (-0.5)
    sums = [((channels, hidden), F32), ((hidden, channels), F32)]
    w_in_sum, w_out_sum, kernel_sum, gain_sum, scale_sum = call(
        functools.partial(unpack_kernel, norm), sums + [(kernel.shape, F32), row, row], [],
        [], [payload, came], 0, 1.5,
    )
    return (
        state.reshape(grid),
        grad_fields.reshape(grid),
        kernel_sum,
        gain_sum.reshape(ln_gain.shape),
        w_in_sum,
        w_out_sum,
        scale_sum.reshape(layer_scale.shape),
    )


def solution(mesh):
    cores = Mesh(mesh.devices.reshape(-1, 4, 2, mesh.devices.shape[1]), TILES + ("dp",))
    banded = P("dp", TILES, None, None, None)
    placed = (banded, banded, P(TILES), P(TILES), P(), P(), P(), P(), P())
    return jax.shard_map(
        shards,
        mesh=cores,
        in_specs=placed,
        out_specs=(banded, banded, P(), P(), P(), P(), P()),
        check_vma=False,
    )
```

```python
import functools

import jax
import jax.numpy as jnp
from jax import lax
from jax.experimental import pallas as pl
from jax.experimental.pallas import tpu as pltpu
from jax.sharding import Mesh, PartitionSpec as P

KSIZE = 7
HALF = KSIZE // 2
TILE = 16
EPS = 1e-06
CHIPS = ("far", "near")
TILES = CHIPS + ("core",)
F32 = jnp.float32
BF16 = jnp.bfloat16
LANES = 128
LEFT = 8
GELU_C = 0.7978845608028654
GELU_A = 0.044715


def dot(lhs, rhs, lhs_dim, rhs_dim):
    return lax.dot_general(
        lhs, rhs, (((lhs_dim,), (rhs_dim,)), ((), ())), preferred_element_type=F32
    )


def chip_index():
    return lax.axis_index("far") * lax.axis_size("near") + lax.axis_index("near")


def cycle_rank():
    count = lax.axis_size(TILES)
    here = chip_index() * lax.axis_size("core") + lax.axis_index("core")
    return jnp.where(here < count // 2, here, count - 1 + count // 2 - here)


def is_even():
    return lax.rem(cycle_rank(), 2) == 0


class Fetch:
    def __init__(self, sems, *pairs):
        self.copies = [
            pltpu.make_async_copy(source, target, sems.at[at]) for at, (source, target) in enumerate(pairs)
        ]
        for copy in self.copies:
            copy.start()

    def wait(self, *which):
        for at in which:
            self.copies[at].wait()


class Shape:
    def __init__(self, slots, channels, hidden):
        self.slots = slots
        self.channels = channels
        self.hidden = hidden
        self.parts = channels // LANES
        self.columns = slots * TILE
        self.pitch = self.columns + 2 * LEFT
        self.cells = slots * TILE * TILE
        self.edge_rows = HALF * TILE
        self.early = 12

    def lanes(self, part):
        return slice(part * LANES, (part + 1) * LANES)


def edge_planes(shape, source, start, stride):
    return [
        jnp.concatenate(
            [source[part, pl.ds(start + col, TILE, stride=stride), :] for part in range(shape.parts)], axis=1
        )
        for col in range(HALF)
    ]


def send_edges(shape, left, right, first, second):
    even = is_even()
    for col in range(HALF):
        rows = pl.ds(col * TILE, TILE)
        first[rows, :] = jnp.where(even, right[col], left[col]).astype(BF16)
        second[rows, :] = jnp.where(even, left[col], right[col]).astype(BF16)


def flip_matrix(size, last):
    to = lax.broadcasted_iota(jnp.int32, (size, size), 0)
    frm = lax.broadcasted_iota(jnp.int32, (size, size), 1)
    return jnp.where(to + frm == last, 1.0, 0.0).astype(BF16)


def owned_of(info):
    return jnp.max(info[...]).astype(jnp.int32)


def prep_kernel(shape, count_hbm, fields, first, second, info, count, work, sems):
    fetch = Fetch(sems, (count_hbm, count))
    for part in range(shape.parts):
        work[part] = fields[:, shape.lanes(part)].astype(F32)
    left = edge_planes(shape, work, 0, TILE)
    fetch.wait(0)
    right = edge_planes(shape, work, (count[0] - 1) * TILE * TILE + TILE - HALF, TILE)
    send_edges(shape, left, right, first, second)
    info[...] = jnp.full(info.shape, count[0].astype(F32), F32)


def top_kernel(shape, info, ocean, fields, fold, live):
    column = lax.broadcasted_iota(jnp.int32, ocean.shape, 1)
    wet = jnp.where(ocean[...] > 0, 1.0, 0.0).astype(F32)
    for slot in range(shape.slots):
        one = jnp.sum(jnp.where(column == slot, wet, 0.0), axis=1, keepdims=True)
        one = jnp.where(info[0:1, 0:1] > slot + 0.5, one, 0.0)
        live[slot] = jnp.broadcast_to(one, live.shape[1:])
    flip = flip_matrix(shape.columns, owned_of(info) * TILE - 1)
    for k in range(HALF):
        cells = jnp.concatenate(
            [
                fields[pl.ds(slot * TILE * TILE + (TILE - 1 - k) * TILE, TILE), :].astype(F32)
                * live[slot, 0:1, :]
                for slot in range(shape.slots)
            ]
        )
        turned = dot(flip, cells.astype(BF16), 1, 0)
        fold[pl.ds(k * shape.columns, shape.columns), :] = turned.astype(BF16)


def band_kernel(shape, info, live, fields, first, second, band, rims):
    used = owned_of(info) * TILE
    even = is_even()
    blank = jnp.zeros((LEFT, LANES), F32)
    per_slot = TILE * TILE
    for part in range(shape.parts):
        band[part, pl.ds(0, HALF * shape.pitch), :] = jnp.zeros((HALF * shape.pitch, LANES), F32)
        for row in range(TILE):
            base = (row + HALF) * shape.pitch
            band[part, pl.ds(base, LEFT), :] = blank
            band[part, pl.ds(base + LEFT + shape.columns, LEFT), :] = blank
    top = HALF * shape.pitch
    for part in range(shape.parts):
        for row in range(TILE):
            base = (row + HALF) * shape.pitch
            for slot in range(shape.slots):
                cells = fields[pl.ds(slot * per_slot + row * TILE, TILE), shape.lanes(part)]
                band[part, pl.ds(base + LEFT + slot * TILE, TILE), :] = cells.astype(F32) * live[slot, 0:1, shape.lanes(part)]
        for col in range(HALF):
            rows = pl.ds(col * TILE, TILE)
            one = first[rows, shape.lanes(part)].astype(F32)
            two = second[rows, shape.lanes(part)].astype(F32)
            west = jnp.where(even, two, one)
            east = jnp.where(even, one, two)
            band[part, pl.ds(top + LEFT - HALF + col, TILE, stride=shape.pitch), :] = west
            band[part, pl.ds(top + LEFT + used + col, TILE, stride=shape.pitch), :] = east
    for k in range(HALF):
        base = (HALF + TILE - 1 - k) * shape.pitch
        east = pl.multiple_of(base + LEFT + used, LEFT)
        for part in range(shape.parts):
            ends = jnp.concatenate([band[part, pl.ds(base, LEFT), :], band[part, pl.ds(east, LEFT), :]])
            rims[pl.ds(k * 2 * LEFT, 2 * LEFT), shape.lanes(part)] = ends.astype(BF16)


def put_fold(shape, used, fold, rims, parts, padded, first_row, work):
    blank = jnp.zeros((LEFT, LANES), F32)
    for at, part in enumerate(parts):
        work[at] = rims[:, shape.lanes(part)].astype(F32)
        for k in range(HALF):
            base = (first_row + k) * shape.pitch
            padded[at, pl.ds(base, LEFT), :] = blank
            padded[at, pl.ds(base + LEFT + shape.columns, LEFT), :] = blank
            cells = fold[pl.ds(k * shape.columns, shape.columns), shape.lanes(part)]
            padded[at, pl.ds(base + LEFT, shape.columns), :] = cells.astype(F32)
            for col in range(HALF):
                west = work[at, pl.ds(k * 2 * LEFT + LEFT - 1 - col, 1), :]
                east = work[at, pl.ds(k * 2 * LEFT + LEFT + col, 1), :]
                padded[at, pl.ds(base + LEFT - 1 - col, 1), :] = east
                padded[at, pl.ds(base + LEFT + used + col, 1), :] = west


def tree_sum(terms):
    while len(terms) > 1:
        pairs = [terms[at] + terms[at + 1] for at in range(0, len(terms) - 1, 2)]
        terms = pairs + terms[len(pairs) * 2 :]
    return terms[0]


def spread_taps(shape, kernel, parts, taps):
    for above in range(KSIZE):
        rows = kernel[above].astype(F32)
        for at, part in enumerate(parts):
            for shift in range(KSIZE):
                row = rows[shift : shift + 1, shape.lanes(part)]
                taps[at, above * KSIZE + shift] = jnp.broadcast_to(row, (8, LANES))


def convolve(shape, rows, padded, taps, convolved):
    run = shape.columns // 8
    pair = 2
    origin = LEFT - HALF

    def two_rows(step, carry):
        row = step * pair
        for part in range(shape.parts):
            sums = [[None] * run for _ in range(pair)]
            for above in range(KSIZE + pair - 1):
                base = (row + above) * shape.pitch + origin
                loaded = [
                    padded[part, pl.ds(base + at, 8, stride=run), :]
                    for at in range(run + KSIZE - 1)
                ]
                for which in range(pair):
                    tap_row = above - which
                    if not 0 <= tap_row < KSIZE:
                        continue
                    for shift in range(KSIZE):
                        weight = taps[part, tap_row * KSIZE + shift]
                        for at in range(run):
                            term = weight * loaded[at + shift]
                            old = sums[which][at]
                            sums[which][at] = term if old is None else old + term
            for which in range(pair):
                for at in range(run):
                    start = (row + which) * shape.columns + at
                    convolved[part, pl.ds(start, 8, stride=run), :] = sums[which][at]
        return carry

    lax.fori_loop(0, rows // pair, two_rows, 0)


def normalise(shape, rows, first_row, convolved, gain, normed, yhat, inverse):
    def one_row(row, carry):
        for slot in range(shape.slots):
            start = pl.multiple_of(row * shape.columns + slot * TILE, TILE)
            at = slot * TILE * TILE + (first_row + row) * TILE
            out = pl.ds(pl.multiple_of(at, TILE), TILE)
            parts = [convolved[part, pl.ds(start, TILE), :] for part in range(shape.parts)]
            mean = jnp.sum(sum(parts), axis=-1, keepdims=True) * (1.0 / shape.channels)
            parts = [value - mean for value in parts]
            square = jnp.sum(sum(value * value for value in parts), axis=-1, keepdims=True)
            scale = lax.rsqrt(square * (1.0 / shape.channels) + EPS)
            inverse[out, :] = jnp.broadcast_to(scale, (TILE, LANES))
            for part in range(shape.parts):
                value = parts[part] * scale
                yhat[out, shape.lanes(part)] = value
                normed[out, shape.lanes(part)] = (value * gain[:, shape.lanes(part)]).astype(BF16)
        return carry

    lax.fori_loop(0, rows, one_row, 0, unroll=4)


def early_kernel(
    shape, live, kernel, gain, w_out, scale, tangent, band,
    normed, yhat, inverse, dproj_t, dact,
    taps, convolved, dproj,
):
    spread_taps(shape, kernel, range(shape.parts), taps)
    convolve(shape, shape.early, band, taps, convolved)
    normalise(shape, shape.early, 0, convolved, gain, normed, yhat, inverse)
    per_slot = TILE * TILE
    for slot in range(shape.slots):
        rows = pl.ds(slot * per_slot, per_slot)
        scaled = (tangent[rows, :].astype(F32) * (scale[...] * live[slot, 0:1, :])).astype(BF16)
        dproj[rows, :] = scaled
        dproj_t[:, slot * per_slot : (slot + 1) * per_slot] = scaled.T
        for h in range(shape.hidden // shape.channels):
            cols = slice(h * shape.channels, (h + 1) * shape.channels)
            dact[rows, cols] = dot(dproj[rows, :], w_out[cols, :], 1, 1)


def late_kernel(
    shape, info, kernel, gain, w_in, band, fold, rims, normed_in, yhat_in, inverse_in, dproj_t, dact,
    keep, give, activated, dpreact, yhat, inverse, padded,
    taps, convolved, normed, normed_t, work, pre,
):
    late = TILE - shape.early
    kept = late + HALF
    for part in range(shape.parts):
        rows = pl.ds(shape.early * shape.pitch, kept * shape.pitch)
        padded[part, pl.ds(0, kept * shape.pitch), :] = band[part, rows, :]
    done = shape.early * TILE
    for slot in range(shape.slots):
        rows = pl.ds(slot * TILE * TILE, done)
        normed[rows, :] = normed_in[rows, :]
        yhat[rows, :] = yhat_in[rows, :]
        inverse[rows, :] = inverse_in[rows, :]
    spread_taps(shape, kernel, range(shape.parts), taps)
    put_fold(shape, owned_of(info) * TILE, fold, rims, range(shape.parts), padded, kept, work)
    convolve(shape, late, padded, taps, convolved)
    normalise(shape, late, shape.early, convolved, gain, normed, yhat, inverse)
    per_slot = TILE * TILE
    for slot in range(shape.slots):
        normed_t[:, slot * per_slot : (slot + 1) * per_slot] = normed[pl.ds(slot * per_slot, per_slot), :].T
    keeps_in = lax.axis_index("core") == 0
    block = shape.channels
    blocks = shape.hidden // block

    def span(h):
        return slice(h * block, (h + 1) * block)

    def expand(step):
        h, slot = divmod(step, shape.slots)
        pre[step % 3] = dot(normed[pl.ds(slot * per_slot, per_slot), :], w_in[:, span(h)], 1, 0)

    def activate(step):
        h, slot = divmod(step, shape.slots)
        rows, cols = pl.ds(slot * per_slot, per_slot), span(h)
        value = pre[step % 3]
        square = value * value
        gate = 0.5 + 0.5 * jnp.tanh(value * (GELU_C + (GELU_C * GELU_A) * square))
        activated[rows, cols] = (value * gate).astype(BF16)
        slope = value * (2.0 * GELU_C + (6.0 * GELU_C * GELU_A) * square)
        grown = gate + slope * (gate - gate * gate)
        dpreact[rows, cols] = (dact[rows, cols] * grown).astype(BF16)

    def reduce_rows(h):
        of_in = dot(normed_t[...], dpreact[:, span(h)], 1, 0)
        of_out = dot(dproj_t[...], activated[:, span(h)], 1, 0)
        keep[span(h), :] = jnp.where(keeps_in, of_in, of_out)
        give[span(h), :] = jnp.where(keeps_in, of_out, of_in).astype(BF16)

    steps = blocks * shape.slots
    expand(0)
    for step in range(steps):
        if step + 1 < steps:
            expand(step + 1)
        activate(step)
        h, slot = divmod(step, shape.slots)
        if slot == 0 and h:
            reduce_rows(h - 1)
    reduce_rows(blocks - 1)


def fold_sum(value):
    return jnp.sum(value.reshape(-1, 8, value.shape[-1]), axis=0)


def norm_grad_kernel(
    shape, w_in, w_out, gain, dpreact, yhat, inverse, activated, tangent, live,
    conv_grad, projected, gain_part, scale_part,
):
    chunk = TILE * TILE
    of_gain = jnp.zeros((8, shape.channels), F32)
    of_scale = jnp.zeros((8, shape.channels), F32)
    for slot in range(shape.slots):
        rows = pl.ds(slot * chunk, chunk)
        dnormed = dot(dpreact[rows, :], w_in[...], 1, 1)
        unit = yhat[rows, :]
        of_gain += fold_sum(dnormed * unit)
        dhat = dnormed * gain[...]
        mean = jnp.sum(dhat, axis=-1, keepdims=True) * (1.0 / shape.channels)
        along = jnp.sum(dhat * unit, axis=-1, keepdims=True) * (1.0 / shape.channels)
        scale = jnp.concatenate([inverse[rows, :]] * shape.parts, axis=1)
        conv_grad[rows, :] = (scale * (dhat - mean - unit * along)).astype(BF16)
        value = dot(activated[rows, :], w_out[...], 1, 0)
        projected[rows, :] = value
        of_scale += live[slot] * fold_sum(tangent[rows, :].astype(F32) * value)
    gain_part[...] = of_gain
    scale_part[...] = of_scale


def state_kernel(shape, fields, scale, projected, live, state, done):
    done[...] = jnp.zeros_like(done)
    chunk = TILE * TILE
    for slot in range(shape.slots):
        rows = pl.ds(slot * chunk, chunk)
        kept = fields[rows, :].astype(F32) + scale[...] * projected[rows, :]
        state[rows, :] = (live[slot, 0:1, :] * kept).astype(BF16)


def place_grad(shape, conv_grad, parts, spaced):
    blank = jnp.zeros((LEFT, LANES), F32)
    for at, part in enumerate(parts):
        for row in range(TILE):
            base = row * shape.pitch
            spaced[at, pl.ds(base, LEFT), :] = blank
            spaced[at, pl.ds(base + LEFT + shape.columns, LEFT), :] = blank
            for slot in range(shape.slots):
                cells = conv_grad[pl.ds(slot * TILE * TILE + row * TILE, TILE), shape.lanes(part)]
                spaced[at, pl.ds(base + LEFT + slot * TILE, TILE), :] = cells.astype(F32)


def taps_kernel(shape, part, band, top, conv_grad, small, padded, spaced):
    place_grad(shape, conv_grad, [part], spaced)
    kept = shape.early * shape.pitch
    padded[0, pl.ds(0, kept), :] = band[part, pl.ds(0, kept), :]
    padded[0, pl.ds(kept, top.shape[1]), :] = top[part]
    run = shape.columns // 8
    origin = LEFT - HALF
    for above in range(KSIZE):

        def one_row(row, sums, above=above):
            base = (row + above) * shape.pitch + origin
            loaded = [padded[0, pl.ds(base + at, 8, stride=run), :] for at in range(run + KSIZE - 1)]
            start = row * shape.pitch + LEFT
            grads = [spaced[0, pl.ds(start + at, 8, stride=run), :] for at in range(run)]
            sums = list(sums)
            for shift in range(KSIZE):
                sums[shift] = sums[shift] + tree_sum([grads[at] * loaded[at + shift] for at in range(run)])
            return tuple(sums)

        blank = tuple(jnp.zeros((8, LANES), F32) for _ in range(KSIZE))
        sums = lax.fori_loop(0, TILE, one_row, blank, unroll=8)
        for shift in range(KSIZE):
            small[pl.ds(above * KSIZE + shift, 1), :] = jnp.sum(sums[shift], axis=0, keepdims=True)


def back_kernel(shape, part, info, kernel, conv_grad, *refs):
    before = refs[:part]
    turns = part == shape.parts - 1
    core_grad, *refs = refs[part:]
    if turns:
        fold, *refs = refs
    spaced, taps = refs
    place_grad(shape, conv_grad, [part], spaced)
    blank = jnp.zeros((LEFT, LANES), F32)
    for row in range(TILE + HALF):
        core_grad[pl.ds(row * shape.pitch, LEFT), :] = blank
        core_grad[pl.ds((row + 1) * shape.pitch - LEFT, LEFT), :] = blank
    spread_taps(shape, kernel, [part], taps)
    run = -(-(shape.columns + 2 * HALF) // 8)

    def one_row(row, tap_rows):
        sums = [None] * run
        for above in tap_rows:
            base = (row - above) * shape.pitch + LEFT
            loaded = [
                spaced[0, pl.ds(base + at - KSIZE + 1, 8, stride=run), :] for at in range(run + KSIZE - 1)
            ]
            weights = [taps[0, above * KSIZE + shift] for shift in range(KSIZE)]
            for at in range(run):
                row_sum = tree_sum([weights[shift] * loaded[at - shift + KSIZE - 1] for shift in range(KSIZE)])
                sums[at] = row_sum if sums[at] is None else sums[at] + row_sum
        start = (row - HALF) * shape.pitch + LEFT - HALF
        for at in range(run):
            core_grad[pl.ds(start + at, 8, stride=run), :] = sums[at]

    inner = (KSIZE - 1, TILE - 1)
    for row in range(HALF, TILE + 2 * HALF):
        if not inner[0] <= row <= inner[1]:
            low = max(0, row - TILE + 1)
            one_row(row, range(low, min(KSIZE - 1, row) + 1))

    def inner_row(step, carry):
        one_row(step, range(KSIZE))
        return carry

    lax.fori_loop(inner[0], inner[1] + 1, inner_row, 0)
    if turns:
        flip = flip_matrix(shape.pitch, owned_of(info) * TILE + 2 * LEFT - 1)
        for k in range(HALF):
            at = pl.ds((TILE + k) * shape.pitch, shape.pitch)
            cells = jnp.concatenate([one[at, :] for one in (*before, core_grad)], axis=1)
            turned = dot(flip, cells.astype(BF16), 1, 0)
            fold[pl.ds(k * shape.pitch, shape.pitch), :] = turned.astype(BF16)


def rims_kernel(shape, info, fold, *refs):
    core_grad = refs[: shape.parts]
    folded, first, second = refs[shape.parts :]
    used = owned_of(info) * TILE
    for part in range(shape.parts):
        folded[part] = core_grad[part][pl.ds(0, TILE * shape.pitch), :]
        for k in range(HALF):
            rows = pl.ds((TILE - 1 - k) * shape.pitch, shape.pitch)
            returned = fold[pl.ds(k * shape.pitch, shape.pitch), shape.lanes(part)]
            folded[part, rows, :] += returned.astype(F32)
    west = edge_planes(shape, folded, LEFT - HALF, shape.pitch)
    east = edge_planes(shape, folded, LEFT + used, shape.pitch)
    send_edges(shape, west, east, first, second)


def final_kernel(
    shape, info, live, tangent, folded, first, second,
    grad_fields, done,
    work,
):
    used = owned_of(info) * TILE
    even = is_even()
    done[...] = jnp.zeros_like(done)
    work[...] = folded[...]
    for part in range(shape.parts):
        for col in range(HALF):
            planes = pl.ds(col * TILE, TILE)
            one = first[planes, shape.lanes(part)].astype(F32)
            two = second[planes, shape.lanes(part)].astype(F32)
            to_tail = jnp.where(even, one, two)
            to_head = jnp.where(even, two, one)
            head = pl.ds(LEFT + col, TILE, stride=shape.pitch)
            work[part, head, :] = work[part, head, :] + to_head
            tail = pl.ds(LEFT + used - HALF + col, TILE, stride=shape.pitch)
            work[part, tail, :] = work[part, tail, :] + to_tail
        for slot in range(shape.slots):
            flag = live[slot, 0:1, shape.lanes(part)]
            for row in range(TILE):
                rows = pl.ds(slot * TILE * TILE + row * TILE, TILE)
                cells = work[part, pl.ds(row * shape.pitch + LEFT + slot * TILE, TILE), :]
                total = tangent[rows, shape.lanes(part)].astype(F32) + cells
                grad_fields[rows, shape.lanes(part)] = (flag * total).astype(BF16)


def unpack_kernel(norm, own, came, w_in, w_out, kernel_sum, gain_sum, scale_sum):
    is_first = lax.axis_index("core") == 0
    hidden, channels = w_out.shape
    for h in range(hidden // channels):
        block = slice(h * channels, (h + 1) * channels)
        mine = own[block, :].astype(F32) * norm
        theirs = came[block, :].astype(F32) * norm
        w_in[:, block] = jnp.where(is_first, mine, theirs)
        w_out[block, :] = jnp.where(is_first, theirs, mine).T
    extra = (own.shape[0] - hidden) // 2
    high, low = pl.ds(hidden, extra), pl.ds(hidden + extra, extra)
    mine = (own[high, :].astype(F32) + own[low, :].astype(F32)) * norm
    theirs = (came[high, :].astype(F32) + came[low, :].astype(F32)) * norm
    small = jnp.concatenate([jnp.where(is_first, mine, theirs), jnp.where(is_first, theirs, mine)])
    for above in range(KSIZE):
        kernel_sum[above] = small[above * KSIZE : (above + 1) * KSIZE, :]
    gain_sum[...] = small[KSIZE * KSIZE : KSIZE * KSIZE + 1, :]
    scale_sum[...] = small[KSIZE * KSIZE + 1 : KSIZE * KSIZE + 2, :]


def pairs_of(kind):
    count = lax.axis_size(TILES)
    half = count // 2
    place = [rank if rank < half else count - 1 + half - rank for rank in range(count)]
    partner = {
        "first": lambda rank: rank ^ 1,
        "second": lambda rank: ((rank + 1) ^ 1) - 1,
        "fold": lambda rank: count - 1 - rank,
    }[kind]
    return [(place[rank], place[partner(rank) % count]) for rank in range(count)]


def swap(block, kind):
    return lax.ppermute(block, TILES, pairs_of(kind))


def core_swap(block):
    return lax.ppermute(block, "core", [(0, 1), (1, 0)])


def stages():
    chip_bits = lax.axis_size(CHIPS).bit_length() - 1
    rest = list(range(2, chip_bits))
    return list(zip([0, -1, 1] + rest, [1, 0, -1] + rest))


def bit_swap(block, stage):
    chips, cores, samples = (lax.axis_size(axis) for axis in (CHIPS, "core", "dp"))
    pairs = []
    for chip in range(chips):
        for core in range(cores):
            for sample in range(samples):
                bit = stage[core]
                to = (chip, sample ^ 1) if bit < 0 else (chip ^ (1 << bit), sample)
                pairs.append(
                    ((chip * cores + core) * samples + sample, (to[0] * cores + core) * samples + to[1])
                )
    return lax.ppermute(block, TILES + ("dp",), pairs)


def bit_here(stage):
    bits = [
        lax.axis_index("dp") if bit < 0 else chip_index() >> bit & 1 for bit in stage
    ]
    return jnp.where(lax.axis_index("core") == 0, bits[0], bits[1])


def half_rows(bit, rows):
    return pl.ds(pl.multiple_of(bit * rows, rows), rows)


def join_kernel(stage, keep, came, mine, send):
    rows = send.shape[0]
    mine[...] = keep[...] + came[...].astype(F32)
    send[...] = mine[half_rows(1 - bit_here(stage), rows), :].astype(BF16)


def halve_kernel(stage, following, whole, came, mine, send):
    rows = mine.shape[0]
    mine[...] = whole[half_rows(bit_here(stage), rows), :] + came[...].astype(F32)
    send[...] = mine[half_rows(1 - bit_here(following), rows // 2), :].astype(BF16)


def pack_kernel(gain_part, scale_part, *refs):
    taps, (keep, send, work) = refs[:-3], refs[-3:]
    half = keep.shape[0]
    work[...] = jnp.zeros_like(work)
    for part, ref in enumerate(taps):
        work[pl.ds(0, ref.shape[0]), part * LANES : (part + 1) * LANES] = ref[...]
    work[pl.ds(KSIZE * KSIZE, 1), :] = jnp.sum(gain_part[...], axis=0, keepdims=True)
    work[pl.ds(KSIZE * KSIZE + 1, 1), :] = jnp.sum(scale_part[...], axis=0, keepdims=True)
    core = lax.axis_index("core")
    keep[...] = work[half_rows(core, half), :]
    value = work[half_rows(1 - core, half), :]
    high = value.astype(BF16)
    send[pl.ds(0, half), :] = high
    send[pl.ds(half, half), :] = (value - high.astype(F32)).astype(BF16)


def turn_kernel(stage, whole, came, keep, extra, payload):
    rows, half = came.shape[0], keep.shape[0]
    share = whole[half_rows(bit_here(stage), rows), :] + came[...].astype(F32)
    payload[pl.ds(0, rows), :] = share.astype(BF16)
    small = keep[...] + (extra[pl.ds(0, half), :].astype(F32) + extra[pl.ds(half, half), :].astype(F32))
    payload[pl.ds(rows, half), :] = small.astype(BF16)


def add_kernel(own, came, payload):
    total = (own[...].astype(F32) + came[...].astype(F32)).astype(BF16)
    if payload.shape == total.shape:
        payload[...] = total
    else:
        for at in range(payload.shape[0]):
            payload[at] = total


def gather_kernel(order, extra, came, payload):
    rows = came.shape[1] - extra
    samples = lax.axis_size("dp")
    is_first = lax.axis_index("core") == 0
    total = jnp.zeros((extra, came.shape[2]), F32)
    for at in range(came.shape[0]):
        near, sample = divmod(at, samples)
        places = []
        for core in range(2):
            place = 0
            for stage in order:
                place = 2 * place + (sample if stage[core] < 0 else near >> stage[core] & 1)
            places.append(place)
        place = jnp.where(is_first, places[0], places[1])
        payload[half_rows(place, rows), :] = came[at, pl.ds(0, rows), :]
        total += came[at, pl.ds(rows, extra), :].astype(F32)
    high = total.astype(BF16)
    full = rows * came.shape[0]
    payload[pl.ds(full, extra), :] = high
    payload[pl.ds(full + extra, extra), :] = (total - high.astype(F32)).astype(BF16)


def double_kernel(stage, extra, own, came, payload):
    rows = own.shape[0] - extra
    bit = bit_here(stage)
    payload[half_rows(bit, rows), :] = own[pl.ds(0, rows), :]
    payload[half_rows(1 - bit, rows), :] = came[pl.ds(0, rows), :]
    total = own[pl.ds(rows, extra), :].astype(F32) + came[pl.ds(rows, extra), :].astype(F32)
    high = total.astype(BF16)
    payload[pl.ds(2 * rows, extra), :] = high
    if payload.shape[0] > 2 * rows + extra:
        payload[pl.ds(2 * rows + extra, extra), :] = (total - high.astype(F32)).astype(BF16)


def halved(mine, send, order):
    for at, stage in enumerate(order[:-1]):
        came = bit_swap(send, stage)
        rows = came.shape[0]
        bit = bit_here(stage)
        mine = lax.dynamic_index_in_dim(mine.reshape(2, rows, -1), bit, 0, keepdims=False) + came.astype(F32)
        bit = bit_here(order[at + 1])
        halves = mine.reshape(2, rows // 2, -1)
        send = lax.dynamic_index_in_dim(halves, 1 - bit, 0, keepdims=False).astype(BF16)
    return mine, send


def call(kernel, outs, scratch, hbm, vmem, copies=0, micros=1.0, after=(), limit=20):
    in_specs = [pl.BlockSpec(memory_space=pl.ANY)] * len(hbm)
    in_specs += [pl.BlockSpec(memory_space=pltpu.VMEM)] * len(vmem)
    in_specs += [pl.BlockSpec(memory_space=pl.ANY)] * len(after)
    shapes = [pltpu.SMEM(*one) if one[1] == jnp.int32 else pltpu.VMEM(*one) for one in scratch]
    if copies:
        shapes.append(pltpu.SemaphoreType.DMA((copies,)))
    taken = len(hbm) + len(vmem)

    def body(*refs):
        kernel(*refs[:taken], *refs[taken + len(after) :])

    return pl.pallas_call(
        body,
        out_shape=[jax.ShapeDtypeStruct(*out) for out in outs],
        in_specs=in_specs,
        out_specs=[pl.BlockSpec(memory_space=pltpu.VMEM)] * len(outs),
        scratch_shapes=shapes,
        cost_estimate=pl.CostEstimate(flops=int(micros * 1e9), bytes_accessed=0, transcendentals=0),
        compiler_params=pltpu.CompilerParams(vmem_limit_bytes=limit * 1024 * 1024),
    )(*hbm, *vmem, *after)


def shards(fields, grad_out, block_count, ocean, kernel, ln_gain, w_in, w_out, layer_scale):
    samples, slots, tile_rows, tile_cols, channels = fields.shape
    hidden = w_in.shape[1]
    shape = Shape(slots, channels, hidden)
    cells, parts, pitch = shape.cells, shape.parts, shape.pitch
    grid = fields.shape
    fields = fields.reshape(cells, channels)
    tangent = grad_out.reshape(cells, channels)
    taps_in = kernel
    gain = ln_gain.reshape(1, channels)
    scale = layer_scale.reshape(1, channels)

    def bind(body):
        return functools.partial(body, shape)

    def strip(rows):
        return ((parts, rows * pitch, LANES), F32)

    edge = ((shape.edge_rows, channels), BF16)
    turned = ((HALF * pitch, channels), BF16)
    whole = ((cells, channels), BF16)
    whole_f = ((cells, channels), F32)
    wide = ((cells, hidden), BF16)
    narrow = ((cells, LANES), F32)
    row = ((1, channels), F32)
    eight = ((8, channels), F32)
    taps = ((parts, KSIZE * KSIZE, 8, LANES), F32)
    count_s = (block_count.shape, jnp.int32)
    flat = ((channels, cells), BF16)
    ends = ((HALF * 2 * LEFT, channels), BF16)
    ends_f = ((parts, HALF * 2 * LEFT, LANES), F32)
    late = TILE - shape.early

    first, second, info = call(
        bind(prep_kernel), [edge, edge, ((8, LANES), F32)],
        [count_s, ((parts, cells, LANES), F32)], [block_count], [fields], 1, 1.0,
    )
    fold, live = call(
        bind(top_kernel), [((HALF * shape.columns, channels), BF16), ((slots, 8, channels), F32)], [],
        [], [info, ocean.reshape(1, slots), fields], 0, 0.5, after=[first],
    )
    first, second = swap(first, "first"), swap(second, "second")
    band, rims = call(
        bind(band_kernel), [strip(TILE + HALF), ends], [],
        [], [info, live, fields, first, second], 0, 1.0, after=[fold],
    )
    fold, rims = swap(fold, "fold"), swap(rims, "fold")
    normed, yhat, inverse, dproj_t, dact = call(
        bind(early_kernel), [whole, whole_f, narrow, flat, ((cells, hidden), F32)],
        [taps, ((parts, shape.early * shape.columns, LANES), F32), whole],
        [], [live, taps_in, gain, w_out, scale, tangent, band], 0, 5.0,
    )
    keep, give, activated, dpreact, yhat, inverse, top = call(
        bind(late_kernel),
        [((hidden, channels), F32), ((hidden, channels), BF16), wide, wide, whole_f, narrow, strip(late + 2 * HALF)],
        [
            taps, ((parts, late * shape.columns, LANES), F32), whole, flat, ends_f,
            ((3, TILE * TILE, channels), F32),
        ],
        [],
        [info, taps_in, gain, w_in, band, fold, rims, normed, yhat, inverse, dproj_t, dact], 0, 5.0,
    )

    order = stages()
    rows = hidden // 2

    def half_step(at, rows):
        return functools.partial(halve_kernel, order[at], order[at + 1]), [
            ((rows, channels), F32), ((rows // 2, channels), BF16),
        ]

    def taps_part(part, after):
        (small,) = call(
            functools.partial(taps_kernel, shape, part), [((small_rows, LANES), F32)],
            [((1, (TILE + 2 * HALF) * pitch, LANES), F32), ((1, TILE * pitch, LANES), F32)],
            [], [band, top, conv_grad], 0, 1.8, after=after,
        )
        return small

    def back_part(part, before, after):
        outs = [(((TILE + HALF) * pitch, LANES), F32)] + [turned] * (part == parts - 1)
        return call(
            functools.partial(back_kernel, shape, part), outs,
            [((1, TILE * pitch, LANES), F32), ((1, KSIZE * KSIZE, 8, LANES), F32)],
            [], [info, taps_in, conv_grad, *before], 0, 2.0, after=after,
        )

    small_rows = -(-(KSIZE * KSIZE + 2) // 32) * 32
    came = core_swap(give)
    conv_grad, projected, gain_part, scale_part = call(
        bind(norm_grad_kernel), [whole, whole_f, eight, eight], [], [],
        [w_in, w_out, gain, dpreact, yhat, inverse, activated, tangent, live], 0, 1.3,
    )
    mine, send = call(
        functools.partial(join_kernel, order[0]),
        [((hidden, channels), F32), ((rows, channels), BF16)], [], [], [keep, came], after=[gain_part], micros=0.3,
    )
    came = bit_swap(send, order[0])
    core_grad = []
    after = [send]
    for part in range(parts):
        one, *fold_back = back_part(part, core_grad, after)
        core_grad += [one]
        after = [one]
    fold_back = swap(fold_back[0], "fold")
    body, outs = half_step(0, rows)
    mine, send = call(body, outs, [], [], [mine, came], after=after, micros=0.3)
    came = bit_swap(send, order[1])
    taps_parts = [taps_part(part, [send]) for part in range(parts)]
    small_rows //= 2
    small, extra = call(
        pack_kernel, [((small_rows, channels), F32), ((2 * small_rows, channels), BF16)],
        [((2 * small_rows, channels), F32)], [], [gain_part, scale_part, *taps_parts], micros=0.3,
    )
    extra = core_swap(extra)
    rows //= 2
    body, outs = half_step(1, rows)
    mine, send = call(body, outs, [], [], [mine, came], after=[small], micros=0.3)
    mine, send = halved(mine, send, order[2:-1])
    came = bit_swap(send, order[-2])
    folded, first, second = call(
        bind(rims_kernel), [strip(TILE), edge, edge], [], [], [info, fold_back, *core_grad], 0, 1.0,
        after=[send],
    )
    first, second = swap(first, "first"), swap(second, "second")
    rows = came.shape[0]
    if rows % 16 == 0:
        (payload,) = call(
            functools.partial(turn_kernel, order[-2]), [((rows + small_rows, channels), BF16)],
            [], [], [mine, came, small, extra], after=[folded], micros=0.3,
        )
    else:
        bit = bit_here(order[-2])
        share = lax.dynamic_index_in_dim(mine.reshape(2, rows, channels), bit, 0, keepdims=False)
        small = small + (extra[:small_rows].astype(F32) + extra[small_rows:].astype(F32))
        payload = jnp.concatenate([share + came.astype(F32), small]).astype(BF16)
    came = bit_swap(payload, order[-1])
    grad_fields, done = call(
        bind(final_kernel), [whole, ((8, LANES), F32)], [strip(TILE)],
        [], [info, live, tangent, folded, first, second], 0, 1.5, after=[payload],
    )
    state, done_too = call(
        bind(state_kernel), [whole, ((8, LANES), F32)], [], [], [fields, scale, projected, live], 0, 1.0, after=[done],
    )
    block = lax.axis_size("near") * lax.axis_size("dp")
    copied = (block, *payload.shape)
    outer = range(block.bit_length() - 1, len(order) - 1)
    (payload,) = call(
        add_kernel, [(payload.shape if outer else copied, BF16)], [], [], [payload, came], after=[done, done_too],
        micros=0.3,
    )
    for at in reversed(outer):
        came = bit_swap(payload, order[at])
        if rows % 16 == 0:
            (payload,) = call(
                functools.partial(double_kernel, order[at], small_rows),
                [((2 * rows + small_rows, channels), BF16)], [], [], [payload, came], micros=0.3,
            )
        else:
            is_low = bit_here(order[at]) == 0
            low, high = payload[:rows], came[:rows]
            both = payload[rows:].astype(F32) + came[rows:].astype(F32)
            joined = [jnp.where(is_low, low, high), jnp.where(is_low, high, low), both.astype(BF16)]
            payload = jnp.concatenate(joined)
        rows *= 2
    if outer:
        payload = jnp.broadcast_to(payload, (block, *payload.shape))
    came = lax.all_to_all(payload, ("near", "dp"), 0, 0, tiled=True)
    (payload,) = call(
        functools.partial(gather_kernel, order[: block.bit_length() - 1], small_rows),
        [((hidden + 2 * small_rows, channels), BF16)], [], [], [came], micros=0.3,
    )
    came = core_swap(payload)
    total = samples * lax.axis_size("dp") * slots * lax.axis_size(TILES) * tile_rows * tile_cols
    norm = total ** (-0.5)
    sums = [((channels, hidden), F32), ((hidden, channels), F32)]
    w_in_sum, w_out_sum, kernel_sum, gain_sum, scale_sum = call(
        functools.partial(unpack_kernel, norm), sums + [(kernel.shape, F32), row, row], [],
        [], [payload, came], 0, 1.5,
    )
    return (
        state.reshape(grid),
        grad_fields.reshape(grid),
        kernel_sum,
        gain_sum.reshape(ln_gain.shape),
        w_in_sum,
        w_out_sum,
        scale_sum.reshape(layer_scale.shape),
    )


def solution(mesh):
    cores = Mesh(mesh.devices.reshape(-1, 4, 2, mesh.devices.shape[1]), TILES + ("dp",))
    banded = P("dp", TILES, None, None, None)
    placed = (banded, banded, P(TILES), P(TILES), P(), P(), P(), P(), P())
    return jax.shard_map(
        shards,
        mesh=cores,
        in_specs=placed,
        out_specs=(banded, banded, P(), P(), P(), P(), P()),
        check_vma=False,
    )
```

```python
import functools

import jax
import jax.numpy as jnp
from jax import lax
from jax.experimental import pallas as pl
from jax.experimental.pallas import tpu as pltpu
from jax.sharding import Mesh, PartitionSpec as P

KSIZE = 7
HALF = KSIZE // 2
TILE = 16
EPS = 1e-06
CHIPS = ("far", "near")
TILES = CHIPS + ("core",)
F32 = jnp.float32
BF16 = jnp.bfloat16
LANES = 128
LEFT = 8
GELU_C = 0.7978845608028654
GELU_A = 0.044715


def dot(lhs, rhs, lhs_dim, rhs_dim):
    return lax.dot_general(
        lhs, rhs, (((lhs_dim,), (rhs_dim,)), ((), ())), preferred_element_type=F32
    )


def chip_index():
    return lax.axis_index("far") * lax.axis_size("near") + lax.axis_index("near")


def cycle_rank():
    count = lax.axis_size(TILES)
    here = chip_index() * lax.axis_size("core") + lax.axis_index("core")
    return jnp.where(here < count // 2, here, count - 1 + count // 2 - here)


def is_even():
    return lax.rem(cycle_rank(), 2) == 0


class Fetch:
    def __init__(self, sems, *pairs):
        self.copies = [
            pltpu.make_async_copy(source, target, sems.at[at]) for at, (source, target) in enumerate(pairs)
        ]
        for copy in self.copies:
            copy.start()

    def wait(self, *which):
        for at in which:
            self.copies[at].wait()


class Shape:
    def __init__(self, slots, channels, hidden):
        self.slots = slots
        self.channels = channels
        self.hidden = hidden
        self.parts = channels // LANES
        self.columns = slots * TILE
        self.pitch = self.columns + 2 * LEFT
        self.cells = slots * TILE * TILE
        self.edge_rows = HALF * TILE
        self.early = 12

    def lanes(self, part):
        return slice(part * LANES, (part + 1) * LANES)


def edge_planes(shape, source, start, stride):
    return [
        jnp.concatenate(
            [source[part, pl.ds(start + col, TILE, stride=stride), :] for part in range(shape.parts)], axis=1
        )
        for col in range(HALF)
    ]


def send_edges(shape, left, right, first, second):
    even = is_even()
    for col in range(HALF):
        rows = pl.ds(col * TILE, TILE)
        first[rows, :] = jnp.where(even, right[col], left[col]).astype(BF16)
        second[rows, :] = jnp.where(even, left[col], right[col]).astype(BF16)


def flip_matrix(size, last):
    to = lax.broadcasted_iota(jnp.int32, (size, size), 0)
    frm = lax.broadcasted_iota(jnp.int32, (size, size), 1)
    return jnp.where(to + frm == last, 1.0, 0.0).astype(BF16)


def owned_of(info):
    return jnp.max(info[...]).astype(jnp.int32)


def prep_kernel(shape, count_hbm, fields, first, second, info, count, work, sems):
    fetch = Fetch(sems, (count_hbm, count))
    for part in range(shape.parts):
        work[part] = fields[:, shape.lanes(part)].astype(F32)
    left = edge_planes(shape, work, 0, TILE)
    fetch.wait(0)
    right = edge_planes(shape, work, (count[0] - 1) * TILE * TILE + TILE - HALF, TILE)
    send_edges(shape, left, right, first, second)
    info[...] = jnp.full(info.shape, count[0].astype(F32), F32)


def top_kernel(shape, info, ocean, fields, fold, live):
    column = lax.broadcasted_iota(jnp.int32, ocean.shape, 1)
    wet = jnp.where(ocean[...] > 0, 1.0, 0.0).astype(F32)
    for slot in range(shape.slots):
        one = jnp.sum(jnp.where(column == slot, wet, 0.0), axis=1, keepdims=True)
        one = jnp.where(info[0:1, 0:1] > slot + 0.5, one, 0.0)
        live[slot] = jnp.broadcast_to(one, live.shape[1:])
    flip = flip_matrix(shape.columns, owned_of(info) * TILE - 1)
    for k in range(HALF):
        cells = jnp.concatenate(
            [
                fields[pl.ds(slot * TILE * TILE + (TILE - 1 - k) * TILE, TILE), :].astype(F32)
                * live[slot, 0:1, :]
                for slot in range(shape.slots)
            ]
        )
        turned = dot(flip, cells.astype(BF16), 1, 0)
        fold[pl.ds(k * shape.columns, shape.columns), :] = turned.astype(BF16)


def band_kernel(shape, info, live, fields, first, second, band, rims):
    used = owned_of(info) * TILE
    even = is_even()
    blank = jnp.zeros((LEFT, LANES), F32)
    per_slot = TILE * TILE
    for part in range(shape.parts):
        band[part, pl.ds(0, HALF * shape.pitch), :] = jnp.zeros((HALF * shape.pitch, LANES), F32)
        for row in range(TILE):
            base = (row + HALF) * shape.pitch
            band[part, pl.ds(base, LEFT), :] = blank
            band[part, pl.ds(base + LEFT + shape.columns, LEFT), :] = blank
    top = HALF * shape.pitch
    for part in range(shape.parts):
        for row in range(TILE):
            base = (row + HALF) * shape.pitch
            for slot in range(shape.slots):
                cells = fields[pl.ds(slot * per_slot + row * TILE, TILE), shape.lanes(part)]
                band[part, pl.ds(base + LEFT + slot * TILE, TILE), :] = cells.astype(F32) * live[slot, 0:1, shape.lanes(part)]
        for col in range(HALF):
            rows = pl.ds(col * TILE, TILE)
            one = first[rows, shape.lanes(part)].astype(F32)
            two = second[rows, shape.lanes(part)].astype(F32)
            west = jnp.where(even, two, one)
            east = jnp.where(even, one, two)
            band[part, pl.ds(top + LEFT - HALF + col, TILE, stride=shape.pitch), :] = west
            band[part, pl.ds(top + LEFT + used + col, TILE, stride=shape.pitch), :] = east
    for k in range(HALF):
        base = (HALF + TILE - 1 - k) * shape.pitch
        east = pl.multiple_of(base + LEFT + used, LEFT)
        for part in range(shape.parts):
            ends = jnp.concatenate([band[part, pl.ds(base, LEFT), :], band[part, pl.ds(east, LEFT), :]])
            rims[pl.ds(k * 2 * LEFT, 2 * LEFT), shape.lanes(part)] = ends.astype(BF16)


def put_fold(shape, used, fold, rims, parts, padded, first_row, work):
    blank = jnp.zeros((LEFT, LANES), F32)
    for at, part in enumerate(parts):
        work[at] = rims[:, shape.lanes(part)].astype(F32)
        for k in range(HALF):
            base = (first_row + k) * shape.pitch
            padded[at, pl.ds(base, LEFT), :] = blank
            padded[at, pl.ds(base + LEFT + shape.columns, LEFT), :] = blank
            cells = fold[pl.ds(k * shape.columns, shape.columns), shape.lanes(part)]
            padded[at, pl.ds(base + LEFT, shape.columns), :] = cells.astype(F32)
            for col in range(HALF):
                west = work[at, pl.ds(k * 2 * LEFT + LEFT - 1 - col, 1), :]
                east = work[at, pl.ds(k * 2 * LEFT + LEFT + col, 1), :]
                padded[at, pl.ds(base + LEFT - 1 - col, 1), :] = east
                padded[at, pl.ds(base + LEFT + used + col, 1), :] = west


def tree_sum(terms):
    while len(terms) > 1:
        pairs = [terms[at] + terms[at + 1] for at in range(0, len(terms) - 1, 2)]
        terms = pairs + terms[len(pairs) * 2 :]
    return terms[0]


def spread_taps(shape, kernel, parts, taps):
    for above in range(KSIZE):
        rows = kernel[above].astype(F32)
        for at, part in enumerate(parts):
            for shift in range(KSIZE):
                row = rows[shift : shift + 1, shape.lanes(part)]
                taps[at, above * KSIZE + shift] = jnp.broadcast_to(row, (8, LANES))


def convolve(shape, rows, padded, taps, convolved):
    run = shape.columns // 8
    pair = 2
    origin = LEFT - HALF

    def two_rows(step, carry):
        row = step * pair
        for part in range(shape.parts):
            sums = [[None] * run for _ in range(pair)]
            for above in range(KSIZE + pair - 1):
                base = (row + above) * shape.pitch + origin
                loaded = [
                    padded[part, pl.ds(base + at, 8, stride=run), :]
                    for at in range(run + KSIZE - 1)
                ]
                for which in range(pair):
                    tap_row = above - which
                    if not 0 <= tap_row < KSIZE:
                        continue
                    for shift in range(KSIZE):
                        weight = taps[part, tap_row * KSIZE + shift]
                        for at in range(run):
                            term = weight * loaded[at + shift]
                            old = sums[which][at]
                            sums[which][at] = term if old is None else old + term
            for which in range(pair):
                for at in range(run):
                    start = (row + which) * shape.columns + at
                    convolved[part, pl.ds(start, 8, stride=run), :] = sums[which][at]
        return carry

    lax.fori_loop(0, rows // pair, two_rows, 0, unroll=2)


def normalise(shape, rows, first_row, convolved, gain, normed, yhat, inverse):
    def one_row(row, carry):
        for slot in range(shape.slots):
            start = pl.multiple_of(row * shape.columns + slot * TILE, TILE)
            at = slot * TILE * TILE + (first_row + row) * TILE
            out = pl.ds(pl.multiple_of(at, TILE), TILE)
            parts = [convolved[part, pl.ds(start, TILE), :] for part in range(shape.parts)]
            mean = jnp.sum(sum(parts), axis=-1, keepdims=True) * (1.0 / shape.channels)
            parts = [value - mean for value in parts]
            square = jnp.sum(sum(value * value for value in parts), axis=-1, keepdims=True)
            scale = lax.rsqrt(square * (1.0 / shape.channels) + EPS)
            inverse[out, :] = jnp.broadcast_to(scale, (TILE, LANES))
            for part in range(shape.parts):
                value = parts[part] * scale
                yhat[out, shape.lanes(part)] = value
                normed[out, shape.lanes(part)] = (value * gain[:, shape.lanes(part)]).astype(BF16)
        return carry

    lax.fori_loop(0, rows, one_row, 0, unroll=min(rows, 6))


def early_kernel(
    shape, live, kernel, gain, w_out, scale, tangent, band,
    normed, yhat, inverse, dproj_t, dact,
    taps, convolved, dproj,
):
    spread_taps(shape, kernel, range(shape.parts), taps)
    convolve(shape, shape.early, band, taps, convolved)
    normalise(shape, shape.early, 0, convolved, gain, normed, yhat, inverse)
    per_slot = TILE * TILE
    for slot in range(shape.slots):
        rows = pl.ds(slot * per_slot, per_slot)
        scaled = (tangent[rows, :].astype(F32) * (scale[...] * live[slot, 0:1, :])).astype(BF16)
        dproj[rows, :] = scaled
        dproj_t[:, slot * per_slot : (slot + 1) * per_slot] = scaled.T
        for h in range(shape.hidden // shape.channels):
            cols = slice(h * shape.channels, (h + 1) * shape.channels)
            dact[rows, cols] = dot(dproj[rows, :], w_out[cols, :], 1, 1)


def late_kernel(
    shape, info, kernel, gain, w_in, band, fold, rims, normed_in, yhat_in, inverse_in, dproj_t, dact,
    keep, give, activated, dpreact, yhat, inverse, padded,
    taps, convolved, normed, normed_t, work, pre,
):
    late = TILE - shape.early
    kept = late + HALF
    for part in range(shape.parts):
        rows = pl.ds(shape.early * shape.pitch, kept * shape.pitch)
        padded[part, pl.ds(0, kept * shape.pitch), :] = band[part, rows, :]
    done = shape.early * TILE
    for slot in range(shape.slots):
        rows = pl.ds(slot * TILE * TILE, done)
        normed[rows, :] = normed_in[rows, :]
        yhat[rows, :] = yhat_in[rows, :]
        inverse[rows, :] = inverse_in[rows, :]
    spread_taps(shape, kernel, range(shape.parts), taps)
    put_fold(shape, owned_of(info) * TILE, fold, rims, range(shape.parts), padded, kept, work)
    convolve(shape, late, padded, taps, convolved)
    normalise(shape, late, shape.early, convolved, gain, normed, yhat, inverse)
    per_slot = TILE * TILE
    for slot in range(shape.slots):
        normed_t[:, slot * per_slot : (slot + 1) * per_slot] = normed[pl.ds(slot * per_slot, per_slot), :].T
    keeps_in = lax.axis_index("core") == 0
    block = shape.channels
    blocks = shape.hidden // block

    def span(h):
        return slice(h * block, (h + 1) * block)

    def expand(step):
        h, slot = divmod(step, shape.slots)
        pre[step % 3] = dot(normed[pl.ds(slot * per_slot, per_slot), :], w_in[:, span(h)], 1, 0)

    def activate(step):
        h, slot = divmod(step, shape.slots)
        rows, cols = pl.ds(slot * per_slot, per_slot), span(h)
        value = pre[step % 3]
        square = value * value
        gate = 0.5 + 0.5 * jnp.tanh(value * (GELU_C + (GELU_C * GELU_A) * square))
        activated[rows, cols] = (value * gate).astype(BF16)
        slope = value * (2.0 * GELU_C + (6.0 * GELU_C * GELU_A) * square)
        grown = gate + slope * (gate - gate * gate)
        dpreact[rows, cols] = (dact[rows, cols] * grown).astype(BF16)

    def reduce_rows(h):
        of_in = dot(normed_t[...], dpreact[:, span(h)], 1, 0)
        of_out = dot(dproj_t[...], activated[:, span(h)], 1, 0)
        keep[span(h), :] = jnp.where(keeps_in, of_in, of_out)
        give[span(h), :] = jnp.where(keeps_in, of_out, of_in).astype(BF16)

    steps = blocks * shape.slots
    expand(0)
    for step in range(steps):
        if step + 1 < steps:
            expand(step + 1)
        activate(step)
        h, slot = divmod(step, shape.slots)
        if slot == 0 and h:
            reduce_rows(h - 1)
    reduce_rows(blocks - 1)


def fold_sum(value):
    return jnp.sum(value.reshape(-1, 8, value.shape[-1]), axis=0)


def norm_grad_kernel(
    shape, w_in, w_out, gain, dpreact, yhat, inverse, activated, tangent, live,
    conv_grad, projected, gain_part, scale_part,
):
    chunk = TILE * TILE
    of_gain = jnp.zeros((8, shape.channels), F32)
    of_scale = jnp.zeros((8, shape.channels), F32)
    for slot in range(shape.slots):
        rows = pl.ds(slot * chunk, chunk)
        dnormed = dot(dpreact[rows, :], w_in[...], 1, 1)
        unit = yhat[rows, :]
        of_gain += fold_sum(dnormed * unit)
        dhat = dnormed * gain[...]
        mean = jnp.sum(dhat, axis=-1, keepdims=True) * (1.0 / shape.channels)
        along = jnp.sum(dhat * unit, axis=-1, keepdims=True) * (1.0 / shape.channels)
        scale = jnp.concatenate([inverse[rows, :]] * shape.parts, axis=1)
        conv_grad[rows, :] = (scale * (dhat - mean - unit * along)).astype(BF16)
        value = dot(activated[rows, :], w_out[...], 1, 0)
        projected[rows, :] = value
        of_scale += live[slot] * fold_sum(tangent[rows, :].astype(F32) * value)
    gain_part[...] = of_gain
    scale_part[...] = of_scale


def state_kernel(shape, fields, scale, projected, live, state, done):
    done[...] = jnp.zeros_like(done)
    chunk = TILE * TILE
    for slot in range(shape.slots):
        rows = pl.ds(slot * chunk, chunk)
        kept = fields[rows, :].astype(F32) + scale[...] * projected[rows, :]
        state[rows, :] = (live[slot, 0:1, :] * kept).astype(BF16)


def place_grad(shape, conv_grad, parts, spaced):
    blank = jnp.zeros((LEFT, LANES), F32)
    for at, part in enumerate(parts):
        for row in range(TILE):
            base = row * shape.pitch
            spaced[at, pl.ds(base, LEFT), :] = blank
            spaced[at, pl.ds(base + LEFT + shape.columns, LEFT), :] = blank
            for slot in range(shape.slots):
                cells = conv_grad[pl.ds(slot * TILE * TILE + row * TILE, TILE), shape.lanes(part)]
                spaced[at, pl.ds(base + LEFT + slot * TILE, TILE), :] = cells.astype(F32)


def taps_kernel(shape, part, band, top, conv_grad, small, padded, spaced):
    place_grad(shape, conv_grad, [part], spaced)
    kept = shape.early * shape.pitch
    padded[0, pl.ds(0, kept), :] = band[part, pl.ds(0, kept), :]
    padded[0, pl.ds(kept, top.shape[1]), :] = top[part]
    run = shape.columns // 8
    origin = LEFT - HALF
    for above in range(KSIZE):

        def one_row(row, sums, above=above):
            base = (row + above) * shape.pitch + origin
            loaded = [padded[0, pl.ds(base + at, 8, stride=run), :] for at in range(run + KSIZE - 1)]
            start = row * shape.pitch + LEFT
            grads = [spaced[0, pl.ds(start + at, 8, stride=run), :] for at in range(run)]
            sums = list(sums)
            for shift in range(KSIZE):
                sums[shift] = sums[shift] + tree_sum([grads[at] * loaded[at + shift] for at in range(run)])
            return tuple(sums)

        blank = tuple(jnp.zeros((8, LANES), F32) for _ in range(KSIZE))
        sums = lax.fori_loop(0, TILE, one_row, blank, unroll=8)
        for shift in range(KSIZE):
            small[pl.ds(above * KSIZE + shift, 1), :] = jnp.sum(sums[shift], axis=0, keepdims=True)


def back_kernel(shape, part, info, kernel, conv_grad, *refs):
    before = refs[:part]
    turns = part == shape.parts - 1
    core_grad, *refs = refs[part:]
    if turns:
        fold, *refs = refs
    spaced, taps = refs
    place_grad(shape, conv_grad, [part], spaced)
    blank = jnp.zeros((LEFT, LANES), F32)
    for row in range(TILE + HALF):
        core_grad[pl.ds(row * shape.pitch, LEFT), :] = blank
        core_grad[pl.ds((row + 1) * shape.pitch - LEFT, LEFT), :] = blank
    spread_taps(shape, kernel, [part], taps)
    run = -(-(shape.columns + 2 * HALF) // 8)

    def one_row(row, tap_rows):
        sums = [None] * run
        for above in tap_rows:
            base = (row - above) * shape.pitch + LEFT
            loaded = [
                spaced[0, pl.ds(base + at - KSIZE + 1, 8, stride=run), :] for at in range(run + KSIZE - 1)
            ]
            weights = [taps[0, above * KSIZE + shift] for shift in range(KSIZE)]
            for at in range(run):
                row_sum = tree_sum([weights[shift] * loaded[at - shift + KSIZE - 1] for shift in range(KSIZE)])
                sums[at] = row_sum if sums[at] is None else sums[at] + row_sum
        start = (row - HALF) * shape.pitch + LEFT - HALF
        for at in range(run):
            core_grad[pl.ds(start + at, 8, stride=run), :] = sums[at]

    inner = (KSIZE - 1, TILE - 1)
    for row in range(HALF, TILE + 2 * HALF):
        if not inner[0] <= row <= inner[1]:
            low = max(0, row - TILE + 1)
            one_row(row, range(low, min(KSIZE - 1, row) + 1))

    def inner_row(step, carry):
        one_row(step, range(KSIZE))
        return carry

    lax.fori_loop(inner[0], inner[1] + 1, inner_row, 0, unroll=5)
    if turns:
        flip = flip_matrix(shape.pitch, owned_of(info) * TILE + 2 * LEFT - 1)
        for k in range(HALF):
            at = pl.ds((TILE + k) * shape.pitch, shape.pitch)
            cells = jnp.concatenate([one[at, :] for one in (*before, core_grad)], axis=1)
            turned = dot(flip, cells.astype(BF16), 1, 0)
            fold[pl.ds(k * shape.pitch, shape.pitch), :] = turned.astype(BF16)


def rims_kernel(shape, info, fold, *refs):
    core_grad = refs[: shape.parts]
    folded, first, second = refs[shape.parts :]
    used = owned_of(info) * TILE
    for part in range(shape.parts):
        folded[part] = core_grad[part][pl.ds(0, TILE * shape.pitch), :]
        for k in range(HALF):
            rows = pl.ds((TILE - 1 - k) * shape.pitch, shape.pitch)
            returned = fold[pl.ds(k * shape.pitch, shape.pitch), shape.lanes(part)]
            folded[part, rows, :] += returned.astype(F32)
    west = edge_planes(shape, folded, LEFT - HALF, shape.pitch)
    east = edge_planes(shape, folded, LEFT + used, shape.pitch)
    send_edges(shape, west, east, first, second)


def final_kernel(
    shape, info, live, tangent, folded, first, second,
    grad_fields, done,
    work,
):
    used = owned_of(info) * TILE
    even = is_even()
    done[...] = jnp.zeros_like(done)
    work[...] = folded[...]
    for part in range(shape.parts):
        for col in range(HALF):
            planes = pl.ds(col * TILE, TILE)
            one = first[planes, shape.lanes(part)].astype(F32)
            two = second[planes, shape.lanes(part)].astype(F32)
            to_tail = jnp.where(even, one, two)
            to_head = jnp.where(even, two, one)
            head = pl.ds(LEFT + col, TILE, stride=shape.pitch)
            work[part, head, :] = work[part, head, :] + to_head
            tail = pl.ds(LEFT + used - HALF + col, TILE, stride=shape.pitch)
            work[part, tail, :] = work[part, tail, :] + to_tail
        for slot in range(shape.slots):
            flag = live[slot, 0:1, shape.lanes(part)]
            for row in range(TILE):
                rows = pl.ds(slot * TILE * TILE + row * TILE, TILE)
                cells = work[part, pl.ds(row * shape.pitch + LEFT + slot * TILE, TILE), :]
                total = tangent[rows, shape.lanes(part)].astype(F32) + cells
                grad_fields[rows, shape.lanes(part)] = (flag * total).astype(BF16)


def unpack_kernel(norm, own, came, w_in, w_out, kernel_sum, gain_sum, scale_sum):
    is_first = lax.axis_index("core") == 0
    hidden, channels = w_out.shape
    for h in range(hidden // channels):
        block = slice(h * channels, (h + 1) * channels)
        mine = own[block, :].astype(F32) * norm
        theirs = came[block, :].astype(F32) * norm
        w_in[:, block] = jnp.where(is_first, mine, theirs)
        w_out[block, :] = jnp.where(is_first, theirs, mine).T
    extra = (own.shape[0] - hidden) // 2
    high, low = pl.ds(hidden, extra), pl.ds(hidden + extra, extra)
    mine = (own[high, :].astype(F32) + own[low, :].astype(F32)) * norm
    theirs = (came[high, :].astype(F32) + came[low, :].astype(F32)) * norm
    small = jnp.concatenate([jnp.where(is_first, mine, theirs), jnp.where(is_first, theirs, mine)])
    for above in range(KSIZE):
        kernel_sum[above] = small[above * KSIZE : (above + 1) * KSIZE, :]
    gain_sum[...] = small[KSIZE * KSIZE : KSIZE * KSIZE + 1, :]
    scale_sum[...] = small[KSIZE * KSIZE + 1 : KSIZE * KSIZE + 2, :]


def pairs_of(kind):
    count = lax.axis_size(TILES)
    half = count // 2
    place = [rank if rank < half else count - 1 + half - rank for rank in range(count)]
    partner = {
        "first": lambda rank: rank ^ 1,
        "second": lambda rank: ((rank + 1) ^ 1) - 1,
        "fold": lambda rank: count - 1 - rank,
    }[kind]
    return [(place[rank], place[partner(rank) % count]) for rank in range(count)]


def swap(block, kind):
    return lax.ppermute(block, TILES, pairs_of(kind))


def core_swap(block):
    return lax.ppermute(block, "core", [(0, 1), (1, 0)])


def stages():
    chip_bits = lax.axis_size(CHIPS).bit_length() - 1
    rest = list(range(2, chip_bits))
    return list(zip([0, -1, 1] + rest, [1, 0, -1] + rest))


def bit_swap(block, stage):
    chips, cores, samples = (lax.axis_size(axis) for axis in (CHIPS, "core", "dp"))
    pairs = []
    for chip in range(chips):
        for core in range(cores):
            for sample in range(samples):
                bit = stage[core]
                to = (chip, sample ^ 1) if bit < 0 else (chip ^ (1 << bit), sample)
                pairs.append(
                    ((chip * cores + core) * samples + sample, (to[0] * cores + core) * samples + to[1])
                )
    return lax.ppermute(block, TILES + ("dp",), pairs)


def bit_here(stage):
    bits = [
        lax.axis_index("dp") if bit < 0 else chip_index() >> bit & 1 for bit in stage
    ]
    return jnp.where(lax.axis_index("core") == 0, bits[0], bits[1])


def half_rows(bit, rows):
    return pl.ds(pl.multiple_of(bit * rows, rows), rows)


def join_kernel(stage, keep, came, mine, send):
    rows = send.shape[0]
    mine[...] = keep[...] + came[...].astype(F32)
    send[...] = mine[half_rows(1 - bit_here(stage), rows), :].astype(BF16)


def halve_kernel(stage, following, whole, came, mine, send):
    rows = mine.shape[0]
    mine[...] = whole[half_rows(bit_here(stage), rows), :] + came[...].astype(F32)
    send[...] = mine[half_rows(1 - bit_here(following), rows // 2), :].astype(BF16)


def pack_kernel(gain_part, scale_part, *refs):
    taps, (keep, send, work) = refs[:-3], refs[-3:]
    half = keep.shape[0]
    work[...] = jnp.zeros_like(work)
    for part, ref in enumerate(taps):
        work[pl.ds(0, ref.shape[0]), part * LANES : (part + 1) * LANES] = ref[...]
    work[pl.ds(KSIZE * KSIZE, 1), :] = jnp.sum(gain_part[...], axis=0, keepdims=True)
    work[pl.ds(KSIZE * KSIZE + 1, 1), :] = jnp.sum(scale_part[...], axis=0, keepdims=True)
    core = lax.axis_index("core")
    keep[...] = work[half_rows(core, half), :]
    value = work[half_rows(1 - core, half), :]
    high = value.astype(BF16)
    send[pl.ds(0, half), :] = high
    send[pl.ds(half, half), :] = (value - high.astype(F32)).astype(BF16)


def turn_kernel(stage, whole, came, keep, extra, payload):
    rows, half = came.shape[0], keep.shape[0]
    share = whole[half_rows(bit_here(stage), rows), :] + came[...].astype(F32)
    payload[pl.ds(0, rows), :] = share.astype(BF16)
    small = keep[...] + (extra[pl.ds(0, half), :].astype(F32) + extra[pl.ds(half, half), :].astype(F32))
    payload[pl.ds(rows, half), :] = small.astype(BF16)


def add_kernel(own, came, payload):
    total = (own[...].astype(F32) + came[...].astype(F32)).astype(BF16)
    if payload.shape == total.shape:
        payload[...] = total
    else:
        for at in range(payload.shape[0]):
            payload[at] = total


def gather_kernel(order, extra, came, payload):
    rows = came.shape[1] - extra
    samples = lax.axis_size("dp")
    is_first = lax.axis_index("core") == 0
    total = jnp.zeros((extra, came.shape[2]), F32)
    for at in range(came.shape[0]):
        near, sample = divmod(at, samples)
        places = []
        for core in range(2):
            place = 0
            for stage in order:
                place = 2 * place + (sample if stage[core] < 0 else near >> stage[core] & 1)
            places.append(place)
        place = jnp.where(is_first, places[0], places[1])
        payload[half_rows(place, rows), :] = came[at, pl.ds(0, rows), :]
        total += came[at, pl.ds(rows, extra), :].astype(F32)
    high = total.astype(BF16)
    full = rows * came.shape[0]
    payload[pl.ds(full, extra), :] = high
    payload[pl.ds(full + extra, extra), :] = (total - high.astype(F32)).astype(BF16)


def double_kernel(stage, extra, own, came, payload):
    rows = own.shape[0] - extra
    bit = bit_here(stage)
    payload[half_rows(bit, rows), :] = own[pl.ds(0, rows), :]
    payload[half_rows(1 - bit, rows), :] = came[pl.ds(0, rows), :]
    total = own[pl.ds(rows, extra), :].astype(F32) + came[pl.ds(rows, extra), :].astype(F32)
    high = total.astype(BF16)
    payload[pl.ds(2 * rows, extra), :] = high
    if payload.shape[0] > 2 * rows + extra:
        payload[pl.ds(2 * rows + extra, extra), :] = (total - high.astype(F32)).astype(BF16)


def halved(mine, send, order):
    for at, stage in enumerate(order[:-1]):
        came = bit_swap(send, stage)
        rows = came.shape[0]
        bit = bit_here(stage)
        mine = lax.dynamic_index_in_dim(mine.reshape(2, rows, -1), bit, 0, keepdims=False) + came.astype(F32)
        bit = bit_here(order[at + 1])
        halves = mine.reshape(2, rows // 2, -1)
        send = lax.dynamic_index_in_dim(halves, 1 - bit, 0, keepdims=False).astype(BF16)
    return mine, send


def call(kernel, outs, scratch, hbm, vmem, copies=0, micros=1.0, after=(), limit=20):
    in_specs = [pl.BlockSpec(memory_space=pl.ANY)] * len(hbm)
    in_specs += [pl.BlockSpec(memory_space=pltpu.VMEM)] * len(vmem)
    in_specs += [pl.BlockSpec(memory_space=pl.ANY)] * len(after)
    shapes = [pltpu.SMEM(*one) if one[1] == jnp.int32 else pltpu.VMEM(*one) for one in scratch]
    if copies:
        shapes.append(pltpu.SemaphoreType.DMA((copies,)))
    taken = len(hbm) + len(vmem)

    def body(*refs):
        kernel(*refs[:taken], *refs[taken + len(after) :])

    return pl.pallas_call(
        body,
        out_shape=[jax.ShapeDtypeStruct(*out) for out in outs],
        in_specs=in_specs,
        out_specs=[pl.BlockSpec(memory_space=pltpu.VMEM)] * len(outs),
        scratch_shapes=shapes,
        cost_estimate=pl.CostEstimate(flops=int(micros * 1e9), bytes_accessed=0, transcendentals=0),
        compiler_params=pltpu.CompilerParams(vmem_limit_bytes=limit * 1024 * 1024),
    )(*hbm, *vmem, *after)


def shards(fields, grad_out, block_count, ocean, kernel, ln_gain, w_in, w_out, layer_scale):
    samples, slots, tile_rows, tile_cols, channels = fields.shape
    hidden = w_in.shape[1]
    shape = Shape(slots, channels, hidden)
    cells, parts, pitch = shape.cells, shape.parts, shape.pitch
    grid = fields.shape
    fields = fields.reshape(cells, channels)
    tangent = grad_out.reshape(cells, channels)
    taps_in = kernel
    gain = ln_gain.reshape(1, channels)
    scale = layer_scale.reshape(1, channels)

    def bind(body):
        return functools.partial(body, shape)

    def strip(rows):
        return ((parts, rows * pitch, LANES), F32)

    edge = ((shape.edge_rows, channels), BF16)
    turned = ((HALF * pitch, channels), BF16)
    whole = ((cells, channels), BF16)
    whole_f = ((cells, channels), F32)
    wide = ((cells, hidden), BF16)
    narrow = ((cells, LANES), F32)
    row = ((1, channels), F32)
    eight = ((8, channels), F32)
    taps = ((parts, KSIZE * KSIZE, 8, LANES), F32)
    count_s = (block_count.shape, jnp.int32)
    flat = ((channels, cells), BF16)
    ends = ((HALF * 2 * LEFT, channels), BF16)
    ends_f = ((parts, HALF * 2 * LEFT, LANES), F32)
    late = TILE - shape.early

    first, second, info = call(
        bind(prep_kernel), [edge, edge, ((8, LANES), F32)],
        [count_s, ((parts, cells, LANES), F32)], [block_count], [fields], 1, 1.0,
    )
    fold, live = call(
        bind(top_kernel), [((HALF * shape.columns, channels), BF16), ((slots, 8, channels), F32)], [],
        [], [info, ocean.reshape(1, slots), fields], 0, 0.5, after=[first],
    )
    first, second = swap(first, "first"), swap(second, "second")
    band, rims = call(
        bind(band_kernel), [strip(TILE + HALF), ends], [],
        [], [info, live, fields, first, second], 0, 1.0, after=[fold],
    )
    fold, rims = swap(fold, "fold"), swap(rims, "fold")
    normed, yhat, inverse, dproj_t, dact = call(
        bind(early_kernel), [whole, whole_f, narrow, flat, ((cells, hidden), F32)],
        [taps, ((parts, shape.early * shape.columns, LANES), F32), whole],
        [], [live, taps_in, gain, w_out, scale, tangent, band], 0, 5.0,
    )
    keep, give, activated, dpreact, yhat, inverse, top = call(
        bind(late_kernel),
        [((hidden, channels), F32), ((hidden, channels), BF16), wide, wide, whole_f, narrow, strip(late + 2 * HALF)],
        [
            taps, ((parts, late * shape.columns, LANES), F32), whole, flat, ends_f,
            ((3, TILE * TILE, channels), F32),
        ],
        [],
        [info, taps_in, gain, w_in, band, fold, rims, normed, yhat, inverse, dproj_t, dact], 0, 5.0,
    )

    order = stages()
    rows = hidden // 2

    def half_step(at, rows):
        return functools.partial(halve_kernel, order[at], order[at + 1]), [
            ((rows, channels), F32), ((rows // 2, channels), BF16),
        ]

    def taps_part(part, after):
        (small,) = call(
            functools.partial(taps_kernel, shape, part), [((small_rows, LANES), F32)],
            [((1, (TILE + 2 * HALF) * pitch, LANES), F32), ((1, TILE * pitch, LANES), F32)],
            [], [band, top, conv_grad], 0, 1.8, after=after,
        )
        return small

    def back_part(part, before, after):
        outs = [(((TILE + HALF) * pitch, LANES), F32)] + [turned] * (part == parts - 1)
        return call(
            functools.partial(back_kernel, shape, part), outs,
            [((1, TILE * pitch, LANES), F32), ((1, KSIZE * KSIZE, 8, LANES), F32)],
            [], [info, taps_in, conv_grad, *before], 0, 2.0, after=after,
        )

    small_rows = -(-(KSIZE * KSIZE + 2) // 32) * 32
    came = core_swap(give)
    conv_grad, projected, gain_part, scale_part = call(
        bind(norm_grad_kernel), [whole, whole_f, eight, eight], [], [],
        [w_in, w_out, gain, dpreact, yhat, inverse, activated, tangent, live], 0, 1.3,
    )
    mine, send = call(
        functools.partial(join_kernel, order[0]),
        [((hidden, channels), F32), ((rows, channels), BF16)], [], [], [keep, came], after=[gain_part], micros=0.3,
    )
    came = bit_swap(send, order[0])
    core_grad = []
    after = [send]
    for part in range(parts):
        one, *fold_back = back_part(part, core_grad, after)
        core_grad += [one]
        after = [one]
    fold_back = swap(fold_back[0], "fold")
    body, outs = half_step(0, rows)
    mine, send = call(body, outs, [], [], [mine, came], after=after, micros=0.3)
    came = bit_swap(send, order[1])
    taps_parts = [taps_part(part, [send]) for part in range(parts)]
    small_rows //= 2
    small, extra = call(
        pack_kernel, [((small_rows, channels), F32), ((2 * small_rows, channels), BF16)],
        [((2 * small_rows, channels), F32)], [], [gain_part, scale_part, *taps_parts], micros=0.3,
    )
    extra = core_swap(extra)
    rows //= 2
    body, outs = half_step(1, rows)
    mine, send = call(body, outs, [], [], [mine, came], after=[small], micros=0.3)
    mine, send = halved(mine, send, order[2:-1])
    came = bit_swap(send, order[-2])
    folded, first, second = call(
        bind(rims_kernel), [strip(TILE), edge, edge], [], [], [info, fold_back, *core_grad], 0, 1.0,
        after=[send],
    )
    first, second = swap(first, "first"), swap(second, "second")
    rows = came.shape[0]
    if rows % 16 == 0:
        (payload,) = call(
            functools.partial(turn_kernel, order[-2]), [((rows + small_rows, channels), BF16)],
            [], [], [mine, came, small, extra], after=[folded], micros=0.3,
        )
    else:
        bit = bit_here(order[-2])
        share = lax.dynamic_index_in_dim(mine.reshape(2, rows, channels), bit, 0, keepdims=False)
        small = small + (extra[:small_rows].astype(F32) + extra[small_rows:].astype(F32))
        payload = jnp.concatenate([share + came.astype(F32), small]).astype(BF16)
    came = bit_swap(payload, order[-1])
    grad_fields, done = call(
        bind(final_kernel), [whole, ((8, LANES), F32)], [strip(TILE)],
        [], [info, live, tangent, folded, first, second], 0, 1.5, after=[payload],
    )
    state, done_too = call(
        bind(state_kernel), [whole, ((8, LANES), F32)], [], [], [fields, scale, projected, live], 0, 1.0, after=[done],
    )
    block = lax.axis_size("near") * lax.axis_size("dp")
    copied = (block, *payload.shape)
    outer = range(block.bit_length() - 1, len(order) - 1)
    (payload,) = call(
        add_kernel, [(payload.shape if outer else copied, BF16)], [], [], [payload, came], after=[done, done_too],
        micros=0.3,
    )
    for at in reversed(outer):
        came = bit_swap(payload, order[at])
        if rows % 16 == 0:
            (payload,) = call(
                functools.partial(double_kernel, order[at], small_rows),
                [((2 * rows + small_rows, channels), BF16)], [], [], [payload, came], micros=0.3,
            )
        else:
            is_low = bit_here(order[at]) == 0
            low, high = payload[:rows], came[:rows]
            both = payload[rows:].astype(F32) + came[rows:].astype(F32)
            joined = [jnp.where(is_low, low, high), jnp.where(is_low, high, low), both.astype(BF16)]
            payload = jnp.concatenate(joined)
        rows *= 2
    if outer:
        payload = jnp.broadcast_to(payload, (block, *payload.shape))
    came = lax.all_to_all(payload, ("near", "dp"), 0, 0, tiled=True)
    (payload,) = call(
        functools.partial(gather_kernel, order[: block.bit_length() - 1], small_rows),
        [((hidden + 2 * small_rows, channels), BF16)], [], [], [came], micros=0.3,
    )
    came = core_swap(payload)
    total = samples * lax.axis_size("dp") * slots * lax.axis_size(TILES) * tile_rows * tile_cols
    norm = total ** (-0.5)
    sums = [((channels, hidden), F32), ((hidden, channels), F32)]
    w_in_sum, w_out_sum, kernel_sum, gain_sum, scale_sum = call(
        functools.partial(unpack_kernel, norm), sums + [(kernel.shape, F32), row, row], [],
        [], [payload, came], 0, 1.5,
    )
    return (
        state.reshape(grid),
        grad_fields.reshape(grid),
        kernel_sum,
        gain_sum.reshape(ln_gain.shape),
        w_in_sum,
        w_out_sum,
        scale_sum.reshape(layer_scale.shape),
    )


def solution(mesh):
    cores = Mesh(mesh.devices.reshape(-1, 4, 2, mesh.devices.shape[1]), TILES + ("dp",))
    banded = P("dp", TILES, None, None, None)
    placed = (banded, banded, P(TILES), P(TILES), P(), P(), P(), P(), P())
    return jax.shard_map(
        shards,
        mesh=cores,
        in_specs=placed,
        out_specs=(banded, banded, P(), P(), P(), P(), P()),
        check_vma=False,
    )
```
